128 devices in a mesh: dp: 8 (over x_lo, z), ctx: 8 (over y, x_hi), tensor: 2 (over core).
Axes of the slice: x: 4 (x_hi: 2, x_lo: 2; x = x_hi * 2 + x_lo), y: 4, z: 4, core: 2. Of those that a mesh axis runs over, the one named last changes fastest.
Arguments:
- hidden_in: bfloat16 [8, 2048, 2048], P('dp', 'ctx', 'tensor'), may hold values from -6 to 6
- grad_out: bfloat16 [8, 2048, 2048], P('dp', 'ctx', 'tensor'), may hold values from -6 to 6
- segment_ids: int32 [8, 2048], P('dp', 'ctx'), may hold values from 0 to 2, as said below
- positions: int32 [8, 2048], P('dp', 'ctx'), may hold values from 0 to 1791, as said below
- qkv_weight: float32 [2048, 3, 2048], P(('dp', 'ctx'), None, 'tensor'), may hold values from -0.125 to 0.125
- dense_weight: float32 [2048, 2048], P(('dp', 'ctx'), 'tensor'), may hold values from -0.5 to 0.5
- fc1_weight: float32 [2048, 8192], P(('dp', 'ctx'), 'tensor'), may hold values from -0.125 to 0.125
- fc2_weight: float32 [2048, 8192], P(('dp', 'ctx'), 'tensor'), may hold values from -0.0625 to 0.0625
- vectors: float32 [2, 11, 1024], P('tensor', None, ('dp', 'ctx')), may hold values from -1.2 to 1.4
- qkv_first: float32 [2048, 3, 2048], P(('dp', 'ctx'), None, 'tensor'), may hold values from -96 to 96
- qkv_second: float32 [2048, 3, 2048], P(('dp', 'ctx'), None, 'tensor'), may hold values from 1245.184 to 4915.2
- dense_first: float32 [2048, 2048], P(('dp', 'ctx'), 'tensor'), may hold values from -20 to 20
- dense_second: float32 [2048, 2048], P(('dp', 'ctx'), 'tensor'), may hold values from 54.0672 to 212.992
- fc1_first: float32 [2048, 8192], P(('dp', 'ctx'), 'tensor'), may hold values from -24 to 24
- fc1_second: float32 [2048, 8192], P(('dp', 'ctx'), 'tensor'), may hold values from 78.6432 to 311.296
- fc2_first: float32 [2048, 8192], P(('dp', 'ctx'), 'tensor'), may hold values from -48 to 48
- fc2_second: float32 [2048, 8192], P(('dp', 'ctx'), 'tensor'), may hold values from 311.296 to 1245.184
- vector_first: float32 [2, 11, 1024], P('tensor', None, ('dp', 'ctx')), may hold values from -80 to 80
- vector_second: float32 [2, 11, 1024], P('tensor', None, ('dp', 'ctx')), may hold values from 868.352 to 3440.64
Outputs:
- hidden_out: bfloat16 [8, 2048, 2048], P('dp', 'ctx', 'tensor')
- grad_in: bfloat16 [8, 2048, 2048], P('dp', 'ctx', 'tensor')
- qkv_first_out: float32 [2048, 3, 2048], P(('dp', 'ctx'), None, 'tensor')
- qkv_second_out: float32 [2048, 3, 2048], P(('dp', 'ctx'), None, 'tensor')
- qkv_weight_out: float32 [2048, 3, 2048], P(('dp', 'ctx'), None, 'tensor')
- dense_first_out: float32 [2048, 2048], P(('dp', 'ctx'), 'tensor')
- dense_second_out: float32 [2048, 2048], P(('dp', 'ctx'), 'tensor')
- dense_weight_out: float32 [2048, 2048], P(('dp', 'ctx'), 'tensor')
- fc1_first_out: float32 [2048, 8192], P(('dp', 'ctx'), 'tensor')
- fc1_second_out: float32 [2048, 8192], P(('dp', 'ctx'), 'tensor')
- fc1_weight_out: float32 [2048, 8192], P(('dp', 'ctx'), 'tensor')
- fc2_first_out: float32 [2048, 8192], P(('dp', 'ctx'), 'tensor')
- fc2_second_out: float32 [2048, 8192], P(('dp', 'ctx'), 'tensor')
- fc2_weight_out: float32 [2048, 8192], P(('dp', 'ctx'), 'tensor')
- vector_first_out: float32 [2, 11, 1024], P('tensor', None, ('dp', 'ctx'))
- vector_second_out: float32 [2, 11, 1024], P('tensor', None, ('dp', 'ctx'))
- vector_out: float32 [2, 11, 1024], P('tensor', None, ('dp', 'ctx'))
The draws below stay inside these ranges and needn't reach their ends.
Inputs may be any that keep to these rules, and one draw needn't show every extreme that they name: `segment_ids`: non-decreasing along each sequence; tokens of one sequence with equal numbers form one document; every sequence holds exactly three documents. `positions`: each token's place counted from the first token of its document, which has 0; no document is longer than 1792 tokens.
All inputs are finite; a program needn't handle non-finite values.
Results may differ from the reference program's by a relative error of at most 0.0084.
Values may be sent and summed in bfloat16 or wider, within the bound.
A program may use at most 320 MiB of HBM per device.

```python
import math
import jax
import jax.numpy as jnp
from jax import lax

D = 2048
H = 32
HD = 64
ROT = 32
FF = 8192
SEQS_DEV = 1
STRETCH = 256
STEP = 10
VROWS = 11
SEQ_LEN = 2048
SEQS = 8
TOKENS = 16384
N_DP = 8
N_TENSOR = 2


def documents(key):
    key_span, key_first, key_second, key_pick = jax.random.split(key, 4)
    position_row = jnp.arange(SEQ_LEN, dtype=jnp.int32)
    span_len = SEQ_LEN - STRETCH
    span_start = jax.random.randint(key_span, (SEQS, 1), 1, STRETCH)
    first_cut = jax.random.randint(key_first, (SEQS, 1), SEQ_LEN // 4, SEQ_LEN // 2)
    second_cut = jax.random.randint(key_second, (SEQS, 1), SEQ_LEN // 2, 3 * SEQ_LEN // 4)
    picked = jax.random.randint(key_pick, (N_DP, 1), 0, SEQS_DEV)
    spanning = (jnp.arange(SEQS_DEV)[None, :] == picked).reshape(SEQS, 1)
    cut_one = jnp.where(spanning, span_start, first_cut)
    cut_two = jnp.where(spanning, span_start + span_len, second_cut)
    starts = (position_row[None, :] == cut_one) | (position_row[None, :] == cut_two)
    segment_num = jnp.cumsum(starts.astype(jnp.int32), axis=1).astype(jnp.int32)
    begin_at = lax.cummax(jnp.where(starts, position_row[None, :], 0).astype(jnp.int32), axis=1)
    return (segment_num, (position_row[None, :] - begin_at).astype(jnp.int32))


def draw_segment_ids(key, part):
    return documents(key)[0]


def draw_positions(key, part):
    return documents(key)[1]


def draw_vectors(key, part):
    key = jax.random.fold_in(key, 7)
    key_main, key_gain = jax.random.split(key)
    layout = (N_TENSOR, VROWS, D // N_TENSOR)
    biases = jnp.clip(0.3 * jax.random.normal(key_main, layout, dtype=jnp.float32), -1.2, 1.2)
    gains = jax.random.uniform(key_gain, layout, dtype=jnp.float32, minval=0.6, maxval=1.4)
    row_index = jnp.arange(VROWS)[None, :, None]
    return jnp.where(row_index == VROWS - 2, gains, biases)


def raised(result, rng, source, target, parts, factor):
    owner, partner = [(jnp.arange(result.shape[position]) // (result.shape[position] // parts)).reshape([-1 if axis == position else 1 for axis in range(result.ndim)]) for position in (source, target)]
    chosen = jax.random.permutation(rng, parts)[partner]
    strong = (owner == chosen) | (owner == (partner + parts // 2) % parts)
    return jnp.where(strong, factor * result, result)


def block_scale(key, extent, pieces, least, top_value):
    def one(position, parts):
        heights = jax.random.uniform(jax.random.fold_in(jax.random.fold_in(key, 6), position), (parts,), jnp.float32, least / len(pieces), top_value / len(pieces))
        return jnp.repeat(jnp.exp(heights), extent[position] // parts).reshape((-1,) + (1,) * (len(extent) - position - 1))

    level = one(*pieces[0])
    for cut in pieces[1:]:
        level = level * one(*cut)
    return level


def gaussian(stream_key, extent, spread, reach, cuts=(), kind=jnp.bfloat16):
    entries = spread * jax.random.normal(stream_key, extent, jnp.float32)
    if cuts:
        entries = entries * block_scale(stream_key, extent, cuts, -0.22, 0.18)
    return jnp.clip(entries, -reach, reach).astype(kind)


def bell_draw_with(rng, shape, spread, bound, cuts, heavy, kind=jnp.bfloat16):
    entries = spread * jax.random.normal(rng, shape, jnp.float32)
    if cuts:
        entries = entries * block_scale(rng, shape, cuts, -0.22, 0.18)
    return jnp.clip(raised(entries, jax.random.fold_in(rng, 3), *heavy), -bound, bound).astype(kind)


def setup_inputs(seed: int = 0) -> dict:
    key_list = jax.random.split(jax.random.key(seed), 20)
    return {
        "hidden_in": gaussian(key_list[0], (SEQS, SEQ_LEN, D), 1.0, 6.0, ((0, 8), (1, 8), (2, 2))),
        "grad_out": bell_draw_with(key_list[1], (SEQS, SEQ_LEN, D), 1.0, 6.0, ((0, 8), (1, 8), (2, 2)), (1, 2, 8, 2.0)),
        "segment_ids": draw_segment_ids(jax.random.fold_in(key_list[19], 71), 0),
        "positions": draw_positions(jax.random.fold_in(key_list[19], 71), 0),
        "qkv_weight": gaussian(key_list[4], (D, 3, D), D ** -0.5, 0.125, ((0, 64), (2, 2)), jnp.float32),
        "dense_weight": gaussian(key_list[5], (D, D), (D // 16) ** -0.5, 0.5, ((0, 64), (1, 2)), jnp.float32),
        "fc1_weight": gaussian(key_list[6], (D, FF), D ** -0.5, 0.125, ((0, 64), (1, 2)), jnp.float32),
        "fc2_weight": gaussian(key_list[7], (D, FF), FF ** -0.5, 0.0625, ((0, 64), (1, 2)), jnp.float32),
        "vectors": draw_vectors(jax.random.fold_in(key_list[19], 71), 0),
        "qkv_first": gaussian(key_list[9], (D, 3, D), (0.13 * TOKENS ** 0.5), 96.0, ((0, 64), (2, 2)), jnp.float32),
        "qkv_second": jnp.clip(jnp.exp(math.log(4915.2) - 1.3730492 * jax.random.uniform(key_list[10], (D, 3, D), jnp.float32) ** block_scale(key_list[10], (D, 3, D), ((0, 64), (2, 2)), -0.2, 0.2)), 1245.184, 4915.2),
        "dense_first": gaussian(key_list[11], (D, D), (0.028 * TOKENS ** 0.5), 20.0, ((0, 64), (1, 2)), jnp.float32),
        "dense_second": jnp.clip(jnp.exp(math.log(212.992) - 1.3710269 * jax.random.uniform(key_list[12], (D, D), jnp.float32) ** block_scale(key_list[12], (D, D), ((0, 64), (1, 2)), -0.2, 0.2)), 54.0672, 212.992),
        "fc1_first": gaussian(key_list[13], (D, FF), (0.033 * TOKENS ** 0.5), 24.0, ((0, 64), (1, 2)), jnp.float32),
        "fc1_second": jnp.clip(jnp.exp(math.log(311.296) - 1.375823 * jax.random.uniform(key_list[14], (D, FF), jnp.float32) ** block_scale(key_list[14], (D, FF), ((0, 64), (1, 2)), -0.2, 0.2)), 78.6432, 311.296),
        "fc2_first": gaussian(key_list[15], (D, FF), (0.066 * TOKENS ** 0.5), 48.0, ((0, 64), (1, 2)), jnp.float32),
        "fc2_second": jnp.clip(jnp.exp(math.log(1245.184) - 1.3862944 * jax.random.uniform(key_list[16], (D, FF), jnp.float32) ** block_scale(key_list[16], (D, FF), ((0, 64), (1, 2)), -0.2, 0.2)), 311.296, 1245.184),
        "vector_first": gaussian(key_list[17], (N_TENSOR, VROWS, D // N_TENSOR), (0.11 * TOKENS ** 0.5), 80.0, ((0, 2), (2, 64)), jnp.float32),
        "vector_second": jnp.clip(jnp.exp(math.log(3440.64) - 1.3768156 * jax.random.uniform(key_list[18], (N_TENSOR, VROWS, D // N_TENSOR), jnp.float32) ** block_scale(key_list[18], (N_TENSOR, VROWS, D // N_TENSOR), ((0, 2), (2, 64)), -0.2, 0.2)), 868.352, 3440.64),
    }


@jax.custom_vjp
def low(v):
    return lax.optimization_barrier(v.astype(jnp.bfloat16)).astype(jnp.float32)

@jax.custom_vjp
def low_back(v):
    return v

def low_keep(v):
    return (low(v), None)

def low_pass(kept, grad):
    return (grad,)

def back_keep(v):
    return (v, None)

def back_low(kept, grad):
    return (low(grad),)
low.defvjp(low_keep, low_pass)
low_back.defvjp(back_keep, back_low)
BETA_ONE = 0.9
BETA_TWO = 0.95
ADAM_EPS = 1e-08
DECAY = 0.1
NORM_EPS = 1e-05
MASKED = -1e+30

def tables(positions):
    freqs = 10000.0 ** (-jnp.arange(ROT // 2, dtype=jnp.float32) * 2.0 / ROT)
    angles = positions.astype(jnp.float32)[..., None] * freqs
    return (jnp.cos(angles)[..., None, :], jnp.sin(angles)[..., None, :])

def rotate(values_in, cosine_table, sine_table):
    half_rot = ROT // 2
    first_part = values_in[..., :half_rot]
    second_part = values_in[..., half_rot:ROT]
    return jnp.concatenate([first_part * cosine_table - second_part * sine_table, second_part * cosine_table + first_part * sine_table, values_in[..., ROT:]], axis=-1)

def attend(block):
    query_block, key_block, value_block, segment_row = block
    score_scale = HD ** (-0.5)
    scores = low_back(jnp.einsum('qhd,khd->hqk', query_block, key_block, precision=lax.Precision.HIGHEST) * score_scale)
    place_row = jnp.arange(SEQ_LEN)
    allowed_pairs = (place_row[None, :] <= place_row[:, None]) & (segment_row[None, :] == segment_row[:, None])
    masked = jnp.where(allowed_pairs[None], scores, MASKED)
    row_max = lax.optimization_barrier(jnp.max(masked, axis=-1, keepdims=True))
    exponent = jnp.exp(masked - row_max)
    probability = exponent / lax.optimization_barrier(jnp.sum(exponent, axis=-1, keepdims=True))
    return jnp.einsum('hqk,khd->qhd', low(probability), value_block, precision=lax.Precision.HIGHEST)

def forward(qkv_weight, dense_weight, fc1_weight, fc2_weight, vectors, hidden, segment_ids, positions):
    qkv_weight = low(qkv_weight)
    dense_weight = low(dense_weight)
    fc1_weight = low(fc1_weight)
    fc2_weight = low(fc2_weight)
    vectors = low(vectors)

    def whole_row(index):
        return vectors[:, index, :].reshape(D)
    base_row = 3 + FF // D
    fc1_bias = vectors[:, 3:base_row, :].reshape(FF)
    dense_bias = whole_row(base_row)
    fc2_bias = whole_row(base_row + 1)
    gain = whole_row(base_row + 2)
    shift = whole_row(base_row + 3)
    qkv_bias = jnp.stack([whole_row(0), whole_row(1), whole_row(2)])
    mean_row = lax.optimization_barrier(jnp.mean(hidden, axis=-1, keepdims=True))
    centred = hidden - mean_row
    variance = lax.optimization_barrier(jnp.mean(centred * centred, axis=-1, keepdims=True))
    normal = centred * lax.rsqrt(variance + NORM_EPS)
    normed = low(normal * gain + shift).reshape(TOKENS, D)
    qkv = low_back(jnp.einsum('td,dcf->tcf', normed, qkv_weight, precision=lax.Precision.HIGHEST) + qkv_bias)
    head_shape = (SEQS, SEQ_LEN, H, HD)
    cosine_table, sine_table = tables(positions)
    query_rows = low(rotate(qkv[:, 0].reshape(head_shape), cosine_table, sine_table))
    key_rows = low(rotate(qkv[:, 1].reshape(head_shape), cosine_table, sine_table))
    value_rows = low(qkv[:, 2].reshape(head_shape))
    group_size = H // 4

    def blocks(values_in):
        grouped = values_in.reshape(SEQS, SEQ_LEN, 4, group_size, HD).transpose(0, 2, 1, 3, 4)
        return grouped.reshape(SEQS * 4, SEQ_LEN, group_size, HD)
    segment_rep = jnp.repeat(segment_ids, 4, axis=0)
    attended = lax.map(jax.checkpoint(attend), (blocks(query_rows), blocks(key_rows), blocks(value_rows), segment_rep))
    attended = attended.reshape(SEQS, 4, SEQ_LEN, group_size, HD).transpose(0, 2, 1, 3, 4).reshape(TOKENS, D)
    attended = low_back(low(attended))
    attn_branch = jnp.dot(attended, dense_weight.T, precision=lax.Precision.HIGHEST) + dense_bias
    pre_act = low_back(jnp.dot(normed, fc1_weight, precision=lax.Precision.HIGHEST) + fc1_bias)
    activated = low(jax.nn.gelu(pre_act, approximate=True))
    mlp_branch = jnp.dot(activated, fc2_weight.T, precision=lax.Precision.HIGHEST) + fc2_bias
    return hidden + (attn_branch + mlp_branch).reshape(SEQS, SEQ_LEN, D)

def adam_step(weight, first, second, gradient, rate):
    first_new = BETA_ONE * first + (1.0 - BETA_ONE) * gradient
    second_new = BETA_TWO * second + (1.0 - BETA_TWO) * gradient * gradient
    fix_one = 1.0 - BETA_ONE ** STEP
    fix_two = 1.0 - BETA_TWO ** STEP
    update = first_new / fix_one / (jnp.sqrt(second_new / fix_two) + ADAM_EPS)
    return (first_new, second_new, weight - rate * (update + DECAY * weight))

def reference(hidden_in, grad_out, segment_ids, positions, qkv_weight, dense_weight, fc1_weight, fc2_weight, vectors, qkv_first, qkv_second, dense_first, dense_second, fc1_first, fc1_second, fc2_first, fc2_second, vector_first, vector_second):
    hidden = hidden_in.astype(jnp.float32)

    def run_block(w_qkv, w_dense, w_fc1, w_fc2, w_vec, x_in):
        return forward(w_qkv, w_dense, w_fc1, w_fc2, w_vec, x_in, segment_ids, positions)
    output, pull_back = jax.vjp(run_block, qkv_weight, dense_weight, fc1_weight, fc2_weight, vectors, hidden)
    gradients = pull_back(grad_out.astype(jnp.float32))
    qkv_new = adam_step(qkv_weight, qkv_first, qkv_second, gradients[0], 2.0 / math.sqrt(D))
    dense_new = adam_step(dense_weight, dense_first, dense_second, gradients[1], 2.0 / math.sqrt(D // 16))
    fc1_new = adam_step(fc1_weight, fc1_first, fc1_second, gradients[2], 2.0 / math.sqrt(D))
    fc2_new = adam_step(fc2_weight, fc2_first, fc2_second, gradients[3], 2.0 / math.sqrt(FF))
    vector_new = adam_step(vectors, vector_first, vector_second, gradients[4], 0.6)
    return (output.astype(jnp.bfloat16), gradients[5].astype(jnp.bfloat16), qkv_new[0], qkv_new[1], qkv_new[2], dense_new[0], dense_new[1], dense_new[2], fc1_new[0], fc1_new[1], fc1_new[2], fc2_new[0], fc2_new[1], fc2_new[2], vector_new[0], vector_new[1], vector_new[2])
```

```python
import functools
import math

import jax
import jax.numpy as jnp
from jax import lax
from jax.experimental import pallas as pl
from jax.experimental.pallas import tpu as pltpu
from jax.sharding import PartitionSpec as P

D = 2048
HD = 64
ROT = 32
FF = 8192
STEP = 10
SEQ = 2048
BLOCK = 256
HALF = 1024
FFS = 512
HEADS = 128
WA = FFS + 3 * HEADS
WB = FFS + HEADS
OWN = 32

BETA_ONE = 0.9
BETA_TWO = 0.95
ADAM_EPS = 1e-08
DECAY = 0.1
NORM_EPS = 1e-05
MASKED = -1e30

MESH = pl.DeviceIdType.MESH
F32 = jnp.float32
BF16 = jnp.bfloat16
OTHERS = tuple((k // 2, k % 2) for k in range(1, 8))


class Plane:
    def __init__(self, over_ctx):
        self.dp = lax.axis_index("dp")
        self.ctx = lax.axis_index("ctx")
        self.core = lax.axis_index("tensor")
        self.over_ctx = over_ctx
        if over_ctx:
            self.ring, self.pair = lax.div(self.ctx, 2), lax.rem(self.ctx, 2)
        else:
            self.ring, self.pair = lax.rem(self.dp, 4), lax.div(self.dp, 4)

    def spot(self, along, flip):
        ring = lax.rem(self.ring + along, 4) if along else self.ring
        pair = 1 - self.pair if flip else self.pair
        return ring * 2 + pair if self.over_ctx else pair * 4 + ring

    def device(self, along, flip):
        spot = self.spot(along, flip)
        return (self.dp, spot, self.core) if self.over_ctx else (spot, self.ctx, self.core)


def rows_at(index, size=BLOCK):
    return pl.ds(pl.multiple_of(index * size, size), size)


def remote(src, dst, sends, recvs, number, device):
    return pltpu.make_async_remote_copy(
        src_ref=src,
        dst_ref=dst,
        send_sem=sends.at[number],
        recv_sem=recvs.at[number],
        device_id=device,
        device_id_type=MESH,
    )


def greet(ctx_plane, dp_plane):
    barrier = pltpu.get_barrier_semaphore()
    partners = [ctx_plane.device(*o) for o in OTHERS] + [dp_plane.device(*o) for o in OTHERS]
    partners.append((ctx_plane.dp, ctx_plane.ctx, 1 - ctx_plane.core))
    for partner in partners:
        pl.semaphore_signal(barrier, inc=1, device_id=partner, device_id_type=MESH)
    pl.semaphore_wait(barrier, len(partners))


class Gather:
    def __init__(self, plane, own, region, sends, recvs, base):
        me = plane.spot(0, 0)

        def message(number, src, spot, part, along, flip):
            dst = region(spot, part)
            return remote(
                dst if src is None else src, dst, sends, recvs, base + number, plane.device(along, flip)
            )

        self.copies = [
            message(0, own, me, None, 1, 0),
            message(1, own, me, None, 3, 0),
            message(2, own, me, None, 0, 1),
            message(3, None, plane.spot(3, 0), 0, 1, 0),
            message(4, None, plane.spot(1, 0), 1, 3, 0),
            message(5, None, plane.spot(0, 1), None, 1, 0),
            message(6, None, plane.spot(0, 1), None, 3, 0),
            message(7, None, plane.spot(3, 1), 0, 1, 0),
            message(8, None, plane.spot(1, 1), 1, 3, 0),
        ]

    def begin(self):
        for k in (2, 0, 1):
            self.copies[k].start()

    def ring(self, flip):
        first, relay = (5, 7) if flip else (0, 3)
        for k in (0, 1):
            self.copies[first + k].wait_recv()
            self.copies[relay + k].start()

    def pair(self):
        self.copies[2].wait_recv()
        self.copies[5].start()
        self.copies[6].start()

    def far(self, flip):
        for k in (7, 8) if flip else (3, 4):
            self.copies[k].wait_recv()

    def end(self):
        for copy in self.copies:
            copy.wait_send()


class GatherCores(Gather):
    def __init__(self, plane, own, region, sends, recvs, base, core_sends, core_recvs, core_base):
        super().__init__(plane, own, region, sends, recvs, base)
        partner = (plane.dp, plane.ctx, 1 - plane.core)
        self.relays = {}
        for number, (along, flip) in enumerate(((0, 0),) + OTHERS):
            dst = region(plane.spot(along, flip), None)
            src = dst if number else own
            self.relays[along, flip] = remote(
                src, dst, core_sends, core_recvs, core_base + number, partner
            )

    def begin(self):
        super().begin()
        self.relays[0, 0].start()

    def ring(self, flip):
        super().ring(flip)
        self.relays[3, flip].start()
        self.relays[1, flip].start()

    def pair(self):
        super().pair()
        self.relays[0, 1].start()

    def far(self, flip):
        super().far(flip)
        self.relays[2, flip].start()

    def end(self):
        super().end()
        for copy in self.relays.values():
            copy.wait()


def gather_kernel(
    hid, grad, wa, wb, vec, place, normed_all, grad_all, wa_all, wb_all, vec_all, place_all, stats,
    other, normed, pieces, tile, table, local, s_act, r_act, s_core, r_core, s_w, r_w, s_small, r_small,
):
    plane, data = Plane(True), Plane(False)
    ctx, dp, core = plane.ctx, plane.dp, plane.core
    greet(plane, data)

    def act_region(ref):
        columns = pl.ds(pl.multiple_of(core * HALF, HALF), HALF)

        def region(spot, part):
            if part is None:
                return ref.at[rows_at(spot), columns]
            start = pl.multiple_of(spot * BLOCK + part * (BLOCK // 2), BLOCK // 2)
            return ref.at[pl.ds(start, BLOCK // 2), columns]

        return region

    def weight_region(ref):
        def region(spot, part):
            if part is None:
                return ref.at[rows_at(spot), :]
            start = pl.multiple_of(spot * BLOCK + part * (BLOCK // 2), BLOCK // 2)
            return ref.at[pl.ds(start, BLOCK // 2), :]

        return region

    def scatter_rows(ref):
        start = pl.multiple_of(dp * BLOCK + ctx * OWN, OWN)
        return ref.at[pl.ds(start, OWN), :]

    hidden_copy = remote(hid, other, s_small, r_small, 0, (dp, ctx, 1 - core))
    hidden_copy.start()
    piece_copies, tile_copies, place_copies, wa_copies, wb_copies = [], [], [], [], []
    for k, o in enumerate(OTHERS):
        to = plane.device(*o)
        spot = plane.spot(*o)
        piece_copies.append(remote(vec, pieces.at[k], s_small, r_small, 1 + k, to))
        place_copies.append(remote(place, place_all.at[ctx], s_small, r_small, 15 + k, to))
        wa_copies.append(remote(wa.at[spot], scatter_rows(wa_all), s_small, r_small, 22 + k, to))
        wb_copies.append(remote(wb.at[spot], scatter_rows(wb_all), s_small, r_small, 29 + k, to))
        columns = pl.ds(pl.multiple_of(dp * 128, 128), 128)
        tile_copies.append(
            remote(tile, table.at[:, columns], s_small, r_small, 8 + k, data.device(*o))
        )
    for copy in piece_copies:
        copy.start()
    for copy in wa_copies + wb_copies + place_copies:
        copy.start()
    locals_ = [
        pltpu.make_async_copy(wa.at[ctx], scatter_rows(wa_all), local.at[0]),
        pltpu.make_async_copy(wb.at[ctx], scatter_rows(wb_all), local.at[1]),
        pltpu.make_async_copy(place, place_all.at[ctx], local.at[2]),
        pltpu.make_async_copy(grad, act_region(grad_all)(ctx, None), local.at[3]),
        pltpu.make_async_copy(normed, act_region(normed_all)(ctx, None), local.at[4]),
    ]
    for copy in locals_[:4]:
        copy.start()

    grad_gather = GatherCores(
        plane, grad, act_region(grad_all), s_act, r_act, 0, s_core, r_core, 0
    )
    normed_gather = GatherCores(
        plane, normed, act_region(normed_all), s_act, r_act, 9, s_core, r_core, 8
    )
    grad_gather.begin()

    for copy in piece_copies:
        copy.wait_recv()
    total = vec[...].astype(F32)
    for k in range(7):
        total = total + pieces[k].astype(F32)
    tile[...] = total.astype(BF16)
    table[:, pl.ds(pl.multiple_of(dp * 128, 128), 128)] = total.astype(BF16)
    for copy in tile_copies:
        copy.start()

    a_region, b_region = weight_region(wa_all), weight_region(wb_all)
    wa_gather = Gather(data, a_region(dp, None), a_region, s_w, r_w, 0)
    wb_gather = Gather(data, b_region(dp, None), b_region, s_w, r_w, 9)
    for copy in wa_copies:
        copy.wait_recv()
    locals_[0].wait()
    wa_gather.begin()
    for copy in wb_copies:
        copy.wait_recv()
    locals_[1].wait()
    wb_gather.begin()

    for copy in tile_copies:
        copy.wait_recv()
    hidden_copy.wait_recv()
    rows = table[...].astype(F32)
    vec_all[...] = rows
    gain, shift = rows[9:10], rows[10:11]
    lanes = lax.broadcasted_iota(jnp.int32, (16, 128), 1)

    def norm(i, carry):
        at = pl.ds(pl.multiple_of(i * 16, 16), 16)
        a, b = hid[at, :].astype(F32), other[at, :].astype(F32)
        mean = (jnp.sum(a, axis=1, keepdims=True) + jnp.sum(b, axis=1, keepdims=True)) / D
        a, b = a - mean, b - mean
        square = jnp.sum(a * a, axis=1, keepdims=True) + jnp.sum(b * b, axis=1, keepdims=True)
        inverse = lax.rsqrt(square / D + NORM_EPS)
        normed[at, :] = (a * inverse * gain + shift).astype(BF16)
        stats[at, :] = jnp.where(lanes < 64, mean, inverse)
        return carry

    lax.fori_loop(0, BLOCK // 16, norm, 0)
    normed_gather.begin()
    locals_[4].start()

    grad_gather.ring(0)
    wa_gather.ring(0)
    grad_gather.pair()
    normed_gather.pair()
    wa_gather.pair()
    wb_gather.ring(0)
    wb_gather.pair()
    normed_gather.ring(0)
    grad_gather.far(0)
    grad_gather.ring(1)
    wa_gather.ring(1)
    normed_gather.far(0)
    normed_gather.ring(1)
    wb_gather.ring(1)
    grad_gather.far(1)
    normed_gather.far(1)
    for gather in (wa_gather, wb_gather):
        gather.far(0)
        gather.far(1)
    for gather in (grad_gather, normed_gather, wa_gather, wb_gather):
        gather.end()
    hidden_copy.wait_send()
    for copy in piece_copies + tile_copies + wa_copies + wb_copies:
        copy.wait_send()
    for copy in place_copies:
        copy.wait()
    for copy in locals_[2:]:
        copy.wait()


def gather_all(hid, grad, wa, wb, vec, place):
    hbm = pl.BlockSpec(memory_space=pl.ANY)
    vmem = pl.BlockSpec(memory_space=pltpu.VMEM)
    dma = pltpu.SemaphoreType.DMA
    return pl.pallas_call(
        gather_kernel,
        out_shape=(
            jax.ShapeDtypeStruct((SEQ, D), BF16),
            jax.ShapeDtypeStruct((SEQ, D), BF16),
            jax.ShapeDtypeStruct((D, WA), BF16),
            jax.ShapeDtypeStruct((D, WB), BF16),
            jax.ShapeDtypeStruct((16, HALF), F32),
            jax.ShapeDtypeStruct((8, 8, BLOCK), jnp.int32),
            jax.ShapeDtypeStruct((BLOCK, 128), F32),
        ),
        in_specs=[vmem, hbm, hbm, hbm, vmem, hbm],
        out_specs=(hbm, hbm, hbm, hbm, vmem, hbm, vmem),
        scratch_shapes=[
            pltpu.VMEM((BLOCK, HALF), BF16),
            pltpu.VMEM((BLOCK, HALF), BF16),
            pltpu.VMEM((7, 16, 128), BF16),
            pltpu.VMEM((16, 128), BF16),
            pltpu.VMEM((16, HALF), BF16),
            dma((5,)),
            dma((18,)),
            dma((18,)),
            dma((16,)),
            dma((16,)),
            dma((18,)),
            dma((18,)),
            dma((36,)),
            dma((36,)),
        ],
        compiler_params=pltpu.CompilerParams(
            collective_id=0, has_side_effects=True, vmem_limit_bytes=32 * 1024 * 1024
        ),
        name="gather_all",
    )(hid, grad, wa, wb, vec, place)


def add_rows(dst, terms, count):
    def step(i, carry):
        at = pl.ds(pl.multiple_of(i * 16, 16), 16)
        total = terms[0][at, :].astype(F32)
        for term in terms[1:]:
            total = total + term[at, :].astype(F32)
        dst[at, :] = total.astype(dst.dtype)
        return carry

    lax.fori_loop(0, count // 16, step, 0)


class Reduce:
    def __init__(self, plane, acc, half_up, half_down, up, down, across, sends, recvs, base):
        self.plane, self.acc, self.across = plane, acc, across
        self.near = (half_up, half_down, up, down)
        half = BLOCK // 2
        self.copies = []
        for j, flip in ((0, 1), (1, 0)):
            far = plane.spot(2, flip)
            for number, (src, dst, along) in enumerate(
                (
                    (acc.at[far, pl.ds(0, half), :], half_up.at[j], 1),
                    (acc.at[far, pl.ds(half, half), :], half_down.at[j], 3),
                    (acc.at[plane.spot(1, flip)], up.at[j], 1),
                    (acc.at[plane.spot(3, flip)], down.at[j], 3),
                )
            ):
                self.copies.append(
                    remote(src, dst, sends, recvs, base + 4 * j + number, plane.device(along, 0))
                )
        self.copies.append(
            remote(acc.at[plane.spot(0, 1)], across, sends, recvs, base + 8, plane.device(0, 1))
        )

    def first(self, j):
        self.copies[4 * j].start()
        self.copies[4 * j + 1].start()

    def second(self, j):
        half = BLOCK // 2
        for number, along in ((0, 1), (1, 3)):
            self.copies[4 * j + number].wait_recv()
            dst = self.acc.at[self.plane.spot(along, 1 - j), pl.ds(number * half, half), :]
            add_rows(dst, [dst, self.near[number].at[j]], half)
            self.copies[4 * j + number + 2].start()

    def third(self):
        self.copies[2].wait_recv()
        self.copies[3].wait_recv()
        dst = self.acc.at[self.plane.spot(0, 1)]
        add_rows(dst, [dst, self.near[2].at[0], self.near[3].at[0]], BLOCK)
        self.copies[8].start()

    def last(self, dst):
        self.copies[6].wait_recv()
        self.copies[7].wait_recv()
        self.copies[8].wait_recv()
        mine = self.acc.at[self.plane.spot(0, 0)]
        add_rows(dst, [mine, self.near[2].at[1], self.near[3].at[1], self.across], BLOCK)

    def end(self):
        for copy in self.copies:
            copy.wait_send()


def reduce_kernel(
    dx_part, out_part, ga_part, gb_part, hid, stats, vec_all, vec_part,
    dx_sum, out_sum, ga_all, gb_all, vec_sum, row_sum,
    dx_acc, dx_in, out_acc, out_in, ga_acc, gb_acc,
    dx_hu, dx_hd, dx_u, dx_d, dx_x, out_hu, out_hd, out_u, out_d, out_x,
    ga_hu, ga_hd, ga_u, ga_d, ga_x, gb_hu, gb_hd, gb_u, gb_d, gb_x,
    ga_done, gb_done, vec, vec_in, vec_tile, tile_in, row_own, row_in,
    local, s_core, r_core, s_red, r_red, s_small, r_small,
):
    plane, data = Plane(True), Plane(False)
    ctx, dp, core = plane.ctx, plane.dp, plane.core
    partner = (dp, ctx, 1 - core)
    greet(plane, data)
    mine = pl.ds(pl.multiple_of(core * HALF, HALF), HALF)
    theirs = pl.ds(pl.multiple_of((1 - core) * HALF, HALF), HALF)
    order = ((2, 1), (2, 0), (1, 1), (3, 1), (1, 0), (3, 0), (0, 1), (0, 0))
    blocks = {}
    for n, (part, acc, landed) in enumerate(
        ((dx_part, dx_acc, dx_in), (out_part, out_acc, out_in))
    ):
        for k, o in enumerate(order):
            spot = plane.spot(*o)
            swap = remote(
                part.at[rows_at(spot), theirs], landed.at[spot], s_core, r_core, 8 * n + k, partner
            )
            keep = pltpu.make_async_copy(
                part.at[rows_at(spot), mine], acc.at[spot], local.at[8 * n + k]
            )
            blocks[n, o] = (swap, keep, acc, landed, spot)

    def launch(n):
        for o in order:
            blocks[n, o][0].start()
            blocks[n, o][1].start()

    def join(n, o):
        swap, keep, acc, landed, spot = blocks[n, o]
        swap.wait_recv()
        keep.wait()
        add_rows(acc.at[spot], [acc.at[spot], landed.at[spot]], BLOCK)

    launch(0)
    grads = []
    for n, (part, acc) in enumerate(((ga_part, ga_acc), (gb_part, gb_acc))):
        for k, o in enumerate(order):
            spot = data.spot(*o)
            copy = pltpu.make_async_copy(
                part.at[rows_at(spot), :], acc.at[spot], local.at[16 + 8 * n + k]
            )
            copy.start()
            grads.append(copy)
    launch(1)

    dx = Reduce(plane, dx_acc, dx_hu, dx_hd, dx_u, dx_d, dx_x, s_red, r_red, 0)
    out = Reduce(plane, out_acc, out_hu, out_hd, out_u, out_d, out_x, s_red, r_red, 9)
    ga = Reduce(data, ga_acc, ga_hu, ga_hd, ga_u, ga_d, ga_x, s_red, r_red, 18)
    gb = Reduce(data, gb_acc, gb_hu, gb_hd, gb_u, gb_d, gb_x, s_red, r_red, 27)

    join(0, (2, 1))
    dx.first(0)
    join(0, (2, 0))
    dx.first(1)
    for copy in grads:
        copy.wait()
    for red in (ga, gb):
        red.first(0)
        red.first(1)
    join(1, (2, 1))
    out.first(0)
    join(1, (2, 0))
    out.first(1)
    for o in order[2:]:
        join(0, o)
    dx.second(0)
    dx.second(1)
    for o in order[2:]:
        join(1, o)
    ga.second(0)
    ga.second(1)
    out.second(0)
    out.second(1)
    gb.second(0)
    gb.second(1)
    dx.third()
    ga.third()
    out.third()
    gb.third()

    dx.last(dx_sum)
    gain = vec_all[9:10, :]
    lanes = lax.broadcasted_iota(jnp.int32, (16, 128), 1)

    def back(i, carry):
        at = pl.ds(pl.multiple_of(i * 16, 16), 16)
        d, h, stat = dx_sum[at, :], hid[at, :].astype(F32), stats[at, :]
        normal = (h - stat[:, 0:1]) * stat[:, 64:65]
        product = d * normal
        one = jnp.sum(d * gain, axis=1, keepdims=True)
        two = jnp.sum(product * gain, axis=1, keepdims=True)
        row_own[at, :] = jnp.where(lanes < 64, one, two)
        return (carry[0] + d, carry[1] + product)

    zero = jnp.zeros((16, HALF), F32)
    shift_rows, gain_rows = lax.fori_loop(0, BLOCK // 16, back, (zero, zero))
    row_copy = remote(row_own, row_in, s_small, r_small, 0, partner)
    row_copy.start()
    number = lax.broadcasted_iota(jnp.int32, (16, HALF), 0)
    gain_grad = jnp.sum(gain_rows, axis=0, keepdims=True)
    shift_grad = jnp.sum(shift_rows, axis=0, keepdims=True)
    vec[...] = jnp.where(
        number == 9, gain_grad, jnp.where(number == 10, shift_grad, vec_part[...])
    )
    vec_copies, tile_copies, ga_copies, gb_copies = [], [], [], []
    for k, o in enumerate(OTHERS):
        columns = pl.ds(pl.multiple_of(data.spot(*o) * 128, 128), 128)
        vec_copies.append(
            remote(vec.at[:, columns], vec_in.at[k], s_small, r_small, 1 + k, data.device(*o))
        )
        to, spot = plane.device(*o), plane.spot(*o)
        tile_copies.append(remote(vec_tile, tile_in.at[k], s_small, r_small, 8 + k, to))
        rows = rows_at(spot, OWN)
        ga_copies.append(
            remote(ga_done.at[rows, :], ga_all.at[ctx], s_small, r_small, 15 + k, to)
        )
        gb_copies.append(
            remote(gb_done.at[rows, :], gb_all.at[ctx], s_small, r_small, 22 + k, to)
        )
    for copy in vec_copies:
        copy.start()

    ga.last(ga_done)
    for copy in ga_copies:
        copy.start()
    ga_keep = pltpu.make_async_copy(ga_done.at[rows_at(ctx, OWN), :], ga_all.at[ctx], local.at[32])
    ga_keep.start()

    for copy in vec_copies:
        copy.wait_recv()
    total = vec[:, pl.ds(pl.multiple_of(dp * 128, 128), 128)]
    for k in range(7):
        total = total + vec_in[k]
    vec_tile[...] = total
    for copy in tile_copies:
        copy.start()

    gb.last(gb_done)
    for copy in gb_copies:
        copy.start()
    gb_keep = pltpu.make_async_copy(gb_done.at[rows_at(ctx, OWN), :], gb_all.at[ctx], local.at[33])
    gb_keep.start()

    out.last(out_sum)
    row_copy.wait()
    row_sum[...] = row_own[...] + row_in[...]
    for copy in tile_copies:
        copy.wait_recv()
    total = vec_tile[...]
    for k in range(7):
        total = total + tile_in[k]
    vec_sum[...] = total

    for copy in ga_copies + gb_copies:
        copy.wait()
    ga_keep.wait()
    gb_keep.wait()
    for copy in vec_copies + tile_copies:
        copy.wait_send()
    for key in blocks:
        blocks[key][0].wait_send()
    for red in (dx, out, ga, gb):
        red.end()


def reduce_all(dx_part, out_part, ga_part, gb_part, hid, stats, vec_all, vec_part):
    hbm = pl.BlockSpec(memory_space=pl.ANY)
    vmem = pl.BlockSpec(memory_space=pltpu.VMEM)
    dma = pltpu.SemaphoreType.DMA

    def landing(width):
        half = pltpu.VMEM((2, BLOCK // 2, width), BF16)
        whole = pltpu.VMEM((2, BLOCK, width), BF16)
        return [half, half, whole, whole, pltpu.VMEM((BLOCK, width), BF16)]

    def eight(width):
        return pltpu.VMEM((8, BLOCK, width), BF16)

    return pl.pallas_call(
        reduce_kernel,
        out_shape=(
            jax.ShapeDtypeStruct((BLOCK, HALF), F32),
            jax.ShapeDtypeStruct((BLOCK, HALF), F32),
            jax.ShapeDtypeStruct((8, OWN, WA), BF16),
            jax.ShapeDtypeStruct((8, OWN, WB), BF16),
            jax.ShapeDtypeStruct((16, 128), F32),
            jax.ShapeDtypeStruct((BLOCK, 128), F32),
        ),
        in_specs=[hbm] * 4 + [vmem] * 4,
        out_specs=(vmem, vmem, hbm, hbm, vmem, vmem),
        scratch_shapes=[
            eight(HALF),
            eight(HALF),
            eight(HALF),
            eight(HALF),
            eight(WA),
            eight(WB),
            *landing(HALF),
            *landing(HALF),
            *landing(WA),
            *landing(WB),
            pltpu.VMEM((BLOCK, WA), BF16),
            pltpu.VMEM((BLOCK, WB), BF16),
            pltpu.VMEM((16, HALF), F32),
            pltpu.VMEM((7, 16, 128), F32),
            pltpu.VMEM((16, 128), F32),
            pltpu.VMEM((7, 16, 128), F32),
            pltpu.VMEM((BLOCK, 128), F32),
            pltpu.VMEM((BLOCK, 128), F32),
            dma((34,)),
            dma((16,)),
            dma((16,)),
            dma((36,)),
            dma((36,)),
            dma((29,)),
            dma((29,)),
        ],
        compiler_params=pltpu.CompilerParams(
            collective_id=1, has_side_effects=True, vmem_limit_bytes=56 * 1024 * 1024
        ),
        name="reduce_all",
    )(dx_part, out_part, ga_part, gb_part, hid, stats, vec_all, vec_part)


def dot_nt(left, right):
    return lax.dot_general(left, right, (((1,), (1,)), ((), ())), preferred_element_type=F32)


def dot_nn(left, right):
    return jnp.dot(left, right, preferred_element_type=F32)


def dot_tn(left, right):
    return lax.dot_general(left, right, (((0,), (0,)), ((), ())), preferred_element_type=F32)


def turn(values, cosine, sine, sign):
    lane = lax.rem(lax.broadcasted_iota(jnp.int32, values.shape, 1), HD)
    low = jnp.where(lane < ROT // 2, sine, 0.0)
    high = sine - low
    up = pltpu.roll(values, HEADS - ROT // 2, 1)
    down = pltpu.roll(values, ROT // 2, 1)
    return values * cosine + sign * (down * high - up * low)


def attention_kernel(
    qkv, d_att, cosine, sine, features, att, d_qkv,
    q_mask, k_mask, q_plain, do_plain, v_all, k_t, v_t, do_t, scores, probs, d_k, d_v,
):
    count = SEQ // BLOCK
    lane = lax.broadcasted_iota(jnp.int32, (BLOCK, HEADS), 1)
    heads = (lane < HD, lane >= HD)
    seg_lane = lax.rem(lane, HD)

    def prepare(i, carry):
        at = rows_at(i)
        c, s = cosine[at, :], sine[at, :]
        q = turn(qkv[at, 0:HEADS], c, s, 1.0).astype(BF16).astype(F32) * (HD**-0.5)
        k = turn(qkv[at, HEADS : 2 * HEADS], c, s, 1.0).astype(BF16).astype(F32)
        v = qkv[at, 2 * HEADS : 3 * HEADS].astype(BF16)
        do = d_att[at, :].astype(F32)
        feature = features[at, :]
        barred = jnp.where(seg_lane < 3, (1.0 - feature) * MASKED, 0.0)
        for h in range(2):
            q_mask[h, at, :] = jnp.where(heads[h], q, barred).astype(BF16)
            k_mask[h, at, :] = jnp.where(heads[h], k, feature).astype(BF16)
            q_plain[h, at, :] = jnp.where(heads[h], q, 0.0).astype(BF16)
            do_plain[h, at, :] = jnp.where(heads[h], do, 0.0).astype(BF16)
        v_all[at, :] = v
        k_t[:, at] = k.T.astype(BF16)
        v_t[:, at] = v.astype(F32).T.astype(BF16)
        do_t[:, at] = do.T
        d_k[at, :] = jnp.zeros((BLOCK, HEADS), F32)
        d_v[at, :] = jnp.zeros((BLOCK, HEADS), F32)
        return carry

    lax.fori_loop(0, count, prepare, 0)
    key_row = lax.broadcasted_iota(jnp.int32, (BLOCK, BLOCK), 0)
    query_col = lax.broadcasted_iota(jnp.int32, (BLOCK, BLOCK), 1)
    causal = key_row <= query_col

    def fold(values, op):
        return op(values.reshape(BLOCK // 8, 8, BLOCK), axis=0)

    for i in range(count):
        own = pl.ds(i * BLOCK, BLOCK)

        def raw(j, h):
            return dot_nt(k_mask[h, rows_at(j), :], q_mask[h, own, :])

        def score(j, carry):
            new = []
            for h in range(2):
                s = raw(j, h)
                scores[h, rows_at(j), :] = s
                new.append(jnp.maximum(carry[h], fold(s, jnp.max)))
            return tuple(new)

        low = jnp.full((8, BLOCK), MASKED, F32)
        maxima = lax.fori_loop(0, i, score, (low, low))
        tops = []
        for h in range(2):
            s = jnp.where(causal, raw(i, h), MASKED)
            scores[h, own, :] = s
            top = jnp.maximum(maxima[h], fold(s, jnp.max))
            tops.append(jnp.max(top, axis=0, keepdims=True))

        def prob(j, carry):
            sums, outs = [], []
            for h in range(2):
                p = jnp.exp(scores[h, rows_at(j), :] - tops[h])
                sums.append(carry[0][h] + fold(p, jnp.sum))
                p = p.astype(BF16)
                probs[h, rows_at(j), :] = p
                outs.append(carry[1][h] + dot_nn(v_t[pl.ds(h * HD, HD), rows_at(j)], p))
            return (tuple(sums), tuple(outs))

        zero_sum, zero_out = jnp.zeros((8, BLOCK), F32), jnp.zeros((HD, BLOCK), F32)
        sums, outs = lax.fori_loop(
            0, i + 1, prob, ((zero_sum, zero_sum), (zero_out, zero_out))
        )
        scale = [1.0 / jnp.sum(sums[h], axis=0, keepdims=True) for h in range(2)]
        outs = [outs[h] * scale[h] for h in range(2)]
        delta = [
            jnp.sum(outs[h] * do_t[pl.ds(h * HD, HD), own], axis=0, keepdims=True)
            for h in range(2)
        ]
        att[own, :] = jnp.concatenate(outs, axis=0).T.astype(BF16)

        def back(j, carry):
            at, new = rows_at(j), []
            add_k, add_v = d_k[at, :], d_v[at, :]
            for h in range(2):
                p = probs[h, at, :].astype(F32) * scale[h]
                d_p = dot_nt(v_all[at, :], do_plain[h, own, :])
                d_s = (p * (d_p - delta[h])).astype(BF16)
                add_v = add_v + dot_nn(p.astype(BF16), do_plain[h, own, :])
                add_k = add_k + dot_nn(d_s, q_plain[h, own, :])
                new.append(carry[h] + dot_nn(k_t[pl.ds(h * HD, HD), at], d_s))
            d_k[at, :] = add_k
            d_v[at, :] = add_v
            return tuple(new)

        d_q = lax.fori_loop(0, i + 1, back, (zero_out, zero_out))
        d_q = jnp.concatenate(d_q, axis=0).T * (HD**-0.5)
        d_qkv[own, 0:HEADS] = turn(d_q, cosine[own, :], sine[own, :], -1.0).astype(BF16)

    def finish(i, carry):
        at = rows_at(i)
        back_k = turn(d_k[at, :], cosine[at, :], sine[at, :], -1.0)
        d_qkv[at, HEADS : 2 * HEADS] = back_k.astype(BF16)
        d_qkv[at, 2 * HEADS : 3 * HEADS] = d_v[at, :].astype(BF16)
        return carry

    lax.fori_loop(0, count, finish, 0)


def attention(qkv, d_att, cosine, sine, features):
    vmem = pl.BlockSpec(memory_space=pltpu.VMEM)
    two = pltpu.VMEM((2, SEQ, HEADS), BF16)
    return pl.pallas_call(
        attention_kernel,
        out_shape=(
            jax.ShapeDtypeStruct((SEQ, HEADS), BF16),
            jax.ShapeDtypeStruct((SEQ, 3 * HEADS), BF16),
        ),
        in_specs=[vmem] * 5,
        out_specs=(vmem, vmem),
        scratch_shapes=[
            two,
            two,
            two,
            two,
            pltpu.VMEM((SEQ, HEADS), BF16),
            pltpu.VMEM((HEADS, SEQ), BF16),
            pltpu.VMEM((HEADS, SEQ), BF16),
            pltpu.VMEM((HEADS, SEQ), F32),
            pltpu.VMEM((2, SEQ, BLOCK), F32),
            pltpu.VMEM((2, SEQ, BLOCK), BF16),
            pltpu.VMEM((SEQ, HEADS), F32),
            pltpu.VMEM((SEQ, HEADS), F32),
        ],
        compiler_params=pltpu.CompilerParams(vmem_limit_bytes=48 * 1024 * 1024),
        name="attention",
    )(qkv, d_att, cosine, sine, features)


def adam_step(weight, first, second, gradient, rate):
    first_new = BETA_ONE * first + (1.0 - BETA_ONE) * gradient
    second_new = BETA_TWO * second + (1.0 - BETA_TWO) * gradient * gradient
    fix_one = 1.0 - BETA_ONE**STEP
    fix_two = 1.0 - BETA_TWO**STEP
    update = first_new / fix_one / (jnp.sqrt(second_new / fix_two) + ADAM_EPS)
    return (first_new, second_new, weight - rate * (update + DECAY * weight))


def tables(positions):
    freqs = 10000.0 ** (-jnp.arange(ROT // 2, dtype=F32) * 2.0 / ROT)
    angles = freqs[:, None] * positions.astype(F32)[None, :]
    lane = jnp.arange(HEADS) % HD
    spread = (lane[None, :] % (ROT // 2) == jnp.arange(ROT // 2)[:, None]) & (lane < ROT)[None, :]
    spread = spread.astype(F32)

    def wide(table):
        return lax.dot_general(
            table, spread, (((0,), (0,)), ((), ())), precision=lax.Precision.HIGHEST
        )

    return wide(jnp.cos(angles)) + (lane >= ROT).astype(F32)[None, :], wide(jnp.sin(angles))


def by_owner(weight, parts):
    return jnp.moveaxis(weight.reshape(OWN, *parts, 8, -1), -2, 0).reshape(8, OWN, -1)


def on_device(
    hidden_in,
    grad_out,
    segment_ids,
    positions,
    qkv_weight,
    dense_weight,
    fc1_weight,
    fc2_weight,
    vectors,
    qkv_first,
    qkv_second,
    dense_first,
    dense_second,
    fc1_first,
    fc1_second,
    fc2_first,
    fc2_second,
    vector_first,
    vector_second,
):
    ctx = lax.axis_index("ctx")
    hid = hidden_in.reshape(BLOCK, HALF)
    grad = grad_out.reshape(BLOCK, HALF)
    wa = jnp.concatenate(
        [by_owner(fc1_weight.astype(BF16), ()), by_owner(qkv_weight.astype(BF16), (3,))], axis=2
    )
    wb = jnp.concatenate(
        [by_owner(fc2_weight.astype(BF16), ()), by_owner(dense_weight.astype(BF16), ())], axis=2
    )
    lane = jnp.arange(128)
    vec = jnp.where(
        (lane // 16 == ctx)[None, :], jnp.tile(vectors[0].astype(BF16), (1, 8)), jnp.zeros((), BF16)
    )
    vec = jnp.pad(vec, ((0, 5), (0, 0)))
    place = jnp.pad(jnp.concatenate([segment_ids, positions], axis=0), ((0, 6), (0, 0)))

    normed, grads, wa_all, wb_all, vec_all, place_all, stats = gather_all(
        hid, grad, wa, wb, vec, place
    )

    segments = place_all[:, 0, :].reshape(SEQ)
    cosine, sine = tables(place_all[:, 1, :].reshape(SEQ))
    features = (segments[:, None] == (lane % HD)[None, :]).astype(F32)
    qkv_bias = lax.dynamic_slice(vec_all, (0, ctx * HEADS), (3, HEADS)).reshape(-1)
    fc1_bias = lax.dynamic_slice(vec_all, (3 + ctx // 2, ctx % 2 * FFS), (1, FFS)).reshape(-1)

    pre = dot_nn(normed, wa_all)
    pre_act = pre[:, :FFS] + fc1_bias
    qkv = pre[:, FFS:] + qkv_bias
    back = dot_nn(grads, wb_all)
    act_float, pull = jax.vjp(lambda inner: jax.nn.gelu(inner, approximate=True), pre_act)
    activated = act_float.astype(BF16)
    d_pre = pull(back[:, :FFS])[0].astype(BF16)
    attended, d_qkv = attention(qkv, back[:, FFS:].astype(BF16), cosine, sine, features)

    right = jnp.concatenate([activated, attended], axis=1)
    left = jnp.concatenate([d_pre, d_qkv], axis=1)
    out_part = dot_nt(right, wb_all).astype(BF16)
    dx_part = dot_nt(left, wa_all).astype(BF16)
    ga_part = dot_tn(normed, left).astype(BF16)
    gb_part = dot_tn(grads, right).astype(BF16)
    bias = jnp.sum(left.astype(F32), axis=0)
    g_sum = jnp.sum(grad.astype(F32), axis=0, keepdims=True)
    vec_part = jnp.zeros((16, HALF), F32)
    vec_part = lax.dynamic_update_slice(vec_part, bias[FFS:].reshape(3, HEADS), (0, ctx * HEADS))
    vec_part = lax.dynamic_update_slice(
        vec_part, bias[:FFS].reshape(1, FFS), (3 + ctx // 2, ctx % 2 * FFS)
    )
    vec_part = lax.dynamic_update_slice(vec_part, jnp.concatenate([g_sum, g_sum]), (7, 0))

    dx_sum, out_sum, ga_all, gb_all, vec_sum, row_sum = reduce_all(
        dx_part, out_part, ga_part, gb_part, hid, stats, vec_all, vec_part
    )

    hidden = hid.astype(F32)
    hidden_out = (hidden + out_sum + (vec_all[7] + vec_all[8])).astype(BF16)
    inverse = stats[:, 64:65]
    normal = (hidden - stats[:, 0:1]) * inverse
    scaled = dx_sum * vec_all[9]
    back_in = inverse * (scaled - row_sum[:, 0:1] / D - normal * (row_sum[:, 64:65] / D))
    grad_in = (grad.astype(F32) + back_in).astype(BF16)

    def owned(grads_in, parts, shape):
        split = grads_in.astype(F32).reshape(8, OWN, *parts, -1)
        return jnp.moveaxis(split, 0, -2).reshape(shape)

    qkv_owned = owned(ga_all[:, :, FFS:], (3,), qkv_weight.shape)
    fc1_owned = owned(ga_all[:, :, :FFS], (), fc1_weight.shape)
    fc2_owned = owned(gb_all[:, :, :FFS], (), fc2_weight.shape)
    dense_owned = owned(gb_all[:, :, FFS:], (), dense_weight.shape)
    vector_owned = lax.dynamic_slice(vec_sum, (0, ctx * 16), (11, 16))[None]
    qkv_new = adam_step(qkv_weight, qkv_first, qkv_second, qkv_owned, 2.0 / math.sqrt(D))
    dense_new = adam_step(
        dense_weight, dense_first, dense_second, dense_owned, 2.0 / math.sqrt(D // 16)
    )
    fc1_new = adam_step(fc1_weight, fc1_first, fc1_second, fc1_owned, 2.0 / math.sqrt(D))
    fc2_new = adam_step(fc2_weight, fc2_first, fc2_second, fc2_owned, 2.0 / math.sqrt(FF))
    vector_new = adam_step(vectors, vector_first, vector_second, vector_owned, 0.6)
    return (
        hidden_out.reshape(hidden_in.shape),
        grad_in.reshape(grad_out.shape),
        *qkv_new,
        *dense_new,
        *fc1_new,
        *fc2_new,
        *vector_new,
    )


def solution(mesh):
    rows = P("dp", "ctx", "tensor")
    tokens = P("dp", "ctx")
    cube = P(("dp", "ctx"), None, "tensor")
    plain = P(("dp", "ctx"), "tensor")
    packed = P("tensor", None, ("dp", "ctx"))
    return jax.shard_map(
        on_device,
        mesh=mesh,
        in_specs=(rows, rows, tokens, tokens, cube, plain, plain, plain, packed)
        + (cube,) * 2
        + (plain,) * 6
        + (packed,) * 2,
        out_specs=(rows, rows) + (cube,) * 3 + (plain,) * 9 + (packed,) * 3,
        check_vma=False,
    )
```

```python
import functools
import math

import jax
import jax.numpy as jnp
from jax import lax
from jax.experimental import pallas as pl
from jax.experimental.pallas import tpu as pltpu
from jax.sharding import PartitionSpec as P

D = 2048
HD = 64
ROT = 32
FF = 8192
STEP = 10
SEQ = 2048
BLOCK = 256
HALF = 1024
FFS = 512
HEADS = 128
WA = FFS + 3 * HEADS
WB = FFS + HEADS
OWN = 32

BETA_ONE = 0.9
BETA_TWO = 0.95
ADAM_EPS = 1e-08
DECAY = 0.1
NORM_EPS = 1e-05
MASKED = -1e30
GELU = math.sqrt(2.0 / math.pi)

MESH = pl.DeviceIdType.MESH
F32 = jnp.float32
BF16 = jnp.bfloat16
OTHERS = tuple((k // 2, k % 2) for k in range(1, 8))


class Plane:
    def __init__(self, over_ctx):
        self.dp = lax.axis_index("dp")
        self.ctx = lax.axis_index("ctx")
        self.core = lax.axis_index("tensor")
        self.over_ctx = over_ctx
        if over_ctx:
            self.ring, self.pair = lax.div(self.ctx, 2), lax.rem(self.ctx, 2)
        else:
            self.ring, self.pair = lax.rem(self.dp, 4), lax.div(self.dp, 4)

    def spot(self, along, flip):
        ring = lax.rem(self.ring + along, 4) if along else self.ring
        pair = 1 - self.pair if flip else self.pair
        return ring * 2 + pair if self.over_ctx else pair * 4 + ring

    def spot_at(self, along, flip):
        ring, pair = lax.rem(self.ring + along, 4), lax.rem(self.pair + flip, 2)
        return ring * 2 + pair if self.over_ctx else pair * 4 + ring

    def device(self, along, flip):
        spot = self.spot(along, flip)
        return (self.dp, spot, self.core) if self.over_ctx else (spot, self.ctx, self.core)


def rows_at(index, size=BLOCK):
    return pl.ds(pl.multiple_of(index * size, size), size)


def remote(src, dst, sends, recvs, number, device):
    return pltpu.make_async_remote_copy(
        src_ref=src,
        dst_ref=dst,
        send_sem=sends.at[number],
        recv_sem=recvs.at[number],
        device_id=device,
        device_id_type=MESH,
    )


def greet(ctx_plane, dp_plane):
    barrier = pltpu.get_barrier_semaphore()
    partners = [ctx_plane.device(*o) for o in OTHERS] + [dp_plane.device(*o) for o in OTHERS]
    partners.append((ctx_plane.dp, ctx_plane.ctx, 1 - ctx_plane.core))
    for partner in partners:
        pl.semaphore_signal(barrier, inc=1, device_id=partner, device_id_type=MESH)
    pl.semaphore_wait(barrier, len(partners))


class Gather:
    def __init__(self, plane, own, region, sends, recvs, base):
        me = plane.spot(0, 0)

        def message(number, src, spot, part, along, flip):
            dst = region(spot, part)
            return remote(
                dst if src is None else src, dst, sends, recvs, base + number, plane.device(along, flip)
            )

        self.copies = [
            message(0, own, me, None, 1, 0),
            message(1, own, me, None, 3, 0),
            message(2, own, me, None, 0, 1),
            message(3, None, plane.spot(3, 0), 0, 1, 0),
            message(4, None, plane.spot(1, 0), 1, 3, 0),
            message(5, None, plane.spot(0, 1), None, 1, 0),
            message(6, None, plane.spot(0, 1), None, 3, 0),
            message(7, None, plane.spot(3, 1), 0, 1, 0),
            message(8, None, plane.spot(1, 1), 1, 3, 0),
        ]

    def begin(self):
        for k in (2, 0, 1):
            self.copies[k].start()

    def ring(self, flip):
        first, relay = (5, 7) if flip else (0, 3)
        for k in (0, 1):
            self.copies[first + k].wait_recv()
            self.copies[relay + k].start()

    def pair(self):
        self.copies[2].wait_recv()
        self.copies[5].start()
        self.copies[6].start()

    def far(self, flip):
        for k in (7, 8) if flip else (3, 4):
            self.copies[k].wait_recv()

    def end(self):
        for copy in self.copies:
            copy.wait_send()


class GatherCores(Gather):
    def __init__(self, plane, own, region, sends, recvs, base, core_sends, core_recvs, core_base):
        super().__init__(plane, own, region, sends, recvs, base)
        partner = (plane.dp, plane.ctx, 1 - plane.core)
        self.relays = {}
        for number, (along, flip) in enumerate(((0, 0),) + OTHERS):
            dst = region(plane.spot(along, flip), None)
            src = dst if number else own
            self.relays[along, flip] = remote(
                src, dst, core_sends, core_recvs, core_base + number, partner
            )

    def begin(self):
        super().begin()
        self.relays[0, 0].start()

    def ring(self, flip):
        super().ring(flip)
        self.relays[3, flip].start()
        self.relays[1, flip].start()

    def pair(self):
        super().pair()
        self.relays[0, 1].start()

    def far(self, flip):
        super().far(flip)
        self.relays[2, flip].start()

    def end(self):
        super().end()
        for copy in self.relays.values():
            copy.wait()


def dot_nt(left, right):
    return lax.dot_general(left, right, (((1,), (1,)), ((), ())), preferred_element_type=F32)


def dot_nn(left, right):
    return jnp.dot(left, right, preferred_element_type=F32)


def turn(values, cosine, sine, sign):
    lane = lax.rem(lax.broadcasted_iota(jnp.int32, values.shape, 1), HD)
    low = jnp.where(lane < ROT // 2, sine, 0.0)
    high = sine - low
    up = pltpu.roll(values, HEADS - ROT // 2, 1)
    down = pltpu.roll(values, ROT // 2, 1)
    return values * cosine + sign * (down * high - up * low)


def fold(values, op):
    return op(values.reshape(BLOCK // 8, 8, BLOCK), axis=0)


def nth_spot(plane, n, flip):
    along = n + lax.div(n, 2) - 2 * lax.div(n, 3)
    return plane.spot_at(along, flip)


def forward_kernel(
    hid, grad, wa, wb, vec, place, freq,
    normed_out, grad_out, wa_out, wb_out, right_out, left_out, right_t, left_t,
    q_out, k_out, v_out, do_out, probs_out, sums_out, wave_out, vec_all, stats, bias_out,
    other, normed, pieces, tile, table, place_all, normed_all, grad_all, wa_all, wb_all,
    slope, right, left, rt, lt, q_mask, k_mask, v_t, k_t, q_own, v_own, do_own,
    scores, probs, att_t, wave, sums,
    local, s_act, r_act, s_core, r_core, s_w, r_w, s_small, r_small, s_pair, r_pair, store, p_sem,
):
    plane, data = Plane(True), Plane(False)
    ctx, dp, core = plane.ctx, plane.dp, plane.core
    partner = (dp, ctx, 1 - core)
    greet(plane, data)

    def act_region(ref):
        columns = pl.ds(pl.multiple_of(core * HALF, HALF), HALF)

        def region(spot, part):
            if part is None:
                return ref.at[rows_at(spot), columns]
            start = pl.multiple_of(spot * BLOCK + part * (BLOCK // 2), BLOCK // 2)
            return ref.at[pl.ds(start, BLOCK // 2), columns]

        return region

    def weight_region(ref):
        def region(spot, part):
            if part is None:
                return ref.at[rows_at(spot), :]
            start = pl.multiple_of(spot * BLOCK + part * (BLOCK // 2), BLOCK // 2)
            return ref.at[pl.ds(start, BLOCK // 2), :]

        return region

    def scatter_rows(ref):
        start = pl.multiple_of(dp * BLOCK + ctx * OWN, OWN)
        return ref.at[pl.ds(start, OWN), :]

    sums[...] = jnp.zeros((8, SEQ), F32)
    hidden_copy = remote(hid, other, s_small, r_small, 0, partner)
    hidden_copy.start()
    piece_copies, tile_copies, place_copies, wa_copies, wb_copies = [], [], [], [], []
    for k, o in enumerate(OTHERS):
        to = plane.device(*o)
        spot = plane.spot(*o)
        piece_copies.append(remote(vec, pieces.at[k], s_small, r_small, 1 + k, to))
        place_copies.append(remote(place, place_all.at[ctx], s_small, r_small, 15 + k, to))
        wa_copies.append(remote(wa.at[spot], scatter_rows(wa_all), s_small, r_small, 22 + k, to))
        wb_copies.append(remote(wb.at[spot], scatter_rows(wb_all), s_small, r_small, 29 + k, to))
        columns = pl.ds(pl.multiple_of(dp * 128, 128), 128)
        tile_copies.append(
            remote(tile, table.at[:, columns], s_small, r_small, 8 + k, data.device(*o))
        )
    for copy in piece_copies:
        copy.start()
    for copy in wa_copies + wb_copies + place_copies:
        copy.start()
    locals_ = [
        pltpu.make_async_copy(wa.at[ctx], scatter_rows(wa_all), local.at[0]),
        pltpu.make_async_copy(wb.at[ctx], scatter_rows(wb_all), local.at[1]),
        pltpu.make_async_copy(place, place_all.at[ctx], local.at[2]),
        pltpu.make_async_copy(grad, act_region(grad_all)(ctx, None), local.at[3]),
        pltpu.make_async_copy(normed, act_region(normed_all)(ctx, None), local.at[4]),
    ]
    for copy in locals_[:4]:
        copy.start()

    normed_gather = GatherCores(
        plane, normed, act_region(normed_all), s_act, r_act, 0, s_core, r_core, 0
    )
    grad_gather = GatherCores(
        plane, grad, act_region(grad_all), s_act, r_act, 9, s_core, r_core, 8
    )

    for copy in piece_copies:
        copy.wait_recv()
    total = vec[...].astype(F32)
    for k in range(7):
        total = total + pieces[k].astype(F32)
    tile[...] = total.astype(BF16)
    table[:, pl.ds(pl.multiple_of(dp * 128, 128), 128)] = total.astype(BF16)
    for copy in tile_copies:
        copy.start()

    a_region, b_region = weight_region(wa_all), weight_region(wb_all)
    wa_gather = Gather(data, a_region(dp, None), a_region, s_w, r_w, 0)
    wb_gather = Gather(data, b_region(dp, None), b_region, s_w, r_w, 9)
    for copy in wa_copies:
        copy.wait_recv()
    locals_[0].wait()
    wa_gather.begin()

    for copy in tile_copies:
        copy.wait_recv()
    hidden_copy.wait_recv()
    rows = table[...].astype(F32)
    vec_all[...] = rows
    gain, shift = rows[9:10], rows[10:11]
    lanes = lax.broadcasted_iota(jnp.int32, (16, 128), 1)

    def norm(i, carry):
        at = pl.ds(pl.multiple_of(i * 16, 16), 16)
        a, b = hid[at, :].astype(F32), other[at, :].astype(F32)
        mean = (jnp.sum(a, axis=1, keepdims=True) + jnp.sum(b, axis=1, keepdims=True)) / D
        a, b = a - mean, b - mean
        square = jnp.sum(a * a, axis=1, keepdims=True) + jnp.sum(b * b, axis=1, keepdims=True)
        inverse = lax.rsqrt(square / D + NORM_EPS)
        normed[at, :] = (a * inverse * gain + shift).astype(BF16)
        stats[at, :] = jnp.where(lanes < 64, mean, inverse)
        return carry

    lax.fori_loop(0, BLOCK // 16, norm, 0)
    normed_gather.begin()
    locals_[4].start()
    grad_gather.begin()
    for copy in wb_copies:
        copy.wait_recv()
    locals_[1].wait()

    for copy in place_copies:
        copy.wait_recv()
    locals_[2].wait()
    lane = lax.broadcasted_iota(jnp.int32, (BLOCK, HEADS), 1)
    inner = lax.rem(lane, HD)
    first_head = lane < HD
    turning = inner < ROT

    def tables(i, carry):
        column = place_all[i].astype(F32).T
        angle = column[:, 1:2] * freq[0:1, :]
        wave[0, rows_at(i), :] = jnp.where(turning, jnp.cos(angle), 1.0)
        wave[1, rows_at(i), :] = jnp.where(turning, jnp.sin(angle), 0.0)
        return carry

    lax.fori_loop(0, 8, tables, 0)

    wa_gather.ring(0)
    wa_gather.pair()
    wb_gather.begin()
    normed_gather.ring(0)
    normed_gather.pair()
    normed_gather.far(0)
    wa_gather.ring(1)
    grad_gather.ring(0)
    grad_gather.pair()
    wb_gather.ring(0)
    wb_gather.pair()
    wa_gather.far(0)
    wa_gather.far(1)
    normed_gather.ring(1)
    my_rows = pl.ds(pl.multiple_of(core * HALF, HALF), HALF)
    their_rows = pl.ds(pl.multiple_of((1 - core) * HALF, HALF), HALF)
    pairs = [
        remote(wa_all.at[their_rows, :], wa_out.at[1], s_pair, r_pair, 0, partner),
        remote(wb_all.at[their_rows, :], wb_out.at[1], s_pair, r_pair, 1, partner),
    ]
    pairs[0].start()
    stores = [
        pltpu.make_async_copy(wa_all.at[my_rows, :], wa_out.at[0], store.at[0]),
        pltpu.make_async_copy(wb_all.at[my_rows, :], wb_out.at[0], store.at[1]),
        pltpu.make_async_copy(wave, wave_out, store.at[2]),
    ]
    stores[0].start()
    stores[2].start()

    qkv_bias = [
        vec_all[c : c + 1, pl.ds(pl.multiple_of(ctx * HEADS, HEADS), HEADS)] for c in range(3)
    ]
    fc1_bias = vec_all[
        pl.ds(3 + lax.div(ctx, 2), 1), pl.ds(pl.multiple_of(lax.rem(ctx, 2) * FFS, FFS), FFS)
    ]

    def project(spot):
        at = rows_at(spot)
        block = normed_all[at, :]
        x = dot_nn(block, wa_all[:, 0:FFS]) + fc1_bias
        square = x * x
        tanh = jnp.tanh(x * (GELU + (GELU * 0.044715) * square))
        half = 0.5 * (1.0 + tanh)
        act = x * half
        bend = GELU + (3.0 * 0.044715 * GELU) * square
        slope[at, :] = half + 0.5 * x * (1.0 - tanh * tanh) * bend
        right[at, 0:FFS] = act.astype(BF16)
        rt[0:FFS, at] = act.T.astype(BF16)
        qkv = dot_nn(block, wa_all[:, FFS:WA])
        c, s = wave[0, at, :], wave[1, at, :]
        q = turn(qkv[:, 0:HEADS] + qkv_bias[0], c, s, 1.0).astype(BF16).astype(F32) * (HD**-0.5)
        k = turn(qkv[:, HEADS : 2 * HEADS] + qkv_bias[1], c, s, 1.0)
        v = qkv[:, 2 * HEADS : 3 * HEADS] + qkv_bias[2]
        segment = place_all[spot].astype(F32).T[:, 0:1]
        feature = jnp.where(segment == inner.astype(F32), 1.0, 0.0)
        barred = jnp.where(inner < 3, (1.0 - feature) * MASKED, 0.0)
        q_mask[0, at, :] = jnp.where(first_head, q, barred).astype(BF16)
        q_mask[1, at, :] = jnp.where(first_head, barred, q).astype(BF16)
        k_mask[0, at, :] = jnp.where(first_head, k, feature).astype(BF16)
        k_mask[1, at, :] = jnp.where(first_head, feature, k).astype(BF16)
        q_own[at, :] = q.astype(BF16)
        v_own[at, :] = v.astype(BF16)
        k_t[:, at] = k.T.astype(BF16)
        v_t[:, at] = v.T.astype(BF16)

    def project_ring(flip, start, end):
        def step(n, carry):
            project(nth_spot(plane, n, flip))
            return carry

        lax.fori_loop(start, end, step, 0)

    locals_[4].wait()
    for o in ((0, 0), (1, 0), (3, 0)):
        normed_gather.relays[o].wait_recv()
    project_ring(0, 0, 2)
    normed_gather.far(1)
    wb_gather.ring(1)
    normed_gather.relays[2, 0].wait_recv()
    project_ring(0, 2, 4)
    for o in ((0, 1), (1, 1), (3, 1), (2, 1)):
        normed_gather.relays[o].wait_recv()
    normed_copy = pltpu.make_async_copy(normed_all, normed_out, store.at[3])
    normed_copy.start()
    project_ring(1, 0, 2)
    grad_gather.far(0)
    project_ring(1, 2, 4)
    grad_gather.ring(1)
    wb_gather.far(0)
    wb_gather.far(1)
    pairs[1].start()
    stores[1].start()
    small_stores = [
        pltpu.make_async_copy(q_own, q_out, store.at[4]),
        pltpu.make_async_copy(k_t, k_out, store.at[5]),
        pltpu.make_async_copy(v_own, v_out, store.at[6]),
    ]
    for copy in small_stores:
        copy.start()

    key_row = lax.broadcasted_iota(jnp.int32, (BLOCK, BLOCK), 0)
    query_col = lax.broadcasted_iota(jnp.int32, (BLOCK, BLOCK), 1)
    causal = key_row <= query_col
    prob_stores, right_copies, right_keeps = {}, [], []
    for i in range(8):
        own = pl.ds(i * BLOCK, BLOCK)
        slot = i % 2

        def raw(j, h):
            return dot_nt(k_mask[h, rows_at(j), :], q_mask[h, own, :])

        def score(j, carry):
            new = []
            for h in range(2):
                s = raw(j, h)
                scores[h, rows_at(j), :] = s
                new.append(jnp.maximum(carry[h], fold(s, jnp.max)))
            return tuple(new)

        low = jnp.full((8, BLOCK), MASKED, F32)
        maxima = lax.fori_loop(0, i, score, (low, low), unroll=True)
        tops = []
        for h in range(2):
            s = jnp.where(causal, raw(i, h), MASKED)
            scores[h, own, :] = s
            top = jnp.maximum(maxima[h], fold(s, jnp.max))
            tops.append(jnp.max(top, axis=0, keepdims=True))
        if i >= 2:
            prob_stores[i - 2].wait()

        def prob(j, carry):
            totals, outs = [], []
            for h in range(2):
                p = jnp.exp(scores[h, rows_at(j), :] - tops[h])
                totals.append(carry[0][h] + fold(p, jnp.sum))
                p = p.astype(BF16)
                probs[slot, h, rows_at(j), :] = p
                outs.append(carry[1][h] + dot_nn(v_t[pl.ds(h * HD, HD), rows_at(j)], p))
            return (tuple(totals), tuple(outs))

        zero_sum, zero_out = jnp.zeros((8, BLOCK), F32), jnp.zeros((HD, BLOCK), F32)
        totals, outs = lax.fori_loop(
            0, i + 1, prob, ((zero_sum, zero_sum), (zero_out, zero_out)), unroll=True
        )
        length = (i + 1) * BLOCK
        prob_stores[i] = pltpu.make_async_copy(
            probs.at[slot, :, pl.ds(0, length), :],
            probs_out.at[i, :, pl.ds(0, length), :],
            p_sem.at[slot],
        )
        prob_stores[i].start()
        scale = [1.0 / jnp.sum(totals[h], axis=0, keepdims=True) for h in range(2)]
        both = jnp.concatenate([outs[h] * scale[h] for h in range(2)], axis=0)
        sums[0:1, own] = scale[0]
        sums[1:2, own] = scale[1]
        att_t[:, own] = both
        rt[FFS:WB, own] = both.astype(BF16)
        right[own, FFS:WB] = both.T.astype(BF16)
        right_copies.append(
            remote(right.at[own, :], right_out.at[1, own, :], s_pair, r_pair, 2 + i, partner)
        )
        right_copies[i].start()
        right_keeps.append(
            pltpu.make_async_copy(right.at[own, :], right_out.at[0, own, :], store.at[7 + i])
        )
        right_keeps[i].start()
        if i == 5:
            grad_gather.far(1)
    rt_copy = pltpu.make_async_copy(rt, right_t, store.at[15])
    rt_copy.start()

    bias_out[...] = jnp.zeros((8, FFS), F32)

    def back(spot):
        at = rows_at(spot)
        block = grad_all[at, :]
        d_pre = dot_nn(block, wb_all[:, 0:FFS]) * slope[at, :]
        rounded = d_pre.astype(BF16)
        left[at, :] = rounded
        lt[:, at] = d_pre.T.astype(BF16)
        whole = rounded.astype(F32)
        bias_out[...] += jnp.sum(whole.reshape(BLOCK // 8, 8, FFS), axis=0)
        d_att = dot_nn(block, wb_all[:, FFS:WB])
        do_own[at, :] = d_att.astype(BF16)
        product = att_t[:, at] * d_att.astype(BF16).astype(F32).T
        sums[2:3, at] = jnp.sum(product[0:HD], axis=0, keepdims=True)
        sums[3:4, at] = jnp.sum(product[HD:], axis=0, keepdims=True)

    def back_ring(flip, start, end):
        def step(n, carry):
            back(nth_spot(plane, n, flip))
            return carry

        lax.fori_loop(start, end, step, 0)

    locals_[3].wait()
    left_copies, left_keeps = [], []

    def send_left(spot):
        k = len(left_copies)
        at = rows_at(spot)
        left_copies.append(
            remote(left.at[at, :], left_out.at[1, at, :], s_pair, r_pair, 10 + k, partner)
        )
        left_keeps.append(
            pltpu.make_async_copy(left.at[at, :], left_out.at[0, at, :], store.at[16 + k])
        )
        left_copies[k].start()
        left_keeps[k].start()

    for o in ((0, 0), (1, 0), (3, 0), (2, 0)):
        grad_gather.relays[o].wait_recv()
    back_ring(0, 0, 4)
    for along in range(4):
        send_left(plane.spot(along, 0))
    for o in ((0, 1), (1, 1), (3, 1), (2, 1)):
        grad_gather.relays[o].wait_recv()
    grad_copy = pltpu.make_async_copy(grad_all, grad_out, store.at[24])
    grad_copy.start()
    back_ring(1, 0, 4)
    for along in range(4):
        send_left(plane.spot(along, 1))
    last_stores = [
        pltpu.make_async_copy(lt, left_t, store.at[25]),
        pltpu.make_async_copy(do_own, do_out, store.at[26]),
        pltpu.make_async_copy(sums, sums_out, store.at[27]),
    ]
    for copy in last_stores:
        copy.start()

    for gather in (grad_gather, normed_gather):
        for copy in gather.copies:
            copy.wait_send()
        for copy in gather.relays.values():
            copy.wait_send()
    wa_gather.end()
    wb_gather.end()
    hidden_copy.wait_send()
    for copy in piece_copies + tile_copies + wa_copies + wb_copies + place_copies:
        copy.wait_send()
    for copy in pairs + right_copies + left_copies:
        copy.wait()
    for copy in stores + small_stores + right_keeps + left_keeps + last_stores:
        copy.wait()
    for copy in (normed_copy, grad_copy, rt_copy, prob_stores[6], prob_stores[7]):
        copy.wait()


def forward(hid, grad, wa, wb, vec, place, freq):
    hbm = pl.BlockSpec(memory_space=pl.ANY)
    vmem = pl.BlockSpec(memory_space=pltpu.VMEM)
    dma = pltpu.SemaphoreType.DMA

    def shape(*dims, kind=BF16):
        return jax.ShapeDtypeStruct(dims, kind)

    return pl.pallas_call(
        forward_kernel,
        out_shape=(
            shape(SEQ, D),
            shape(SEQ, D),
            shape(2, HALF, WA),
            shape(2, HALF, WB),
            shape(2, SEQ, WB),
            shape(2, SEQ, FFS),
            shape(WB, SEQ),
            shape(FFS, SEQ),
            shape(SEQ, HEADS),
            shape(HEADS, SEQ),
            shape(SEQ, HEADS),
            shape(SEQ, HEADS),
            shape(8, 2, SEQ, BLOCK),
            shape(8, SEQ, kind=F32),
            shape(2, SEQ, HEADS, kind=F32),
            shape(16, HALF, kind=F32),
            shape(BLOCK, 128, kind=F32),
            shape(8, FFS, kind=F32),
        ),
        in_specs=[vmem, hbm, hbm, hbm, vmem, hbm, vmem],
        out_specs=(hbm,) * 15 + (vmem,) * 3,
        scratch_shapes=[
            pltpu.VMEM((BLOCK, HALF), BF16),
            pltpu.VMEM((BLOCK, HALF), BF16),
            pltpu.VMEM((7, 16, 128), BF16),
            pltpu.VMEM((16, 128), BF16),
            pltpu.VMEM((16, HALF), BF16),
            pltpu.VMEM((8, 8, BLOCK), jnp.int32),
            pltpu.VMEM((SEQ, D), BF16),
            pltpu.VMEM((SEQ, D), BF16),
            pltpu.VMEM((D, WA), BF16),
            pltpu.VMEM((D, WB), BF16),
            pltpu.VMEM((SEQ, FFS), F32),
            pltpu.VMEM((SEQ, WB), BF16),
            pltpu.VMEM((SEQ, FFS), BF16),
            pltpu.VMEM((WB, SEQ), BF16),
            pltpu.VMEM((FFS, SEQ), BF16),
            pltpu.VMEM((2, SEQ, HEADS), BF16),
            pltpu.VMEM((2, SEQ, HEADS), BF16),
            pltpu.VMEM((HEADS, SEQ), BF16),
            pltpu.VMEM((HEADS, SEQ), BF16),
            pltpu.VMEM((SEQ, HEADS), BF16),
            pltpu.VMEM((SEQ, HEADS), BF16),
            pltpu.VMEM((SEQ, HEADS), BF16),
            pltpu.VMEM((2, SEQ, BLOCK), F32),
            pltpu.VMEM((2, 2, SEQ, BLOCK), BF16),
            pltpu.VMEM((HEADS, SEQ), F32),
            pltpu.VMEM((2, SEQ, HEADS), F32),
            pltpu.VMEM((8, SEQ), F32),
            dma((5,)),
            dma((18,)),
            dma((18,)),
            dma((16,)),
            dma((16,)),
            dma((18,)),
            dma((18,)),
            dma((36,)),
            dma((36,)),
            dma((18,)),
            dma((18,)),
            dma((28,)),
            dma((2,)),
        ],
        compiler_params=pltpu.CompilerParams(
            collective_id=0, has_side_effects=True, vmem_limit_bytes=62 * 1024 * 1024
        ),
        name="forward",
    )(hid, grad, wa, wb, vec, place, freq)


def add_rows(dst, terms, count, chunk):
    def step(i, carry):
        at = pl.ds(pl.multiple_of(i * chunk, chunk), chunk)
        total = terms[0][at, :].astype(F32)
        for term in terms[1:]:
            total = total + term[at, :].astype(F32)
        dst[at, :] = total.astype(dst.dtype)
        return carry

    lax.fori_loop(0, count // chunk, step, 0)


class Reduce:
    def __init__(self, plane, acc, landing, sends, recvs, base):
        half_up, half_down, up, down, across = landing
        self.plane, self.acc, self.across = plane, acc, across
        self.near = (half_up, half_down, up, down)
        self.rows = across.shape[0]
        self.chunk = 16 * 1024 // across.shape[1]
        half = self.half = self.rows // 2
        self.copies = []
        for j, flip in ((0, 1), (1, 0)):
            far = plane.spot(2, flip)
            for number, (src, dst, along) in enumerate(
                (
                    (acc.at[far, pl.ds(0, half), :], half_up.at[j], 1),
                    (acc.at[far, pl.ds(half, half), :], half_down.at[j], 3),
                    (acc.at[plane.spot(1, flip)], up.at[j], 1),
                    (acc.at[plane.spot(3, flip)], down.at[j], 3),
                )
            ):
                self.copies.append(
                    remote(src, dst, sends, recvs, base + 4 * j + number, plane.device(along, 0))
                )
        self.copies.append(
            remote(acc.at[plane.spot(0, 1)], across, sends, recvs, base + 8, plane.device(0, 1))
        )

    def first(self):
        for k in (0, 1, 4, 5):
            self.copies[k].start()

    def second(self, j):
        half = self.half
        for number, along in ((0, 1), (1, 3)):
            self.copies[4 * j + number].wait_recv()
            dst = self.acc.at[self.plane.spot(along, 1 - j), pl.ds(number * half, half), :]
            add_rows(dst, [dst, self.near[number].at[j]], half, self.chunk)
            self.copies[4 * j + number + 2].start()

    def third(self):
        self.copies[2].wait_recv()
        self.copies[3].wait_recv()
        dst = self.acc.at[self.plane.spot(0, 1)]
        add_rows(dst, [dst, self.near[2].at[0], self.near[3].at[0]], self.rows, self.chunk)
        self.copies[8].start()

    def arrived(self):
        for k in (6, 7, 8):
            self.copies[k].wait_recv()
        mine = self.acc.at[self.plane.spot(0, 0)]
        return [mine, self.near[2].at[1], self.near[3].at[1], self.across]

    def last(self, dst):
        add_rows(dst, self.arrived(), self.rows, self.chunk)

    def last_turned(self, dst):
        terms = self.arrived()

        def step(i, carry):
            at = pl.ds(pl.multiple_of(i * 128, 128), 128)
            total = terms[0][at, :].astype(F32)
            for term in terms[1:]:
                total = total + term[at, :].astype(F32)
            dst[:, at] = total.T.astype(dst.dtype)
            return carry

        lax.fori_loop(0, self.rows // 128, step, 0)

    def end(self):
        for copy in self.copies:
            copy.wait_send()


def backward_kernel(
    right_in, wb_in, left_in, wa_in, normed, grads, right_t, left_t, q_in, k_in, v_in, do_in,
    probs_in, sums, wave_in, hid, grad, stats, vec_all, bias_in,
    hidden_out, grad_in, gb_all, gf_all, gq_all, vec_sum,
    left, weight, rt, lt, stream, q_all, k_t, v_all, do_all, probs_odd, probs_even, wave, d_k, d_v,
    out_acc, dx_acc, gb_acc, gf_acc, gq_acc,
    out_a, out_b, out_c, out_d, out_e, dx_a, dx_b, dx_c, dx_d, dx_e, gb_a, gb_b, gb_c, gb_d, gb_e,
    gf_a, gf_b, gf_c, gf_d, gf_e, gq_a, gq_b, gq_c, gq_d, gq_e,
    gb_done, gf_done, gq_done, bias, final, vec, vec_in, vec_tile, tile_in, row_own, row_in,
    load, s_stream, s_probs, s_pair, r_pair, s_red, r_red, s_small, r_small, keep,
):
    plane, data = Plane(True), Plane(False)
    ctx, dp, core = plane.ctx, plane.dp, plane.core
    partner = (dp, ctx, 1 - core)
    loads = {
        "weight": pltpu.make_async_copy(wb_in, weight.at[:, :, pl.ds(0, WB)], load.at[0]),
        "right": pltpu.make_async_copy(right_in, left.at[:, :, pl.ds(0, WB)], load.at[1]),
        "rt": pltpu.make_async_copy(right_t, rt, load.at[2]),
        "lt": pltpu.make_async_copy(left_t, lt, load.at[3]),
        "q": pltpu.make_async_copy(q_in, q_all, load.at[4]),
        "k": pltpu.make_async_copy(k_in, k_t, load.at[5]),
        "v": pltpu.make_async_copy(v_in, v_all, load.at[6]),
        "do": pltpu.make_async_copy(do_in, do_all, load.at[7]),
    }
    for copy in loads.values():
        copy.start()
    greet(plane, data)

    out = Reduce(plane, out_acc, (out_a, out_b, out_c, out_d, out_e), s_red, r_red, 0)
    dx = Reduce(plane, dx_acc, (dx_a, dx_b, dx_c, dx_d, dx_e), s_red, r_red, 9)
    gb = Reduce(data, gb_acc, (gb_a, gb_b, gb_c, gb_d, gb_e), s_red, r_red, 18)
    gf = Reduce(data, gf_acc, (gf_a, gf_b, gf_c, gf_d, gf_e), s_red, r_red, 27)
    gq = Reduce(data, gq_acc, (gq_a, gq_b, gq_c, gq_d, gq_e), s_red, r_red, 36)

    def spot_of(where, n):
        group = lax.div(n + 2, 4)
        inside = n + 2 - 4 * group
        near = 1 - lax.rem(group + 1, 2)
        along = near * (1 + 2 * lax.rem(inside, 2)) + (1 - near) * (2 - group)
        flip = near * (1 - lax.div(inside, 2)) + (1 - near) * (1 - lax.rem(inside, 2))
        return where.spot_at(along, flip)

    def out_block(n, carry):
        spot = spot_of(plane, n)
        at = rows_at(spot)
        total = dot_nt(left[0, at, 0:WB], weight[0, :, 0:WB])
        total = total + dot_nt(left[1, at, 0:WB], weight[1, :, 0:WB])
        out_acc[spot] = total.astype(BF16)
        return carry

    def dx_block(n, carry):
        spot = spot_of(plane, n)
        at = rows_at(spot)
        total = dot_nt(left[0, at, 0:FFS], weight[0, :, 0:FFS])
        total = total + dot_nt(left[1, at, 0:FFS], weight[1, :, 0:FFS])
        total = total + dot_nt(left[0, at, WB:HALF], weight[0, :, FFS:WA])
        total = total + dot_nt(left[1, at, WB:HALF], weight[1, :, FFS:WA])
        dx_acc[spot] = total.astype(BF16)
        return carry

    def fetch(source, n):
        columns = rows_at(spot_of(data, n))
        slot = lax.rem(n, 2)
        return pltpu.make_async_copy(source.at[:, columns], stream.at[slot], s_stream.at[slot])

    def weight_blocks(source, factor, rows, acc, start, end):
        def step(n, carry):
            @pl.when(n < 7)
            def _():
                fetch(source, n + 1).start()

            fetch(source, n).wait()
            total = dot_nn(factor[0:rows, :], stream[lax.rem(n, 2)])
            acc[spot_of(data, n)] = total.astype(BF16)
            return carry

        lax.fori_loop(start, end, step, 0)

    fetch(grads, 0).start()
    loads["weight"].wait()
    loads["right"].wait()
    lax.fori_loop(0, 2, out_block, 0)
    out.first()
    loads["rt"].wait()
    weight_blocks(grads, rt, WB, gb_acc, 0, 2)
    gb.first()
    lax.fori_loop(2, 8, out_block, 0)
    left_load = pltpu.make_async_copy(left_in, left.at[:, :, pl.ds(0, FFS)], load.at[8])
    weight_load = pltpu.make_async_copy(wa_in, weight, load.at[9])
    left_load.start()
    weight_load.start()
    out.second(0)
    weight_blocks(grads, rt, WB, gb_acc, 2, 8)
    gb.second(0)
    gb.second(1)
    out.second(1)
    loads["lt"].wait()
    fetch(normed, 0).start()
    weight_blocks(normed, lt, FFS, gf_acc, 0, 2)
    gf.first()
    weight_blocks(normed, lt, FFS, gf_acc, 2, 8)
    gf.second(0)
    gf.second(1)

    lane = lax.broadcasted_iota(jnp.int32, (BLOCK, HEADS), 1)
    heads = (lane < HD, lane >= HD)
    bias[...] = jnp.zeros((8, 3 * HEADS), F32)

    def clear(i, carry):
        d_k[rows_at(i), :] = jnp.zeros((BLOCK, HEADS), F32)
        d_v[rows_at(i), :] = jnp.zeros((BLOCK, HEADS), F32)
        return carry

    lax.fori_loop(0, 8, clear, 0)

    def probs_of(i):
        length = pl.ds(0, (i + 1) * BLOCK)
        buffer = probs_odd if i % 2 else probs_even
        return [
            pltpu.make_async_copy(
                probs_in.at[i, :, length, :], buffer.at[:, length, :], s_probs.at[i % 2]
            ),
            pltpu.make_async_copy(
                wave_in.at[:, pl.ds(i * BLOCK, BLOCK), :], wave.at[i % 2], s_probs.at[2 + i % 2]
            ),
        ]

    for name in ("q", "k", "v", "do"):
        loads[name].wait()
    arriving = {7: probs_of(7)}
    for copy in arriving[7]:
        copy.start()
    swaps = []
    for i in range(7, -1, -1):
        own = pl.ds(i * BLOCK, BLOCK)
        if i:
            arriving[i - 1] = probs_of(i - 1)
            for copy in arriving[i - 1]:
                copy.start()
        for copy in arriving[i]:
            copy.wait()
        probs = probs_odd if i % 2 else probs_even
        scale = [sums[h : h + 1, own] for h in range(2)]
        delta = [sums[2 + h : 3 + h, own] for h in range(2)]
        q, do = q_all[own, :].astype(F32), do_all[own, :].astype(F32)
        q_plain = [jnp.where(heads[h], q, 0.0).astype(BF16) for h in range(2)]
        do_plain = [jnp.where(heads[h], do, 0.0).astype(BF16) for h in range(2)]

        def back(j, carry):
            at, new = rows_at(j), []
            add_k, add_v = d_k[at, :], d_v[at, :]
            for h in range(2):
                p = probs[h, at, :].astype(F32) * scale[h]
                d_p = dot_nt(v_all[at, :], do_plain[h])
                d_s = (p * (d_p - delta[h])).astype(BF16)
                add_v = add_v + dot_nn(p.astype(BF16), do_plain[h])
                add_k = add_k + dot_nn(d_s, q_plain[h])
                new.append(carry[h] + dot_nn(k_t[pl.ds(h * HD, HD), at], d_s))
            d_k[at, :] = add_k
            d_v[at, :] = add_v
            return tuple(new)

        zero_out = jnp.zeros((HD, BLOCK), F32)
        d_q = lax.fori_loop(0, i + 1, back, (zero_out, zero_out), unroll=True)
        d_q = jnp.concatenate(d_q, axis=0).T * (HD**-0.5)
        c, s = wave[i % 2, 0], wave[i % 2, 1]
        parts = (turn(d_q, c, s, -1.0), turn(d_k[own, :], c, s, -1.0), d_v[own, :])
        for k, part in enumerate(parts):
            rounded = part.astype(BF16)
            whole = rounded.astype(F32)
            left[0, own, WB + k * HEADS : WB + (k + 1) * HEADS] = rounded
            rt[k * HEADS : (k + 1) * HEADS, own] = whole.T.astype(BF16)
            columns = slice(k * HEADS, (k + 1) * HEADS)
            bias[:, columns] += jnp.sum(whole.reshape(BLOCK // 8, 8, HEADS), axis=0)
        span = pl.ds(WB, 3 * HEADS)
        swap = remote(
            left.at[0, own, span], left.at[1, own, span], s_pair, r_pair, i, partner
        )
        swap.start()
        swaps.append(swap)
        if i == 5:
            out.third()
        if i == 3:
            gb.third()
        if i == 1:
            gf.third()

    left_load.wait()
    weight_load.wait()
    for swap in swaps:
        swap.wait_recv()
    lax.fori_loop(0, 2, dx_block, 0)
    dx.first()
    fetch(normed, 0).start()
    lax.fori_loop(2, 6, dx_block, 0)
    dx.second(0)
    weight_blocks(normed, rt, 3 * HEADS, gq_acc, 0, 2)
    gq.first()
    dx.second(1)
    lax.fori_loop(6, 8, dx_block, 0)
    weight_blocks(normed, rt, 3 * HEADS, gq_acc, 2, 8)
    gq.second(0)
    gq.second(1)

    copies = {}
    keeps = []
    for n, (name, done, landed) in enumerate(
        (("gb", gb_done, gb_all), ("gf", gf_done, gf_all), ("gq", gq_done, gq_all))
    ):
        copies[name] = [
            remote(
                done.at[rows_at(plane.spot(*o), OWN), :],
                landed.at[ctx],
                s_small,
                r_small,
                15 + 7 * n + k,
                plane.device(*o),
            )
            for k, o in enumerate(OTHERS)
        ]
        keeps.append(
            pltpu.make_async_copy(done.at[rows_at(ctx, OWN), :], landed.at[ctx], keep.at[n])
        )
    for n, (name, red, done) in enumerate((("gb", gb, gb_done), ("gf", gf, gf_done))):
        red.last_turned(done)
        for copy in copies[name]:
            copy.start()
        keeps[n].start()

    out.last(final)
    bias_rows = vec_all[7:8, :] + vec_all[8:9, :]

    def add_hidden(i, carry):
        at = pl.ds(pl.multiple_of(i * 16, 16), 16)
        hidden_out[at, :] = (hid[at, :].astype(F32) + final[at, :] + bias_rows).astype(BF16)
        return carry

    lax.fori_loop(0, BLOCK // 16, add_hidden, 0)
    dx.third()
    gq.third()
    gq.last_turned(gq_done)
    for copy in copies["gq"]:
        copy.start()
    keeps[2].start()

    dx.last(final)
    gain = vec_all[9:10, :]
    lanes = lax.broadcasted_iota(jnp.int32, (16, 128), 1)

    def lean(i, carry):
        at = pl.ds(pl.multiple_of(i * 16, 16), 16)
        d, h, stat = final[at, :], hid[at, :].astype(F32), stats[at, :]
        normal = (h - stat[:, 0:1]) * stat[:, 64:65]
        product = d * normal
        one = jnp.sum(d * gain, axis=1, keepdims=True)
        two = jnp.sum(product * gain, axis=1, keepdims=True)
        row_own[at, :] = jnp.where(lanes < 64, one, two)
        return (carry[0] + d, carry[1] + product, carry[2] + grad[at, :].astype(F32))

    zero = jnp.zeros((16, HALF), F32)
    rows = lax.fori_loop(0, BLOCK // 16, lean, (zero, zero, zero))
    row_copy = remote(row_own, row_in, s_small, r_small, 0, partner)
    row_copy.start()
    shift_grad, gain_grad, bias_grad = [jnp.sum(r, axis=0, keepdims=True) for r in rows]
    number = lax.broadcasted_iota(jnp.int32, (16, HALF), 0)
    vec[...] = jnp.where(
        number == 9,
        gain_grad,
        jnp.where(
            number == 10, shift_grad, jnp.where((number == 7) | (number == 8), bias_grad, 0.0)
        ),
    )
    columns = pl.ds(pl.multiple_of(ctx * HEADS, HEADS), HEADS)
    for k in range(3):
        part = jnp.sum(bias[:, k * HEADS : (k + 1) * HEADS], axis=0, keepdims=True)
        vec[k : k + 1, columns] = part
    columns = pl.ds(pl.multiple_of(lax.rem(ctx, 2) * FFS, FFS), FFS)
    part = jnp.sum(bias_in[...], axis=0, keepdims=True)
    vec[:, columns] = jnp.where(
        lax.broadcasted_iota(jnp.int32, (16, FFS), 0) == 3 + lax.div(ctx, 2), part, vec[:, columns]
    )
    vec_copies, tile_copies = [], []
    for k, o in enumerate(OTHERS):
        columns = pl.ds(pl.multiple_of(data.spot(*o) * 128, 128), 128)
        vec_copies.append(
            remote(vec.at[:, columns], vec_in.at[k], s_small, r_small, 1 + k, data.device(*o))
        )
        tile_copies.append(
            remote(vec_tile, tile_in.at[k], s_small, r_small, 8 + k, plane.device(*o))
        )
    for copy in vec_copies:
        copy.start()
    for copy in vec_copies:
        copy.wait_recv()
    total = vec[:, pl.ds(pl.multiple_of(dp * 128, 128), 128)]
    for k in range(7):
        total = total + vec_in[k]
    vec_tile[...] = total
    for copy in tile_copies:
        copy.start()

    row_copy.wait()

    def tilt(i, carry):
        at = pl.ds(pl.multiple_of(i * 16, 16), 16)
        d, h, stat = final[at, :], hid[at, :].astype(F32), stats[at, :]
        inverse = stat[:, 64:65]
        normal = (h - stat[:, 0:1]) * inverse
        row = (row_own[at, :] + row_in[at, :]) / D
        change = inverse * (d * gain - row[:, 0:1] - normal * row[:, 64:65])
        grad_in[at, :] = (grad[at, :].astype(F32) + change).astype(BF16)
        return carry

    lax.fori_loop(0, BLOCK // 16, tilt, 0)
    for copy in tile_copies:
        copy.wait_recv()
    total = vec_tile[...]
    for k in range(7):
        total = total + tile_in[k]
    vec_sum[...] = total

    for name in copies:
        for copy in copies[name]:
            copy.wait()
    for copy in keeps:
        copy.wait()
    for copy in vec_copies + tile_copies + swaps:
        copy.wait_send()
    for red in (dx, out, gb, gf, gq):
        red.end()


def backward(*args):
    hbm = pl.BlockSpec(memory_space=pl.ANY)
    vmem = pl.BlockSpec(memory_space=pltpu.VMEM)
    dma = pltpu.SemaphoreType.DMA

    def landing(rows, width):
        half = pltpu.VMEM((2, rows // 2, width), BF16)
        whole = pltpu.VMEM((2, rows, width), BF16)
        return [half, half, whole, whole, pltpu.VMEM((rows, width), BF16)]

    def shape(*dims, kind=BF16):
        return jax.ShapeDtypeStruct(dims, kind)

    return pl.pallas_call(
        backward_kernel,
        out_shape=(
            shape(BLOCK, HALF),
            shape(BLOCK, HALF),
            shape(8, OWN, WB),
            shape(8, OWN, FFS),
            shape(8, OWN, 3 * HEADS),
            shape(16, 128, kind=F32),
        ),
        in_specs=[hbm] * 13 + [vmem, hbm] + [vmem] * 5,
        out_specs=(vmem, vmem, hbm, hbm, hbm, vmem),
        scratch_shapes=[
            pltpu.VMEM((2, SEQ, HALF), BF16),
            pltpu.VMEM((2, HALF, WA), BF16),
            pltpu.VMEM((WB, SEQ), BF16),
            pltpu.VMEM((FFS, SEQ), BF16),
            pltpu.VMEM((2, SEQ, BLOCK), BF16),
            pltpu.VMEM((SEQ, HEADS), BF16),
            pltpu.VMEM((HEADS, SEQ), BF16),
            pltpu.VMEM((SEQ, HEADS), BF16),
            pltpu.VMEM((SEQ, HEADS), BF16),
            pltpu.VMEM((2, SEQ, BLOCK), BF16),
            pltpu.VMEM((2, SEQ - BLOCK, BLOCK), BF16),
            pltpu.VMEM((2, 2, BLOCK, HEADS), F32),
            pltpu.VMEM((SEQ, HEADS), F32),
            pltpu.VMEM((SEQ, HEADS), F32),
            pltpu.VMEM((8, BLOCK, HALF), BF16),
            pltpu.VMEM((8, BLOCK, HALF), BF16),
            pltpu.VMEM((8, WB, BLOCK), BF16),
            pltpu.VMEM((8, FFS, BLOCK), BF16),
            pltpu.VMEM((8, 3 * HEADS, BLOCK), BF16),
            *landing(BLOCK, HALF),
            *landing(BLOCK, HALF),
            *landing(WB, BLOCK),
            *landing(FFS, BLOCK),
            *landing(3 * HEADS, BLOCK),
            pltpu.VMEM((BLOCK, WB), BF16),
            pltpu.VMEM((BLOCK, FFS), BF16),
            pltpu.VMEM((BLOCK, 3 * HEADS), BF16),
            pltpu.VMEM((8, 3 * HEADS), F32),
            pltpu.VMEM((BLOCK, HALF), F32),
            pltpu.VMEM((16, HALF), F32),
            pltpu.VMEM((7, 16, 128), F32),
            pltpu.VMEM((16, 128), F32),
            pltpu.VMEM((7, 16, 128), F32),
            pltpu.VMEM((BLOCK, 128), F32),
            pltpu.VMEM((BLOCK, 128), F32),
            dma((10,)),
            dma((2,)),
            dma((4,)),
            dma((8,)),
            dma((8,)),
            dma((45,)),
            dma((45,)),
            dma((36,)),
            dma((36,)),
            dma((3,)),
        ],
        compiler_params=pltpu.CompilerParams(
            collective_id=1, has_side_effects=True, vmem_limit_bytes=62 * 1024 * 1024
        ),
        name="backward",
    )(*args)


def adam_step(weight, first, second, gradient, rate):
    first_new = BETA_ONE * first + (1.0 - BETA_ONE) * gradient
    second_new = BETA_TWO * second + (1.0 - BETA_TWO) * gradient * gradient
    fix_one = 1.0 - BETA_ONE**STEP
    fix_two = 1.0 - BETA_TWO**STEP
    update = first_new / fix_one / (jnp.sqrt(second_new / fix_two) + ADAM_EPS)
    return (first_new, second_new, weight - rate * (update + DECAY * weight))


def by_owner(weight, parts):
    return jnp.moveaxis(weight.reshape(OWN, *parts, 8, -1), -2, 0).reshape(8, OWN, -1)


def on_device(
    hidden_in,
    grad_out,
    segment_ids,
    positions,
    qkv_weight,
    dense_weight,
    fc1_weight,
    fc2_weight,
    vectors,
    qkv_first,
    qkv_second,
    dense_first,
    dense_second,
    fc1_first,
    fc1_second,
    fc2_first,
    fc2_second,
    vector_first,
    vector_second,
):
    ctx = lax.axis_index("ctx")
    hid = hidden_in.reshape(BLOCK, HALF)
    grad = grad_out.reshape(BLOCK, HALF)
    wa = jnp.concatenate(
        [by_owner(fc1_weight.astype(BF16), ()), by_owner(qkv_weight.astype(BF16), (3,))], axis=2
    )
    wb = jnp.concatenate(
        [by_owner(fc2_weight.astype(BF16), ()), by_owner(dense_weight.astype(BF16), ())], axis=2
    )
    lane = jnp.arange(128)
    vec = jnp.where(
        (lane // 16 == ctx)[None, :], jnp.tile(vectors[0].astype(BF16), (1, 8)), jnp.zeros((), BF16)
    )
    vec = jnp.pad(vec, ((0, 5), (0, 0)))
    place = jnp.pad(jnp.concatenate([segment_ids, positions], axis=0), ((0, 6), (0, 0)))

    freqs = 10000.0 ** (-jnp.arange(ROT // 2, dtype=F32) * 2.0 / ROT)
    freq = jnp.broadcast_to(jnp.tile(freqs, HEADS // (ROT // 2))[None], (8, HEADS))

    (
        normed, grads, wa2, wb2, right, left, right_t, left_t, q, k_t, v, do, probs, sums, wave,
        vec_all, stats, bias,
    ) = forward(hid, grad, wa, wb, vec, place, freq)
    hidden_out, grad_in, gb_all, gf_all, gq_all, vec_sum = backward(
        right, wb2, left, wa2, normed, grads, right_t, left_t, q, k_t, v, do, probs, sums, wave,
        hid, grad, stats, vec_all, bias,
    )

    def owned(grads_in, parts, shape):
        split = grads_in.astype(F32).reshape(8, OWN, *parts, -1)
        return jnp.moveaxis(split, 0, -2).reshape(shape)

    qkv_owned = owned(gq_all, (3,), qkv_weight.shape)
    fc1_owned = owned(gf_all, (), fc1_weight.shape)
    fc2_owned = owned(gb_all[:, :, :FFS], (), fc2_weight.shape)
    dense_owned = owned(gb_all[:, :, FFS:], (), dense_weight.shape)
    vector_owned = lax.dynamic_slice(vec_sum, (0, ctx * 16), (11, 16))[None]
    qkv_new = adam_step(qkv_weight, qkv_first, qkv_second, qkv_owned, 2.0 / math.sqrt(D))
    dense_new = adam_step(
        dense_weight, dense_first, dense_second, dense_owned, 2.0 / math.sqrt(D // 16)
    )
    fc1_new = adam_step(fc1_weight, fc1_first, fc1_second, fc1_owned, 2.0 / math.sqrt(D))
    fc2_new = adam_step(fc2_weight, fc2_first, fc2_second, fc2_owned, 2.0 / math.sqrt(FF))
    vector_new = adam_step(vectors, vector_first, vector_second, vector_owned, 0.6)
    return (
        hidden_out.reshape(hidden_in.shape),
        grad_in.reshape(grad_out.shape),
        *qkv_new,
        *dense_new,
        *fc1_new,
        *fc2_new,
        *vector_new,
    )


def solution(mesh):
    rows = P("dp", "ctx", "tensor")
    tokens = P("dp", "ctx")
    cube = P(("dp", "ctx"), None, "tensor")
    plain = P(("dp", "ctx"), "tensor")
    packed = P("tensor", None, ("dp", "ctx"))
    return jax.shard_map(
        on_device,
        mesh=mesh,
        in_specs=(rows, rows, tokens, tokens, cube, plain, plain, plain, packed)
        + (cube,) * 2
        + (plain,) * 6
        + (packed,) * 2,
        out_specs=(rows, rows) + (cube,) * 3 + (plain,) * 9 + (packed,) * 3,
        check_vma=False,
    )
```

```python
import functools
import math

import jax
import jax.numpy as jnp
import numpy as np
from jax import lax
from jax.experimental import pallas as pl
from jax.experimental.pallas import tpu as pltpu
from jax.sharding import PartitionSpec as P

D = 2048
HD = 64
ROT = 32
FF = 8192
STEP = 10
SEQ = 2048
BLOCK = 256
HALF = 1024
FFS = 512
HEADS = 128
WA = FFS + 3 * HEADS
WB = FFS + HEADS
OWN = 32

BETA_ONE = 0.9
BETA_TWO = 0.95
ADAM_EPS = 1e-08
DECAY = 0.1
NORM_EPS = 1e-05
MASKED = -1e30
GELU = math.sqrt(2.0 / math.pi)

RATES = (2.0 / math.sqrt(D), 2.0 / math.sqrt(FF), 2.0 / math.sqrt(D // 16), 0.6)
MESH = pl.DeviceIdType.MESH
F32 = jnp.float32
BF16 = jnp.bfloat16
OTHERS = tuple((k // 2, k % 2) for k in range(1, 8))


class Plane:
    def __init__(self, over_ctx):
        self.dp = lax.axis_index("dp")
        self.ctx = lax.axis_index("ctx")
        self.core = lax.axis_index("tensor")
        self.over_ctx = over_ctx
        if over_ctx:
            self.ring, self.pair = lax.div(self.ctx, 2), lax.rem(self.ctx, 2)
        else:
            self.ring, self.pair = lax.rem(self.dp, 4), lax.div(self.dp, 4)

    def spot(self, along, flip):
        ring = lax.rem(self.ring + along, 4) if along else self.ring
        pair = 1 - self.pair if flip else self.pair
        return ring * 2 + pair if self.over_ctx else pair * 4 + ring

    def spot_at(self, along, flip):
        ring, pair = lax.rem(self.ring + along, 4), lax.rem(self.pair + flip, 2)
        return ring * 2 + pair if self.over_ctx else pair * 4 + ring

    def device(self, along, flip):
        spot = self.spot(along, flip)
        return (self.dp, spot, self.core) if self.over_ctx else (spot, self.ctx, self.core)


def rows_at(index, size=BLOCK):
    return pl.ds(pl.multiple_of(index * size, size), size)


def remote(src, dst, sends, recvs, number, device):
    return pltpu.make_async_remote_copy(
        src_ref=src,
        dst_ref=dst,
        send_sem=sends.at[number],
        recv_sem=recvs.at[number],
        device_id=device,
        device_id_type=MESH,
    )


def greet(ctx_plane, dp_plane):
    barrier = pltpu.get_barrier_semaphore()
    partners = [ctx_plane.device(*o) for o in OTHERS] + [dp_plane.device(*o) for o in OTHERS]
    partners.append((ctx_plane.dp, ctx_plane.ctx, 1 - ctx_plane.core))
    for partner in partners:
        pl.semaphore_signal(barrier, inc=1, device_id=partner, device_id_type=MESH)
    pl.semaphore_wait(barrier, len(partners))


class Gather:
    def __init__(self, plane, own, region, sends, recvs, base):
        me = plane.spot(0, 0)

        def message(number, src, spot, part, along, flip):
            dst = region(spot, part)
            return remote(
                dst if src is None else src, dst, sends, recvs, base + number, plane.device(along, flip)
            )

        self.copies = [
            message(0, own, me, None, 1, 0),
            message(1, own, me, None, 3, 0),
            message(2, own, me, None, 0, 1),
            message(3, None, plane.spot(3, 0), 0, 1, 0),
            message(4, None, plane.spot(1, 0), 1, 3, 0),
            message(5, None, plane.spot(0, 1), None, 1, 0),
            message(6, None, plane.spot(0, 1), None, 3, 0),
            message(7, None, plane.spot(3, 1), 0, 1, 0),
            message(8, None, plane.spot(1, 1), 1, 3, 0),
        ]

    def begin_ring(self):
        self.copies[0].start()
        self.copies[1].start()

    def begin_pair(self):
        self.copies[2].start()

    def ring(self, flip):
        first, relay = (5, 7) if flip else (0, 3)
        for k in (0, 1):
            self.copies[first + k].wait_recv()
            self.copies[relay + k].start()

    def pair(self):
        self.copies[2].wait_recv()
        self.copies[5].start()
        self.copies[6].start()

    def far(self, flip):
        for k in (7, 8) if flip else (3, 4):
            self.copies[k].wait_recv()

    def end(self):
        for copy in self.copies:
            copy.wait_send()


class GatherCores(Gather):
    def __init__(self, plane, own, region, sends, recvs, base, core_sends, core_recvs, core_base):
        super().__init__(plane, own, region, sends, recvs, base)
        partner = (plane.dp, plane.ctx, 1 - plane.core)
        self.relays = {}
        for number, (along, flip) in enumerate(((0, 0),) + OTHERS):
            dst = region(plane.spot(along, flip), None)
            src = dst if number else own
            self.relays[along, flip] = remote(
                src, dst, core_sends, core_recvs, core_base + number, partner
            )

    def begin_ring(self):
        super().begin_ring()
        self.relays[0, 0].start()

    def ring(self, flip):
        super().ring(flip)
        self.relays[3, flip].start()
        self.relays[1, flip].start()

    def pair(self):
        super().pair()
        self.relays[0, 1].start()

    def far(self, flip):
        super().far(flip)
        self.relays[2, flip].start()

    def end(self):
        super().end()
        for copy in self.relays.values():
            copy.wait()


def dot_nt(left, right):
    return lax.dot_general(left, right, (((1,), (1,)), ((), ())), preferred_element_type=F32)


def dot_nn(left, right):
    return jnp.dot(left, right, preferred_element_type=F32)


def dot_tn(left, right):
    return lax.dot_general(left, right, (((0,), (0,)), ((), ())), preferred_element_type=F32)


def turn(values, cosine, sine, sign):
    lane = lax.rem(lax.broadcasted_iota(jnp.int32, values.shape, 1), HD)
    low = jnp.where(lane < ROT // 2, sine, 0.0)
    high = sine - low
    up = pltpu.roll(values, HEADS - ROT // 2, 1)
    down = pltpu.roll(values, ROT // 2, 1)
    return values * cosine + sign * (down * high - up * low)


def fold(values, op):
    return op(values.reshape(BLOCK // 8, 8, BLOCK), axis=0)


def nth_spot(plane, n, flip):
    along = n + lax.div(n, 2) - 2 * lax.div(n, 3)
    return plane.spot_at(along, flip)


def forward_kernel(
    hid, grad, fc1, qkv_w, fc2, dense, vectors, segments, positions,
    normed_out, grad_out, wa_out, wb_out, right_out, left_out,
    q_out, k_out, v_out, do_out, probs_out, sums_out, wave_out, vec_all, stats, bias_out,
    wa, wb, vec, place, joined, other, normed, pieces, tile, table, place_all,
    normed_all, grad_all, wa_all, wb_all, slope, right, left, q_mask, k_mask, v_t, k_t, q_own, v_own, do_own,
    scores, probs, att_t, wave, sums,
    local, s_act, r_act, s_core, r_core, s_w, r_w, s_small, r_small, s_pair, r_pair, store, p_sem,
):
    plane, data = Plane(True), Plane(False)
    ctx, dp, core = plane.ctx, plane.dp, plane.core
    partner = (dp, ctx, 1 - core)

    def act_region(ref):
        columns = pl.ds(pl.multiple_of(core * HALF, HALF), HALF)

        def region(spot, part):
            if part is None:
                return ref.at[rows_at(spot), columns]
            start = pl.multiple_of(spot * BLOCK + part * (BLOCK // 2), BLOCK // 2)
            return ref.at[pl.ds(start, BLOCK // 2), columns]

        return region

    def weight_region(ref):
        def region(spot, part):
            if part is None:
                return ref.at[rows_at(spot), :]
            start = pl.multiple_of(spot * BLOCK + part * (BLOCK // 2), BLOCK // 2)
            return ref.at[pl.ds(start, BLOCK // 2), :]

        return region

    def scatter_rows(ref):
        start = pl.multiple_of(dp * BLOCK + ctx * OWN, OWN)
        return ref.at[pl.ds(start, OWN), :]

    sums[...] = jnp.zeros((8, SEQ), F32)
    vec_lane = lax.broadcasted_iota(jnp.int32, (11, 128), 1)
    spread = jnp.concatenate([vectors[...]] * 8, axis=1)
    vec[...] = jnp.zeros((16, 128), F32)
    vec[0:11, :] = jnp.where(lax.div(vec_lane, 16) == ctx, spread, 0.0)
    place[...] = jnp.zeros((8, BLOCK), jnp.int32)
    place[0:1, :] = segments[...]
    place[1:2, :] = positions[...]
    place_all[ctx] = place[...]
    tile[...] = vec[...].astype(BF16)
    for c in range(8):
        wa[c, :, 0:FFS] = fc1[:, c * FFS : (c + 1) * FFS].astype(BF16)
        wb[c, :, 0:FFS] = fc2[:, c * FFS : (c + 1) * FFS].astype(BF16)
        columns = slice(c * HEADS, (c + 1) * HEADS)
        wb[c, :, FFS:WB] = dense[:, columns].astype(BF16)
        for k in range(3):
            wa[c, :, FFS + k * HEADS : FFS + (k + 1) * HEADS] = qkv_w[:, k, columns].astype(BF16)

    greet(plane, data)
    hidden_copy = remote(hid, other, s_small, r_small, 0, partner)
    hidden_copy.start()
    piece_copies, tile_copies, place_copies, wa_copies, wb_copies = [], [], [], [], []
    for k, o in enumerate(OTHERS):
        to = plane.device(*o)
        spot = plane.spot(*o)
        piece_copies.append(remote(tile, pieces.at[k], s_small, r_small, 1 + k, to))
        place_copies.append(remote(place, place_all.at[ctx], s_small, r_small, 15 + k, to))
        wa_copies.append(remote(wa.at[spot], scatter_rows(wa_all), s_small, r_small, 22 + k, to))
        wb_copies.append(remote(wb.at[spot], scatter_rows(wb_all), s_small, r_small, 29 + k, to))
        columns = pl.ds(pl.multiple_of(dp * 128, 128), 128)
        tile_copies.append(
            remote(joined, table.at[:, columns], s_small, r_small, 8 + k, data.device(*o))
        )
    for copy in piece_copies + wa_copies + wb_copies + place_copies:
        copy.start()
    locals_ = [
        pltpu.make_async_copy(wa.at[ctx], scatter_rows(wa_all), local.at[0]),
        pltpu.make_async_copy(wb.at[ctx], scatter_rows(wb_all), local.at[1]),
        pltpu.make_async_copy(grad, act_region(grad_all)(ctx, None), local.at[2]),
        pltpu.make_async_copy(normed, act_region(normed_all)(ctx, None), local.at[3]),
    ]
    for copy in locals_[:3]:
        copy.start()

    normed_gather = GatherCores(
        plane, normed, act_region(normed_all), s_act, r_act, 0, s_core, r_core, 0
    )
    grad_gather = GatherCores(
        plane, grad, act_region(grad_all), s_act, r_act, 9, s_core, r_core, 8
    )

    for copy in piece_copies:
        copy.wait_recv()
    total = tile[...].astype(F32)
    for k in range(7):
        total = total + pieces[k].astype(F32)
    joined[...] = total.astype(BF16)
    table[:, pl.ds(pl.multiple_of(dp * 128, 128), 128)] = total.astype(BF16)
    for copy in tile_copies:
        copy.start()

    a_region, b_region = weight_region(wa_all), weight_region(wb_all)
    wa_gather = Gather(data, a_region(dp, None), a_region, s_w, r_w, 0)
    wb_gather = Gather(data, b_region(dp, None), b_region, s_w, r_w, 9)
    for copy in wa_copies:
        copy.wait_recv()
    locals_[0].wait()
    wa_gather.begin_pair()
    wa_gather.begin_ring()
    grad_gather.begin_ring()

    for copy in tile_copies:
        copy.wait_recv()
    hidden_copy.wait_recv()
    rows = table[...].astype(F32)
    vec_all[...] = rows
    gain, shift = rows[9:10], rows[10:11]
    lanes = lax.broadcasted_iota(jnp.int32, (16, 128), 1)

    def norm(i, carry):
        at = pl.ds(pl.multiple_of(i * 16, 16), 16)
        a, b = hid[at, :].astype(F32), other[at, :].astype(F32)
        mean = (jnp.sum(a, axis=1, keepdims=True) + jnp.sum(b, axis=1, keepdims=True)) / D
        a, b = a - mean, b - mean
        square = jnp.sum(a * a, axis=1, keepdims=True) + jnp.sum(b * b, axis=1, keepdims=True)
        inverse = lax.rsqrt(square / D + NORM_EPS)
        normed[at, :] = (a * inverse * gain + shift).astype(BF16)
        stats[at, :] = jnp.where(lanes < 64, mean, inverse)
        return carry

    lax.fori_loop(0, BLOCK // 16, norm, 0)
    normed_gather.begin_pair()
    normed_gather.begin_ring()
    locals_[3].start()
    for copy in place_copies:
        copy.wait_recv()
    lane = lax.broadcasted_iota(jnp.int32, (BLOCK, HEADS), 1)
    inner = lax.rem(lane, HD)
    first_head = lane < HD
    turning = inner < ROT
    wheel = lax.rem(lax.broadcasted_iota(jnp.int32, (1, HEADS), 1), ROT // 2)
    freq = jnp.zeros((1, HEADS), F32)
    for k in range(ROT // 2):
        freq = jnp.where(wheel == k, float(np.float32(10000.0 ** (-2.0 * k / ROT))), freq)

    def tables(i, carry):
        column = place_all[i].astype(F32).T
        angle = column[:, 1:2] * freq
        wave[0, rows_at(i), :] = jnp.where(turning, jnp.cos(angle), 1.0)
        wave[1, rows_at(i), :] = jnp.where(turning, jnp.sin(angle), 0.0)
        return carry

    lax.fori_loop(0, 8, tables, 0)

    wa_gather.ring(0)
    wa_gather.pair()
    for copy in wb_copies:
        copy.wait_recv()
    locals_[1].wait()
    normed_gather.pair()
    grad_gather.begin_pair()
    normed_gather.ring(0)
    wb_gather.begin_pair()
    wb_gather.begin_ring()
    wa_gather.ring(1)
    wa_gather.far(0)
    wa_gather.far(1)
    my_rows = pl.ds(pl.multiple_of(core * HALF, HALF), HALF)
    their_rows = pl.ds(pl.multiple_of((1 - core) * HALF, HALF), HALF)
    pairs = [
        remote(wa_all.at[their_rows, :], wa_out.at[1], s_pair, r_pair, 0, partner),
        remote(wb_all.at[their_rows, :], wb_out.at[1], s_pair, r_pair, 1, partner),
    ]
    pairs[0].start()
    stores = [
        pltpu.make_async_copy(wa_all.at[my_rows, :], wa_out.at[0], store.at[0]),
        pltpu.make_async_copy(wb_all.at[my_rows, :], wb_out.at[0], store.at[1]),
        pltpu.make_async_copy(wave, wave_out, store.at[2]),
    ]
    stores[0].start()
    stores[2].start()

    qkv_bias = [
        vec_all[c : c + 1, pl.ds(pl.multiple_of(ctx * HEADS, HEADS), HEADS)] for c in range(3)
    ]
    fc1_bias = vec_all[
        pl.ds(3 + lax.div(ctx, 2), 1), pl.ds(pl.multiple_of(lax.rem(ctx, 2) * FFS, FFS), FFS)
    ]

    def project(spot):
        at = rows_at(spot)
        block = normed_all[at, :]
        x = dot_nn(block, wa_all[:, 0:FFS]) + fc1_bias
        square = x * x
        tanh = jnp.tanh(x * (GELU + (GELU * 0.044715) * square))
        half = 0.5 * (1.0 + tanh)
        bend = GELU + (3.0 * 0.044715 * GELU) * square
        slope[at, :] = half + 0.5 * x * (1.0 - tanh * tanh) * bend
        right[at, 0:FFS] = (x * half).astype(BF16)
        qkv = dot_nn(block, wa_all[:, FFS:WA])
        c, s = wave[0, at, :], wave[1, at, :]
        q = turn(qkv[:, 0:HEADS] + qkv_bias[0], c, s, 1.0).astype(BF16).astype(F32) * (HD**-0.5)
        k = turn(qkv[:, HEADS : 2 * HEADS] + qkv_bias[1], c, s, 1.0)
        v = qkv[:, 2 * HEADS : 3 * HEADS] + qkv_bias[2]
        segment = place_all[spot].astype(F32).T[:, 0:1]
        feature = jnp.where(segment == inner.astype(F32), 1.0, 0.0)
        barred = jnp.where(inner < 3, (1.0 - feature) * MASKED, 0.0)
        q_mask[0, at, :] = jnp.where(first_head, q, barred).astype(BF16)
        q_mask[1, at, :] = jnp.where(first_head, barred, q).astype(BF16)
        k_mask[0, at, :] = jnp.where(first_head, k, feature).astype(BF16)
        k_mask[1, at, :] = jnp.where(first_head, feature, k).astype(BF16)
        q_own[at, :] = q.astype(BF16)
        v_own[at, :] = v.astype(BF16)
        k_t[:, at] = k.T.astype(BF16)
        v_t[:, at] = v.T.astype(BF16)

    def project_ring(flip, start, end):
        def step(n, carry):
            project(nth_spot(plane, n, flip))
            return carry

        lax.fori_loop(start, end, step, 0)

    def keep_block(ref, out, o, number):
        at = rows_at(plane.spot(*o))
        copy = pltpu.make_async_copy(ref.at[at, :], out.at[at, :], store.at[number])
        copy.start()
        return copy

    locals_[3].wait()
    for o in ((0, 0), (1, 0), (3, 0)):
        normed_gather.relays[o].wait_recv()
    project_ring(0, 0, 2)
    wb_gather.ring(0)
    wb_gather.pair()
    project_ring(0, 2, 3)
    normed_gather.far(0)
    normed_gather.ring(1)
    normed_gather.relays[2, 0].wait_recv()
    project_ring(0, 3, 4)
    for o in ((0, 1), (1, 1), (3, 1)):
        normed_gather.relays[o].wait_recv()
    project_ring(1, 0, 2)
    normed_gather.far(1)
    grad_gather.ring(0)
    grad_gather.pair()
    project_ring(1, 2, 3)
    wb_gather.ring(1)
    normed_gather.relays[2, 1].wait_recv()
    project_ring(1, 3, 4)
    normed_copies = [
        keep_block(normed_all, normed_out, (along, flip), 16 + 2 * along + flip)
        for flip in (0, 1)
        for along in range(4)
    ]
    small_stores = [
        pltpu.make_async_copy(q_own, q_out, store.at[4]),
        pltpu.make_async_copy(k_t, k_out, store.at[5]),
        pltpu.make_async_copy(v_own, v_out, store.at[6]),
    ]
    for copy in small_stores:
        copy.start()

    key_row = lax.broadcasted_iota(jnp.int32, (BLOCK, BLOCK), 0)
    query_col = lax.broadcasted_iota(jnp.int32, (BLOCK, BLOCK), 1)
    causal = key_row <= query_col
    prob_stores, right_copies, right_keeps = {}, [], []
    for i in range(8):
        own = pl.ds(i * BLOCK, BLOCK)
        slot = i % 2

        def raw(j, h):
            return dot_nt(k_mask[h, rows_at(j), :], q_mask[h, own, :])

        def score(j, carry):
            new = []
            for h in range(2):
                s = raw(j, h)
                scores[h, rows_at(j), :] = s
                new.append(jnp.maximum(carry[h], fold(s, jnp.max)))
            return tuple(new)

        low = jnp.full((8, BLOCK), MASKED, F32)
        maxima = lax.fori_loop(0, i, score, (low, low), unroll=True)
        tops = []
        for h in range(2):
            s = jnp.where(causal, raw(i, h), MASKED)
            scores[h, own, :] = s
            top = jnp.maximum(maxima[h], fold(s, jnp.max))
            tops.append(jnp.max(top, axis=0, keepdims=True))
        if i >= 2:
            prob_stores[i - 2].wait()

        def prob(j, carry):
            totals, outs = [], []
            for h in range(2):
                p = jnp.exp(scores[h, rows_at(j), :] - tops[h])
                totals.append(carry[0][h] + fold(p, jnp.sum))
                p = p.astype(BF16)
                probs[slot, h, rows_at(j), :] = p
                outs.append(carry[1][h] + dot_nn(v_t[pl.ds(h * HD, HD), rows_at(j)], p))
            return (tuple(totals), tuple(outs))

        zero_sum, zero_out = jnp.zeros((8, BLOCK), F32), jnp.zeros((HD, BLOCK), F32)
        totals, outs = lax.fori_loop(
            0, i + 1, prob, ((zero_sum, zero_sum), (zero_out, zero_out)), unroll=True
        )
        length = (i + 1) * BLOCK
        prob_stores[i] = pltpu.make_async_copy(
            probs.at[slot, :, pl.ds(0, length), :],
            probs_out.at[i, :, pl.ds(0, length), :],
            p_sem.at[slot],
        )
        prob_stores[i].start()
        scale = [1.0 / jnp.sum(totals[h], axis=0, keepdims=True) for h in range(2)]
        both = jnp.concatenate([outs[h] * scale[h] for h in range(2)], axis=0)
        sums[0:1, own] = scale[0]
        sums[1:2, own] = scale[1]
        att_t[:, own] = both
        right[own, FFS:WB] = both.T.astype(BF16)
        right_copies.append(
            remote(right.at[own, :], right_out.at[1, own, :], s_pair, r_pair, 2 + i, partner)
        )
        right_copies[i].start()
        right_keeps.append(
            pltpu.make_async_copy(right.at[own, :], right_out.at[0, own, :], store.at[7 + i])
        )
        right_keeps[i].start()
        if i == 3:
            wb_gather.far(0)
            wb_gather.far(1)
            pairs[1].start()
            stores[1].start()
        if i == 4:
            grad_gather.far(0)
        if i == 6:
            grad_gather.ring(1)

    bias_out[...] = jnp.zeros((8, FFS), F32)

    def back(spot):
        at = rows_at(spot)
        block = grad_all[at, :]
        d_pre = dot_nn(block, wb_all[:, 0:FFS]) * slope[at, :]
        rounded = d_pre.astype(BF16)
        left[at, :] = rounded
        whole = rounded.astype(F32)
        bias_out[...] += jnp.sum(whole.reshape(BLOCK // 8, 8, FFS), axis=0)
        d_att = dot_nn(block, wb_all[:, FFS:WB])
        do_own[at, :] = d_att.astype(BF16)
        product = att_t[:, at] * d_att.astype(BF16).astype(F32).T
        sums[2:3, at] = jnp.sum(product[0:HD], axis=0, keepdims=True)
        sums[3:4, at] = jnp.sum(product[HD:], axis=0, keepdims=True)

    def back_ring(flip, start, end):
        def step(n, carry):
            back(nth_spot(plane, n, flip))
            return carry

        lax.fori_loop(start, end, step, 0)

    locals_[2].wait()
    left_copies, left_keeps = [], []

    def send_left(o):
        k = len(left_copies)
        at = rows_at(plane.spot(*o))
        left_copies.append(
            remote(left.at[at, :], left_out.at[1, at, :], s_pair, r_pair, 10 + k, partner)
        )
        left_keeps.append(
            pltpu.make_async_copy(left.at[at, :], left_out.at[0, at, :], store.at[24 + k])
        )
        left_copies[k].start()
        left_keeps[k].start()

    for along in range(4):
        grad_gather.relays[along, 0].wait_recv()
    grad_copies = [
        keep_block(grad_all, grad_out, (along, 0), 32 + 2 * along) for along in range(4)
    ]
    back_ring(0, 0, 4)
    for along in range(4):
        send_left((along, 0))
    for along in (0, 1, 3):
        grad_gather.relays[along, 1].wait_recv()
        grad_copies.append(keep_block(grad_all, grad_out, (along, 1), 33 + 2 * along))
    back_ring(1, 0, 2)
    grad_gather.far(1)
    back_ring(1, 2, 3)
    for along in (0, 1, 3):
        send_left((along, 1))
    grad_gather.relays[2, 1].wait_recv()
    grad_copies.append(keep_block(grad_all, grad_out, (2, 1), 37))
    back_ring(1, 3, 4)
    send_left((2, 1))
    last_stores = [
        pltpu.make_async_copy(do_own, do_out, store.at[40]),
        pltpu.make_async_copy(sums, sums_out, store.at[41]),
    ]
    for copy in last_stores:
        copy.start()

    for gather in (grad_gather, normed_gather):
        for copy in gather.copies:
            copy.wait_send()
        for copy in gather.relays.values():
            copy.wait_send()
    wa_gather.end()
    wb_gather.end()
    hidden_copy.wait_send()
    for copy in piece_copies + tile_copies + wa_copies + wb_copies + place_copies:
        copy.wait_send()
    for copy in pairs + right_copies + left_copies:
        copy.wait()
    for copy in stores + small_stores + right_keeps + left_keeps + last_stores:
        copy.wait()
    for copy in normed_copies + grad_copies + [prob_stores[6], prob_stores[7]]:
        copy.wait()


def forward(*args):
    hbm = pl.BlockSpec(memory_space=pl.ANY)
    vmem = pl.BlockSpec(memory_space=pltpu.VMEM)
    dma = pltpu.SemaphoreType.DMA

    def shape(*dims, kind=BF16):
        return jax.ShapeDtypeStruct(dims, kind)

    return pl.pallas_call(
        forward_kernel,
        out_shape=(
            shape(SEQ, D),
            shape(SEQ, D),
            shape(2, HALF, WA),
            shape(2, HALF, WB),
            shape(2, SEQ, WB),
            shape(2, SEQ, FFS),
            shape(SEQ, HEADS),
            shape(HEADS, SEQ),
            shape(SEQ, HEADS),
            shape(SEQ, HEADS),
            shape(8, 2, SEQ, BLOCK),
            shape(8, SEQ, kind=F32),
            shape(2, SEQ, HEADS, kind=F32),
            shape(16, HALF, kind=F32),
            shape(BLOCK, 128, kind=F32),
            shape(8, FFS, kind=F32),
        ),
        in_specs=[vmem, hbm] + [vmem] * 7,
        out_specs=(hbm,) * 13 + (vmem,) * 3,
        scratch_shapes=[
            pltpu.VMEM((8, OWN, WA), BF16),
            pltpu.VMEM((8, OWN, WB), BF16),
            pltpu.VMEM((16, 128), F32),
            pltpu.VMEM((8, BLOCK), jnp.int32),
            pltpu.VMEM((16, 128), BF16),
            pltpu.VMEM((BLOCK, HALF), BF16),
            pltpu.VMEM((BLOCK, HALF), BF16),
            pltpu.VMEM((7, 16, 128), BF16),
            pltpu.VMEM((16, 128), BF16),
            pltpu.VMEM((16, HALF), BF16),
            pltpu.VMEM((8, 8, BLOCK), jnp.int32),
            pltpu.VMEM((SEQ, D), BF16),
            pltpu.VMEM((SEQ, D), BF16),
            pltpu.VMEM((D, WA), BF16),
            pltpu.VMEM((D, WB), BF16),
            pltpu.VMEM((SEQ, FFS), F32),
            pltpu.VMEM((SEQ, WB), BF16),
            pltpu.VMEM((SEQ, FFS), BF16),
            pltpu.VMEM((2, SEQ, HEADS), BF16),
            pltpu.VMEM((2, SEQ, HEADS), BF16),
            pltpu.VMEM((HEADS, SEQ), BF16),
            pltpu.VMEM((HEADS, SEQ), BF16),
            pltpu.VMEM((SEQ, HEADS), BF16),
            pltpu.VMEM((SEQ, HEADS), BF16),
            pltpu.VMEM((SEQ, HEADS), BF16),
            pltpu.VMEM((2, SEQ, BLOCK), F32),
            pltpu.VMEM((2, 2, SEQ, BLOCK), BF16),
            pltpu.VMEM((HEADS, SEQ), F32),
            pltpu.VMEM((2, SEQ, HEADS), F32),
            pltpu.VMEM((8, SEQ), F32),
            dma((4,)),
            dma((18,)),
            dma((18,)),
            dma((16,)),
            dma((16,)),
            dma((18,)),
            dma((18,)),
            dma((36,)),
            dma((36,)),
            dma((18,)),
            dma((18,)),
            dma((42,)),
            dma((2,)),
        ],
        compiler_params=pltpu.CompilerParams(
            collective_id=0, has_side_effects=True, vmem_limit_bytes=62 * 1024 * 1024
        ),
        name="forward",
    )(*args)


def add_rows(dst, terms, count, chunk):
    def step(i, carry):
        at = pl.ds(pl.multiple_of(i * chunk, chunk), chunk)
        total = terms[0][at, :].astype(F32)
        for term in terms[1:]:
            total = total + term[at, :].astype(F32)
        dst[at, :] = total.astype(dst.dtype)
        return carry

    lax.fori_loop(0, count // chunk, step, 0)


class Reduce:
    def __init__(self, plane, acc, landing, sends, recvs, base):
        half_up, half_down, up, down, across = landing
        self.plane, self.acc, self.across = plane, acc, across
        self.near = (half_up, half_down, up, down)
        self.rows = across.shape[0]
        self.chunk = 16
        half = self.half = self.rows // 2
        self.copies = []
        for j, flip in ((0, 1), (1, 0)):
            far = plane.spot(2, flip)
            for number, (src, dst, along) in enumerate(
                (
                    (acc.at[far, pl.ds(0, half), :], half_up.at[j], 1),
                    (acc.at[far, pl.ds(half, half), :], half_down.at[j], 3),
                    (acc.at[plane.spot(1, flip)], up.at[j], 1),
                    (acc.at[plane.spot(3, flip)], down.at[j], 3),
                )
            ):
                self.copies.append(
                    remote(src, dst, sends, recvs, base + 4 * j + number, plane.device(along, 0))
                )
        self.copies.append(
            remote(acc.at[plane.spot(0, 1)], across, sends, recvs, base + 8, plane.device(0, 1))
        )

    def first(self, j):
        self.copies[4 * j].start()
        self.copies[4 * j + 1].start()

    def second(self, j):
        half = self.half
        for number, along in ((0, 1), (1, 3)):
            self.copies[4 * j + number].wait_recv()
            dst = self.acc.at[self.plane.spot(along, 1 - j), pl.ds(number * half, half), :]
            add_rows(dst, [dst, self.near[number].at[j]], half, self.chunk)
            self.copies[4 * j + number + 2].start()

    def third(self):
        self.copies[2].wait_recv()
        self.copies[3].wait_recv()
        dst = self.acc.at[self.plane.spot(0, 1)]
        add_rows(dst, [dst, self.near[2].at[0], self.near[3].at[0]], self.rows, self.chunk)
        self.copies[8].start()

    def arrived(self):
        for k in (6, 7, 8):
            self.copies[k].wait_recv()
        mine = self.acc.at[self.plane.spot(0, 0)]
        return [mine, self.near[2].at[1], self.near[3].at[1], self.across]

    def last(self, dst):
        add_rows(dst, self.arrived(), self.rows, self.chunk)

    def end(self):
        for copy in self.copies:
            copy.wait_send()


def backward_kernel(
    right_in, wb_in, left_in, wa_in, normed, grads, q_in, k_in, v_in, do_in,
    probs_in, sums, wave_in, hid, grad, stats, vec_all, bias_in,
    hidden_out, grad_in, gb_all, ga_all, vec_sum,
    left, weight, stream, q_all, k_t, v_all, do_all, probs_odd, probs_even, wave, d_k, d_v,
    out_acc, dx_acc, gb_acc, ga_acc,
    out_a, out_b, out_c, out_d, out_e, dx_a, dx_b, dx_c, dx_d, dx_e, gb_a, gb_b, gb_c, gb_d, gb_e,
    ga_a, ga_b, ga_c, ga_d, ga_e, gb_done, ga_done, bias, final, vec, vec_in, vec_tile, tile_in, row_own, row_in,
    load, s_stream, s_probs, s_pair, r_pair, s_red, r_red, s_small, r_small, keep,
):
    plane, data = Plane(True), Plane(False)
    ctx, dp, core = plane.ctx, plane.dp, plane.core
    partner = (dp, ctx, 1 - core)
    loads = {
        "weight": pltpu.make_async_copy(wb_in, weight.at[:, :, pl.ds(0, WB)], load.at[0]),
        "right": pltpu.make_async_copy(right_in, left.at[:, :, pl.ds(0, WB)], load.at[1]),
        "q": pltpu.make_async_copy(q_in, q_all, load.at[4]),
        "k": pltpu.make_async_copy(k_in, k_t, load.at[5]),
        "v": pltpu.make_async_copy(v_in, v_all, load.at[6]),
        "do": pltpu.make_async_copy(do_in, do_all, load.at[7]),
    }
    for copy in loads.values():
        copy.start()
    greet(plane, data)

    out = Reduce(plane, out_acc, (out_a, out_b, out_c, out_d, out_e), s_red, r_red, 0)
    dx = Reduce(plane, dx_acc, (dx_a, dx_b, dx_c, dx_d, dx_e), s_red, r_red, 9)
    gb = Reduce(data, gb_acc, (gb_a, gb_b, gb_c, gb_d, gb_e), s_red, r_red, 18)
    ga = Reduce(data, ga_acc, (ga_a, ga_b, ga_c, ga_d, ga_e), s_red, r_red, 27)

    def spot_of(where, n):
        group = lax.div(n + 2, 4)
        inside = n + 2 - 4 * group
        near = 1 - lax.rem(group + 1, 2)
        along = near * (1 + 2 * lax.rem(inside, 2)) + (1 - near) * (2 - group)
        flip = near * (1 - lax.div(inside, 2)) + (1 - near) * (1 - lax.rem(inside, 2))
        return where.spot_at(along, flip)

    def out_block(n, carry):
        spot = spot_of(plane, n)
        at = rows_at(spot)
        total = dot_nt(left[0, at, 0:WB], weight[0, :, 0:WB])
        total = total + dot_nt(left[1, at, 0:WB], weight[1, :, 0:WB])
        out_acc[spot] = total.astype(BF16)
        return carry

    def dx_block(n, carry):
        spot = spot_of(plane, n)
        at = rows_at(spot)
        total = dot_nt(left[0, at, 0:FFS], weight[0, :, 0:FFS])
        total = total + dot_nt(left[1, at, 0:FFS], weight[1, :, 0:FFS])
        total = total + dot_nt(left[0, at, WB:HALF], weight[0, :, FFS:WA])
        total = total + dot_nt(left[1, at, WB:HALF], weight[1, :, FFS:WA])
        dx_acc[spot] = total.astype(BF16)
        return carry

    def fetch(source, n):
        columns = rows_at(spot_of(data, n))
        slot = lax.rem(n, 2)
        return pltpu.make_async_copy(source.at[:, columns], stream.at[slot], s_stream.at[slot])

    def weight_blocks(source, parts, acc, start, end):
        def step(n, carry):
            @pl.when(n < 7)
            def _():
                fetch(source, n + 1).start()

            fetch(source, n).wait()
            columns, spot = 0, spot_of(data, n)
            for first, width in parts:
                total = dot_tn(stream[lax.rem(n, 2)], left[0, :, first : first + width])
                acc[spot, :, columns : columns + width] = total.astype(BF16)
                columns += width
            return carry

        lax.fori_loop(start, end, step, 0)

    b_parts, a_parts = ((0, WB),), ((0, FFS), (WB, 3 * HEADS))
    fetch(grads, 0).start()
    loads["weight"].wait()
    loads["right"].wait()
    lax.fori_loop(0, 1, out_block, 0)
    out.first(0)
    lax.fori_loop(1, 4, out_block, 0)
    weight_blocks(grads, b_parts, gb_acc, 0, 1)
    gb.first(0)
    out.second(0)
    out.first(1)
    lax.fori_loop(4, 8, out_block, 0)
    weight_load = pltpu.make_async_copy(wa_in, weight, load.at[9])
    weight_load.start()
    weight_blocks(grads, b_parts, gb_acc, 1, 4)
    gb.second(0)
    gb.first(1)
    out.second(1)
    weight_blocks(grads, b_parts, gb_acc, 4, 8)
    gb.second(1)
    left_load = pltpu.make_async_copy(left_in, left.at[:, :, pl.ds(0, FFS)], load.at[8])
    left_load.start()
    out.third()

    lane = lax.broadcasted_iota(jnp.int32, (BLOCK, HEADS), 1)
    heads = (lane < HD, lane >= HD)
    bias[...] = jnp.zeros((8, 3 * HEADS), F32)

    def clear(i, carry):
        d_k[rows_at(i), :] = jnp.zeros((BLOCK, HEADS), F32)
        d_v[rows_at(i), :] = jnp.zeros((BLOCK, HEADS), F32)
        return carry

    lax.fori_loop(0, 8, clear, 0)

    def probs_of(i):
        length = pl.ds(0, (i + 1) * BLOCK)
        buffer = probs_odd if i % 2 else probs_even
        return [
            pltpu.make_async_copy(
                probs_in.at[i, :, length, :], buffer.at[:, length, :], s_probs.at[i % 2]
            ),
            pltpu.make_async_copy(
                wave_in.at[:, pl.ds(i * BLOCK, BLOCK), :], wave.at[i % 2], s_probs.at[2 + i % 2]
            ),
        ]

    for name in ("q", "k", "v", "do"):
        loads[name].wait()
    arriving = {7: probs_of(7)}
    for copy in arriving[7]:
        copy.start()
    swaps = []
    for i in range(7, -1, -1):
        own = pl.ds(i * BLOCK, BLOCK)
        if i:
            arriving[i - 1] = probs_of(i - 1)
            for copy in arriving[i - 1]:
                copy.start()
        for copy in arriving[i]:
            copy.wait()
        probs = probs_odd if i % 2 else probs_even
        scale = [sums[h : h + 1, own] for h in range(2)]
        delta = [sums[2 + h : 3 + h, own] for h in range(2)]
        q, do = q_all[own, :].astype(F32), do_all[own, :].astype(F32)
        q_plain = [jnp.where(heads[h], q, 0.0).astype(BF16) for h in range(2)]
        do_plain = [jnp.where(heads[h], do, 0.0).astype(BF16) for h in range(2)]

        def back(j, carry):
            at, new = rows_at(j), []
            add_k, add_v = d_k[at, :], d_v[at, :]
            for h in range(2):
                p = probs[h, at, :].astype(F32) * scale[h]
                d_p = dot_nt(v_all[at, :], do_plain[h])
                d_s = (p * (d_p - delta[h])).astype(BF16)
                add_v = add_v + dot_nn(p.astype(BF16), do_plain[h])
                add_k = add_k + dot_nn(d_s, q_plain[h])
                new.append(carry[h] + dot_nn(k_t[pl.ds(h * HD, HD), at], d_s))
            d_k[at, :] = add_k
            d_v[at, :] = add_v
            return tuple(new)

        zero_out = jnp.zeros((HD, BLOCK), F32)
        d_q = lax.fori_loop(0, i + 1, back, (zero_out, zero_out), unroll=True)
        d_q = jnp.concatenate(d_q, axis=0).T * (HD**-0.5)
        c, s = wave[i % 2, 0], wave[i % 2, 1]
        parts = (turn(d_q, c, s, -1.0), turn(d_k[own, :], c, s, -1.0), d_v[own, :])
        for k, part in enumerate(parts):
            rounded = part.astype(BF16)
            whole = rounded.astype(F32)
            left[0, own, WB + k * HEADS : WB + (k + 1) * HEADS] = rounded
            columns = slice(k * HEADS, (k + 1) * HEADS)
            bias[:, columns] += jnp.sum(whole.reshape(BLOCK // 8, 8, HEADS), axis=0)
        span = pl.ds(WB, 3 * HEADS)
        swap = remote(
            left.at[0, own, span], left.at[1, own, span], s_pair, r_pair, i, partner
        )
        swap.start()
        swaps.append(swap)
        if i == 4:
            gb.third()
        if i == 0:
            gb.last(gb_done)

    left_load.wait()
    weight_load.wait()
    for swap in swaps:
        swap.wait_recv()
    fetch(normed, 0).start()
    lax.fori_loop(0, 1, dx_block, 0)
    dx.first(0)
    lax.fori_loop(1, 4, dx_block, 0)
    dx.second(0)
    dx.first(1)
    weight_blocks(normed, a_parts, ga_acc, 0, 1)
    ga.first(0)
    lax.fori_loop(4, 6, dx_block, 0)
    weight_blocks(normed, a_parts, ga_acc, 1, 4)
    ga.second(0)
    ga.first(1)
    dx.second(1)
    lax.fori_loop(6, 8, dx_block, 0)
    dx.third()
    weight_blocks(normed, a_parts, ga_acc, 4, 8)
    ga.second(1)

    copies = {}
    keeps = []
    for n, (name, done, landed) in enumerate(
        (("gb", gb_done, gb_all), ("ga", ga_done, ga_all))
    ):
        copies[name] = [
            remote(
                done.at[rows_at(plane.spot(*o), OWN), :],
                landed.at[ctx],
                s_small,
                r_small,
                15 + 7 * n + k,
                plane.device(*o),
            )
            for k, o in enumerate(OTHERS)
        ]
        keeps.append(
            pltpu.make_async_copy(done.at[rows_at(ctx, OWN), :], landed.at[ctx], keep.at[n])
        )
    for copy in copies["gb"]:
        copy.start()
    keeps[0].start()

    out.last(final)
    bias_rows = vec_all[7:8, :] + vec_all[8:9, :]

    def add_hidden(i, carry):
        at = pl.ds(pl.multiple_of(i * 16, 16), 16)
        hidden_out[at, :] = (hid[at, :].astype(F32) + final[at, :] + bias_rows).astype(BF16)
        return carry

    lax.fori_loop(0, BLOCK // 16, add_hidden, 0)
    ga.third()
    dx.last(final)
    gain = vec_all[9:10, :]
    lanes = lax.broadcasted_iota(jnp.int32, (16, 128), 1)

    def lean(i, carry):
        at = pl.ds(pl.multiple_of(i * 16, 16), 16)
        d, h, stat = final[at, :], hid[at, :].astype(F32), stats[at, :]
        normal = (h - stat[:, 0:1]) * stat[:, 64:65]
        product = d * normal
        one = jnp.sum(d * gain, axis=1, keepdims=True)
        two = jnp.sum(product * gain, axis=1, keepdims=True)
        row_own[at, :] = jnp.where(lanes < 64, one, two)
        return (carry[0] + d, carry[1] + product, carry[2] + grad[at, :].astype(F32))

    zero = jnp.zeros((16, HALF), F32)
    rows = lax.fori_loop(0, BLOCK // 16, lean, (zero, zero, zero))
    row_copy = remote(row_own, row_in, s_small, r_small, 0, partner)
    row_copy.start()
    shift_grad, gain_grad, bias_grad = [jnp.sum(r, axis=0, keepdims=True) for r in rows]
    number = lax.broadcasted_iota(jnp.int32, (16, HALF), 0)
    vec[...] = jnp.where(
        number == 9,
        gain_grad,
        jnp.where(
            number == 10, shift_grad, jnp.where((number == 7) | (number == 8), bias_grad, 0.0)
        ),
    )
    columns = pl.ds(pl.multiple_of(ctx * HEADS, HEADS), HEADS)
    for k in range(3):
        part = jnp.sum(bias[:, k * HEADS : (k + 1) * HEADS], axis=0, keepdims=True)
        vec[k : k + 1, columns] = part
    columns = pl.ds(pl.multiple_of(lax.rem(ctx, 2) * FFS, FFS), FFS)
    part = jnp.sum(bias_in[...], axis=0, keepdims=True)
    vec[:, columns] = jnp.where(
        lax.broadcasted_iota(jnp.int32, (16, FFS), 0) == 3 + lax.div(ctx, 2), part, vec[:, columns]
    )
    vec_copies, tile_copies = [], []
    for k, o in enumerate(OTHERS):
        columns = pl.ds(pl.multiple_of(data.spot(*o) * 128, 128), 128)
        vec_copies.append(
            remote(vec.at[:, columns], vec_in.at[k], s_small, r_small, 1 + k, data.device(*o))
        )
        tile_copies.append(
            remote(vec_tile, tile_in.at[k], s_small, r_small, 8 + k, plane.device(*o))
        )
    for copy in vec_copies:
        copy.start()
    ga.last(ga_done)
    for copy in copies["ga"]:
        copy.start()
    keeps[1].start()
    for copy in vec_copies:
        copy.wait_recv()
    total = vec[:, pl.ds(pl.multiple_of(dp * 128, 128), 128)]
    for k in range(7):
        total = total + vec_in[k]
    vec_tile[...] = total
    for copy in tile_copies:
        copy.start()

    row_copy.wait()

    def tilt(i, carry):
        at = pl.ds(pl.multiple_of(i * 16, 16), 16)
        d, h, stat = final[at, :], hid[at, :].astype(F32), stats[at, :]
        inverse = stat[:, 64:65]
        normal = (h - stat[:, 0:1]) * inverse
        row = (row_own[at, :] + row_in[at, :]) / D
        change = inverse * (d * gain - row[:, 0:1] - normal * row[:, 64:65])
        grad_in[at, :] = (grad[at, :].astype(F32) + change).astype(BF16)
        return carry

    lax.fori_loop(0, BLOCK // 16, tilt, 0)
    for copy in tile_copies:
        copy.wait_recv()
    total = vec_tile[...]
    for k in range(7):
        total = total + tile_in[k]
    vec_sum[...] = total

    for name in copies:
        for copy in copies[name]:
            copy.wait()
    for copy in keeps:
        copy.wait()
    for copy in vec_copies + tile_copies + swaps:
        copy.wait_send()
    for red in (dx, out, gb, ga):
        red.end()


def backward(*args):
    hbm = pl.BlockSpec(memory_space=pl.ANY)
    vmem = pl.BlockSpec(memory_space=pltpu.VMEM)
    dma = pltpu.SemaphoreType.DMA

    def landing(rows, width):
        half = pltpu.VMEM((2, rows // 2, width), BF16)
        whole = pltpu.VMEM((2, rows, width), BF16)
        return [half, half, whole, whole, pltpu.VMEM((rows, width), BF16)]

    def shape(*dims, kind=BF16):
        return jax.ShapeDtypeStruct(dims, kind)

    return pl.pallas_call(
        backward_kernel,
        out_shape=(
            shape(BLOCK, HALF),
            shape(BLOCK, HALF),
            shape(8, OWN, WB),
            shape(8, OWN, WA),
            shape(16, 128, kind=F32),
        ),
        in_specs=[hbm] * 11 + [vmem, hbm] + [vmem] * 5,
        out_specs=(vmem, vmem, hbm, hbm, vmem),
        scratch_shapes=[
            pltpu.VMEM((2, SEQ, HALF), BF16),
            pltpu.VMEM((2, HALF, WA), BF16),
            pltpu.VMEM((2, SEQ, BLOCK), BF16),
            pltpu.VMEM((SEQ, HEADS), BF16),
            pltpu.VMEM((HEADS, SEQ), BF16),
            pltpu.VMEM((SEQ, HEADS), BF16),
            pltpu.VMEM((SEQ, HEADS), BF16),
            pltpu.VMEM((2, SEQ, BLOCK), BF16),
            pltpu.VMEM((2, SEQ - BLOCK, BLOCK), BF16),
            pltpu.VMEM((2, 2, BLOCK, HEADS), F32),
            pltpu.VMEM((SEQ, HEADS), F32),
            pltpu.VMEM((SEQ, HEADS), F32),
            pltpu.VMEM((8, BLOCK, HALF), BF16),
            pltpu.VMEM((8, BLOCK, HALF), BF16),
            pltpu.VMEM((8, BLOCK, WB), BF16),
            pltpu.VMEM((8, BLOCK, WA), BF16),
            *landing(BLOCK, HALF),
            *landing(BLOCK, HALF),
            *landing(BLOCK, WB),
            *landing(BLOCK, WA),
            pltpu.VMEM((BLOCK, WB), BF16),
            pltpu.VMEM((BLOCK, WA), BF16),
            pltpu.VMEM((8, 3 * HEADS), F32),
            pltpu.VMEM((BLOCK, HALF), F32),
            pltpu.VMEM((16, HALF), F32),
            pltpu.VMEM((7, 16, 128), F32),
            pltpu.VMEM((16, 128), F32),
            pltpu.VMEM((7, 16, 128), F32),
            pltpu.VMEM((BLOCK, 128), F32),
            pltpu.VMEM((BLOCK, 128), F32),
            dma((10,)),
            dma((2,)),
            dma((4,)),
            dma((8,)),
            dma((8,)),
            dma((45,)),
            dma((45,)),
            dma((36,)),
            dma((36,)),
            dma((3,)),
        ],
        compiler_params=pltpu.CompilerParams(
            collective_id=1, has_side_effects=True, vmem_limit_bytes=62 * 1024 * 1024
        ),
        name="backward",
    )(*args)


def adam_step(weight, first, second, gradient, rate):
    first_new = BETA_ONE * first + (1.0 - BETA_ONE) * gradient
    second_new = BETA_TWO * second + (1.0 - BETA_TWO) * gradient * gradient
    fix_one = 1.0 - BETA_ONE**STEP
    fix_two = 1.0 - BETA_TWO**STEP
    update = first_new / fix_one / (jnp.sqrt(second_new / fix_two) + ADAM_EPS)
    return (first_new, second_new, weight - rate * (update + DECAY * weight))


def update_kernel(
    ga, gb, vec_sum, hidden, back,
    qkv_w, qkv_m, qkv_v, dense_w, dense_m, dense_v, fc1_w, fc1_m, fc1_v, fc2_w, fc2_m, fc2_v,
    vec_w, vec_m, vec_v,
    hidden_out, back_out,
    qkv_mo, qkv_vo, qkv_wo, dense_mo, dense_vo, dense_wo, fc1_mo, fc1_vo, fc1_wo,
    fc2_mo, fc2_vo, fc2_wo, vec_mo, vec_vo, vec_wo,
):
    hidden_out[...] = hidden[...]
    back_out[...] = back[...]

    def step(w, m, v, mo, vo, wo, gradient, rate):
        mo[...], vo[...], wo[...] = adam_step(w[...], m[...], v[...], gradient, rate)

    step(fc1_w, fc1_m, fc1_v, fc1_mo, fc1_vo, fc1_wo, ga[0, :, 0:FFS].astype(F32), RATES[0])
    step(fc2_w, fc2_m, fc2_v, fc2_mo, fc2_vo, fc2_wo, gb[0, :, 0:FFS].astype(F32), RATES[1])
    step(
        dense_w, dense_m, dense_v, dense_mo, dense_vo, dense_wo, gb[0, :, FFS:WB].astype(F32), RATES[2]
    )
    for k in range(3):
        gradient = ga[0, :, FFS + k * HEADS : FFS + (k + 1) * HEADS].astype(F32)
        new = adam_step(qkv_w[:, k, :], qkv_m[:, k, :], qkv_v[:, k, :], gradient, RATES[0])
        qkv_mo[:, k, :], qkv_vo[:, k, :], qkv_wo[:, k, :] = new

    @pl.when(pl.program_id(0) == 0)
    def _():
        mine = pltpu.roll(vec_sum[...], lax.rem(128 - 16 * lax.axis_index("ctx"), 128), 1)
        step(vec_w, vec_m, vec_v, vec_mo, vec_vo, vec_wo, mine[0:11, 0:16], RATES[3])


def update(ga, gb, vec_sum, hidden, back, *state):
    def part(rows, width):
        return pl.BlockSpec((rows, width), lambda c: (0, c))

    vec = pl.BlockSpec((11, 16), lambda c: (0, 0))
    token = pl.BlockSpec((OWN, HALF), lambda c: (c, 0))
    sets = (
        [pl.BlockSpec((OWN, 3, HEADS), lambda c: (0, 0, c))] * 3
        + [part(OWN, HEADS)] * 3
        + [part(OWN, FFS)] * 6
        + [vec] * 3
    )
    wide = [pl.BlockSpec((1, OWN, w), lambda c: (c, 0, 0)) for w in (WA, WB)]
    shapes = [jax.ShapeDtypeStruct(x.shape, x.dtype) for x in (hidden, back, *state)]
    return pl.pallas_call(
        update_kernel,
        grid=(8,),
        out_shape=shapes,
        in_specs=wide + [pl.BlockSpec((16, 128), lambda c: (0, 0)), token, token] + sets,
        out_specs=[token, token] + sets,
        name="update",
    )(ga, gb, vec_sum, hidden, back, *state)


def on_device(
    hidden_in,
    grad_out,
    segment_ids,
    positions,
    qkv_weight,
    dense_weight,
    fc1_weight,
    fc2_weight,
    vectors,
    qkv_first,
    qkv_second,
    dense_first,
    dense_second,
    fc1_first,
    fc1_second,
    fc2_first,
    fc2_second,
    vector_first,
    vector_second,
):
    hid = hidden_in.reshape(BLOCK, HALF)
    grad = grad_out.reshape(BLOCK, HALF)
    (
        normed, grads, wa2, wb2, right, left, q, k_t, v, do, probs, sums, wave, vec_all, stats, bias,
    ) = forward(
        hid, grad, fc1_weight, qkv_weight, fc2_weight, dense_weight, vectors[0], segment_ids,
        positions,
    )
    hidden_out, grad_in, gb_all, ga_all, vec_sum = backward(
        right, wb2, left, wa2, normed, grads, q, k_t, v, do, probs, sums, wave,
        hid, grad, stats, vec_all, bias,
    )
    new = update(
        ga_all, gb_all, vec_sum, hidden_out, grad_in,
        qkv_weight, qkv_first, qkv_second, dense_weight, dense_first, dense_second,
        fc1_weight, fc1_first, fc1_second, fc2_weight, fc2_first, fc2_second,
        vectors[0], vector_first[0], vector_second[0],
    )
    return (
        new[0].reshape(hidden_in.shape),
        new[1].reshape(grad_out.shape),
        *new[2:14],
        *(x[None] for x in new[14:]),
    )


def solution(mesh):
    rows = P("dp", "ctx", "tensor")
    tokens = P("dp", "ctx")
    cube = P(("dp", "ctx"), None, "tensor")
    plain = P(("dp", "ctx"), "tensor")
    packed = P("tensor", None, ("dp", "ctx"))
    return jax.shard_map(
        on_device,
        mesh=mesh,
        in_specs=(rows, rows, tokens, tokens, cube, plain, plain, plain, packed)
        + (cube,) * 2
        + (plain,) * 6
        + (packed,) * 2,
        out_specs=(rows, rows) + (cube,) * 3 + (plain,) * 9 + (packed,) * 3,
        check_vma=False,
    )
```

```python
import functools
import math

import jax
import jax.numpy as jnp
import numpy as np
from jax import lax
from jax.experimental import pallas as pl
from jax.experimental.pallas import tpu as pltpu
from jax.sharding import PartitionSpec as P

D = 2048
HD = 64
ROT = 32
FF = 8192
STEP = 10
SEQ = 2048
BLOCK = 256
HALF = 1024
FFS = 512
HEADS = 128
WA = FFS + 3 * HEADS
WB = FFS + HEADS
OWN = 32

BETA_ONE = 0.9
BETA_TWO = 0.95
ADAM_EPS = 1e-08
DECAY = 0.1
NORM_EPS = 1e-05
MASKED = -1e30
GELU = math.sqrt(2.0 / math.pi)

RATES = (2.0 / math.sqrt(D), 2.0 / math.sqrt(FF), 2.0 / math.sqrt(D // 16), 0.6)
MESH = pl.DeviceIdType.MESH
F32 = jnp.float32
BF16 = jnp.bfloat16
OTHERS = tuple((k // 2, k % 2) for k in range(1, 8))


class Plane:
    def __init__(self, over_ctx):
        self.dp = lax.axis_index("dp")
        self.ctx = lax.axis_index("ctx")
        self.core = lax.axis_index("tensor")
        self.over_ctx = over_ctx
        if over_ctx:
            self.ring, self.pair = lax.div(self.ctx, 2), lax.rem(self.ctx, 2)
        else:
            self.ring, self.pair = lax.rem(self.dp, 4), lax.div(self.dp, 4)

    def spot(self, along, flip):
        ring = lax.rem(self.ring + along, 4) if along else self.ring
        pair = 1 - self.pair if flip else self.pair
        return ring * 2 + pair if self.over_ctx else pair * 4 + ring

    def spot_at(self, along, flip):
        ring, pair = lax.rem(self.ring + along, 4), lax.rem(self.pair + flip, 2)
        return ring * 2 + pair if self.over_ctx else pair * 4 + ring

    def device(self, along, flip):
        spot = self.spot(along, flip)
        return (self.dp, spot, self.core) if self.over_ctx else (spot, self.ctx, self.core)


def rows_at(index, size=BLOCK):
    return pl.ds(pl.multiple_of(index * size, size), size)


def remote(src, dst, sends, recvs, number, device):
    return pltpu.make_async_remote_copy(
        src_ref=src,
        dst_ref=dst,
        send_sem=sends.at[number],
        recv_sem=recvs.at[number],
        device_id=device,
        device_id_type=MESH,
    )


def greet(ctx_plane, dp_plane):
    barrier = pltpu.get_barrier_semaphore()
    partners = [ctx_plane.device(*o) for o in OTHERS] + [dp_plane.device(*o) for o in OTHERS]
    partners.append((ctx_plane.dp, ctx_plane.ctx, 1 - ctx_plane.core))
    for partner in partners:
        pl.semaphore_signal(barrier, inc=1, device_id=partner, device_id_type=MESH)
    pl.semaphore_wait(barrier, len(partners))


class Gather:
    def __init__(self, plane, own, region, sends, recvs, base):
        me = plane.spot(0, 0)

        def message(number, src, spot, part, along, flip):
            dst = region(spot, part)
            return remote(
                dst if src is None else src, dst, sends, recvs, base + number, plane.device(along, flip)
            )

        self.copies = [
            message(0, own, me, None, 1, 0),
            message(1, own, me, None, 3, 0),
            message(2, own, me, None, 0, 1),
            message(3, None, plane.spot(3, 0), 0, 1, 0),
            message(4, None, plane.spot(1, 0), 1, 3, 0),
            message(5, None, plane.spot(0, 1), None, 1, 0),
            message(6, None, plane.spot(0, 1), None, 3, 0),
            message(7, None, plane.spot(3, 1), 0, 1, 0),
            message(8, None, plane.spot(1, 1), 1, 3, 0),
        ]

    def begin_ring(self):
        self.copies[0].start()
        self.copies[1].start()

    def begin_pair(self):
        self.copies[2].start()

    def ring(self, flip):
        first, relay = (5, 7) if flip else (0, 3)
        for k in (0, 1):
            self.copies[first + k].wait_recv()
            self.copies[relay + k].start()

    def pair(self):
        self.copies[2].wait_recv()
        self.copies[5].start()
        self.copies[6].start()

    def far(self, flip):
        for k in (7, 8) if flip else (3, 4):
            self.copies[k].wait_recv()

    def end(self):
        for copy in self.copies:
            copy.wait_send()


class GatherCores(Gather):
    def __init__(self, plane, own, region, sends, recvs, base, core_sends, core_recvs, core_base):
        super().__init__(plane, own, region, sends, recvs, base)
        partner = (plane.dp, plane.ctx, 1 - plane.core)
        self.relays = {}
        for number, (along, flip) in enumerate(((0, 0),) + OTHERS):
            dst = region(plane.spot(along, flip), None)
            src = dst if number else own
            self.relays[along, flip] = remote(
                src, dst, core_sends, core_recvs, core_base + number, partner
            )

    def begin_ring(self):
        super().begin_ring()
        self.relays[0, 0].start()

    def ring(self, flip):
        super().ring(flip)
        self.relays[3, flip].start()
        self.relays[1, flip].start()

    def pair(self):
        super().pair()
        self.relays[0, 1].start()

    def far(self, flip):
        super().far(flip)
        self.relays[2, flip].start()

    def end(self):
        super().end()
        for copy in self.relays.values():
            copy.wait()


def dot_nt(left, right):
    return lax.dot_general(left, right, (((1,), (1,)), ((), ())), preferred_element_type=F32)


def dot_nn(left, right):
    return jnp.dot(left, right, preferred_element_type=F32)


def dot_tn(left, right):
    return lax.dot_general(left, right, (((0,), (0,)), ((), ())), preferred_element_type=F32)


def turn(values, cosine, sine, sign):
    lane = lax.rem(lax.broadcasted_iota(jnp.int32, values.shape, 1), HD)
    low = jnp.where(lane < ROT // 2, sine, 0.0)
    high = sine - low
    up = pltpu.roll(values, HEADS - ROT // 2, 1)
    down = pltpu.roll(values, ROT // 2, 1)
    return values * cosine + sign * (down * high - up * low)


def fold(values, op):
    return op(values.reshape(BLOCK // 8, 8, BLOCK), axis=0)


def nth_spot(plane, n, flip):
    along = n + lax.div(n, 2) - 2 * lax.div(n, 3)
    return plane.spot_at(along, flip)


def forward_kernel(
    hid, grad, fc1_in, qkv_in, fc2_in, dense_in, vectors, segments, positions,
    normed_out, grad_out, wa_out, wb_out, right_out, left_out,
    q_out, k_out, v_out, do_out, probs_out, sums_out, wave_out, vec_all, stats, bias_out,
    fc1, qkv_w, fc2, dense, wa, wb, vec, place, joined, other, normed, pieces, tile, table, place_all,
    normed_all, grad_all, wa_all, wb_all, slope, right, left, q_mask, k_mask, v_t, k_t, q_own, v_own, do_own,
    scores, probs, att_t, wave, sums,
    load, local, s_act, r_act, s_core, r_core, s_w, r_w, s_small, r_small, s_pair, r_pair, store, p_sem,
):
    plane, data = Plane(True), Plane(False)
    ctx, dp, core = plane.ctx, plane.dp, plane.core
    partner = (dp, ctx, 1 - core)

    def act_region(ref):
        columns = pl.ds(pl.multiple_of(core * HALF, HALF), HALF)

        def region(spot, part):
            if part is None:
                return ref.at[rows_at(spot), columns]
            start = pl.multiple_of(spot * BLOCK + part * (BLOCK // 2), BLOCK // 2)
            return ref.at[pl.ds(start, BLOCK // 2), columns]

        return region

    def weight_region(ref):
        def region(spot, part):
            if part is None:
                return ref.at[rows_at(spot), :]
            start = pl.multiple_of(spot * BLOCK + part * (BLOCK // 2), BLOCK // 2)
            return ref.at[pl.ds(start, BLOCK // 2), :]

        return region

    def scatter_rows(ref):
        start = pl.multiple_of(dp * BLOCK + ctx * OWN, OWN)
        return ref.at[pl.ds(start, OWN), :]

    sums[...] = jnp.zeros((8, SEQ), F32)
    vec_lane = lax.broadcasted_iota(jnp.int32, (1, 128), 1)
    loads = [
        pltpu.make_async_copy(src, dst, load.at[k])
        for k, (src, dst) in enumerate(
            ((fc1_in, fc1), (qkv_in, qkv_w), (fc2_in, fc2), (dense_in, dense))
        )
    ]
    for copy in loads:
        copy.start()
    greet(plane, data)
    hidden_copy = remote(hid, other, s_small, r_small, 0, partner)
    hidden_copy.start()
    vec[...] = jnp.zeros((16, 128), F32)
    for k in range(11):
        spread = jnp.concatenate([vectors[k]] * 8, axis=1)
        vec[k : k + 1, :] = jnp.where(lax.div(vec_lane, 16) == ctx, spread, 0.0)
    place[...] = jnp.zeros((8, BLOCK), jnp.int32)
    place[0:1, :] = segments[...]
    place[1:2, :] = positions[...]
    place_all[ctx] = place[...]
    tile[...] = vec[...].astype(BF16)
    piece_copies, tile_copies, place_copies, wa_copies, wb_copies = [], [], [], [], []
    for k, o in enumerate(OTHERS):
        to = plane.device(*o)
        spot = plane.spot(*o)
        piece_copies.append(remote(tile, pieces.at[k], s_small, r_small, 1 + k, to))
        place_copies.append(remote(place, place_all.at[ctx], s_small, r_small, 15 + k, to))
        wa_copies.append(remote(wa.at[spot], scatter_rows(wa_all), s_small, r_small, 22 + k, to))
        wb_copies.append(remote(wb.at[spot], scatter_rows(wb_all), s_small, r_small, 29 + k, to))
        columns = pl.ds(pl.multiple_of(dp * 128, 128), 128)
        tile_copies.append(
            remote(joined, table.at[:, columns], s_small, r_small, 8 + k, data.device(*o))
        )
    for copy in piece_copies + place_copies:
        copy.start()
    for copy in loads:
        copy.wait()
    for c in range(8):
        wa[c, :, 0:FFS] = fc1[:, c * FFS : (c + 1) * FFS].astype(BF16)
        wb[c, :, 0:FFS] = fc2[:, c * FFS : (c + 1) * FFS].astype(BF16)
        columns = slice(c * HEADS, (c + 1) * HEADS)
        wb[c, :, FFS:WB] = dense[:, columns].astype(BF16)
        for k in range(3):
            wa[c, :, FFS + k * HEADS : FFS + (k + 1) * HEADS] = qkv_w[k, :, columns].astype(BF16)
    for copy in wa_copies + wb_copies:
        copy.start()
    locals_ = [
        pltpu.make_async_copy(wa.at[ctx], scatter_rows(wa_all), local.at[0]),
        pltpu.make_async_copy(wb.at[ctx], scatter_rows(wb_all), local.at[1]),
        pltpu.make_async_copy(grad, act_region(grad_all)(ctx, None), local.at[2]),
        pltpu.make_async_copy(normed, act_region(normed_all)(ctx, None), local.at[3]),
    ]
    for copy in locals_[:3]:
        copy.start()

    normed_gather = GatherCores(
        plane, normed, act_region(normed_all), s_act, r_act, 0, s_core, r_core, 0
    )
    grad_gather = GatherCores(
        plane, grad, act_region(grad_all), s_act, r_act, 9, s_core, r_core, 8
    )

    for copy in piece_copies:
        copy.wait_recv()
    total = tile[...].astype(F32)
    for k in range(7):
        total = total + pieces[k].astype(F32)
    joined[...] = total.astype(BF16)
    table[:, pl.ds(pl.multiple_of(dp * 128, 128), 128)] = total.astype(BF16)
    for copy in tile_copies:
        copy.start()

    a_region, b_region = weight_region(wa_all), weight_region(wb_all)
    wa_gather = Gather(data, a_region(dp, None), a_region, s_w, r_w, 0)
    wb_gather = Gather(data, b_region(dp, None), b_region, s_w, r_w, 9)
    for copy in tile_copies:
        copy.wait_recv()
    hidden_copy.wait_recv()
    rows = table[...].astype(F32)
    vec_all[...] = rows
    gain, shift = rows[9:10], rows[10:11]
    lanes = lax.broadcasted_iota(jnp.int32, (16, 128), 1)

    def norm(i, carry):
        at = pl.ds(pl.multiple_of(i * 16, 16), 16)
        a, b = hid[at, :].astype(F32), other[at, :].astype(F32)
        mean = (jnp.sum(a, axis=1, keepdims=True) + jnp.sum(b, axis=1, keepdims=True)) / D
        a, b = a - mean, b - mean
        square = jnp.sum(a * a, axis=1, keepdims=True) + jnp.sum(b * b, axis=1, keepdims=True)
        inverse = lax.rsqrt(square / D + NORM_EPS)
        normed[at, :] = (a * inverse * gain + shift).astype(BF16)
        stats[at, :] = jnp.where(lanes < 64, mean, inverse)
        return carry

    lax.fori_loop(0, BLOCK // 16, norm, 0)
    for copy in wa_copies:
        copy.wait_recv()
    locals_[0].wait()
    wa_gather.begin_pair()
    wa_gather.begin_ring()
    normed_gather.begin_pair()
    normed_gather.begin_ring()
    locals_[3].start()
    for copy in place_copies:
        copy.wait_recv()
    lane = lax.broadcasted_iota(jnp.int32, (BLOCK, HEADS), 1)
    inner = lax.rem(lane, HD)
    first_head = lane < HD
    turning = inner < ROT
    wheel = lax.rem(lax.broadcasted_iota(jnp.int32, (1, HEADS), 1), ROT // 2)
    freq = jnp.zeros((1, HEADS), F32)
    for k in range(ROT // 2):
        freq = jnp.where(wheel == k, float(np.float32(10000.0 ** (-2.0 * k / ROT))), freq)

    def tables(i, carry):
        column = place_all[i].astype(F32).T
        angle = column[:, 1:2] * freq
        wave[0, rows_at(i), :] = jnp.where(turning, jnp.cos(angle), 1.0)
        wave[1, rows_at(i), :] = jnp.where(turning, jnp.sin(angle), 0.0)
        return carry

    lax.fori_loop(0, 8, tables, 0)

    for copy in wb_copies:
        copy.wait_recv()
    locals_[1].wait()
    wa_gather.ring(0)
    wa_gather.pair()
    normed_gather.ring(0)
    normed_gather.pair()
    grad_gather.begin_pair()
    wb_gather.begin_pair()
    wb_gather.begin_ring()
    wa_gather.ring(1)
    normed_gather.far(0)
    wa_gather.far(0)
    wa_gather.far(1)
    normed_gather.ring(1)
    my_rows = pl.ds(pl.multiple_of(core * HALF, HALF), HALF)
    their_rows = pl.ds(pl.multiple_of((1 - core) * HALF, HALF), HALF)
    pairs = [
        remote(wa_all.at[their_rows, :], wa_out.at[1], s_pair, r_pair, 0, partner),
        remote(wb_all.at[their_rows, :], wb_out.at[1], s_pair, r_pair, 1, partner),
    ]
    pairs[0].start()
    stores = [
        pltpu.make_async_copy(wa_all.at[my_rows, :], wa_out.at[0], store.at[0]),
        pltpu.make_async_copy(wb_all.at[my_rows, :], wb_out.at[0], store.at[1]),
        pltpu.make_async_copy(wave, wave_out, store.at[2]),
    ]
    stores[0].start()
    stores[2].start()

    qkv_bias = [
        vec_all[c : c + 1, pl.ds(pl.multiple_of(ctx * HEADS, HEADS), HEADS)] for c in range(3)
    ]
    fc1_bias = vec_all[
        pl.ds(3 + lax.div(ctx, 2), 1), pl.ds(pl.multiple_of(lax.rem(ctx, 2) * FFS, FFS), FFS)
    ]

    def project(spot):
        at = rows_at(spot)
        block = normed_all[at, :]
        x = dot_nn(block, wa_all[:, 0:FFS]) + fc1_bias
        square = x * x
        tanh = jnp.tanh(x * (GELU + (GELU * 0.044715) * square))
        half = 0.5 * (1.0 + tanh)
        bend = GELU + (3.0 * 0.044715 * GELU) * square
        slope[at, :] = half + 0.5 * x * (1.0 - tanh * tanh) * bend
        right[at, 0:FFS] = (x * half).astype(BF16)
        qkv = dot_nn(block, wa_all[:, FFS:WA])
        c, s = wave[0, at, :], wave[1, at, :]
        q = turn(qkv[:, 0:HEADS] + qkv_bias[0], c, s, 1.0).astype(BF16).astype(F32) * (HD**-0.5)
        k = turn(qkv[:, HEADS : 2 * HEADS] + qkv_bias[1], c, s, 1.0)
        v = qkv[:, 2 * HEADS : 3 * HEADS] + qkv_bias[2]
        segment = place_all[spot].astype(F32).T[:, 0:1]
        feature = jnp.where(segment == inner.astype(F32), 1.0, 0.0)
        barred = jnp.where(inner < 3, (1.0 - feature) * MASKED, 0.0)
        q_mask[0, at, :] = jnp.where(first_head, q, barred).astype(BF16)
        q_mask[1, at, :] = jnp.where(first_head, barred, q).astype(BF16)
        k_mask[0, at, :] = jnp.where(first_head, k, feature).astype(BF16)
        k_mask[1, at, :] = jnp.where(first_head, feature, k).astype(BF16)
        q_own[at, :] = q.astype(BF16)
        v_own[at, :] = v.astype(BF16)
        k_t[:, at] = k.T.astype(BF16)
        v_t[:, at] = v.T.astype(BF16)

    def project_ring(flip, start, end):
        def step(n, carry):
            project(nth_spot(plane, n, flip))
            return carry

        lax.fori_loop(start, end, step, 0)

    def keep_block(ref, out, o, number):
        at = rows_at(plane.spot(*o))
        copy = pltpu.make_async_copy(ref.at[at, :], out.at[at, :], store.at[number])
        copy.start()
        return copy

    locals_[3].wait()
    for o in ((0, 0), (1, 0), (3, 0), (2, 0)):
        normed_gather.relays[o].wait_recv()
    project_ring(0, 0, 2)
    normed_gather.far(1)
    grad_gather.begin_ring()
    wb_gather.ring(0)
    wb_gather.pair()
    project_ring(0, 2, 4)
    for o in ((0, 1), (1, 1), (3, 1), (2, 1)):
        normed_gather.relays[o].wait_recv()
    project_ring(1, 0, 2)
    wb_gather.ring(1)
    grad_gather.ring(0)
    grad_gather.pair()
    project_ring(1, 2, 4)
    normed_copies = [
        keep_block(normed_all, normed_out, (along, flip), 16 + 2 * along + flip)
        for flip in (0, 1)
        for along in range(4)
    ]
    small_stores = [
        pltpu.make_async_copy(q_own, q_out, store.at[4]),
        pltpu.make_async_copy(k_t, k_out, store.at[5]),
        pltpu.make_async_copy(v_own, v_out, store.at[6]),
    ]
    for copy in small_stores:
        copy.start()

    key_row = lax.broadcasted_iota(jnp.int32, (BLOCK, BLOCK), 0)
    query_col = lax.broadcasted_iota(jnp.int32, (BLOCK, BLOCK), 1)
    causal = key_row <= query_col
    prob_stores, right_copies, right_keeps = {}, [], []
    for i in range(8):
        own = pl.ds(i * BLOCK, BLOCK)
        slot = i % 2

        def raw(j, h):
            return dot_nt(k_mask[h, rows_at(j), :], q_mask[h, own, :])

        def score(j, carry):
            new = []
            for h in range(2):
                s = raw(j, h)
                scores[h, rows_at(j), :] = s
                new.append(jnp.maximum(carry[h], fold(s, jnp.max)))
            return tuple(new)

        low = jnp.full((8, BLOCK), MASKED, F32)
        maxima = lax.fori_loop(0, i, score, (low, low), unroll=True)
        tops = []
        for h in range(2):
            s = jnp.where(causal, raw(i, h), MASKED)
            scores[h, own, :] = s
            top = jnp.maximum(maxima[h], fold(s, jnp.max))
            tops.append(jnp.max(top, axis=0, keepdims=True))
        if i >= 2:
            prob_stores[i - 2].wait()

        def prob(j, carry):
            totals, outs = [], []
            for h in range(2):
                p = jnp.exp(scores[h, rows_at(j), :] - tops[h])
                totals.append(carry[0][h] + fold(p, jnp.sum))
                p = p.astype(BF16)
                probs[slot, h, rows_at(j), :] = p
                outs.append(carry[1][h] + dot_nn(v_t[pl.ds(h * HD, HD), rows_at(j)], p))
            return (tuple(totals), tuple(outs))

        zero_sum, zero_out = jnp.zeros((8, BLOCK), F32), jnp.zeros((HD, BLOCK), F32)
        totals, outs = lax.fori_loop(
            0, i + 1, prob, ((zero_sum, zero_sum), (zero_out, zero_out)), unroll=True
        )
        length = (i + 1) * BLOCK
        prob_stores[i] = pltpu.make_async_copy(
            probs.at[slot, :, pl.ds(0, length), :],
            probs_out.at[i, :, pl.ds(0, length), :],
            p_sem.at[slot],
        )
        prob_stores[i].start()
        scale = [1.0 / jnp.sum(totals[h], axis=0, keepdims=True) for h in range(2)]
        both = jnp.concatenate([outs[h] * scale[h] for h in range(2)], axis=0)
        sums[0:1, own] = scale[0]
        sums[1:2, own] = scale[1]
        att_t[:, own] = both
        right[own, FFS:WB] = both.T.astype(BF16)
        right_copies.append(
            remote(right.at[own, :], right_out.at[1, own, :], s_pair, r_pair, 2 + i, partner)
        )
        right_copies[i].start()
        right_keeps.append(
            pltpu.make_async_copy(right.at[own, :], right_out.at[0, own, :], store.at[7 + i])
        )
        right_keeps[i].start()
        if i == 3:
            wb_gather.far(0)
            wb_gather.far(1)
            pairs[1].start()
            stores[1].start()
        if i == 4:
            grad_gather.far(0)
        if i == 6:
            grad_gather.ring(1)

    bias_out[...] = jnp.zeros((8, FFS), F32)

    def back(spot):
        at = rows_at(spot)
        block = grad_all[at, :]
        d_pre = dot_nn(block, wb_all[:, 0:FFS]) * slope[at, :]
        rounded = d_pre.astype(BF16)
        left[at, :] = rounded
        whole = rounded.astype(F32)
        bias_out[...] += jnp.sum(whole.reshape(BLOCK // 8, 8, FFS), axis=0)
        d_att = dot_nn(block, wb_all[:, FFS:WB])
        do_own[at, :] = d_att.astype(BF16)
        product = att_t[:, at] * d_att.astype(BF16).astype(F32).T
        sums[2:3, at] = jnp.sum(product[0:HD], axis=0, keepdims=True)
        sums[3:4, at] = jnp.sum(product[HD:], axis=0, keepdims=True)

    def back_ring(flip, start, end):
        def step(n, carry):
            back(nth_spot(plane, n, flip))
            return carry

        lax.fori_loop(start, end, step, 0)

    locals_[2].wait()
    left_copies, left_keeps = [], []

    def send_left(o):
        k = len(left_copies)
        at = rows_at(plane.spot(*o))
        left_copies.append(
            remote(left.at[at, :], left_out.at[1, at, :], s_pair, r_pair, 10 + k, partner)
        )
        left_keeps.append(
            pltpu.make_async_copy(left.at[at, :], left_out.at[0, at, :], store.at[24 + k])
        )
        left_copies[k].start()
        left_keeps[k].start()

    for along in range(4):
        grad_gather.relays[along, 0].wait_recv()
    grad_copies = [
        keep_block(grad_all, grad_out, (along, 0), 32 + 2 * along) for along in range(4)
    ]
    back_ring(0, 0, 4)
    for along in range(4):
        send_left((along, 0))
    for along in (0, 1, 3):
        grad_gather.relays[along, 1].wait_recv()
        grad_copies.append(keep_block(grad_all, grad_out, (along, 1), 33 + 2 * along))
    back_ring(1, 0, 2)
    grad_gather.far(1)
    back_ring(1, 2, 3)
    for along in (0, 1, 3):
        send_left((along, 1))
    grad_gather.relays[2, 1].wait_recv()
    grad_copies.append(keep_block(grad_all, grad_out, (2, 1), 37))
    back_ring(1, 3, 4)
    send_left((2, 1))
    last_stores = [
        pltpu.make_async_copy(do_own, do_out, store.at[40]),
        pltpu.make_async_copy(sums, sums_out, store.at[41]),
    ]
    for copy in last_stores:
        copy.start()

    for gather in (grad_gather, normed_gather):
        for copy in gather.copies:
            copy.wait_send()
        for copy in gather.relays.values():
            copy.wait_send()
    wa_gather.end()
    wb_gather.end()
    hidden_copy.wait_send()
    for copy in piece_copies + tile_copies + wa_copies + wb_copies + place_copies:
        copy.wait_send()
    for copy in pairs + right_copies + left_copies:
        copy.wait()
    for copy in stores + small_stores + right_keeps + left_keeps + last_stores:
        copy.wait()
    for copy in normed_copies + grad_copies + [prob_stores[6], prob_stores[7]]:
        copy.wait()


def forward(*args):
    hbm = pl.BlockSpec(memory_space=pl.ANY)
    vmem = pl.BlockSpec(memory_space=pltpu.VMEM)
    dma = pltpu.SemaphoreType.DMA

    def shape(*dims, kind=BF16):
        return jax.ShapeDtypeStruct(dims, kind)

    return pl.pallas_call(
        forward_kernel,
        out_shape=(
            shape(SEQ, D),
            shape(SEQ, D),
            shape(2, HALF, WA),
            shape(2, HALF, WB),
            shape(2, SEQ, WB),
            shape(2, SEQ, FFS),
            shape(SEQ, HEADS),
            shape(HEADS, SEQ),
            shape(SEQ, HEADS),
            shape(SEQ, HEADS),
            shape(8, 2, SEQ, BLOCK),
            shape(8, SEQ, kind=F32),
            shape(2, SEQ, HEADS, kind=F32),
            shape(16, HALF, kind=F32),
            shape(BLOCK, 128, kind=F32),
            shape(8, FFS, kind=F32),
        ),
        in_specs=[vmem] + [hbm] * 5 + [vmem] * 3,
        out_specs=(hbm,) * 13 + (vmem,) * 3,
        scratch_shapes=[
            pltpu.VMEM((OWN, FF // 2), F32),
            pltpu.VMEM((3, OWN, HALF), F32),
            pltpu.VMEM((OWN, FF // 2), F32),
            pltpu.VMEM((OWN, HALF), F32),
            pltpu.VMEM((8, OWN, WA), BF16),
            pltpu.VMEM((8, OWN, WB), BF16),
            pltpu.VMEM((16, 128), F32),
            pltpu.VMEM((8, BLOCK), jnp.int32),
            pltpu.VMEM((16, 128), BF16),
            pltpu.VMEM((BLOCK, HALF), BF16),
            pltpu.VMEM((BLOCK, HALF), BF16),
            pltpu.VMEM((7, 16, 128), BF16),
            pltpu.VMEM((16, 128), BF16),
            pltpu.VMEM((16, HALF), BF16),
            pltpu.VMEM((8, 8, BLOCK), jnp.int32),
            pltpu.VMEM((SEQ, D), BF16),
            pltpu.VMEM((SEQ, D), BF16),
            pltpu.VMEM((D, WA), BF16),
            pltpu.VMEM((D, WB), BF16),
            pltpu.VMEM((SEQ, FFS), F32),
            pltpu.VMEM((SEQ, WB), BF16),
            pltpu.VMEM((SEQ, FFS), BF16),
            pltpu.VMEM((2, SEQ, HEADS), BF16),
            pltpu.VMEM((2, SEQ, HEADS), BF16),
            pltpu.VMEM((HEADS, SEQ), BF16),
            pltpu.VMEM((HEADS, SEQ), BF16),
            pltpu.VMEM((SEQ, HEADS), BF16),
            pltpu.VMEM((SEQ, HEADS), BF16),
            pltpu.VMEM((SEQ, HEADS), BF16),
            pltpu.VMEM((2, SEQ, BLOCK), F32),
            pltpu.VMEM((2, 2, SEQ, BLOCK), BF16),
            pltpu.VMEM((HEADS, SEQ), F32),
            pltpu.VMEM((2, SEQ, HEADS), F32),
            pltpu.VMEM((8, SEQ), F32),
            dma((4,)),
            dma((4,)),
            dma((18,)),
            dma((18,)),
            dma((16,)),
            dma((16,)),
            dma((18,)),
            dma((18,)),
            dma((36,)),
            dma((36,)),
            dma((18,)),
            dma((18,)),
            dma((42,)),
            dma((2,)),
        ],
        compiler_params=pltpu.CompilerParams(
            collective_id=0, has_side_effects=True, vmem_limit_bytes=62 * 1024 * 1024
        ),
        name="forward",
    )(*args)


def add_rows(dst, terms, count, chunk):
    def step(i, carry):
        at = pl.ds(pl.multiple_of(i * chunk, chunk), chunk)
        total = terms[0][at, :].astype(F32)
        for term in terms[1:]:
            total = total + term[at, :].astype(F32)
        dst[at, :] = total.astype(dst.dtype)
        return carry

    lax.fori_loop(0, count // chunk, step, 0)


class Reduce:
    def __init__(self, plane, acc, landing, sends, recvs, base):
        half_up, half_down, up, down, across = landing
        self.plane, self.acc, self.across = plane, acc, across
        self.near = (half_up, half_down, up, down)
        self.rows = across.shape[0]
        self.chunk = 16
        half = self.half = self.rows // 2
        self.copies = []
        for j, flip in ((0, 1), (1, 0)):
            far = plane.spot(2, flip)
            for number, (src, dst, along) in enumerate(
                (
                    (acc.at[far, pl.ds(0, half), :], half_up.at[j], 1),
                    (acc.at[far, pl.ds(half, half), :], half_down.at[j], 3),
                    (acc.at[plane.spot(1, flip)], up.at[j], 1),
                    (acc.at[plane.spot(3, flip)], down.at[j], 3),
                )
            ):
                self.copies.append(
                    remote(src, dst, sends, recvs, base + 4 * j + number, plane.device(along, 0))
                )
        self.copies.append(
            remote(acc.at[plane.spot(0, 1)], across, sends, recvs, base + 8, plane.device(0, 1))
        )

    def first(self, j):
        self.copies[4 * j].start()
        self.copies[4 * j + 1].start()

    def second(self, j):
        half = self.half
        for number, along in ((0, 1), (1, 3)):
            self.copies[4 * j + number].wait_recv()
            dst = self.acc.at[self.plane.spot(along, 1 - j), pl.ds(number * half, half), :]
            add_rows(dst, [dst, self.near[number].at[j]], half, self.chunk)
            self.copies[4 * j + number + 2].start()

    def third(self):
        self.copies[2].wait_recv()
        self.copies[3].wait_recv()
        dst = self.acc.at[self.plane.spot(0, 1)]
        add_rows(dst, [dst, self.near[2].at[0], self.near[3].at[0]], self.rows, self.chunk)
        self.copies[8].start()

    def arrived(self):
        for k in (6, 7, 8):
            self.copies[k].wait_recv()
        mine = self.acc.at[self.plane.spot(0, 0)]
        return [mine, self.near[2].at[1], self.near[3].at[1], self.across]

    def last(self, dst):
        add_rows(dst, self.arrived(), self.rows, self.chunk)

    def end(self):
        for copy in self.copies:
            copy.wait_send()


def backward_kernel(
    right_in, wb_in, left_in, wa_in, normed, grads, q_in, k_in, v_in, do_in,
    probs_in, sums, wave_in, hid, grad, stats, vec_all, bias_in,
    hidden_out, grad_in, gb_all, ga_all, vec_sum,
    right, left, weight, stream, q_all, k_t, v_all, do_all, probs_odd, probs_even, wave, d_k, d_v,
    out_acc, dx_acc, gb_acc, ga_acc,
    out_a, out_b, out_c, out_d, out_e, dx_a, dx_b, dx_c, dx_d, dx_e, gb_a, gb_b, gb_c, gb_d, gb_e,
    ga_a, ga_b, ga_c, ga_d, ga_e, gb_done, ga_done, bias, final, vec, vec_in, vec_tile, tile_in, row_own, row_in,
    load, s_stream, s_probs, s_pair, r_pair, s_red, r_red, s_small, r_small, keep,
):
    plane, data = Plane(True), Plane(False)
    ctx, dp, core = plane.ctx, plane.dp, plane.core
    partner = (dp, ctx, 1 - core)
    loads = {
        "weight": pltpu.make_async_copy(wb_in, weight.at[:, :, pl.ds(0, WB)], load.at[0]),
        "right": pltpu.make_async_copy(right_in, right, load.at[1]),
        "left": pltpu.make_async_copy(left_in, left.at[:, :, pl.ds(0, FFS)], load.at[2]),
        "q": pltpu.make_async_copy(q_in, q_all, load.at[4]),
        "k": pltpu.make_async_copy(k_in, k_t, load.at[5]),
        "v": pltpu.make_async_copy(v_in, v_all, load.at[6]),
        "do": pltpu.make_async_copy(do_in, do_all, load.at[7]),
    }
    for copy in loads.values():
        copy.start()
    greet(plane, data)

    out = Reduce(plane, out_acc, (out_a, out_b, out_c, out_d, out_e), s_red, r_red, 0)
    dx = Reduce(plane, dx_acc, (dx_a, dx_b, dx_c, dx_d, dx_e), s_red, r_red, 9)
    gb = Reduce(data, gb_acc, (gb_a, gb_b, gb_c, gb_d, gb_e), s_red, r_red, 18)
    ga = Reduce(data, ga_acc, (ga_a, ga_b, ga_c, ga_d, ga_e), s_red, r_red, 27)

    def spot_of(where, n):
        group = lax.div(n + 2, 4)
        inside = n + 2 - 4 * group
        near = 1 - lax.rem(group + 1, 2)
        along = near * (1 + 2 * lax.rem(inside, 2)) + (1 - near) * (2 - group)
        flip = near * (1 - lax.div(inside, 2)) + (1 - near) * (1 - lax.rem(inside, 2))
        return where.spot_at(along, flip)

    def out_block(n, carry):
        spot = spot_of(plane, n)
        at = rows_at(spot)
        total = dot_nt(right[0, at, :], weight[0, :, 0:WB])
        total = total + dot_nt(right[1, at, :], weight[1, :, 0:WB])
        out_acc[spot] = total.astype(BF16)
        return carry

    def dx_block(n, carry):
        spot = spot_of(plane, n)
        at = rows_at(spot)
        total = dot_nt(left[0, at, :], weight[0])
        total = total + dot_nt(left[1, at, :], weight[1])
        dx_acc[spot] = total.astype(BF16)
        return carry

    def fetch(source, n):
        columns = rows_at(spot_of(data, n))
        slot = lax.rem(n, 2)
        return pltpu.make_async_copy(source.at[:, columns], stream.at[slot], s_stream.at[slot])

    def weight_blocks(source, factor, acc, start, end):
        def step(n, carry):
            @pl.when(n < 7)
            def _():
                fetch(source, n + 1).start()

            fetch(source, n).wait()
            total = dot_tn(stream[lax.rem(n, 2)], factor[0])
            acc[spot_of(data, n)] = total.astype(BF16)
            return carry

        lax.fori_loop(start, end, step, 0)

    loads["weight"].wait()
    loads["right"].wait()
    lax.fori_loop(0, 1, out_block, 0)
    out.first(0)
    lax.fori_loop(1, 4, out_block, 0)
    fetch(grads, 0).start()
    out.second(0)
    out.first(1)
    lax.fori_loop(4, 8, out_block, 0)
    weight_load = pltpu.make_async_copy(wa_in, weight, load.at[8])
    weight_load.start()

    lane = lax.broadcasted_iota(jnp.int32, (BLOCK, HEADS), 1)
    heads = (lane < HD, lane >= HD)
    bias[...] = jnp.zeros((8, 3 * HEADS), F32)

    def clear(i, carry):
        d_k[rows_at(i), :] = jnp.zeros((BLOCK, HEADS), F32)
        d_v[rows_at(i), :] = jnp.zeros((BLOCK, HEADS), F32)
        return carry

    lax.fori_loop(0, 8, clear, 0)

    def probs_of(i):
        length = pl.ds(0, (i + 1) * BLOCK)
        buffer = probs_odd if i % 2 else probs_even
        return [
            pltpu.make_async_copy(
                probs_in.at[i, :, length, :], buffer.at[:, length, :], s_probs.at[i % 2]
            ),
            pltpu.make_async_copy(
                wave_in.at[:, pl.ds(i * BLOCK, BLOCK), :], wave.at[i % 2], s_probs.at[2 + i % 2]
            ),
        ]

    for name in ("q", "k", "v", "do"):
        loads[name].wait()
    arriving = {7: probs_of(7)}
    for copy in arriving[7]:
        copy.start()
    swaps = []
    for i in range(7, -1, -1):
        own = pl.ds(i * BLOCK, BLOCK)
        if i:
            arriving[i - 1] = probs_of(i - 1)
            for copy in arriving[i - 1]:
                copy.start()
        for copy in arriving[i]:
            copy.wait()
        probs = probs_odd if i % 2 else probs_even
        scale = [sums[h : h + 1, own] for h in range(2)]
        delta = [sums[2 + h : 3 + h, own] for h in range(2)]
        q, do = q_all[own, :].astype(F32), do_all[own, :].astype(F32)
        q_plain = [jnp.where(heads[h], q, 0.0).astype(BF16) for h in range(2)]
        do_plain = [jnp.where(heads[h], do, 0.0).astype(BF16) for h in range(2)]

        def back(j, carry):
            at, new = rows_at(j), []
            add_k, add_v = d_k[at, :], d_v[at, :]
            for h in range(2):
                p = probs[h, at, :].astype(F32) * scale[h]
                d_p = dot_nt(v_all[at, :], do_plain[h])
                d_s = (p * (d_p - delta[h])).astype(BF16)
                add_v = add_v + dot_nn(p.astype(BF16), do_plain[h])
                add_k = add_k + dot_nn(d_s, q_plain[h])
                new.append(carry[h] + dot_nn(k_t[pl.ds(h * HD, HD), at], d_s))
            d_k[at, :] = add_k
            d_v[at, :] = add_v
            return tuple(new)

        zero_out = jnp.zeros((HD, BLOCK), F32)
        d_q = lax.fori_loop(0, i + 1, back, (zero_out, zero_out), unroll=True)
        d_q = jnp.concatenate(d_q, axis=0).T * (HD**-0.5)
        c, s = wave[i % 2, 0], wave[i % 2, 1]
        parts = (turn(d_q, c, s, -1.0), turn(d_k[own, :], c, s, -1.0), d_v[own, :])
        for k, part in enumerate(parts):
            rounded = part.astype(BF16)
            whole = rounded.astype(F32)
            left[0, own, FFS + k * HEADS : FFS + (k + 1) * HEADS] = rounded
            columns = slice(k * HEADS, (k + 1) * HEADS)
            bias[:, columns] += jnp.sum(whole.reshape(BLOCK // 8, 8, HEADS), axis=0)
        span = pl.ds(FFS, 3 * HEADS)
        swap = remote(
            left.at[0, own, span], left.at[1, own, span], s_pair, r_pair, i, partner
        )
        swap.start()
        swaps.append(swap)
        if i == 5:
            out.second(1)

    out.third()
    loads["left"].wait()
    weight_load.wait()
    weight_blocks(grads, right, gb_acc, 0, 1)
    gb.first(0)
    weight_blocks(grads, right, gb_acc, 1, 4)
    for swap in swaps:
        swap.wait_recv()
    lax.fori_loop(0, 1, dx_block, 0)
    dx.first(0)
    gb.second(0)
    gb.first(1)
    lax.fori_loop(1, 4, dx_block, 0)
    dx.second(0)
    dx.first(1)
    weight_blocks(grads, right, gb_acc, 4, 8)
    fetch(normed, 0).start()
    gb.second(1)
    lax.fori_loop(4, 6, dx_block, 0)
    weight_blocks(normed, left, ga_acc, 0, 1)
    ga.first(0)
    weight_blocks(normed, left, ga_acc, 1, 3)
    dx.second(1)
    gb.third()
    weight_blocks(normed, left, ga_acc, 3, 4)
    ga.second(0)
    ga.first(1)
    lax.fori_loop(6, 8, dx_block, 0)
    dx.third()
    weight_blocks(normed, left, ga_acc, 4, 8)
    ga.second(1)
    gb.last(gb_done)

    copies = {}
    keeps = []
    for n, (name, done, landed) in enumerate(
        (("gb", gb_done, gb_all), ("ga", ga_done, ga_all))
    ):
        copies[name] = [
            remote(
                done.at[rows_at(plane.spot(*o), OWN), :],
                landed.at[ctx],
                s_small,
                r_small,
                15 + 7 * n + k,
                plane.device(*o),
            )
            for k, o in enumerate(OTHERS)
        ]
        keeps.append(
            pltpu.make_async_copy(done.at[rows_at(ctx, OWN), :], landed.at[ctx], keep.at[n])
        )
    for copy in copies["gb"]:
        copy.start()
    keeps[0].start()

    out.last(final)
    bias_rows = vec_all[7:8, :] + vec_all[8:9, :]

    def add_hidden(i, carry):
        at = pl.ds(pl.multiple_of(i * 16, 16), 16)
        hidden_out[at, :] = (hid[at, :].astype(F32) + final[at, :] + bias_rows).astype(BF16)
        return carry

    lax.fori_loop(0, BLOCK // 16, add_hidden, 0)
    ga.third()
    dx.last(final)
    gain = vec_all[9:10, :]
    lanes = lax.broadcasted_iota(jnp.int32, (16, 128), 1)

    def lean(i, carry):
        at = pl.ds(pl.multiple_of(i * 16, 16), 16)
        d, h, stat = final[at, :], hid[at, :].astype(F32), stats[at, :]
        normal = (h - stat[:, 0:1]) * stat[:, 64:65]
        product = d * normal
        one = jnp.sum(d * gain, axis=1, keepdims=True)
        two = jnp.sum(product * gain, axis=1, keepdims=True)
        row_own[at, :] = jnp.where(lanes < 64, one, two)
        return (carry[0] + d, carry[1] + product, carry[2] + grad[at, :].astype(F32))

    zero = jnp.zeros((16, HALF), F32)
    rows = lax.fori_loop(0, BLOCK // 16, lean, (zero, zero, zero))
    row_copy = remote(row_own, row_in, s_small, r_small, 0, partner)
    row_copy.start()
    shift_grad, gain_grad, bias_grad = [jnp.sum(r, axis=0, keepdims=True) for r in rows]
    number = lax.broadcasted_iota(jnp.int32, (16, HALF), 0)
    vec[...] = jnp.where(
        number == 9,
        gain_grad,
        jnp.where(
            number == 10, shift_grad, jnp.where((number == 7) | (number == 8), bias_grad, 0.0)
        ),
    )
    columns = pl.ds(pl.multiple_of(ctx * HEADS, HEADS), HEADS)
    for k in range(3):
        part = jnp.sum(bias[:, k * HEADS : (k + 1) * HEADS], axis=0, keepdims=True)
        vec[k : k + 1, columns] = part
    columns = pl.ds(pl.multiple_of(lax.rem(ctx, 2) * FFS, FFS), FFS)
    part = jnp.sum(bias_in[...], axis=0, keepdims=True)
    vec[:, columns] = jnp.where(
        lax.broadcasted_iota(jnp.int32, (16, FFS), 0) == 3 + lax.div(ctx, 2), part, vec[:, columns]
    )
    vec_copies, tile_copies = [], []
    for k, o in enumerate(OTHERS):
        columns = pl.ds(pl.multiple_of(data.spot(*o) * 128, 128), 128)
        vec_copies.append(
            remote(vec.at[:, columns], vec_in.at[k], s_small, r_small, 1 + k, data.device(*o))
        )
        tile_copies.append(
            remote(vec_tile, tile_in.at[k], s_small, r_small, 8 + k, plane.device(*o))
        )
    for copy in vec_copies:
        copy.start()
    ga.last(ga_done)
    for copy in copies["ga"]:
        copy.start()
    keeps[1].start()
    for copy in vec_copies:
        copy.wait_recv()
    total = vec[:, pl.ds(pl.multiple_of(dp * 128, 128), 128)]
    for k in range(7):
        total = total + vec_in[k]
    vec_tile[...] = total
    for copy in tile_copies:
        copy.start()

    row_copy.wait()

    def tilt(i, carry):
        at = pl.ds(pl.multiple_of(i * 16, 16), 16)
        d, h, stat = final[at, :], hid[at, :].astype(F32), stats[at, :]
        inverse = stat[:, 64:65]
        normal = (h - stat[:, 0:1]) * inverse
        row = (row_own[at, :] + row_in[at, :]) / D
        change = inverse * (d * gain - row[:, 0:1] - normal * row[:, 64:65])
        grad_in[at, :] = (grad[at, :].astype(F32) + change).astype(BF16)
        return carry

    lax.fori_loop(0, BLOCK // 16, tilt, 0)
    for copy in tile_copies:
        copy.wait_recv()
    total = vec_tile[...]
    for k in range(7):
        total = total + tile_in[k]
    vec_sum[...] = total

    for name in copies:
        for copy in copies[name]:
            copy.wait()
    for copy in keeps:
        copy.wait()
    for copy in vec_copies + tile_copies + swaps:
        copy.wait_send()
    for red in (dx, out, gb, ga):
        red.end()


def backward(*args):
    hbm = pl.BlockSpec(memory_space=pl.ANY)
    vmem = pl.BlockSpec(memory_space=pltpu.VMEM)
    dma = pltpu.SemaphoreType.DMA

    def landing(rows, width):
        half = pltpu.VMEM((2, rows // 2, width), BF16)
        whole = pltpu.VMEM((2, rows, width), BF16)
        return [half, half, whole, whole, pltpu.VMEM((rows, width), BF16)]

    def shape(*dims, kind=BF16):
        return jax.ShapeDtypeStruct(dims, kind)

    return pl.pallas_call(
        backward_kernel,
        out_shape=(
            shape(BLOCK, HALF),
            shape(BLOCK, HALF),
            shape(8, OWN, WB),
            shape(8, OWN, WA),
            shape(16, 128, kind=F32),
        ),
        in_specs=[hbm] * 11 + [vmem, hbm] + [vmem] * 5,
        out_specs=(vmem, vmem, hbm, hbm, vmem),
        scratch_shapes=[
            pltpu.VMEM((2, SEQ, WB), BF16),
            pltpu.VMEM((2, SEQ, WA), BF16),
            pltpu.VMEM((2, HALF, WA), BF16),
            pltpu.VMEM((2, SEQ, BLOCK), BF16),
            pltpu.VMEM((SEQ, HEADS), BF16),
            pltpu.VMEM((HEADS, SEQ), BF16),
            pltpu.VMEM((SEQ, HEADS), BF16),
            pltpu.VMEM((SEQ, HEADS), BF16),
            pltpu.VMEM((2, SEQ, BLOCK), BF16),
            pltpu.VMEM((2, SEQ - BLOCK, BLOCK), BF16),
            pltpu.VMEM((2, 2, BLOCK, HEADS), F32),
            pltpu.VMEM((SEQ, HEADS), F32),
            pltpu.VMEM((SEQ, HEADS), F32),
            pltpu.VMEM((8, BLOCK, HALF), BF16),
            pltpu.VMEM((8, BLOCK, HALF), BF16),
            pltpu.VMEM((8, BLOCK, WB), BF16),
            pltpu.VMEM((8, BLOCK, WA), BF16),
            *landing(BLOCK, HALF),
            *landing(BLOCK, HALF),
            *landing(BLOCK, WB),
            *landing(BLOCK, WA),
            pltpu.VMEM((BLOCK, WB), BF16),
            pltpu.VMEM((BLOCK, WA), BF16),
            pltpu.VMEM((8, 3 * HEADS), F32),
            pltpu.VMEM((BLOCK, HALF), F32),
            pltpu.VMEM((16, HALF), F32),
            pltpu.VMEM((7, 16, 128), F32),
            pltpu.VMEM((16, 128), F32),
            pltpu.VMEM((7, 16, 128), F32),
            pltpu.VMEM((BLOCK, 128), F32),
            pltpu.VMEM((BLOCK, 128), F32),
            dma((10,)),
            dma((2,)),
            dma((4,)),
            dma((8,)),
            dma((8,)),
            dma((45,)),
            dma((45,)),
            dma((36,)),
            dma((36,)),
            dma((3,)),
        ],
        compiler_params=pltpu.CompilerParams(
            collective_id=1, has_side_effects=True, vmem_limit_bytes=62 * 1024 * 1024
        ),
        name="backward",
    )(*args)


def adam_step(weight, first, second, gradient, rate):
    first_new = BETA_ONE * first + (1.0 - BETA_ONE) * gradient
    second_new = BETA_TWO * second + (1.0 - BETA_TWO) * gradient * gradient
    fix_one = 1.0 - BETA_ONE**STEP
    fix_two = 1.0 - BETA_TWO**STEP
    update = first_new / fix_one / (jnp.sqrt(second_new / fix_two) + ADAM_EPS)
    return (first_new, second_new, weight - rate * (update + DECAY * weight))


def update_kernel(
    ga, gb, vec_sum, hidden, back,
    qkv_w, qkv_m, qkv_v, dense_w, dense_m, dense_v, fc1_w, fc1_m, fc1_v, fc2_w, fc2_m, fc2_v,
    vec_w, vec_m, vec_v,
    hidden_out, back_out,
    qkv_mo, qkv_vo, qkv_wo, dense_mo, dense_vo, dense_wo, fc1_mo, fc1_vo, fc1_wo,
    fc2_mo, fc2_vo, fc2_wo, vec_mo, vec_vo, vec_wo,
):
    hidden_out[...] = hidden[...]
    back_out[...] = back[...]

    fc1 = (fc1_w, fc1_m, fc1_v, fc1_mo, fc1_vo, fc1_wo)
    fc2 = (fc2_w, fc2_m, fc2_v, fc2_mo, fc2_vo, fc2_wo)
    dense = (dense_w, dense_m, dense_v, dense_mo, dense_vo, dense_wo)
    qkv = (qkv_w, qkv_m, qkv_v, qkv_mo, qkv_vo, qkv_wo)
    vec = (vec_w, vec_m, vec_v, vec_mo, vec_vo, vec_wo)

    def step(refs, gradient, rate, *at):
        w, m, v, mo, vo, wo = refs
        mo[at], vo[at], wo[at] = adam_step(w[at], m[at], v[at], gradient, rate)

    for c in range(8):
        wide, narrow = slice(c * FFS, (c + 1) * FFS), slice(c * HEADS, (c + 1) * HEADS)
        step(fc1, ga[c, :, 0:FFS].astype(F32), RATES[0], slice(None), wide)
        step(fc2, gb[c, :, 0:FFS].astype(F32), RATES[1], slice(None), wide)
        step(dense, gb[c, :, FFS:WB].astype(F32), RATES[2], slice(None), narrow)
        for k in range(3):
            columns = slice(FFS + k * HEADS, FFS + (k + 1) * HEADS)
            step(qkv, ga[c, :, columns].astype(F32), RATES[0], k, slice(None), narrow)

    @pl.when(pl.program_id(0) == 0)
    def _():
        mine = pltpu.roll(vec_sum[...], lax.rem(128 - 16 * lax.axis_index("ctx"), 128), 1)
        for k in range(11):
            step(vec, mine[k : k + 1, 0:16], RATES[3], k)


def update(ga, gb, vec_sum, hidden, back, *state):
    steps = 2
    rows = OWN // steps

    def part(width):
        return pl.BlockSpec((rows, width), lambda n: (n, 0))

    vec = pl.BlockSpec((11, 1, 16), lambda n: (0, 0, 0))
    token = pl.BlockSpec((BLOCK // steps, HALF), lambda n: (n, 0))
    sets = (
        [pl.BlockSpec((3, rows, HALF), lambda n: (0, n, 0))] * 3
        + [part(HALF)] * 3
        + [part(FF // 2)] * 6
        + [vec] * 3
    )
    wide = [pl.BlockSpec((8, rows, w), lambda n: (0, n, 0)) for w in (WA, WB)]
    shapes = [jax.ShapeDtypeStruct(x.shape, x.dtype) for x in (hidden, back, *state)]
    return pl.pallas_call(
        update_kernel,
        grid=(steps,),
        out_shape=shapes,
        in_specs=wide + [pl.BlockSpec((16, 128), lambda n: (0, 0)), token, token] + sets,
        out_specs=[token, token] + sets,
        compiler_params=pltpu.CompilerParams(vmem_limit_bytes=40 * 1024 * 1024),
        name="update",
    )(ga, gb, vec_sum, hidden, back, *state)


def on_device(
    hidden_in,
    grad_out,
    segment_ids,
    positions,
    qkv_weight,
    dense_weight,
    fc1_weight,
    fc2_weight,
    vectors,
    qkv_first,
    qkv_second,
    dense_first,
    dense_second,
    fc1_first,
    fc1_second,
    fc2_first,
    fc2_second,
    vector_first,
    vector_second,
):
    hid = hidden_in.reshape(BLOCK, HALF)
    grad = grad_out.reshape(BLOCK, HALF)

    def turned(array):
        return jnp.moveaxis(array, 1, 0)

    (
        normed, grads, wa2, wb2, right, left, q, k_t, v, do, probs, sums, wave, vec_all, stats, bias,
    ) = forward(
        hid, grad, fc1_weight, turned(qkv_weight), fc2_weight, dense_weight, turned(vectors),
        segment_ids, positions,
    )
    hidden_out, grad_in, gb_all, ga_all, vec_sum = backward(
        right, wb2, left, wa2, normed, grads, q, k_t, v, do, probs, sums, wave,
        hid, grad, stats, vec_all, bias,
    )
    new = update(
        ga_all, gb_all, vec_sum, hidden_out, grad_in,
        turned(qkv_weight), turned(qkv_first), turned(qkv_second),
        dense_weight, dense_first, dense_second,
        fc1_weight, fc1_first, fc1_second, fc2_weight, fc2_first, fc2_second,
        turned(vectors), turned(vector_first), turned(vector_second),
    )
    return (
        new[0].reshape(hidden_in.shape),
        new[1].reshape(grad_out.shape),
        *(turned(x) for x in new[2:5]),
        *new[5:14],
        *(turned(x) for x in new[14:]),
    )


def solution(mesh):
    rows = P("dp", "ctx", "tensor")
    tokens = P("dp", "ctx")
    cube = P(("dp", "ctx"), None, "tensor")
    plain = P(("dp", "ctx"), "tensor")
    packed = P("tensor", None, ("dp", "ctx"))
    return jax.shard_map(
        on_device,
        mesh=mesh,
        in_specs=(rows, rows, tokens, tokens, cube, plain, plain, plain, packed)
        + (cube,) * 2
        + (plain,) * 6
        + (packed,) * 2,
        out_specs=(rows, rows) + (cube,) * 3 + (plain,) * 9 + (packed,) * 3,
        check_vma=False,
    )
```

```python
import functools
import math

import jax
import jax.numpy as jnp
import numpy as np
from jax import lax
from jax.experimental import pallas as pl
from jax.experimental.pallas import tpu as pltpu
from jax.sharding import PartitionSpec as P

D = 2048
HD = 64
ROT = 32
FF = 8192
STEP = 10
SEQ = 2048
BLOCK = 256
HALF = 1024
FFS = 512
HEADS = 128
WA = FFS + 3 * HEADS
WB = FFS + HEADS
OWN = 32

BETA_ONE = 0.9
BETA_TWO = 0.95
ADAM_EPS = 1e-08
DECAY = 0.1
NORM_EPS = 1e-05
MASKED = -1e30
GELU = math.sqrt(2.0 / math.pi)

RATES = (2.0 / math.sqrt(D), 2.0 / math.sqrt(FF), 2.0 / math.sqrt(D // 16), 0.6)
MESH = pl.DeviceIdType.MESH
F32 = jnp.float32
BF16 = jnp.bfloat16
OTHERS = tuple((k // 2, k % 2) for k in range(1, 8))


class Plane:
    def __init__(self, over_ctx):
        self.dp = lax.axis_index("dp")
        self.ctx = lax.axis_index("ctx")
        self.core = lax.axis_index("tensor")
        self.over_ctx = over_ctx
        if over_ctx:
            self.ring, self.pair = lax.div(self.ctx, 2), lax.rem(self.ctx, 2)
        else:
            self.ring, self.pair = lax.rem(self.dp, 4), lax.div(self.dp, 4)

    def spot(self, along, flip):
        ring = lax.rem(self.ring + along, 4) if along else self.ring
        pair = 1 - self.pair if flip else self.pair
        return ring * 2 + pair if self.over_ctx else pair * 4 + ring

    def spot_at(self, along, flip):
        ring, pair = lax.rem(self.ring + along, 4), lax.rem(self.pair + flip, 2)
        return ring * 2 + pair if self.over_ctx else pair * 4 + ring

    def device(self, along, flip):
        spot = self.spot(along, flip)
        return (self.dp, spot, self.core) if self.over_ctx else (spot, self.ctx, self.core)


def rows_at(index, size=BLOCK):
    return pl.ds(pl.multiple_of(index * size, size), size)


def remote(src, dst, sends, recvs, number, device):
    return pltpu.make_async_remote_copy(
        src_ref=src,
        dst_ref=dst,
        send_sem=sends.at[number],
        recv_sem=recvs.at[number],
        device_id=device,
        device_id_type=MESH,
    )


def greet(ctx_plane, dp_plane):
    barrier = pltpu.get_barrier_semaphore()
    partners = [ctx_plane.device(*o) for o in OTHERS] + [dp_plane.device(*o) for o in OTHERS]
    partners.append((ctx_plane.dp, ctx_plane.ctx, 1 - ctx_plane.core))
    for partner in partners:
        pl.semaphore_signal(barrier, inc=1, device_id=partner, device_id_type=MESH)
    pl.semaphore_wait(barrier, len(partners))


class Gather:
    def __init__(self, plane, own, region, sends, recvs, base):
        me = plane.spot(0, 0)

        def message(number, src, spot, part, along, flip):
            dst = region(spot, part)
            return remote(
                dst if src is None else src, dst, sends, recvs, base + number, plane.device(along, flip)
            )

        self.copies = [
            message(0, own, me, None, 1, 0),
            message(1, own, me, None, 3, 0),
            message(2, own, me, None, 0, 1),
            message(3, None, plane.spot(3, 0), 0, 1, 0),
            message(4, None, plane.spot(1, 0), 1, 3, 0),
            message(5, None, plane.spot(0, 1), None, 1, 0),
            message(6, None, plane.spot(0, 1), None, 3, 0),
            message(7, None, plane.spot(3, 1), 0, 1, 0),
            message(8, None, plane.spot(1, 1), 1, 3, 0),
        ]

    def begin_ring(self):
        self.copies[0].start()
        self.copies[1].start()

    def begin_pair(self):
        self.copies[2].start()

    def ring(self, flip):
        first, relay = (5, 7) if flip else (0, 3)
        for k in (0, 1):
            self.copies[first + k].wait_recv()
            self.copies[relay + k].start()

    def pair(self):
        self.copies[2].wait_recv()
        self.copies[5].start()
        self.copies[6].start()

    def far(self, flip):
        for k in (7, 8) if flip else (3, 4):
            self.copies[k].wait_recv()

    def end(self):
        for copy in self.copies:
            copy.wait_send()


class GatherCores(Gather):
    def __init__(self, plane, own, region, sends, recvs, base, core_sends, core_recvs, core_base):
        super().__init__(plane, own, region, sends, recvs, base)
        partner = (plane.dp, plane.ctx, 1 - plane.core)
        self.relays = {}
        for number, (along, flip) in enumerate(((0, 0),) + OTHERS):
            dst = region(plane.spot(along, flip), None)
            src = dst if number else own
            self.relays[along, flip] = remote(
                src, dst, core_sends, core_recvs, core_base + number, partner
            )

    def begin_ring(self):
        super().begin_ring()
        self.relays[0, 0].start()

    def ring(self, flip):
        super().ring(flip)
        self.relays[3, flip].start()
        self.relays[1, flip].start()

    def pair(self):
        super().pair()
        self.relays[0, 1].start()

    def far(self, flip):
        super().far(flip)
        self.relays[2, flip].start()

    def end(self):
        super().end()
        for copy in self.relays.values():
            copy.wait()


def dot_nt(left, right):
    return lax.dot_general(left, right, (((1,), (1,)), ((), ())), preferred_element_type=F32)


def dot_nn(left, right):
    return jnp.dot(left, right, preferred_element_type=F32)


def dot_tn(left, right):
    return lax.dot_general(left, right, (((0,), (0,)), ((), ())), preferred_element_type=F32)


def turn(values, cosine, sine, sign):
    lane = lax.rem(lax.broadcasted_iota(jnp.int32, values.shape, 1), HD)
    low = jnp.where(lane < ROT // 2, sine, 0.0)
    high = sine - low
    up = pltpu.roll(values, HEADS - ROT // 2, 1)
    down = pltpu.roll(values, ROT // 2, 1)
    return values * cosine + sign * (down * high - up * low)


def fold(values, op):
    return op(values.reshape(BLOCK // 8, 8, BLOCK), axis=0)


def nth_spot(plane, n, flip):
    along = n + lax.div(n, 2) - 2 * lax.div(n, 3)
    return plane.spot_at(along, flip)


def forward_kernel(
    hid, grad, fc1_in, qkv_in, fc2_in, dense_in, vectors, segments, positions,
    normed_out, grad_out, wa_out, wb_out, right_out, left_out,
    q_out, k_out, v_out, do_out, probs_out, sums_out, wave_out, vec_all, stats, bias_out,
    fc1, qkv_w, fc2, dense, wa, wb, vec, place, joined, other, normed, pieces, tile, table, place_all,
    normed_all, grad_all, wa_all, wb_all, slope, right, left, q_mask, k_mask, v_t, k_t, q_own, v_own, do_own,
    scores, probs, att_t, wave, sums,
    load, local, s_act, r_act, s_core, r_core, s_w, r_w, s_small, r_small, s_pair, r_pair, store, p_sem,
):
    plane, data = Plane(True), Plane(False)
    ctx, dp, core = plane.ctx, plane.dp, plane.core
    partner = (dp, ctx, 1 - core)

    def act_region(ref):
        columns = pl.ds(pl.multiple_of(core * HALF, HALF), HALF)

        def region(spot, part):
            if part is None:
                return ref.at[rows_at(spot), columns]
            start = pl.multiple_of(spot * BLOCK + part * (BLOCK // 2), BLOCK // 2)
            return ref.at[pl.ds(start, BLOCK // 2), columns]

        return region

    def weight_region(ref):
        def region(spot, part):
            if part is None:
                return ref.at[rows_at(spot), :]
            start = pl.multiple_of(spot * BLOCK + part * (BLOCK // 2), BLOCK // 2)
            return ref.at[pl.ds(start, BLOCK // 2), :]

        return region

    def scatter_rows(ref):
        start = pl.multiple_of(dp * BLOCK + ctx * OWN, OWN)
        return ref.at[pl.ds(start, OWN), :]

    sums[...] = jnp.zeros((8, SEQ), F32)
    vec_lane = lax.broadcasted_iota(jnp.int32, (1, 128), 1)
    loads = [
        pltpu.make_async_copy(src, dst, load.at[k])
        for k, (src, dst) in enumerate(
            ((fc1_in, fc1), (qkv_in, qkv_w), (fc2_in, fc2), (dense_in, dense))
        )
    ]
    for copy in loads:
        copy.start()
    greet(plane, data)
    hidden_copy = remote(hid, other, s_small, r_small, 0, partner)
    hidden_copy.start()
    vec[...] = jnp.zeros((16, 128), F32)
    for k in range(11):
        spread = jnp.concatenate([vectors[k]] * 8, axis=1)
        vec[k : k + 1, :] = jnp.where(lax.div(vec_lane, 16) == ctx, spread, 0.0)
    place[...] = jnp.zeros((8, BLOCK), jnp.int32)
    place[0:1, :] = segments[...]
    place[1:2, :] = positions[...]
    place_all[ctx] = place[...]
    tile[...] = vec[...].astype(BF16)
    piece_copies, tile_copies, place_copies, wa_copies, wb_copies = [], [], [], [], []
    for k, o in enumerate(OTHERS):
        to = plane.device(*o)
        spot = plane.spot(*o)
        piece_copies.append(remote(tile, pieces.at[k], s_small, r_small, 1 + k, to))
        place_copies.append(remote(place, place_all.at[ctx], s_small, r_small, 15 + k, to))
        wa_copies.append(remote(wa.at[spot], scatter_rows(wa_all), s_small, r_small, 22 + k, to))
        wb_copies.append(remote(wb.at[spot], scatter_rows(wb_all), s_small, r_small, 29 + k, to))
        columns = pl.ds(pl.multiple_of(dp * 128, 128), 128)
        tile_copies.append(
            remote(joined, table.at[:, columns], s_small, r_small, 8 + k, data.device(*o))
        )
    for copy in piece_copies + place_copies:
        copy.start()
    for copy in loads:
        copy.wait()
    for c in range(8):
        wa[c, :, 0:FFS] = fc1[:, c * FFS : (c + 1) * FFS].astype(BF16)
        columns = slice(c * HEADS, (c + 1) * HEADS)
        for k in range(3):
            wa[c, :, FFS + k * HEADS : FFS + (k + 1) * HEADS] = qkv_w[k, :, columns].astype(BF16)
    for copy in wa_copies:
        copy.start()
    for c in range(8):
        wb[c, :, 0:FFS] = fc2[:, c * FFS : (c + 1) * FFS].astype(BF16)
        wb[c, :, FFS:WB] = dense[:, c * HEADS : (c + 1) * HEADS].astype(BF16)
    locals_ = [
        pltpu.make_async_copy(wa.at[ctx], scatter_rows(wa_all), local.at[0]),
        pltpu.make_async_copy(wb.at[ctx], scatter_rows(wb_all), local.at[1]),
        pltpu.make_async_copy(grad, act_region(grad_all)(ctx, None), local.at[2]),
        pltpu.make_async_copy(normed, act_region(normed_all)(ctx, None), local.at[3]),
    ]
    for copy in locals_[:3]:
        copy.start()

    normed_gather = GatherCores(
        plane, normed, act_region(normed_all), s_act, r_act, 0, s_core, r_core, 0
    )
    grad_gather = GatherCores(
        plane, grad, act_region(grad_all), s_act, r_act, 9, s_core, r_core, 8
    )

    for copy in piece_copies:
        copy.wait_recv()
    total = tile[...].astype(F32)
    for k in range(7):
        total = total + pieces[k].astype(F32)
    joined[...] = total.astype(BF16)
    table[:, pl.ds(pl.multiple_of(dp * 128, 128), 128)] = total.astype(BF16)
    for copy in tile_copies:
        copy.start()

    a_region, b_region = weight_region(wa_all), weight_region(wb_all)
    wa_gather = Gather(data, a_region(dp, None), a_region, s_w, r_w, 0)
    wb_gather = Gather(data, b_region(dp, None), b_region, s_w, r_w, 9)
    for copy in wa_copies:
        copy.wait_recv()
    locals_[0].wait()
    wa_gather.begin_pair()
    wa_gather.begin_ring()
    for copy in wb_copies:
        copy.start()
    grad_gather.begin_ring()
    for copy in tile_copies:
        copy.wait_recv()
    hidden_copy.wait_recv()
    rows = table[...].astype(F32)
    vec_all[...] = rows
    gain, shift = rows[9:10], rows[10:11]
    lanes = lax.broadcasted_iota(jnp.int32, (16, 128), 1)

    def norm(i, carry):
        at = pl.ds(pl.multiple_of(i * 16, 16), 16)
        a, b = hid[at, :].astype(F32), other[at, :].astype(F32)
        mean = (jnp.sum(a, axis=1, keepdims=True) + jnp.sum(b, axis=1, keepdims=True)) / D
        a, b = a - mean, b - mean
        square = jnp.sum(a * a, axis=1, keepdims=True) + jnp.sum(b * b, axis=1, keepdims=True)
        inverse = lax.rsqrt(square / D + NORM_EPS)
        normed[at, :] = (a * inverse * gain + shift).astype(BF16)
        stats[at, :] = jnp.where(lanes < 64, mean, inverse)
        return carry

    lax.fori_loop(0, BLOCK // 16, norm, 0)
    normed_gather.begin_pair()
    normed_gather.begin_ring()
    locals_[3].start()
    for copy in place_copies:
        copy.wait_recv()
    lane = lax.broadcasted_iota(jnp.int32, (BLOCK, HEADS), 1)
    inner = lax.rem(lane, HD)
    first_head = lane < HD
    turning = inner < ROT
    wheel = lax.rem(lax.broadcasted_iota(jnp.int32, (1, HEADS), 1), ROT // 2)
    freq = jnp.zeros((1, HEADS), F32)
    for k in range(ROT // 2):
        freq = jnp.where(wheel == k, float(np.float32(10000.0 ** (-2.0 * k / ROT))), freq)

    def tables(i, carry):
        column = place_all[i].astype(F32).T
        angle = column[:, 1:2] * freq
        wave[0, rows_at(i), :] = jnp.where(turning, jnp.cos(angle), 1.0)
        wave[1, rows_at(i), :] = jnp.where(turning, jnp.sin(angle), 0.0)
        return carry

    lax.fori_loop(0, 8, tables, 0)

    for copy in wb_copies:
        copy.wait_recv()
    locals_[1].wait()
    wa_gather.ring(0)
    wa_gather.pair()
    normed_gather.pair()
    wb_gather.begin_pair()
    wb_gather.begin_ring()
    wa_gather.ring(1)
    normed_gather.ring(0)
    grad_gather.begin_pair()
    wb_gather.ring(0)
    wb_gather.pair()
    normed_gather.ring(1)
    grad_gather.ring(0)
    wa_gather.far(0)
    wa_gather.far(1)
    normed_gather.far(0)
    my_rows = pl.ds(pl.multiple_of(core * HALF, HALF), HALF)
    their_rows = pl.ds(pl.multiple_of((1 - core) * HALF, HALF), HALF)
    pairs = [
        remote(wa_all.at[their_rows, :], wa_out.at[1], s_pair, r_pair, 0, partner),
        remote(wb_all.at[their_rows, :], wb_out.at[1], s_pair, r_pair, 1, partner),
    ]
    pairs[0].start()
    stores = [
        pltpu.make_async_copy(wa_all.at[my_rows, :], wa_out.at[0], store.at[0]),
        pltpu.make_async_copy(wb_all.at[my_rows, :], wb_out.at[0], store.at[1]),
        pltpu.make_async_copy(wave, wave_out, store.at[2]),
    ]
    stores[0].start()
    stores[2].start()

    qkv_bias = [
        vec_all[c : c + 1, pl.ds(pl.multiple_of(ctx * HEADS, HEADS), HEADS)] for c in range(3)
    ]
    fc1_bias = vec_all[
        pl.ds(3 + lax.div(ctx, 2), 1), pl.ds(pl.multiple_of(lax.rem(ctx, 2) * FFS, FFS), FFS)
    ]

    def project(spot):
        at = rows_at(spot)
        block = normed_all[at, :]
        x = dot_nn(block, wa_all[:, 0:FFS]) + fc1_bias
        square = x * x
        tanh = jnp.tanh(x * (GELU + (GELU * 0.044715) * square))
        half = 0.5 * (1.0 + tanh)
        bend = GELU + (3.0 * 0.044715 * GELU) * square
        slope[at, :] = half + 0.5 * x * (1.0 - tanh * tanh) * bend
        right[at, 0:FFS] = (x * half).astype(BF16)
        qkv = dot_nn(block, wa_all[:, FFS:WA])
        c, s = wave[0, at, :], wave[1, at, :]
        q = turn(qkv[:, 0:HEADS] + qkv_bias[0], c, s, 1.0).astype(BF16).astype(F32) * (HD**-0.5)
        k = turn(qkv[:, HEADS : 2 * HEADS] + qkv_bias[1], c, s, 1.0)
        v = qkv[:, 2 * HEADS : 3 * HEADS] + qkv_bias[2]
        segment = place_all[spot].astype(F32).T[:, 0:1]
        feature = jnp.where(segment == inner.astype(F32), 1.0, 0.0)
        barred = jnp.where(inner < 3, (1.0 - feature) * MASKED, 0.0)
        q_mask[0, at, :] = jnp.where(first_head, q, barred).astype(BF16)
        q_mask[1, at, :] = jnp.where(first_head, barred, q).astype(BF16)
        k_mask[0, at, :] = jnp.where(first_head, k, feature).astype(BF16)
        k_mask[1, at, :] = jnp.where(first_head, feature, k).astype(BF16)
        q_own[at, :] = q.astype(BF16)
        v_own[at, :] = v.astype(BF16)
        k_t[:, at] = k.T.astype(BF16)
        v_t[:, at] = v.T.astype(BF16)

    def project_ring(flip, start, end):
        def step(n, carry):
            project(nth_spot(plane, n, flip))
            return carry

        lax.fori_loop(start, end, step, 0)

    def keep_block(ref, out, o, number):
        at = rows_at(plane.spot(*o))
        copy = pltpu.make_async_copy(ref.at[at, :], out.at[at, :], store.at[number])
        copy.start()
        return copy

    locals_[3].wait()
    for o in ((0, 0), (1, 0), (3, 0), (2, 0)):
        normed_gather.relays[o].wait_recv()
    project_ring(0, 0, 2)
    grad_gather.pair()
    wb_gather.ring(1)
    project_ring(0, 2, 4)
    normed_gather.far(1)
    for o in ((0, 1), (1, 1), (3, 1), (2, 1)):
        normed_gather.relays[o].wait_recv()
    project_ring(1, 0, 4)
    normed_copies = [
        keep_block(normed_all, normed_out, (along, flip), 16 + 2 * along + flip)
        for flip in (0, 1)
        for along in range(4)
    ]
    small_stores = [
        pltpu.make_async_copy(q_own, q_out, store.at[4]),
        pltpu.make_async_copy(k_t, k_out, store.at[5]),
        pltpu.make_async_copy(v_own, v_out, store.at[6]),
    ]
    for copy in small_stores:
        copy.start()

    key_row = lax.broadcasted_iota(jnp.int32, (BLOCK, BLOCK), 0)
    query_col = lax.broadcasted_iota(jnp.int32, (BLOCK, BLOCK), 1)
    causal = key_row <= query_col
    prob_stores, right_copies, right_keeps = {}, [], []
    for i in range(8):
        own = pl.ds(i * BLOCK, BLOCK)
        slot = i % 2

        def raw(j, h):
            return dot_nt(k_mask[h, rows_at(j), :], q_mask[h, own, :])

        def score(j, carry):
            new = []
            for h in range(2):
                s = raw(j, h)
                scores[h, rows_at(j), :] = s
                new.append(jnp.maximum(carry[h], fold(s, jnp.max)))
            return tuple(new)

        low = jnp.full((8, BLOCK), MASKED, F32)
        maxima = lax.fori_loop(0, i, score, (low, low), unroll=True)
        tops = []
        for h in range(2):
            s = jnp.where(causal, raw(i, h), MASKED)
            scores[h, own, :] = s
            top = jnp.maximum(maxima[h], fold(s, jnp.max))
            tops.append(jnp.max(top, axis=0, keepdims=True))
        if i >= 2:
            prob_stores[i - 2].wait()

        def prob(j, carry):
            totals, outs = [], []
            for h in range(2):
                p = jnp.exp(scores[h, rows_at(j), :] - tops[h])
                totals.append(carry[0][h] + fold(p, jnp.sum))
                p = p.astype(BF16)
                probs[slot, h, rows_at(j), :] = p
                outs.append(carry[1][h] + dot_nn(v_t[pl.ds(h * HD, HD), rows_at(j)], p))
            return (tuple(totals), tuple(outs))

        zero_sum, zero_out = jnp.zeros((8, BLOCK), F32), jnp.zeros((HD, BLOCK), F32)
        totals, outs = lax.fori_loop(
            0, i + 1, prob, ((zero_sum, zero_sum), (zero_out, zero_out)), unroll=True
        )
        length = (i + 1) * BLOCK
        prob_stores[i] = pltpu.make_async_copy(
            probs.at[slot, :, pl.ds(0, length), :],
            probs_out.at[i, :, pl.ds(0, length), :],
            p_sem.at[slot],
        )
        prob_stores[i].start()
        scale = [1.0 / jnp.sum(totals[h], axis=0, keepdims=True) for h in range(2)]
        both = jnp.concatenate([outs[h] * scale[h] for h in range(2)], axis=0)
        sums[0:1, own] = scale[0]
        sums[1:2, own] = scale[1]
        att_t[:, own] = both
        right[own, FFS:WB] = both.T.astype(BF16)
        right_copies.append(
            remote(right.at[own, :], right_out.at[1, own, :], s_pair, r_pair, 2 + i, partner)
        )
        right_copies[i].start()
        right_keeps.append(
            pltpu.make_async_copy(right.at[own, :], right_out.at[0, own, :], store.at[7 + i])
        )
        right_keeps[i].start()
        if i == 2:
            wb_gather.far(0)
            wb_gather.far(1)
            pairs[1].start()
            stores[1].start()
        if i == 4:
            grad_gather.far(0)
            grad_gather.ring(1)
    bias_out[...] = jnp.zeros((8, FFS), F32)

    def back(spot):
        at = rows_at(spot)
        block = grad_all[at, :]
        d_pre = dot_nn(block, wb_all[:, 0:FFS]) * slope[at, :]
        rounded = d_pre.astype(BF16)
        left[at, :] = rounded
        whole = rounded.astype(F32)
        bias_out[...] += jnp.sum(whole.reshape(BLOCK // 8, 8, FFS), axis=0)
        d_att = dot_nn(block, wb_all[:, FFS:WB])
        do_own[at, :] = d_att.astype(BF16)
        product = att_t[:, at] * d_att.astype(BF16).astype(F32).T
        sums[2:3, at] = jnp.sum(product[0:HD], axis=0, keepdims=True)
        sums[3:4, at] = jnp.sum(product[HD:], axis=0, keepdims=True)

    def back_ring(flip, start, end):
        def step(n, carry):
            back(nth_spot(plane, n, flip))
            return carry

        lax.fori_loop(start, end, step, 0)

    locals_[2].wait()
    left_copies, left_keeps = [], []

    def send_left(o):
        k = len(left_copies)
        at = rows_at(plane.spot(*o))
        left_copies.append(
            remote(left.at[at, :], left_out.at[1, at, :], s_pair, r_pair, 10 + k, partner)
        )
        left_keeps.append(
            pltpu.make_async_copy(left.at[at, :], left_out.at[0, at, :], store.at[24 + k])
        )
        left_copies[k].start()
        left_keeps[k].start()

    for along in range(4):
        grad_gather.relays[along, 0].wait_recv()
    grad_copies = [
        keep_block(grad_all, grad_out, (along, 0), 32 + 2 * along) for along in range(4)
    ]
    back_ring(0, 0, 4)
    for along in range(4):
        send_left((along, 0))
    for along in (0, 1, 3):
        grad_gather.relays[along, 1].wait_recv()
        grad_copies.append(keep_block(grad_all, grad_out, (along, 1), 33 + 2 * along))
    back_ring(1, 0, 2)
    grad_gather.far(1)
    back_ring(1, 2, 3)
    for along in (0, 1, 3):
        send_left((along, 1))
    grad_gather.relays[2, 1].wait_recv()
    grad_copies.append(keep_block(grad_all, grad_out, (2, 1), 37))
    back_ring(1, 3, 4)
    send_left((2, 1))
    last_stores = [
        pltpu.make_async_copy(do_own, do_out, store.at[40]),
        pltpu.make_async_copy(sums, sums_out, store.at[41]),
    ]
    for copy in last_stores:
        copy.start()

    for gather in (grad_gather, normed_gather):
        for copy in gather.copies:
            copy.wait_send()
        for copy in gather.relays.values():
            copy.wait_send()
    wa_gather.end()
    wb_gather.end()
    hidden_copy.wait_send()
    for copy in piece_copies + tile_copies + wa_copies + wb_copies + place_copies:
        copy.wait_send()
    for copy in pairs + right_copies + left_copies:
        copy.wait()
    for copy in stores + small_stores + right_keeps + left_keeps + last_stores:
        copy.wait()
    for copy in normed_copies + grad_copies + [prob_stores[6], prob_stores[7]]:
        copy.wait()


def forward(*args):
    hbm = pl.BlockSpec(memory_space=pl.ANY)
    vmem = pl.BlockSpec(memory_space=pltpu.VMEM)
    dma = pltpu.SemaphoreType.DMA

    def shape(*dims, kind=BF16):
        return jax.ShapeDtypeStruct(dims, kind)

    return pl.pallas_call(
        forward_kernel,
        out_shape=(
            shape(SEQ, D),
            shape(SEQ, D),
            shape(2, HALF, WA),
            shape(2, HALF, WB),
            shape(2, SEQ, WB),
            shape(2, SEQ, FFS),
            shape(SEQ, HEADS),
            shape(HEADS, SEQ),
            shape(SEQ, HEADS),
            shape(SEQ, HEADS),
            shape(8, 2, SEQ, BLOCK),
            shape(8, SEQ, kind=F32),
            shape(2, SEQ, HEADS, kind=F32),
            shape(16, HALF, kind=F32),
            shape(BLOCK, 128, kind=F32),
            shape(8, FFS, kind=F32),
        ),
        in_specs=[vmem] + [hbm] * 5 + [vmem] * 3,
        out_specs=(hbm,) * 13 + (vmem,) * 3,
        scratch_shapes=[
            pltpu.VMEM((OWN, FF // 2), F32),
            pltpu.VMEM((3, OWN, HALF), F32),
            pltpu.VMEM((OWN, FF // 2), F32),
            pltpu.VMEM((OWN, HALF), F32),
            pltpu.VMEM((8, OWN, WA), BF16),
            pltpu.VMEM((8, OWN, WB), BF16),
            pltpu.VMEM((16, 128), F32),
            pltpu.VMEM((8, BLOCK), jnp.int32),
            pltpu.VMEM((16, 128), BF16),
            pltpu.VMEM((BLOCK, HALF), BF16),
            pltpu.VMEM((BLOCK, HALF), BF16),
            pltpu.VMEM((7, 16, 128), BF16),
            pltpu.VMEM((16, 128), BF16),
            pltpu.VMEM((16, HALF), BF16),
            pltpu.VMEM((8, 8, BLOCK), jnp.int32),
            pltpu.VMEM((SEQ, D), BF16),
            pltpu.VMEM((SEQ, D), BF16),
            pltpu.VMEM((D, WA), BF16),
            pltpu.VMEM((D, WB), BF16),
            pltpu.VMEM((SEQ, FFS), F32),
            pltpu.VMEM((SEQ, WB), BF16),
            pltpu.VMEM((SEQ, FFS), BF16),
            pltpu.VMEM((2, SEQ, HEADS), BF16),
            pltpu.VMEM((2, SEQ, HEADS), BF16),
            pltpu.VMEM((HEADS, SEQ), BF16),
            pltpu.VMEM((HEADS, SEQ), BF16),
            pltpu.VMEM((SEQ, HEADS), BF16),
            pltpu.VMEM((SEQ, HEADS), BF16),
            pltpu.VMEM((SEQ, HEADS), BF16),
            pltpu.VMEM((2, SEQ, BLOCK), F32),
            pltpu.VMEM((2, 2, SEQ, BLOCK), BF16),
            pltpu.VMEM((HEADS, SEQ), F32),
            pltpu.VMEM((2, SEQ, HEADS), F32),
            pltpu.VMEM((8, SEQ), F32),
            dma((4,)),
            dma((4,)),
            dma((18,)),
            dma((18,)),
            dma((16,)),
            dma((16,)),
            dma((18,)),
            dma((18,)),
            dma((36,)),
            dma((36,)),
            dma((18,)),
            dma((18,)),
            dma((42,)),
            dma((2,)),
        ],
        compiler_params=pltpu.CompilerParams(
            collective_id=0, has_side_effects=True, vmem_limit_bytes=62 * 1024 * 1024
        ),
        name="forward",
    )(*args)


def add_rows(dst, terms, count, chunk):
    def step(i, carry):
        at = pl.ds(pl.multiple_of(i * chunk, chunk), chunk)
        total = terms[0][at, :].astype(F32)
        for term in terms[1:]:
            total = total + term[at, :].astype(F32)
        dst[at, :] = total.astype(dst.dtype)
        return carry

    lax.fori_loop(0, count // chunk, step, 0)


class Reduce:
    def __init__(self, plane, acc, landing, sends, recvs, base):
        half_up, half_down, up, down, across = landing
        self.plane, self.acc, self.across = plane, acc, across
        self.near = (half_up, half_down, up, down)
        self.rows = across.shape[0]
        self.chunk = 16
        half = self.half = self.rows // 2
        self.copies = []
        for j, flip in ((0, 1), (1, 0)):
            far = plane.spot(2, flip)
            for number, (src, dst, along) in enumerate(
                (
                    (acc.at[far, pl.ds(0, half), :], half_up.at[j], 1),
                    (acc.at[far, pl.ds(half, half), :], half_down.at[j], 3),
                    (acc.at[plane.spot(1, flip)], up.at[j], 1),
                    (acc.at[plane.spot(3, flip)], down.at[j], 3),
                )
            ):
                self.copies.append(
                    remote(src, dst, sends, recvs, base + 4 * j + number, plane.device(along, 0))
                )
        self.copies.append(
            remote(acc.at[plane.spot(0, 1)], across, sends, recvs, base + 8, plane.device(0, 1))
        )

    def first(self, j):
        self.copies[4 * j].start()
        self.copies[4 * j + 1].start()

    def second(self, j):
        half = self.half
        for number, along in ((0, 1), (1, 3)):
            self.copies[4 * j + number].wait_recv()
            dst = self.acc.at[self.plane.spot(along, 1 - j), pl.ds(number * half, half), :]
            add_rows(dst, [dst, self.near[number].at[j]], half, self.chunk)
            self.copies[4 * j + number + 2].start()

    def third(self):
        self.copies[2].wait_recv()
        self.copies[3].wait_recv()
        dst = self.acc.at[self.plane.spot(0, 1)]
        add_rows(dst, [dst, self.near[2].at[0], self.near[3].at[0]], self.rows, self.chunk)
        self.copies[8].start()

    def arrived(self):
        for k in (6, 7, 8):
            self.copies[k].wait_recv()
        mine = self.acc.at[self.plane.spot(0, 0)]
        return [mine, self.near[2].at[1], self.near[3].at[1], self.across]

    def last(self, dst):
        add_rows(dst, self.arrived(), self.rows, self.chunk)

    def end(self):
        for copy in self.copies:
            copy.wait_send()


def backward_kernel(
    right_in, wb_in, left_in, wa_in, normed, grads, q_in, k_in, v_in, do_in,
    probs_in, sums, wave_in, hid, grad, stats, vec_all, bias_in,
    hidden_out, grad_in, gb_all, ga_all, vec_sum,
    right, left, weight, stream, q_all, k_t, v_all, do_all, probs_odd, probs_even, wave, d_k, d_v,
    out_acc, dx_acc, gb_acc, ga_acc,
    out_a, out_b, out_c, out_d, out_e, dx_a, dx_b, dx_c, dx_d, dx_e, gb_a, gb_b, gb_c, gb_d, gb_e,
    ga_a, ga_b, ga_c, ga_d, ga_e, gb_done, ga_done, bias, final, vec, vec_in, vec_tile, tile_in, row_own, row_in,
    load, s_stream, s_probs, s_pair, r_pair, s_red, r_red, s_small, r_small, keep,
):
    plane, data = Plane(True), Plane(False)
    ctx, dp, core = plane.ctx, plane.dp, plane.core
    partner = (dp, ctx, 1 - core)
    loads = {
        "weight": pltpu.make_async_copy(wb_in, weight.at[:, :, pl.ds(0, WB)], load.at[0]),
        "right": pltpu.make_async_copy(right_in, right, load.at[1]),
        "left": pltpu.make_async_copy(left_in, left.at[:, :, pl.ds(0, FFS)], load.at[2]),
        "q": pltpu.make_async_copy(q_in, q_all, load.at[4]),
        "k": pltpu.make_async_copy(k_in, k_t, load.at[5]),
        "v": pltpu.make_async_copy(v_in, v_all, load.at[6]),
        "do": pltpu.make_async_copy(do_in, do_all, load.at[7]),
    }
    for copy in loads.values():
        copy.start()
    greet(plane, data)

    out = Reduce(plane, out_acc, (out_a, out_b, out_c, out_d, out_e), s_red, r_red, 0)
    dx = Reduce(plane, dx_acc, (dx_a, dx_b, dx_c, dx_d, dx_e), s_red, r_red, 9)
    gb = Reduce(data, gb_acc, (gb_a, gb_b, gb_c, gb_d, gb_e), s_red, r_red, 18)
    ga = Reduce(data, ga_acc, (ga_a, ga_b, ga_c, ga_d, ga_e), s_red, r_red, 27)

    def spot_of(where, n):
        group = lax.div(n + 2, 4)
        inside = n + 2 - 4 * group
        near = 1 - lax.rem(group + 1, 2)
        along = near * (1 + 2 * lax.rem(inside, 2)) + (1 - near) * (2 - group)
        flip = near * (1 - lax.div(inside, 2)) + (1 - near) * (1 - lax.rem(inside, 2))
        return where.spot_at(along, flip)

    def out_block(n, carry):
        spot = spot_of(plane, n)
        at = rows_at(spot)
        total = dot_nt(right[0, at, :], weight[0, :, 0:WB])
        total = total + dot_nt(right[1, at, :], weight[1, :, 0:WB])
        out_acc[spot] = total.astype(BF16)
        return carry

    def dx_block(n, carry):
        spot = spot_of(plane, n)
        at = rows_at(spot)
        total = dot_nt(left[0, at, :], weight[0])
        total = total + dot_nt(left[1, at, :], weight[1])
        dx_acc[spot] = total.astype(BF16)
        return carry

    def fetch(source, n):
        columns = rows_at(spot_of(data, n))
        slot = lax.rem(n, 2)
        return pltpu.make_async_copy(source.at[:, columns], stream.at[slot], s_stream.at[slot])

    def weight_blocks(source, factor, acc, start, end):
        def step(n, carry):
            @pl.when(n < 7)
            def _():
                fetch(source, n + 1).start()

            fetch(source, n).wait()
            total = dot_tn(stream[lax.rem(n, 2)], factor[0])
            acc[spot_of(data, n)] = total.astype(BF16)
            return carry

        lax.fori_loop(start, end, step, 0)

    loads["weight"].wait()
    loads["right"].wait()
    lax.fori_loop(0, 1, out_block, 0)
    out.first(0)
    fetch(grads, 0).start()
    lax.fori_loop(1, 8, out_block, 0)
    weight_load = pltpu.make_async_copy(wa_in, weight, load.at[8])
    weight_load.start()
    out.second(0)
    out.first(1)
    weight_blocks(grads, right, gb_acc, 0, 1)
    gb.first(0)
    weight_blocks(grads, right, gb_acc, 1, 4)

    lane = lax.broadcasted_iota(jnp.int32, (BLOCK, HEADS), 1)
    heads = (lane < HD, lane >= HD)
    bias[...] = jnp.zeros((8, 3 * HEADS), F32)

    def clear(i, carry):
        d_k[rows_at(i), :] = jnp.zeros((BLOCK, HEADS), F32)
        d_v[rows_at(i), :] = jnp.zeros((BLOCK, HEADS), F32)
        return carry

    lax.fori_loop(0, 8, clear, 0)

    def probs_of(i):
        length = pl.ds(0, (i + 1) * BLOCK)
        buffer = probs_odd if i % 2 else probs_even
        return [
            pltpu.make_async_copy(
                probs_in.at[i, :, length, :], buffer.at[:, length, :], s_probs.at[i % 2]
            ),
            pltpu.make_async_copy(
                wave_in.at[:, pl.ds(i * BLOCK, BLOCK), :], wave.at[i % 2], s_probs.at[2 + i % 2]
            ),
        ]

    for name in ("q", "k", "v", "do"):
        loads[name].wait()
    arriving = {7: probs_of(7)}
    for copy in arriving[7]:
        copy.start()
    swaps = []
    for i in range(7, -1, -1):
        own = pl.ds(i * BLOCK, BLOCK)
        if i:
            arriving[i - 1] = probs_of(i - 1)
            for copy in arriving[i - 1]:
                copy.start()
        for copy in arriving[i]:
            copy.wait()
        probs = probs_odd if i % 2 else probs_even
        scale = [sums[h : h + 1, own] for h in range(2)]
        delta = [sums[2 + h : 3 + h, own] for h in range(2)]
        q, do = q_all[own, :].astype(F32), do_all[own, :].astype(F32)
        q_plain = [jnp.where(heads[h], q, 0.0).astype(BF16) for h in range(2)]
        do_plain = [jnp.where(heads[h], do, 0.0).astype(BF16) for h in range(2)]

        def back(j, carry):
            at, new = rows_at(j), []
            add_k, add_v = d_k[at, :], d_v[at, :]
            for h in range(2):
                p = probs[h, at, :].astype(F32) * scale[h]
                d_p = dot_nt(v_all[at, :], do_plain[h])
                d_s = (p * (d_p - delta[h])).astype(BF16)
                add_v = add_v + dot_nn(p.astype(BF16), do_plain[h])
                add_k = add_k + dot_nn(d_s, q_plain[h])
                new.append(carry[h] + dot_nn(k_t[pl.ds(h * HD, HD), at], d_s))
            d_k[at, :] = add_k
            d_v[at, :] = add_v
            return tuple(new)

        zero_out = jnp.zeros((HD, BLOCK), F32)
        d_q = lax.fori_loop(0, i + 1, back, (zero_out, zero_out), unroll=True)
        d_q = jnp.concatenate(d_q, axis=0).T * (HD**-0.5)
        c, s = wave[i % 2, 0], wave[i % 2, 1]
        parts = (turn(d_q, c, s, -1.0), turn(d_k[own, :], c, s, -1.0), d_v[own, :])
        for k, part in enumerate(parts):
            rounded = part.astype(BF16)
            whole = rounded.astype(F32)
            left[0, own, FFS + k * HEADS : FFS + (k + 1) * HEADS] = rounded
            columns = slice(k * HEADS, (k + 1) * HEADS)
            bias[:, columns] += jnp.sum(whole.reshape(BLOCK // 8, 8, HEADS), axis=0)
        span = pl.ds(FFS, 3 * HEADS)
        swap = remote(
            left.at[0, own, span], left.at[1, own, span], s_pair, r_pair, i, partner
        )
        swap.start()
        swaps.append(swap)
        if i == 7:
            gb.second(0)
            gb.first(1)
        if i == 5:
            out.second(1)
        if i == 3:
            out.third()

    loads["left"].wait()
    weight_load.wait()
    for swap in swaps:
        swap.wait_recv()
    lax.fori_loop(0, 1, dx_block, 0)
    dx.first(0)
    weight_blocks(grads, right, gb_acc, 4, 6)
    gb.second(1)
    weight_blocks(grads, right, gb_acc, 6, 8)
    fetch(normed, 0).start()
    gb.third()
    weight_blocks(normed, left, ga_acc, 0, 1)
    ga.first(0)
    lax.fori_loop(1, 4, dx_block, 0)
    dx.second(0)
    dx.first(1)
    weight_blocks(normed, left, ga_acc, 1, 4)
    ga.second(0)
    ga.first(1)
    lax.fori_loop(4, 8, dx_block, 0)
    gb.last(gb_done)
    weight_blocks(normed, left, ga_acc, 4, 6)
    dx.second(1)
    ga.second(1)
    weight_blocks(normed, left, ga_acc, 6, 8)
    dx.third()

    copies = {}
    keeps = []
    for n, (name, done, landed) in enumerate(
        (("gb", gb_done, gb_all), ("ga", ga_done, ga_all))
    ):
        copies[name] = [
            remote(
                done.at[rows_at(plane.spot(*o), OWN), :],
                landed.at[ctx],
                s_small,
                r_small,
                15 + 7 * n + k,
                plane.device(*o),
            )
            for k, o in enumerate(OTHERS)
        ]
        keeps.append(
            pltpu.make_async_copy(done.at[rows_at(ctx, OWN), :], landed.at[ctx], keep.at[n])
        )
    for copy in copies["gb"]:
        copy.start()
    keeps[0].start()

    out.last(final)
    bias_rows = vec_all[7:8, :] + vec_all[8:9, :]

    def add_hidden(i, carry):
        at = pl.ds(pl.multiple_of(i * 16, 16), 16)
        hidden_out[at, :] = (hid[at, :].astype(F32) + final[at, :] + bias_rows).astype(BF16)
        return carry

    lax.fori_loop(0, BLOCK // 16, add_hidden, 0)
    ga.third()
    dx.last(final)
    gain = vec_all[9:10, :]
    lanes = lax.broadcasted_iota(jnp.int32, (16, 128), 1)

    def lean(i, carry):
        at = pl.ds(pl.multiple_of(i * 16, 16), 16)
        d, h, stat = final[at, :], hid[at, :].astype(F32), stats[at, :]
        normal = (h - stat[:, 0:1]) * stat[:, 64:65]
        product = d * normal
        one = jnp.sum(d * gain, axis=1, keepdims=True)
        two = jnp.sum(product * gain, axis=1, keepdims=True)
        row_own[at, :] = jnp.where(lanes < 64, one, two)
        return (carry[0] + d, carry[1] + product, carry[2] + grad[at, :].astype(F32))

    zero = jnp.zeros((16, HALF), F32)
    rows = lax.fori_loop(0, BLOCK // 16, lean, (zero, zero, zero))
    row_copy = remote(row_own, row_in, s_small, r_small, 0, partner)
    row_copy.start()
    shift_grad, gain_grad, bias_grad = [jnp.sum(r, axis=0, keepdims=True) for r in rows]
    number = lax.broadcasted_iota(jnp.int32, (16, HALF), 0)
    vec[...] = jnp.where(
        number == 9,
        gain_grad,
        jnp.where(
            number == 10, shift_grad, jnp.where((number == 7) | (number == 8), bias_grad, 0.0)
        ),
    )
    columns = pl.ds(pl.multiple_of(ctx * HEADS, HEADS), HEADS)
    for k in range(3):
        part = jnp.sum(bias[:, k * HEADS : (k + 1) * HEADS], axis=0, keepdims=True)
        vec[k : k + 1, columns] = part
    columns = pl.ds(pl.multiple_of(lax.rem(ctx, 2) * FFS, FFS), FFS)
    part = jnp.sum(bias_in[...], axis=0, keepdims=True)
    vec[:, columns] = jnp.where(
        lax.broadcasted_iota(jnp.int32, (16, FFS), 0) == 3 + lax.div(ctx, 2), part, vec[:, columns]
    )
    vec_copies, tile_copies = [], []
    for k, o in enumerate(OTHERS):
        columns = pl.ds(pl.multiple_of(data.spot(*o) * 128, 128), 128)
        vec_copies.append(
            remote(vec.at[:, columns], vec_in.at[k], s_small, r_small, 1 + k, data.device(*o))
        )
        tile_copies.append(
            remote(vec_tile, tile_in.at[k], s_small, r_small, 8 + k, plane.device(*o))
        )
    for copy in vec_copies:
        copy.start()
    ga.last(ga_done)
    for copy in copies["ga"]:
        copy.start()
    keeps[1].start()
    for copy in vec_copies:
        copy.wait_recv()
    total = vec[:, pl.ds(pl.multiple_of(dp * 128, 128), 128)]
    for k in range(7):
        total = total + vec_in[k]
    vec_tile[...] = total
    for copy in tile_copies:
        copy.start()

    row_copy.wait()

    def tilt(i, carry):
        at = pl.ds(pl.multiple_of(i * 16, 16), 16)
        d, h, stat = final[at, :], hid[at, :].astype(F32), stats[at, :]
        inverse = stat[:, 64:65]
        normal = (h - stat[:, 0:1]) * inverse
        row = (row_own[at, :] + row_in[at, :]) / D
        change = inverse * (d * gain - row[:, 0:1] - normal * row[:, 64:65])
        grad_in[at, :] = (grad[at, :].astype(F32) + change).astype(BF16)
        return carry

    lax.fori_loop(0, BLOCK // 16, tilt, 0)
    for copy in tile_copies:
        copy.wait_recv()
    total = vec_tile[...]
    for k in range(7):
        total = total + tile_in[k]
    vec_sum[...] = total

    for name in copies:
        for copy in copies[name]:
            copy.wait()
    for copy in keeps:
        copy.wait()
    for copy in vec_copies + tile_copies + swaps:
        copy.wait_send()
    for red in (dx, out, gb, ga):
        red.end()


def backward(*args):
    hbm = pl.BlockSpec(memory_space=pl.ANY)
    vmem = pl.BlockSpec(memory_space=pltpu.VMEM)
    dma = pltpu.SemaphoreType.DMA

    def landing(rows, width):
        half = pltpu.VMEM((2, rows // 2, width), BF16)
        whole = pltpu.VMEM((2, rows, width), BF16)
        return [half, half, whole, whole, pltpu.VMEM((rows, width), BF16)]

    def shape(*dims, kind=BF16):
        return jax.ShapeDtypeStruct(dims, kind)

    return pl.pallas_call(
        backward_kernel,
        out_shape=(
            shape(BLOCK, HALF),
            shape(BLOCK, HALF),
            shape(8, OWN, WB),
            shape(8, OWN, WA),
            shape(16, 128, kind=F32),
        ),
        in_specs=[hbm] * 11 + [vmem, hbm] + [vmem] * 5,
        out_specs=(vmem, vmem, hbm, hbm, vmem),
        scratch_shapes=[
            pltpu.VMEM((2, SEQ, WB), BF16),
            pltpu.VMEM((2, SEQ, WA), BF16),
            pltpu.VMEM((2, HALF, WA), BF16),
            pltpu.VMEM((2, SEQ, BLOCK), BF16),
            pltpu.VMEM((SEQ, HEADS), BF16),
            pltpu.VMEM((HEADS, SEQ), BF16),
            pltpu.VMEM((SEQ, HEADS), BF16),
            pltpu.VMEM((SEQ, HEADS), BF16),
            pltpu.VMEM((2, SEQ, BLOCK), BF16),
            pltpu.VMEM((2, SEQ - BLOCK, BLOCK), BF16),
            pltpu.VMEM((2, 2, BLOCK, HEADS), F32),
            pltpu.VMEM((SEQ, HEADS), F32),
            pltpu.VMEM((SEQ, HEADS), F32),
            pltpu.VMEM((8, BLOCK, HALF), BF16),
            pltpu.VMEM((8, BLOCK, HALF), BF16),
            pltpu.VMEM((8, BLOCK, WB), BF16),
            pltpu.VMEM((8, BLOCK, WA), BF16),
            *landing(BLOCK, HALF),
            *landing(BLOCK, HALF),
            *landing(BLOCK, WB),
            *landing(BLOCK, WA),
            pltpu.VMEM((BLOCK, WB), BF16),
            pltpu.VMEM((BLOCK, WA), BF16),
            pltpu.VMEM((8, 3 * HEADS), F32),
            pltpu.VMEM((BLOCK, HALF), F32),
            pltpu.VMEM((16, HALF), F32),
            pltpu.VMEM((7, 16, 128), F32),
            pltpu.VMEM((16, 128), F32),
            pltpu.VMEM((7, 16, 128), F32),
            pltpu.VMEM((BLOCK, 128), F32),
            pltpu.VMEM((BLOCK, 128), F32),
            dma((10,)),
            dma((2,)),
            dma((4,)),
            dma((8,)),
            dma((8,)),
            dma((45,)),
            dma((45,)),
            dma((36,)),
            dma((36,)),
            dma((3,)),
        ],
        compiler_params=pltpu.CompilerParams(
            collective_id=1, has_side_effects=True, vmem_limit_bytes=62 * 1024 * 1024
        ),
        name="backward",
    )(*args)


def adam_step(weight, first, second, gradient, rate):
    first_new = BETA_ONE * first + (1.0 - BETA_ONE) * gradient
    second_new = BETA_TWO * second + (1.0 - BETA_TWO) * gradient * gradient
    fix_one = 1.0 - BETA_ONE**STEP
    fix_two = 1.0 - BETA_TWO**STEP
    update = first_new / fix_one / (jnp.sqrt(second_new / fix_two) + ADAM_EPS)
    return (first_new, second_new, weight - rate * (update + DECAY * weight))


def update_kernel(
    ga, gb, vec_sum, hidden, back,
    qkv_w, qkv_m, qkv_v, dense_w, dense_m, dense_v, fc1_w, fc1_m, fc1_v, fc2_w, fc2_m, fc2_v,
    vec_w, vec_m, vec_v,
    hidden_out, back_out,
    qkv_mo, qkv_vo, qkv_wo, dense_mo, dense_vo, dense_wo, fc1_mo, fc1_vo, fc1_wo,
    fc2_mo, fc2_vo, fc2_wo, vec_mo, vec_vo, vec_wo,
):
    hidden_out[...] = hidden[...]
    back_out[...] = back[...]

    fc1 = (fc1_w, fc1_m, fc1_v, fc1_mo, fc1_vo, fc1_wo)
    fc2 = (fc2_w, fc2_m, fc2_v, fc2_mo, fc2_vo, fc2_wo)
    dense = (dense_w, dense_m, dense_v, dense_mo, dense_vo, dense_wo)
    qkv = (qkv_w, qkv_m, qkv_v, qkv_mo, qkv_vo, qkv_wo)
    vec = (vec_w, vec_m, vec_v, vec_mo, vec_vo, vec_wo)

    def step(refs, gradient, rate, *at):
        w, m, v, mo, vo, wo = refs
        mo[at], vo[at], wo[at] = adam_step(w[at], m[at], v[at], gradient, rate)

    for c in range(8):
        wide, narrow = slice(c * FFS, (c + 1) * FFS), slice(c * HEADS, (c + 1) * HEADS)
        step(fc1, ga[c, :, 0:FFS].astype(F32), RATES[0], slice(None), wide)
        step(fc2, gb[c, :, 0:FFS].astype(F32), RATES[1], slice(None), wide)
        step(dense, gb[c, :, FFS:WB].astype(F32), RATES[2], slice(None), narrow)
        for k in range(3):
            columns = slice(FFS + k * HEADS, FFS + (k + 1) * HEADS)
            step(qkv, ga[c, :, columns].astype(F32), RATES[0], k, slice(None), narrow)

    @pl.when(pl.program_id(0) == 0)
    def _():
        mine = pltpu.roll(vec_sum[...], lax.rem(128 - 16 * lax.axis_index("ctx"), 128), 1)
        for k in range(11):
            step(vec, mine[k : k + 1, 0:16], RATES[3], k)


def update(ga, gb, vec_sum, hidden, back, *state):
    steps = 2
    rows = OWN // steps

    def part(width):
        return pl.BlockSpec((rows, width), lambda n: (n, 0))

    vec = pl.BlockSpec((11, 1, 16), lambda n: (0, 0, 0))
    token = pl.BlockSpec((BLOCK // steps, HALF), lambda n: (n, 0))
    sets = (
        [pl.BlockSpec((3, rows, HALF), lambda n: (0, n, 0))] * 3
        + [part(HALF)] * 3
        + [part(FF // 2)] * 6
        + [vec] * 3
    )
    wide = [pl.BlockSpec((8, rows, w), lambda n: (0, n, 0)) for w in (WA, WB)]
    shapes = [jax.ShapeDtypeStruct(x.shape, x.dtype) for x in (hidden, back, *state)]
    return pl.pallas_call(
        update_kernel,
        grid=(steps,),
        out_shape=shapes,
        in_specs=wide + [pl.BlockSpec((16, 128), lambda n: (0, 0)), token, token] + sets,
        out_specs=[token, token] + sets,
        compiler_params=pltpu.CompilerParams(vmem_limit_bytes=62 * 1024 * 1024),
        name="update",
    )(ga, gb, vec_sum, hidden, back, *state)


def on_device(
    hidden_in,
    grad_out,
    segment_ids,
    positions,
    qkv_weight,
    dense_weight,
    fc1_weight,
    fc2_weight,
    vectors,
    qkv_first,
    qkv_second,
    dense_first,
    dense_second,
    fc1_first,
    fc1_second,
    fc2_first,
    fc2_second,
    vector_first,
    vector_second,
):
    hid = hidden_in.reshape(BLOCK, HALF)
    grad = grad_out.reshape(BLOCK, HALF)

    def turned(array):
        return jnp.moveaxis(array, 1, 0)

    (
        normed, grads, wa2, wb2, right, left, q, k_t, v, do, probs, sums, wave, vec_all, stats, bias,
    ) = forward(
        hid, grad, fc1_weight, turned(qkv_weight), fc2_weight, dense_weight, turned(vectors),
        segment_ids, positions,
    )
    hidden_out, grad_in, gb_all, ga_all, vec_sum = backward(
        right, wb2, left, wa2, normed, grads, q, k_t, v, do, probs, sums, wave,
        hid, grad, stats, vec_all, bias,
    )
    new = update(
        ga_all, gb_all, vec_sum, hidden_out, grad_in,
        turned(qkv_weight), turned(qkv_first), turned(qkv_second),
        dense_weight, dense_first, dense_second,
        fc1_weight, fc1_first, fc1_second, fc2_weight, fc2_first, fc2_second,
        turned(vectors), turned(vector_first), turned(vector_second),
    )
    return (
        new[0].reshape(hidden_in.shape),
        new[1].reshape(grad_out.shape),
        *(turned(x) for x in new[2:5]),
        *new[5:14],
        *(turned(x) for x in new[14:]),
    )


def solution(mesh):
    rows = P("dp", "ctx", "tensor")
    tokens = P("dp", "ctx")
    cube = P(("dp", "ctx"), None, "tensor")
    plain = P(("dp", "ctx"), "tensor")
    packed = P("tensor", None, ("dp", "ctx"))
    return jax.shard_map(
        on_device,
        mesh=mesh,
        in_specs=(rows, rows, tokens, tokens, cube, plain, plain, plain, packed)
        + (cube,) * 2
        + (plain,) * 6
        + (packed,) * 2,
        out_specs=(rows, rows) + (cube,) * 3 + (plain,) * 9 + (packed,) * 3,
        check_vma=False,
    )
```

```python
import functools
import math

import jax
import jax.numpy as jnp
import numpy as np
from jax import lax
from jax.experimental import pallas as pl
from jax.experimental.pallas import tpu as pltpu
from jax.sharding import PartitionSpec as P

D = 2048
HD = 64
ROT = 32
FF = 8192
STEP = 10
SEQ = 2048
BLOCK = 256
HALF = 1024
FFS = 512
HEADS = 128
WA = FFS + 3 * HEADS
WB = FFS + HEADS
OWN = 32
DIRECT = 64

BETA_ONE = 0.9
BETA_TWO = 0.95
ADAM_EPS = 1e-08
DECAY = 0.1
NORM_EPS = 1e-05
MASKED = -1e30
GELU = math.sqrt(2.0 / math.pi)

RATES = (2.0 / math.sqrt(D), 2.0 / math.sqrt(FF), 2.0 / math.sqrt(D // 16), 0.6)
MESH = pl.DeviceIdType.MESH
F32 = jnp.float32
BF16 = jnp.bfloat16
OTHERS = tuple((k // 2, k % 2) for k in range(1, 8))


class Plane:
    def __init__(self, over_ctx):
        self.dp = lax.axis_index("dp")
        self.ctx = lax.axis_index("ctx")
        self.core = lax.axis_index("tensor")
        self.over_ctx = over_ctx
        if over_ctx:
            self.ring, self.pair = lax.div(self.ctx, 2), lax.rem(self.ctx, 2)
        else:
            self.ring, self.pair = lax.rem(self.dp, 4), lax.div(self.dp, 4)

    def spot(self, along, flip):
        ring = lax.rem(self.ring + along, 4) if along else self.ring
        pair = 1 - self.pair if flip else self.pair
        return ring * 2 + pair if self.over_ctx else pair * 4 + ring

    def spot_at(self, along, flip):
        ring, pair = lax.rem(self.ring + along, 4), lax.rem(self.pair + flip, 2)
        return ring * 2 + pair if self.over_ctx else pair * 4 + ring

    def device(self, along, flip):
        spot = self.spot(along, flip)
        return (self.dp, spot, self.core) if self.over_ctx else (spot, self.ctx, self.core)


def rows_at(index, size=BLOCK):
    return pl.ds(pl.multiple_of(index * size, size), size)


def remote(src, dst, sends, recvs, number, device):
    return pltpu.make_async_remote_copy(
        src_ref=src,
        dst_ref=dst,
        send_sem=sends.at[number],
        recv_sem=recvs.at[number],
        device_id=device,
        device_id_type=MESH,
    )


def partners_of(ctx_plane, dp_plane):
    partners = [ctx_plane.device(*o) for o in OTHERS] + [dp_plane.device(*o) for o in OTHERS]
    return partners + [(ctx_plane.dp, ctx_plane.ctx, 1 - ctx_plane.core)]


def greet(partners):
    barrier = pltpu.get_barrier_semaphore()
    for partner in partners:
        pl.semaphore_signal(barrier, inc=1, device_id=partner, device_id_type=MESH)


def meet(partners):
    pl.semaphore_wait(pltpu.get_barrier_semaphore(), len(partners))


class Gather:
    def __init__(self, plane, own, region, sends, recvs, base, direct=0):
        self.direct = direct
        near, half = BLOCK - direct, BLOCK // 2
        whole, most, rest = (0, BLOCK), (0, near), (near, direct)
        plans = [
            ((0, 0), whole, (1, 0)),
            ((0, 0), whole, (3, 0)),
            ((0, 0), whole, (0, 1)),
            ((3, 0), (0, half), (1, 0)),
            ((1, 0), (half, half), (3, 0)),
            ((0, 1), most, (1, 0)),
            ((0, 1), most, (3, 0)),
            ((3, 1), (0, near // 2), (1, 0)),
            ((1, 1), (near // 2, near // 2), (3, 0)),
        ]
        if direct:
            plans += [((along, 0), rest, (0, 1)) for along in (3, 1, 2)]
        self.copies = []
        for number, (block, span, to) in enumerate(plans):
            dst = region(plane.spot(*block), *span)
            src = own if number < 3 else dst
            self.copies.append(
                remote(src, dst, sends, recvs, base + number, plane.device(*to))
            )

    def begin_ring(self):
        self.copies[0].start()
        self.copies[1].start()

    def begin_pair(self):
        self.copies[2].start()

    def ring(self, flip):
        first, relay = (5, 7) if flip else (0, 3)
        for k in (0, 1):
            self.copies[first + k].wait_recv()
            self.copies[relay + k].start()
            if self.direct and not flip:
                self.copies[9 + k].start()
        if self.direct and flip:
            self.copies[9].wait_recv()
            self.copies[10].wait_recv()

    def pair(self):
        self.copies[2].wait_recv()
        self.copies[5].start()
        self.copies[6].start()

    def far(self, flip):
        for k in (7, 8) if flip else (3, 4):
            self.copies[k].wait_recv()
        if self.direct:
            if flip:
                self.copies[11].wait_recv()
            else:
                self.copies[11].start()

    def end(self):
        for copy in self.copies:
            copy.wait_send()


class GatherCores(Gather):
    def __init__(self, plane, own, region, sends, recvs, base, core_sends, core_recvs, core_base):
        super().__init__(plane, own, region, sends, recvs, base, DIRECT)
        partner = (plane.dp, plane.ctx, 1 - plane.core)
        self.relays = {}
        for number, (along, flip) in enumerate(((0, 0),) + OTHERS):
            dst = region(plane.spot(along, flip), 0, BLOCK)
            src = dst if number else own
            self.relays[along, flip] = remote(
                src, dst, core_sends, core_recvs, core_base + number, partner
            )

    def begin_ring(self):
        super().begin_ring()
        self.relays[0, 0].start()

    def ring(self, flip):
        super().ring(flip)
        self.relays[3, flip].start()
        self.relays[1, flip].start()

    def pair(self):
        super().pair()
        self.relays[0, 1].start()

    def far(self, flip):
        super().far(flip)
        self.relays[2, flip].start()

    def end(self):
        super().end()
        for copy in self.relays.values():
            copy.wait()


def dot_nt(left, right):
    return lax.dot_general(left, right, (((1,), (1,)), ((), ())), preferred_element_type=F32)


def dot_nn(left, right):
    return jnp.dot(left, right, preferred_element_type=F32)


def dot_tn(left, right):
    return lax.dot_general(left, right, (((0,), (0,)), ((), ())), preferred_element_type=F32)


def turn(values, cosine, sine, sign):
    lane = lax.rem(lax.broadcasted_iota(jnp.int32, values.shape, 1), HD)
    low = jnp.where(lane < ROT // 2, sine, 0.0)
    high = sine - low
    up = pltpu.roll(values, HEADS - ROT // 2, 1)
    down = pltpu.roll(values, ROT // 2, 1)
    return values * cosine + sign * (down * high - up * low)


def fold(values, op):
    return op(values.reshape(BLOCK // 8, 8, BLOCK), axis=0)


def nth_spot(plane, n, flip):
    along = n + lax.div(n, 2) - 2 * lax.div(n, 3)
    return plane.spot_at(along, flip)


def forward_kernel(
    hid, grad, fc1_in, qkv_in, fc2_in, dense_in, vectors, segments, positions,
    normed_out, grad_out, wa_out, wb_out, right_out, left_out,
    q_out, k_out, v_out, do_out, probs_out, sums_out, wave_out, vec_all, stats, bias_out,
    fc1, qkv_w, fc2, dense, wa, wb, vec, place, joined, other, normed, pieces, tile, table, place_all,
    normed_all, grad_all, wa_all, wb_all, slope, right, left, q_mask, k_mask, v_t, k_t, q_own, v_own, do_own,
    scores, probs, att_t, wave, sums,
    load, local, s_act, r_act, s_core, r_core, s_w, r_w, s_small, r_small, s_pair, r_pair, store, p_sem,
):
    plane, data = Plane(True), Plane(False)
    ctx, dp, core = plane.ctx, plane.dp, plane.core
    partner = (dp, ctx, 1 - core)

    def span_at(spot, start, size):
        return pl.ds(pl.multiple_of(spot * BLOCK + start, 32), size)

    def act_region(ref):
        columns = pl.ds(pl.multiple_of(core * HALF, HALF), HALF)
        return lambda *span: ref.at[span_at(*span), columns]

    def weight_region(ref):
        return lambda *span: ref.at[span_at(*span), :]

    def scatter_rows(ref):
        start = pl.multiple_of(dp * BLOCK + ctx * OWN, OWN)
        return ref.at[pl.ds(start, OWN), :]

    normed_gather = GatherCores(
        plane, normed, act_region(normed_all), s_act, r_act, 0, s_core, r_core, 0
    )
    grad_gather = GatherCores(
        plane, grad, act_region(grad_all), s_act, r_act, 12, s_core, r_core, 8
    )

    loads = [
        pltpu.make_async_copy(src, dst, load.at[k])
        for k, (src, dst) in enumerate(
            ((fc1_in, fc1), (qkv_in, qkv_w), (fc2_in, fc2), (dense_in, dense))
        )
    ]
    for copy in loads:
        copy.start()
    partners = partners_of(plane, data)
    greet(partners)
    vec_lane = lax.broadcasted_iota(jnp.int32, (1, 128), 1)
    vec[...] = jnp.zeros((16, 128), F32)
    for k in range(11):
        spread = jnp.concatenate([vectors[k]] * 8, axis=1)
        vec[k : k + 1, :] = jnp.where(lax.div(vec_lane, 16) == ctx, spread, 0.0)
    tile[...] = vec[...].astype(BF16)
    place[...] = jnp.zeros((8, BLOCK), jnp.int32)
    place[0:1, :] = segments[...]
    place[1:2, :] = positions[...]
    place_all[ctx] = place[...]
    for copy in loads:
        copy.wait()
    for c in range(8):
        wa[c, :, 0:FFS] = fc1[:, c * FFS : (c + 1) * FFS].astype(BF16)
        wb[c, :, 0:FFS] = fc2[:, c * FFS : (c + 1) * FFS].astype(BF16)
        columns = slice(c * HEADS, (c + 1) * HEADS)
        wb[c, :, FFS:WB] = dense[:, columns].astype(BF16)
        for k in range(3):
            wa[c, :, FFS + k * HEADS : FFS + (k + 1) * HEADS] = qkv_w[k, :, columns].astype(BF16)

    piece_copies, tile_copies, place_copies, wa_copies, wb_copies = [], [], [], [], []
    for k, o in enumerate(OTHERS):
        to = plane.device(*o)
        spot = plane.spot(*o)
        piece_copies.append(remote(tile, pieces.at[k], s_small, r_small, 1 + k, to))
        place_copies.append(remote(place, place_all.at[ctx], s_small, r_small, 15 + k, to))
        wa_copies.append(remote(wa.at[spot], scatter_rows(wa_all), s_small, r_small, 22 + k, to))
        wb_copies.append(remote(wb.at[spot], scatter_rows(wb_all), s_small, r_small, 29 + k, to))
        columns = pl.ds(pl.multiple_of(dp * 128, 128), 128)
        tile_copies.append(
            remote(joined, table.at[:, columns], s_small, r_small, 8 + k, data.device(*o))
        )
    hidden_copy = remote(hid, other, s_small, r_small, 0, partner)
    meet(partners)
    for copy in piece_copies:
        copy.start()
    hidden_copy.start()
    locals_ = [
        pltpu.make_async_copy(wa.at[ctx], scatter_rows(wa_all), local.at[0]),
        pltpu.make_async_copy(wb.at[ctx], scatter_rows(wb_all), local.at[1]),
        pltpu.make_async_copy(grad, act_region(grad_all)(ctx, 0, BLOCK), local.at[2]),
        pltpu.make_async_copy(normed, act_region(normed_all)(ctx, 0, BLOCK), local.at[3]),
    ]
    for copy in locals_[:3]:
        copy.start()

    for copy in piece_copies:
        copy.wait_recv()
    total = tile[...].astype(F32)
    for k in range(7):
        total = total + pieces[k].astype(F32)
    joined[...] = total.astype(BF16)
    table[:, pl.ds(pl.multiple_of(dp * 128, 128), 128)] = total.astype(BF16)
    for copy in tile_copies + wa_copies + place_copies + wb_copies:
        copy.start()
    grad_gather.begin_ring()
    sums[...] = jnp.zeros((8, SEQ), F32)

    a_region, b_region = weight_region(wa_all), weight_region(wb_all)
    wa_gather = Gather(data, a_region(dp, 0, BLOCK), a_region, s_w, r_w, 0)
    wb_gather = Gather(data, b_region(dp, 0, BLOCK), b_region, s_w, r_w, 9)
    for copy in wa_copies:
        copy.wait_recv()
    locals_[0].wait()
    wa_gather.begin_pair()
    wa_gather.begin_ring()
    for copy in tile_copies:
        copy.wait_recv()
    hidden_copy.wait_recv()
    rows = table[...].astype(F32)
    vec_all[...] = rows
    gain, shift = rows[9:10], rows[10:11]
    lanes = lax.broadcasted_iota(jnp.int32, (16, 128), 1)

    def norm(i, carry):
        at = pl.ds(pl.multiple_of(i * 16, 16), 16)
        a, b = hid[at, :].astype(F32), other[at, :].astype(F32)
        mean = (jnp.sum(a, axis=1, keepdims=True) + jnp.sum(b, axis=1, keepdims=True)) / D
        a, b = a - mean, b - mean
        square = jnp.sum(a * a, axis=1, keepdims=True) + jnp.sum(b * b, axis=1, keepdims=True)
        inverse = lax.rsqrt(square / D + NORM_EPS)
        normed[at, :] = (a * inverse * gain + shift).astype(BF16)
        stats[at, :] = jnp.where(lanes < 64, mean, inverse)
        return carry

    lax.fori_loop(0, BLOCK // 16, norm, 0)
    normed_gather.begin_pair()
    normed_gather.begin_ring()
    locals_[3].start()
    for copy in place_copies:
        copy.wait_recv()
    lane = lax.broadcasted_iota(jnp.int32, (BLOCK, HEADS), 1)
    inner = lax.rem(lane, HD)
    first_head = lane < HD
    turning = inner < ROT
    wheel = lax.rem(lax.broadcasted_iota(jnp.int32, (1, HEADS), 1), ROT // 2)
    freq = jnp.zeros((1, HEADS), F32)
    for k in range(ROT // 2):
        freq = jnp.where(wheel == k, float(np.float32(10000.0 ** (-2.0 * k / ROT))), freq)

    def tables(i, carry):
        column = place_all[i].astype(F32).T
        angle = column[:, 1:2] * freq
        wave[0, rows_at(i), :] = jnp.where(turning, jnp.cos(angle), 1.0)
        wave[1, rows_at(i), :] = jnp.where(turning, jnp.sin(angle), 0.0)
        return carry

    lax.fori_loop(0, 8, tables, 0)

    for copy in wb_copies:
        copy.wait_recv()
    locals_[1].wait()
    wa_gather.ring(0)
    wa_gather.pair()
    normed_gather.pair()
    wb_gather.begin_pair()
    wb_gather.begin_ring()
    wa_gather.ring(1)
    normed_gather.ring(0)
    grad_gather.begin_pair()
    wb_gather.ring(0)
    wb_gather.pair()
    normed_gather.ring(1)
    grad_gather.ring(0)
    wa_gather.far(0)
    wa_gather.far(1)
    normed_gather.far(0)
    my_rows = pl.ds(pl.multiple_of(core * HALF, HALF), HALF)
    their_rows = pl.ds(pl.multiple_of((1 - core) * HALF, HALF), HALF)
    pairs = [
        remote(wa_all.at[their_rows, :], wa_out.at[1], s_pair, r_pair, 0, partner),
        remote(wb_all.at[their_rows, :], wb_out.at[1], s_pair, r_pair, 1, partner),
    ]
    pairs[0].start()
    stores = [
        pltpu.make_async_copy(wa_all.at[my_rows, :], wa_out.at[0], store.at[0]),
        pltpu.make_async_copy(wb_all.at[my_rows, :], wb_out.at[0], store.at[1]),
        pltpu.make_async_copy(wave, wave_out, store.at[2]),
    ]
    stores[0].start()
    stores[2].start()

    qkv_bias = [
        vec_all[c : c + 1, pl.ds(pl.multiple_of(ctx * HEADS, HEADS), HEADS)] for c in range(3)
    ]
    fc1_bias = vec_all[
        pl.ds(3 + lax.div(ctx, 2), 1), pl.ds(pl.multiple_of(lax.rem(ctx, 2) * FFS, FFS), FFS)
    ]

    def project(spot):
        at = rows_at(spot)
        block = normed_all[at, :]
        x = dot_nn(block, wa_all[:, 0:FFS]) + fc1_bias
        square = x * x
        tanh = jnp.tanh(x * (GELU + (GELU * 0.044715) * square))
        half = 0.5 * (1.0 + tanh)
        bend = GELU + (3.0 * 0.044715 * GELU) * square
        slope[at, :] = half + 0.5 * x * (1.0 - tanh * tanh) * bend
        right[at, 0:FFS] = (x * half).astype(BF16)
        qkv = dot_nn(block, wa_all[:, FFS:WA])
        c, s = wave[0, at, :], wave[1, at, :]
        q = turn(qkv[:, 0:HEADS] + qkv_bias[0], c, s, 1.0).astype(BF16).astype(F32) * (HD**-0.5)
        k = turn(qkv[:, HEADS : 2 * HEADS] + qkv_bias[1], c, s, 1.0)
        v = qkv[:, 2 * HEADS : 3 * HEADS] + qkv_bias[2]
        segment = place_all[spot].astype(F32).T[:, 0:1]
        feature = jnp.where(segment == inner.astype(F32), 1.0, 0.0)
        barred = jnp.where(inner < 3, (1.0 - feature) * MASKED, 0.0)
        q_mask[0, at, :] = jnp.where(first_head, q, barred).astype(BF16)
        q_mask[1, at, :] = jnp.where(first_head, barred, q).astype(BF16)
        k_mask[0, at, :] = jnp.where(first_head, k, feature).astype(BF16)
        k_mask[1, at, :] = jnp.where(first_head, feature, k).astype(BF16)
        q_own[at, :] = q.astype(BF16)
        v_own[at, :] = v.astype(BF16)
        k_t[:, at] = k.T.astype(BF16)
        v_t[:, at] = v.T.astype(BF16)

    def project_ring(flip, start, end):
        def step(n, carry):
            project(nth_spot(plane, n, flip))
            return carry

        lax.fori_loop(start, end, step, 0)

    def keep_block(ref, out, o, number):
        at = rows_at(plane.spot(*o))
        copy = pltpu.make_async_copy(ref.at[at, :], out.at[at, :], store.at[number])
        copy.start()
        return copy

    locals_[3].wait()
    for o in ((0, 0), (1, 0), (3, 0), (2, 0)):
        normed_gather.relays[o].wait_recv()
    project_ring(0, 0, 2)
    grad_gather.pair()
    wb_gather.ring(1)
    project_ring(0, 2, 4)
    normed_gather.far(1)
    for o in ((0, 1), (1, 1), (3, 1), (2, 1)):
        normed_gather.relays[o].wait_recv()
    project_ring(1, 0, 4)
    normed_copies = [
        keep_block(normed_all, normed_out, (along, flip), 16 + 2 * along + flip)
        for flip in (0, 1)
        for along in range(4)
    ]
    small_stores = [
        pltpu.make_async_copy(q_own, q_out, store.at[4]),
        pltpu.make_async_copy(k_t, k_out, store.at[5]),
        pltpu.make_async_copy(v_own, v_out, store.at[6]),
    ]
    for copy in small_stores:
        copy.start()

    key_row = lax.broadcasted_iota(jnp.int32, (BLOCK, BLOCK), 0)
    query_col = lax.broadcasted_iota(jnp.int32, (BLOCK, BLOCK), 1)
    causal = key_row <= query_col
    prob_stores, right_copies, right_keeps = {}, [], []
    for i in range(8):
        own = pl.ds(i * BLOCK, BLOCK)
        slot = i % 2

        def raw(j, h):
            return dot_nt(k_mask[h, rows_at(j), :], q_mask[h, own, :])

        def score(j, carry):
            new = []
            for h in range(2):
                s = raw(j, h)
                scores[h, rows_at(j), :] = s
                new.append(jnp.maximum(carry[h], fold(s, jnp.max)))
            return tuple(new)

        low = jnp.full((8, BLOCK), MASKED, F32)
        maxima = lax.fori_loop(0, i, score, (low, low), unroll=True)
        tops = []
        for h in range(2):
            s = jnp.where(causal, raw(i, h), MASKED)
            scores[h, own, :] = s
            top = jnp.maximum(maxima[h], fold(s, jnp.max))
            tops.append(jnp.max(top, axis=0, keepdims=True))
        if i >= 2:
            prob_stores[i - 2].wait()

        def prob(j, carry):
            totals, outs = [], []
            for h in range(2):
                p = jnp.exp(scores[h, rows_at(j), :] - tops[h])
                totals.append(carry[0][h] + fold(p, jnp.sum))
                p = p.astype(BF16)
                probs[slot, h, rows_at(j), :] = p
                outs.append(carry[1][h] + dot_nn(v_t[pl.ds(h * HD, HD), rows_at(j)], p))
            return (tuple(totals), tuple(outs))

        zero_sum, zero_out = jnp.zeros((8, BLOCK), F32), jnp.zeros((HD, BLOCK), F32)
        totals, outs = lax.fori_loop(
            0, i + 1, prob, ((zero_sum, zero_sum), (zero_out, zero_out)), unroll=True
        )
        length = (i + 1) * BLOCK
        prob_stores[i] = pltpu.make_async_copy(
            probs.at[slot, :, pl.ds(0, length), :],
            probs_out.at[i, :, pl.ds(0, length), :],
            p_sem.at[slot],
        )
        prob_stores[i].start()
        scale = [1.0 / jnp.sum(totals[h], axis=0, keepdims=True) for h in range(2)]
        both = jnp.concatenate([outs[h] * scale[h] for h in range(2)], axis=0)
        sums[0:1, own] = scale[0]
        sums[1:2, own] = scale[1]
        att_t[:, own] = both
        right[own, FFS:WB] = both.T.astype(BF16)
        right_copies.append(
            remote(right.at[own, :], right_out.at[1, own, :], s_pair, r_pair, 2 + i, partner)
        )
        right_copies[i].start()
        right_keeps.append(
            pltpu.make_async_copy(right.at[own, :], right_out.at[0, own, :], store.at[7 + i])
        )
        right_keeps[i].start()
        if i == 2:
            wb_gather.far(0)
            wb_gather.far(1)
            pairs[1].start()
            stores[1].start()
        if i == 4:
            grad_gather.far(0)
            grad_gather.ring(1)
    bias_out[...] = jnp.zeros((8, FFS), F32)

    def back(spot):
        at = rows_at(spot)
        block = grad_all[at, :]
        d_pre = dot_nn(block, wb_all[:, 0:FFS]) * slope[at, :]
        rounded = d_pre.astype(BF16)
        left[at, :] = rounded
        whole = rounded.astype(F32)
        bias_out[...] += jnp.sum(whole.reshape(BLOCK // 8, 8, FFS), axis=0)
        d_att = dot_nn(block, wb_all[:, FFS:WB])
        do_own[at, :] = d_att.astype(BF16)
        product = att_t[:, at] * d_att.astype(BF16).astype(F32).T
        sums[2:3, at] = jnp.sum(product[0:HD], axis=0, keepdims=True)
        sums[3:4, at] = jnp.sum(product[HD:], axis=0, keepdims=True)

    def back_ring(flip, start, end):
        def step(n, carry):
            back(nth_spot(plane, n, flip))
            return carry

        lax.fori_loop(start, end, step, 0)

    locals_[2].wait()
    left_copies, left_keeps = [], []

    def send_left(o):
        k = len(left_copies)
        at = rows_at(plane.spot(*o))
        left_copies.append(
            remote(left.at[at, :], left_out.at[1, at, :], s_pair, r_pair, 10 + k, partner)
        )
        left_keeps.append(
            pltpu.make_async_copy(left.at[at, :], left_out.at[0, at, :], store.at[24 + k])
        )
        left_copies[k].start()
        left_keeps[k].start()

    for along in range(4):
        grad_gather.relays[along, 0].wait_recv()
    grad_copies = [
        keep_block(grad_all, grad_out, (along, 0), 32 + 2 * along) for along in range(4)
    ]
    back_ring(0, 0, 4)
    for along in range(4):
        send_left((along, 0))
    for along in (0, 1, 3):
        grad_gather.relays[along, 1].wait_recv()
        grad_copies.append(keep_block(grad_all, grad_out, (along, 1), 33 + 2 * along))
    back_ring(1, 0, 2)
    grad_gather.far(1)
    back_ring(1, 2, 3)
    for along in (0, 1, 3):
        send_left((along, 1))
    grad_gather.relays[2, 1].wait_recv()
    grad_copies.append(keep_block(grad_all, grad_out, (2, 1), 37))
    back_ring(1, 3, 4)
    send_left((2, 1))
    last_stores = [
        pltpu.make_async_copy(do_own, do_out, store.at[40]),
        pltpu.make_async_copy(sums, sums_out, store.at[41]),
    ]
    for copy in last_stores:
        copy.start()

    for gather in (grad_gather, normed_gather):
        for copy in gather.copies:
            copy.wait_send()
        for copy in gather.relays.values():
            copy.wait_send()
    wa_gather.end()
    wb_gather.end()
    hidden_copy.wait_send()
    for copy in piece_copies + tile_copies + wa_copies + wb_copies + place_copies:
        copy.wait_send()
    for copy in pairs + right_copies + left_copies:
        copy.wait()
    for copy in stores + small_stores + right_keeps + left_keeps + last_stores:
        copy.wait()
    for copy in normed_copies + grad_copies + [prob_stores[6], prob_stores[7]]:
        copy.wait()


def forward(*args):
    hbm = pl.BlockSpec(memory_space=pl.ANY)
    vmem = pl.BlockSpec(memory_space=pltpu.VMEM)
    dma = pltpu.SemaphoreType.DMA

    def shape(*dims, kind=BF16):
        return jax.ShapeDtypeStruct(dims, kind)

    return pl.pallas_call(
        forward_kernel,
        out_shape=(
            shape(SEQ, D),
            shape(SEQ, D),
            shape(2, HALF, WA),
            shape(2, HALF, WB),
            shape(2, SEQ, WB),
            shape(2, SEQ, FFS),
            shape(SEQ, HEADS),
            shape(HEADS, SEQ),
            shape(SEQ, HEADS),
            shape(SEQ, HEADS),
            shape(8, 2, SEQ, BLOCK),
            shape(8, SEQ, kind=F32),
            shape(2, SEQ, HEADS, kind=F32),
            shape(16, HALF, kind=F32),
            shape(BLOCK, 128, kind=F32),
            shape(8, FFS, kind=F32),
        ),
        in_specs=[vmem] + [hbm] * 5 + [vmem] * 3,
        out_specs=(hbm,) * 13 + (vmem,) * 3,
        scratch_shapes=[
            pltpu.VMEM((OWN, FF // 2), F32),
            pltpu.VMEM((3, OWN, HALF), F32),
            pltpu.VMEM((OWN, FF // 2), F32),
            pltpu.VMEM((OWN, HALF), F32),
            pltpu.VMEM((8, OWN, WA), BF16),
            pltpu.VMEM((8, OWN, WB), BF16),
            pltpu.VMEM((16, 128), F32),
            pltpu.VMEM((8, BLOCK), jnp.int32),
            pltpu.VMEM((16, 128), BF16),
            pltpu.VMEM((BLOCK, HALF), BF16),
            pltpu.VMEM((BLOCK, HALF), BF16),
            pltpu.VMEM((7, 16, 128), BF16),
            pltpu.VMEM((16, 128), BF16),
            pltpu.VMEM((16, HALF), BF16),
            pltpu.VMEM((8, 8, BLOCK), jnp.int32),
            pltpu.VMEM((SEQ, D), BF16),
            pltpu.VMEM((SEQ, D), BF16),
            pltpu.VMEM((D, WA), BF16),
            pltpu.VMEM((D, WB), BF16),
            pltpu.VMEM((SEQ, FFS), F32),
            pltpu.VMEM((SEQ, WB), BF16),
            pltpu.VMEM((SEQ, FFS), BF16),
            pltpu.VMEM((2, SEQ, HEADS), BF16),
            pltpu.VMEM((2, SEQ, HEADS), BF16),
            pltpu.VMEM((HEADS, SEQ), BF16),
            pltpu.VMEM((HEADS, SEQ), BF16),
            pltpu.VMEM((SEQ, HEADS), BF16),
            pltpu.VMEM((SEQ, HEADS), BF16),
            pltpu.VMEM((SEQ, HEADS), BF16),
            pltpu.VMEM((2, SEQ, BLOCK), F32),
            pltpu.VMEM((2, 2, SEQ, BLOCK), BF16),
            pltpu.VMEM((HEADS, SEQ), F32),
            pltpu.VMEM((2, SEQ, HEADS), F32),
            pltpu.VMEM((8, SEQ), F32),
            dma((4,)),
            dma((4,)),
            dma((24,)),
            dma((24,)),
            dma((16,)),
            dma((16,)),
            dma((18,)),
            dma((18,)),
            dma((36,)),
            dma((36,)),
            dma((18,)),
            dma((18,)),
            dma((42,)),
            dma((2,)),
        ],
        compiler_params=pltpu.CompilerParams(
            collective_id=0, has_side_effects=True, vmem_limit_bytes=62 * 1024 * 1024
        ),
        name="forward",
    )(*args)


def add_rows(dst, terms, count, chunk):
    def step(i, carry):
        at = pl.ds(pl.multiple_of(i * chunk, chunk), chunk)
        total = terms[0][at, :].astype(F32)
        for term in terms[1:]:
            total = total + term[at, :].astype(F32)
        dst[at, :] = total.astype(dst.dtype)
        return carry

    lax.fori_loop(0, count // chunk, step, 0)


class Reduce:
    def __init__(self, plane, acc, landing, sends, recvs, base):
        half_up, half_down, up, down, across = landing[:5]
        self.plane, self.acc, self.across = plane, acc, across
        self.near = (half_up, half_down, up, down)
        self.rows = across.shape[0]
        self.early = landing[5] if len(landing) > 5 else None
        self.direct = DIRECT if self.early is not None else 0
        self.sizes = (self.rows - self.direct, self.rows)
        self.copies = []
        for j, flip in ((0, 1), (1, 0)):
            far, size = plane.spot(2, flip), self.sizes[j]
            low, high, most = pl.ds(0, size // 2), pl.ds(size // 2, size // 2), pl.ds(0, size)
            for number, (src, dst, along) in enumerate(
                (
                    (acc.at[far, low, :], half_up.at[j, low, :], 1),
                    (acc.at[far, high, :], half_down.at[j, low, :], 3),
                    (acc.at[plane.spot(1, flip), most, :], up.at[j, most, :], 1),
                    (acc.at[plane.spot(3, flip), most, :], down.at[j, most, :], 3),
                )
            ):
                self.copies.append(
                    remote(src, dst, sends, recvs, base + 4 * j + number, plane.device(along, 0))
                )
        across_device = plane.device(0, 1)
        self.copies.append(
            remote(acc.at[plane.spot(0, 1)], across, sends, recvs, base + 8, across_device)
        )
        if self.direct:
            self.rest = pl.ds(self.sizes[0], self.direct)
            for k, along in enumerate((2, 1, 3)):
                src = acc.at[plane.spot(along, 1), self.rest, :]
                self.copies.append(
                    remote(src, self.early.at[k], sends, recvs, base + 9 + k, across_device)
                )

    def send_early(self):
        self.copies[10].start()
        self.copies[11].start()

    def add_early(self, k, along):
        self.copies[9 + k].wait_recv()
        dst = self.acc.at[self.plane.spot(along, 0), self.rest, :]
        add_rows(dst, [dst, self.early.at[k]], self.direct, 16)

    def first(self, j):
        if self.direct and j:
            self.add_early(0, 2)
        self.copies[4 * j].start()
        self.copies[4 * j + 1].start()
        if self.direct and not j:
            self.copies[9].start()

    def second(self, j):
        if self.direct and j:
            self.add_early(1, 1)
            self.add_early(2, 3)
        half = self.sizes[j] // 2
        for number, along in ((0, 1), (1, 3)):
            self.copies[4 * j + number].wait_recv()
            dst = self.acc.at[self.plane.spot(along, 1 - j), pl.ds(number * half, half), :]
            add_rows(dst, [dst, self.near[number].at[j]], half, 16)
            self.copies[4 * j + number + 2].start()

    def third(self):
        self.copies[2].wait_recv()
        self.copies[3].wait_recv()
        dst = self.acc.at[self.plane.spot(0, 1)]
        add_rows(dst, [dst, self.near[2].at[0], self.near[3].at[0]], self.sizes[0], 16)
        self.copies[8].start()

    def arrived(self):
        for k in (6, 7, 8):
            self.copies[k].wait_recv()
        mine = self.acc.at[self.plane.spot(0, 0)]
        return [mine, self.near[2].at[1], self.near[3].at[1], self.across]

    def last(self, dst):
        add_rows(dst, self.arrived(), self.rows, 16)

    def end(self):
        for copy in self.copies:
            copy.wait_send()


def backward_kernel(
    right_in, wb_in, left_in, wa_in, normed, grads, q_in, k_in, v_in, do_in,
    probs_in, sums, wave_in, hid, grad, stats, vec_all, bias_in,
    hidden_out, grad_in, gb_all, ga_all, vec_sum,
    right, left, weight, stream, q_all, k_t, v_all, do_all, probs_odd, probs_even, wave, d_k, d_v,
    out_acc, dx_acc, gb_acc, ga_acc,
    out_a, out_b, out_c, out_d, out_e, out_f, dx_a, dx_b, dx_c, dx_d, dx_e, dx_f, gb_a, gb_b, gb_c, gb_d, gb_e,
    ga_a, ga_b, ga_c, ga_d, ga_e, gb_done, ga_done, bias, final, vec, vec_in, vec_tile, tile_in, row_own, row_in,
    load, s_stream, s_probs, s_pair, r_pair, s_red, r_red, s_small, r_small, keep,
):
    plane, data = Plane(True), Plane(False)
    ctx, dp, core = plane.ctx, plane.dp, plane.core
    partner = (dp, ctx, 1 - core)
    loads = {
        "weight": pltpu.make_async_copy(wb_in, weight.at[:, :, pl.ds(0, WB)], load.at[0]),
        "right": pltpu.make_async_copy(right_in, right, load.at[1]),
        "left": pltpu.make_async_copy(left_in, left.at[:, :, pl.ds(0, FFS)], load.at[2]),
        "q": pltpu.make_async_copy(q_in, q_all, load.at[4]),
        "k": pltpu.make_async_copy(k_in, k_t, load.at[5]),
        "v": pltpu.make_async_copy(v_in, v_all, load.at[6]),
        "do": pltpu.make_async_copy(do_in, do_all, load.at[7]),
    }
    loads["weight"].start()
    loads["right"].start()
    partners = partners_of(plane, data)
    greet(partners)

    out = Reduce(plane, out_acc, (out_a, out_b, out_c, out_d, out_e, out_f), s_red, r_red, 0)
    dx = Reduce(plane, dx_acc, (dx_a, dx_b, dx_c, dx_d, dx_e, dx_f), s_red, r_red, 12)
    gb = Reduce(data, gb_acc, (gb_a, gb_b, gb_c, gb_d, gb_e), s_red, r_red, 24)
    ga = Reduce(data, ga_acc, (ga_a, ga_b, ga_c, ga_d, ga_e), s_red, r_red, 33)

    def spot_of(where, n):
        group = lax.div(n + 2, 4)
        inside = n + 2 - 4 * group
        near = 1 - lax.rem(group + 1, 2)
        along = near * (1 + 2 * lax.rem(inside, 2)) + (1 - near) * (2 - group)
        flip = near * (1 - lax.div(inside, 2)) + (1 - near) * (1 - lax.rem(inside, 2))
        return where.spot_at(along, flip)

    def out_block(n, carry):
        spot = spot_of(plane, n)
        at = rows_at(spot)
        total = dot_nt(right[0, at, :], weight[0, :, 0:WB])
        total = total + dot_nt(right[1, at, :], weight[1, :, 0:WB])
        out_acc[spot] = total.astype(BF16)
        return carry

    def dx_block(n, carry):
        spot = spot_of(plane, n)
        at = rows_at(spot)
        total = dot_nt(left[0, at, :], weight[0])
        total = total + dot_nt(left[1, at, :], weight[1])
        dx_acc[spot] = total.astype(BF16)
        return carry

    def fetch(source, n):
        columns = rows_at(spot_of(data, n))
        slot = lax.rem(n, 2)
        return pltpu.make_async_copy(source.at[:, columns], stream.at[slot], s_stream.at[slot])

    def weight_blocks(source, factor, acc, start, end):
        def step(n, carry):
            @pl.when(n < 7)
            def _():
                fetch(source, n + 1).start()

            fetch(source, n).wait()
            total = dot_tn(stream[lax.rem(n, 2)], factor[0])
            acc[spot_of(data, n)] = total.astype(BF16)
            return carry

        lax.fori_loop(start, end, step, 0)

    loads["weight"].wait()
    loads["right"].wait()
    fetch(grads, 0).start()
    lax.fori_loop(0, 1, out_block, 0)
    meet(partners)
    out.first(0)
    for name in ("q", "k", "v", "do", "left"):
        loads[name].start()
    lax.fori_loop(1, 4, out_block, 0)
    out.send_early()
    lax.fori_loop(4, 8, out_block, 0)
    weight_load = pltpu.make_async_copy(wa_in, weight, load.at[8])
    weight_load.start()
    out.second(0)
    out.first(1)
    weight_blocks(grads, right, gb_acc, 0, 1)
    gb.first(0)
    weight_blocks(grads, right, gb_acc, 1, 6)
    gb.second(0)
    gb.first(1)
    weight_blocks(grads, right, gb_acc, 6, 8)
    fetch(normed, 0).start()

    lane = lax.broadcasted_iota(jnp.int32, (BLOCK, HEADS), 1)
    heads = (lane < HD, lane >= HD)
    bias[...] = jnp.zeros((8, 3 * HEADS), F32)

    def clear(i, carry):
        d_k[rows_at(i), :] = jnp.zeros((BLOCK, HEADS), F32)
        d_v[rows_at(i), :] = jnp.zeros((BLOCK, HEADS), F32)
        return carry

    lax.fori_loop(0, 8, clear, 0)

    def probs_of(i):
        length = pl.ds(0, (i + 1) * BLOCK)
        buffer = probs_odd if i % 2 else probs_even
        return [
            pltpu.make_async_copy(
                probs_in.at[i, :, length, :], buffer.at[:, length, :], s_probs.at[i % 2]
            ),
            pltpu.make_async_copy(
                wave_in.at[:, pl.ds(i * BLOCK, BLOCK), :], wave.at[i % 2], s_probs.at[2 + i % 2]
            ),
        ]

    for name in ("q", "k", "v", "do"):
        loads[name].wait()
    arriving = {7: probs_of(7)}
    for copy in arriving[7]:
        copy.start()
    swaps = []
    for i in range(7, -1, -1):
        own = pl.ds(i * BLOCK, BLOCK)
        if i:
            arriving[i - 1] = probs_of(i - 1)
            for copy in arriving[i - 1]:
                copy.start()
        for copy in arriving[i]:
            copy.wait()
        probs = probs_odd if i % 2 else probs_even
        scale = [sums[h : h + 1, own] for h in range(2)]
        delta = [sums[2 + h : 3 + h, own] for h in range(2)]
        q, do = q_all[own, :].astype(F32), do_all[own, :].astype(F32)
        q_plain = [jnp.where(heads[h], q, 0.0).astype(BF16) for h in range(2)]
        do_plain = [jnp.where(heads[h], do, 0.0).astype(BF16) for h in range(2)]

        def back(j, carry):
            at, new = rows_at(j), []
            add_k, add_v = d_k[at, :], d_v[at, :]
            for h in range(2):
                p = probs[h, at, :].astype(F32) * scale[h]
                d_p = dot_nt(v_all[at, :], do_plain[h])
                d_s = (p * (d_p - delta[h])).astype(BF16)
                add_v = add_v + dot_nn(p.astype(BF16), do_plain[h])
                add_k = add_k + dot_nn(d_s, q_plain[h])
                new.append(carry[h] + dot_nn(k_t[pl.ds(h * HD, HD), at], d_s))
            d_k[at, :] = add_k
            d_v[at, :] = add_v
            return tuple(new)

        zero_out = jnp.zeros((HD, BLOCK), F32)
        d_q = lax.fori_loop(0, i + 1, back, (zero_out, zero_out), unroll=True)
        d_q = jnp.concatenate(d_q, axis=0).T * (HD**-0.5)
        c, s = wave[i % 2, 0], wave[i % 2, 1]
        parts = (turn(d_q, c, s, -1.0), turn(d_k[own, :], c, s, -1.0), d_v[own, :])
        for k, part in enumerate(parts):
            rounded = part.astype(BF16)
            whole = rounded.astype(F32)
            left[0, own, FFS + k * HEADS : FFS + (k + 1) * HEADS] = rounded
            columns = slice(k * HEADS, (k + 1) * HEADS)
            bias[:, columns] += jnp.sum(whole.reshape(BLOCK // 8, 8, HEADS), axis=0)
        span = pl.ds(FFS, 3 * HEADS)
        swap = remote(
            left.at[0, own, span], left.at[1, own, span], s_pair, r_pair, i, partner
        )
        swap.start()
        swaps.append(swap)
        if i == 7:
            gb.second(1)
        if i == 6:
            out.second(1)
        if i == 3:
            out.third()
            gb.third()

    loads["left"].wait()
    weight_load.wait()
    for swap in swaps:
        swap.wait_recv()
    lax.fori_loop(0, 1, dx_block, 0)
    dx.first(0)
    weight_blocks(normed, left, ga_acc, 0, 1)
    ga.first(0)
    lax.fori_loop(1, 4, dx_block, 0)
    dx.send_early()
    weight_blocks(normed, left, ga_acc, 1, 2)
    dx.second(0)
    dx.first(1)
    weight_blocks(normed, left, ga_acc, 2, 4)
    ga.second(0)
    ga.first(1)
    lax.fori_loop(4, 8, dx_block, 0)
    weight_blocks(normed, left, ga_acc, 4, 6)
    dx.second(1)
    ga.second(1)
    weight_blocks(normed, left, ga_acc, 6, 8)
    gb.last(gb_done)
    dx.third()

    copies = {}
    keeps = []
    for n, (name, done, landed) in enumerate(
        (("gb", gb_done, gb_all), ("ga", ga_done, ga_all))
    ):
        copies[name] = [
            remote(
                done.at[rows_at(plane.spot(*o), OWN), :],
                landed.at[ctx],
                s_small,
                r_small,
                15 + 7 * n + k,
                plane.device(*o),
            )
            for k, o in enumerate(OTHERS)
        ]
        keeps.append(
            pltpu.make_async_copy(done.at[rows_at(ctx, OWN), :], landed.at[ctx], keep.at[n])
        )
    for copy in copies["gb"]:
        copy.start()
    keeps[0].start()

    ga.third()
    out.last(final)
    bias_rows = vec_all[7:8, :] + vec_all[8:9, :]

    def add_hidden(i, carry):
        at = pl.ds(pl.multiple_of(i * 16, 16), 16)
        hidden_out[at, :] = (hid[at, :].astype(F32) + final[at, :] + bias_rows).astype(BF16)
        return carry

    lax.fori_loop(0, BLOCK // 16, add_hidden, 0)
    dx.last(final)
    gain = vec_all[9:10, :]
    lanes = lax.broadcasted_iota(jnp.int32, (16, 128), 1)

    def lean(i, carry):
        at = pl.ds(pl.multiple_of(i * 16, 16), 16)
        d, h, stat = final[at, :], hid[at, :].astype(F32), stats[at, :]
        normal = (h - stat[:, 0:1]) * stat[:, 64:65]
        product = d * normal
        one = jnp.sum(d * gain, axis=1, keepdims=True)
        two = jnp.sum(product * gain, axis=1, keepdims=True)
        row_own[at, :] = jnp.where(lanes < 64, one, two)
        return (carry[0] + d, carry[1] + product, carry[2] + grad[at, :].astype(F32))

    zero = jnp.zeros((16, HALF), F32)
    rows = lax.fori_loop(0, BLOCK // 16, lean, (zero, zero, zero))
    row_copy = remote(row_own, row_in, s_small, r_small, 0, partner)
    row_copy.start()
    shift_grad, gain_grad, bias_grad = [jnp.sum(r, axis=0, keepdims=True) for r in rows]
    number = lax.broadcasted_iota(jnp.int32, (16, HALF), 0)
    vec[...] = jnp.where(
        number == 9,
        gain_grad,
        jnp.where(
            number == 10, shift_grad, jnp.where((number == 7) | (number == 8), bias_grad, 0.0)
        ),
    )
    columns = pl.ds(pl.multiple_of(ctx * HEADS, HEADS), HEADS)
    for k in range(3):
        part = jnp.sum(bias[:, k * HEADS : (k + 1) * HEADS], axis=0, keepdims=True)
        vec[k : k + 1, columns] = part
    columns = pl.ds(pl.multiple_of(lax.rem(ctx, 2) * FFS, FFS), FFS)
    part = jnp.sum(bias_in[...], axis=0, keepdims=True)
    vec[:, columns] = jnp.where(
        lax.broadcasted_iota(jnp.int32, (16, FFS), 0) == 3 + lax.div(ctx, 2), part, vec[:, columns]
    )
    vec_copies, tile_copies = [], []
    for k, o in enumerate(OTHERS):
        columns = pl.ds(pl.multiple_of(data.spot(*o) * 128, 128), 128)
        vec_copies.append(
            remote(vec.at[:, columns], vec_in.at[k], s_small, r_small, 1 + k, data.device(*o))
        )
        tile_copies.append(
            remote(vec_tile, tile_in.at[k], s_small, r_small, 8 + k, plane.device(*o))
        )
    for copy in vec_copies:
        copy.start()
    ga.last(ga_done)
    for copy in copies["ga"]:
        copy.start()
    keeps[1].start()
    for copy in vec_copies:
        copy.wait_recv()
    total = vec[:, pl.ds(pl.multiple_of(dp * 128, 128), 128)]
    for k in range(7):
        total = total + vec_in[k]
    vec_tile[...] = total
    for copy in tile_copies:
        copy.start()

    row_copy.wait()

    def tilt(i, carry):
        at = pl.ds(pl.multiple_of(i * 16, 16), 16)
        d, h, stat = final[at, :], hid[at, :].astype(F32), stats[at, :]
        inverse = stat[:, 64:65]
        normal = (h - stat[:, 0:1]) * inverse
        row = (row_own[at, :] + row_in[at, :]) / D
        change = inverse * (d * gain - row[:, 0:1] - normal * row[:, 64:65])
        grad_in[at, :] = (grad[at, :].astype(F32) + change).astype(BF16)
        return carry

    lax.fori_loop(0, BLOCK // 16, tilt, 0)
    for copy in tile_copies:
        copy.wait_recv()
    total = vec_tile[...]
    for k in range(7):
        total = total + tile_in[k]
    vec_sum[...] = total

    for name in copies:
        for copy in copies[name]:
            copy.wait()
    for copy in keeps:
        copy.wait()
    for copy in vec_copies + tile_copies + swaps:
        copy.wait_send()
    for red in (dx, out, gb, ga):
        red.end()


def backward(*args):
    hbm = pl.BlockSpec(memory_space=pl.ANY)
    vmem = pl.BlockSpec(memory_space=pltpu.VMEM)
    dma = pltpu.SemaphoreType.DMA

    def landing(rows, width):
        half = pltpu.VMEM((2, rows // 2, width), BF16)
        whole = pltpu.VMEM((2, rows, width), BF16)
        return [half, half, whole, whole, pltpu.VMEM((rows, width), BF16)]

    def shape(*dims, kind=BF16):
        return jax.ShapeDtypeStruct(dims, kind)

    return pl.pallas_call(
        backward_kernel,
        out_shape=(
            shape(BLOCK, HALF),
            shape(BLOCK, HALF),
            shape(8, OWN, WB),
            shape(8, OWN, WA),
            shape(16, 128, kind=F32),
        ),
        in_specs=[hbm] * 11 + [vmem, hbm] + [vmem] * 5,
        out_specs=(vmem, vmem, hbm, hbm, vmem),
        scratch_shapes=[
            pltpu.VMEM((2, SEQ, WB), BF16),
            pltpu.VMEM((2, SEQ, WA), BF16),
            pltpu.VMEM((2, HALF, WA), BF16),
            pltpu.VMEM((2, SEQ, BLOCK), BF16),
            pltpu.VMEM((SEQ, HEADS), BF16),
            pltpu.VMEM((HEADS, SEQ), BF16),
            pltpu.VMEM((SEQ, HEADS), BF16),
            pltpu.VMEM((SEQ, HEADS), BF16),
            pltpu.VMEM((2, SEQ, BLOCK), BF16),
            pltpu.VMEM((2, SEQ - BLOCK, BLOCK), BF16),
            pltpu.VMEM((2, 2, BLOCK, HEADS), F32),
            pltpu.VMEM((SEQ, HEADS), F32),
            pltpu.VMEM((SEQ, HEADS), F32),
            pltpu.VMEM((8, BLOCK, HALF), BF16),
            pltpu.VMEM((8, BLOCK, HALF), BF16),
            pltpu.VMEM((8, BLOCK, WB), BF16),
            pltpu.VMEM((8, BLOCK, WA), BF16),
            *landing(BLOCK, HALF),
            pltpu.VMEM((3, DIRECT, HALF), BF16),
            *landing(BLOCK, HALF),
            pltpu.VMEM((3, DIRECT, HALF), BF16),
            *landing(BLOCK, WB),
            *landing(BLOCK, WA),
            pltpu.VMEM((BLOCK, WB), BF16),
            pltpu.VMEM((BLOCK, WA), BF16),
            pltpu.VMEM((8, 3 * HEADS), F32),
            pltpu.VMEM((BLOCK, HALF), F32),
            pltpu.VMEM((16, HALF), F32),
            pltpu.VMEM((7, 16, 128), F32),
            pltpu.VMEM((16, 128), F32),
            pltpu.VMEM((7, 16, 128), F32),
            pltpu.VMEM((BLOCK, 128), F32),
            pltpu.VMEM((BLOCK, 128), F32),
            dma((10,)),
            dma((2,)),
            dma((4,)),
            dma((8,)),
            dma((8,)),
            dma((42,)),
            dma((42,)),
            dma((36,)),
            dma((36,)),
            dma((3,)),
        ],
        compiler_params=pltpu.CompilerParams(
            collective_id=1, has_side_effects=True, vmem_limit_bytes=62 * 1024 * 1024
        ),
        name="backward",
    )(*args)


def adam_step(weight, first, second, gradient, rate):
    first_new = BETA_ONE * first + (1.0 - BETA_ONE) * gradient
    second_new = BETA_TWO * second + (1.0 - BETA_TWO) * gradient * gradient
    fix_one = 1.0 - BETA_ONE**STEP
    fix_two = 1.0 - BETA_TWO**STEP
    update = first_new / fix_one / (jnp.sqrt(second_new / fix_two) + ADAM_EPS)
    return (first_new, second_new, weight - rate * (update + DECAY * weight))


def update_kernel(
    ga, gb, vec_sum, hidden, back,
    qkv_w, qkv_m, qkv_v, dense_w, dense_m, dense_v, fc1_w, fc1_m, fc1_v, fc2_w, fc2_m, fc2_v,
    vec_w, vec_m, vec_v,
    hidden_out, back_out,
    qkv_mo, qkv_vo, qkv_wo, dense_mo, dense_vo, dense_wo, fc1_mo, fc1_vo, fc1_wo,
    fc2_mo, fc2_vo, fc2_wo, vec_mo, vec_vo, vec_wo,
):
    hidden_out[...] = hidden[...]
    back_out[...] = back[...]

    fc1 = (fc1_w, fc1_m, fc1_v, fc1_mo, fc1_vo, fc1_wo)
    fc2 = (fc2_w, fc2_m, fc2_v, fc2_mo, fc2_vo, fc2_wo)
    dense = (dense_w, dense_m, dense_v, dense_mo, dense_vo, dense_wo)
    qkv = (qkv_w, qkv_m, qkv_v, qkv_mo, qkv_vo, qkv_wo)
    vec = (vec_w, vec_m, vec_v, vec_mo, vec_vo, vec_wo)

    def step(refs, gradient, rate, *at):
        w, m, v, mo, vo, wo = refs
        mo[at], vo[at], wo[at] = adam_step(w[at], m[at], v[at], gradient, rate)

    for c in range(8):
        wide, narrow = slice(c * FFS, (c + 1) * FFS), slice(c * HEADS, (c + 1) * HEADS)
        step(fc1, ga[c, :, 0:FFS].astype(F32), RATES[0], slice(None), wide)
        step(fc2, gb[c, :, 0:FFS].astype(F32), RATES[1], slice(None), wide)
        step(dense, gb[c, :, FFS:WB].astype(F32), RATES[2], slice(None), narrow)
        for k in range(3):
            columns = slice(FFS + k * HEADS, FFS + (k + 1) * HEADS)
            step(qkv, ga[c, :, columns].astype(F32), RATES[0], k, slice(None), narrow)

    @pl.when(pl.program_id(0) == 0)
    def _():
        mine = pltpu.roll(vec_sum[...], lax.rem(128 - 16 * lax.axis_index("ctx"), 128), 1)
        for k in range(11):
            step(vec, mine[k : k + 1, 0:16], RATES[3], k)


def update(ga, gb, vec_sum, hidden, back, *state):
    steps = 2
    rows = OWN // steps

    def part(width):
        return pl.BlockSpec((rows, width), lambda n: (n, 0))

    vec = pl.BlockSpec((11, 1, 16), lambda n: (0, 0, 0))
    token = pl.BlockSpec((BLOCK // steps, HALF), lambda n: (n, 0))
    sets = (
        [pl.BlockSpec((3, rows, HALF), lambda n: (0, n, 0))] * 3
        + [part(HALF)] * 3
        + [part(FF // 2)] * 6
        + [vec] * 3
    )
    wide = [pl.BlockSpec((8, rows, w), lambda n: (0, n, 0)) for w in (WA, WB)]
    shapes = [jax.ShapeDtypeStruct(x.shape, x.dtype) for x in (hidden, back, *state)]
    return pl.pallas_call(
        update_kernel,
        grid=(steps,),
        out_shape=shapes,
        in_specs=wide + [pl.BlockSpec((16, 128), lambda n: (0, 0)), token, token] + sets,
        out_specs=[token, token] + sets,
        compiler_params=pltpu.CompilerParams(vmem_limit_bytes=62 * 1024 * 1024),
        name="update",
    )(ga, gb, vec_sum, hidden, back, *state)


def on_device(
    hidden_in,
    grad_out,
    segment_ids,
    positions,
    qkv_weight,
    dense_weight,
    fc1_weight,
    fc2_weight,
    vectors,
    qkv_first,
    qkv_second,
    dense_first,
    dense_second,
    fc1_first,
    fc1_second,
    fc2_first,
    fc2_second,
    vector_first,
    vector_second,
):
    hid = hidden_in.reshape(BLOCK, HALF)
    grad = grad_out.reshape(BLOCK, HALF)

    def turned(array):
        return jnp.moveaxis(array, 1, 0)

    (
        normed, grads, wa2, wb2, right, left, q, k_t, v, do, probs, sums, wave, vec_all, stats, bias,
    ) = forward(
        hid, grad, fc1_weight, turned(qkv_weight), fc2_weight, dense_weight, turned(vectors),
        segment_ids, positions,
    )
    hidden_out, grad_in, gb_all, ga_all, vec_sum = backward(
        right, wb2, left, wa2, normed, grads, q, k_t, v, do, probs, sums, wave,
        hid, grad, stats, vec_all, bias,
    )
    new = update(
        ga_all, gb_all, vec_sum, hidden_out, grad_in,
        turned(qkv_weight), turned(qkv_first), turned(qkv_second),
        dense_weight, dense_first, dense_second,
        fc1_weight, fc1_first, fc1_second, fc2_weight, fc2_first, fc2_second,
        turned(vectors), turned(vector_first), turned(vector_second),
    )
    return (
        new[0].reshape(hidden_in.shape),
        new[1].reshape(grad_out.shape),
        *(turned(x) for x in new[2:5]),
        *new[5:14],
        *(turned(x) for x in new[14:]),
    )


def solution(mesh):
    rows = P("dp", "ctx", "tensor")
    tokens = P("dp", "ctx")
    cube = P(("dp", "ctx"), None, "tensor")
    plain = P(("dp", "ctx"), "tensor")
    packed = P("tensor", None, ("dp", "ctx"))
    return jax.shard_map(
        on_device,
        mesh=mesh,
        in_specs=(rows, rows, tokens, tokens, cube, plain, plain, plain, packed)
        + (cube,) * 2
        + (plain,) * 6
        + (packed,) * 2,
        out_specs=(rows, rows) + (cube,) * 3 + (plain,) * 9 + (packed,) * 3,
        check_vma=False,
    )
```

```python
import functools
import math

import jax
import jax.numpy as jnp
import numpy as np
from jax import lax
from jax.experimental import pallas as pl
from jax.experimental.pallas import tpu as pltpu
from jax.sharding import PartitionSpec as P

D = 2048
HD = 64
ROT = 32
FF = 8192
STEP = 10
SEQ = 2048
BLOCK = 256
HALF = 1024
FFS = 512
HEADS = 128
WA = FFS + 3 * HEADS
WB = FFS + HEADS
OWN = 32
DIRECT = 64

BETA_ONE = 0.9
BETA_TWO = 0.95
ADAM_EPS = 1e-08
DECAY = 0.1
NORM_EPS = 1e-05
MASKED = -1e30
GELU = math.sqrt(2.0 / math.pi)

RATES = (2.0 / math.sqrt(D), 2.0 / math.sqrt(FF), 2.0 / math.sqrt(D // 16), 0.6)
MESH = pl.DeviceIdType.MESH
F32 = jnp.float32
BF16 = jnp.bfloat16
OTHERS = tuple((k // 2, k % 2) for k in range(1, 8))


class Plane:
    def __init__(self, over_ctx):
        self.dp = lax.axis_index("dp")
        self.ctx = lax.axis_index("ctx")
        self.core = lax.axis_index("tensor")
        self.over_ctx = over_ctx
        if over_ctx:
            self.ring, self.pair = lax.div(self.ctx, 2), lax.rem(self.ctx, 2)
        else:
            self.ring, self.pair = lax.rem(self.dp, 4), lax.div(self.dp, 4)

    def spot(self, along, flip):
        ring = lax.rem(self.ring + along, 4) if along else self.ring
        pair = 1 - self.pair if flip else self.pair
        return ring * 2 + pair if self.over_ctx else pair * 4 + ring

    def spot_at(self, along, flip):
        ring, pair = lax.rem(self.ring + along, 4), lax.rem(self.pair + flip, 2)
        return ring * 2 + pair if self.over_ctx else pair * 4 + ring

    def device(self, along, flip):
        spot = self.spot(along, flip)
        return (self.dp, spot, self.core) if self.over_ctx else (spot, self.ctx, self.core)


def rows_at(index, size=BLOCK):
    return pl.ds(pl.multiple_of(index * size, size), size)


def remote(src, dst, sends, recvs, number, device):
    return pltpu.make_async_remote_copy(
        src_ref=src,
        dst_ref=dst,
        send_sem=sends.at[number],
        recv_sem=recvs.at[number],
        device_id=device,
        device_id_type=MESH,
    )


def partners_of(ctx_plane, dp_plane):
    partners = [ctx_plane.device(*o) for o in OTHERS] + [dp_plane.device(*o) for o in OTHERS]
    return partners + [(ctx_plane.dp, ctx_plane.ctx, 1 - ctx_plane.core)]


def greet(partners):
    barrier = pltpu.get_barrier_semaphore()
    for partner in partners:
        pl.semaphore_signal(barrier, inc=1, device_id=partner, device_id_type=MESH)


def meet(partners):
    pl.semaphore_wait(pltpu.get_barrier_semaphore(), len(partners))


class Gather:
    def __init__(self, plane, own, region, sends, recvs, base, direct=0):
        self.direct = direct
        near, half = BLOCK - direct, BLOCK // 2
        whole, most, rest = (0, BLOCK), (0, near), (near, direct)
        plans = [
            ((0, 0), whole, (1, 0)),
            ((0, 0), whole, (3, 0)),
            ((0, 0), whole, (0, 1)),
            ((3, 0), (0, half), (1, 0)),
            ((1, 0), (half, half), (3, 0)),
            ((0, 1), most, (1, 0)),
            ((0, 1), most, (3, 0)),
            ((3, 1), (0, near // 2), (1, 0)),
            ((1, 1), (near // 2, near // 2), (3, 0)),
        ]
        if direct:
            plans += [((along, 0), rest, (0, 1)) for along in (3, 1, 2)]
        self.copies = []
        for number, (block, span, to) in enumerate(plans):
            dst = region(plane.spot(*block), *span)
            src = own if number < 3 else dst
            self.copies.append(
                remote(src, dst, sends, recvs, base + number, plane.device(*to))
            )

    def begin_ring(self):
        self.copies[0].start()
        self.copies[1].start()

    def begin_pair(self):
        self.copies[2].start()

    def ring(self, flip):
        first, relay = (5, 7) if flip else (0, 3)
        for k in (0, 1):
            self.copies[first + k].wait_recv()
            self.copies[relay + k].start()
            if self.direct and not flip:
                self.copies[9 + k].start()
        if self.direct and flip:
            self.copies[9].wait_recv()
            self.copies[10].wait_recv()

    def pair(self):
        self.copies[2].wait_recv()
        self.copies[5].start()
        self.copies[6].start()

    def far(self, flip):
        for k in (7, 8) if flip else (3, 4):
            self.copies[k].wait_recv()
        if self.direct:
            if flip:
                self.copies[11].wait_recv()
            else:
                self.copies[11].start()

    def end(self):
        for copy in self.copies:
            copy.wait_send()


class GatherCores(Gather):
    def __init__(self, plane, own, region, sends, recvs, base, core_sends, core_recvs, core_base):
        super().__init__(plane, own, region, sends, recvs, base, DIRECT)
        partner = (plane.dp, plane.ctx, 1 - plane.core)
        self.relays = {}
        for number, (along, flip) in enumerate(((0, 0),) + OTHERS):
            dst = region(plane.spot(along, flip), 0, BLOCK)
            src = dst if number else own
            self.relays[along, flip] = remote(
                src, dst, core_sends, core_recvs, core_base + number, partner
            )

    def begin_ring(self):
        super().begin_ring()
        self.relays[0, 0].start()

    def ring(self, flip):
        super().ring(flip)
        self.relays[3, flip].start()
        self.relays[1, flip].start()

    def pair(self):
        super().pair()
        self.relays[0, 1].start()

    def far(self, flip):
        super().far(flip)
        self.relays[2, flip].start()

    def end(self):
        super().end()
        for copy in self.relays.values():
            copy.wait()


def dot_nt(left, right):
    return lax.dot_general(left, right, (((1,), (1,)), ((), ())), preferred_element_type=F32)


def dot_nn(left, right):
    return jnp.dot(left, right, preferred_element_type=F32)


def dot_tn(left, right):
    return lax.dot_general(left, right, (((0,), (0,)), ((), ())), preferred_element_type=F32)


def turn(values, cosine, sine, sign):
    lane = lax.rem(lax.broadcasted_iota(jnp.int32, values.shape, 1), HD)
    low = jnp.where(lane < ROT // 2, sine, 0.0)
    high = sine - low
    up = pltpu.roll(values, HEADS - ROT // 2, 1)
    down = pltpu.roll(values, ROT // 2, 1)
    return values * cosine + sign * (down * high - up * low)


def fold(values, op):
    return op(values.reshape(BLOCK // 8, 8, BLOCK), axis=0)


def nth_spot(plane, n, flip):
    along = n + lax.div(n, 2) - 2 * lax.div(n, 3)
    return plane.spot_at(along, flip)


def forward_kernel(
    hid, grad, fc1_in, qkv_in, fc2_in, dense_in, vectors, segments, positions,
    normed_out, grad_out, wa_out, wb_out, right_out, left_out,
    q_out, k_out, v_out, do_out, probs_out, sums_out, wave_out, vec_all, stats, bias_out,
    fc1, qkv_w, fc2, dense, wa, wb, vec, place, joined, other, normed, pieces, tile, table, place_all,
    normed_all, grad_all, wa_all, wb_all, slope, right, left, q_mask, k_mask, v_t, k_t, q_own, v_own, do_own,
    scores, probs, att_t, wave, sums,
    load, local, s_act, r_act, s_core, r_core, s_w, r_w, s_small, r_small, s_pair, r_pair, store, p_sem,
):
    plane, data = Plane(True), Plane(False)
    ctx, dp, core = plane.ctx, plane.dp, plane.core
    partner = (dp, ctx, 1 - core)

    def span_at(spot, start, size):
        return pl.ds(pl.multiple_of(spot * BLOCK + start, 32), size)

    def act_region(ref):
        columns = pl.ds(pl.multiple_of(core * HALF, HALF), HALF)
        return lambda *span: ref.at[span_at(*span), columns]

    def weight_region(ref):
        return lambda *span: ref.at[span_at(*span), :]

    def scatter_rows(ref):
        start = pl.multiple_of(dp * BLOCK + ctx * OWN, OWN)
        return ref.at[pl.ds(start, OWN), :]

    normed_gather = GatherCores(
        plane, normed, act_region(normed_all), s_act, r_act, 0, s_core, r_core, 0
    )
    grad_gather = GatherCores(
        plane, grad, act_region(grad_all), s_act, r_act, 12, s_core, r_core, 8
    )

    loads = [
        pltpu.make_async_copy(src, dst, load.at[k])
        for k, (src, dst) in enumerate(
            ((fc1_in, fc1), (qkv_in, qkv_w), (fc2_in, fc2), (dense_in, dense))
        )
    ]
    for copy in loads:
        copy.start()
    partners = partners_of(plane, data)
    greet(partners)
    vec_lane = lax.broadcasted_iota(jnp.int32, (1, 128), 1)
    vec[...] = jnp.zeros((16, 128), F32)
    for k in range(11):
        spread = jnp.concatenate([vectors[k]] * 8, axis=1)
        vec[k : k + 1, :] = jnp.where(lax.div(vec_lane, 16) == ctx, spread, 0.0)
    tile[...] = vec[...].astype(BF16)
    place[...] = jnp.zeros((8, BLOCK), jnp.int32)
    place[0:1, :] = segments[...]
    place[1:2, :] = positions[...]
    place_all[ctx] = place[...]
    for copy in loads:
        copy.wait()
    for c in range(8):
        wa[c, :, 0:FFS] = fc1[:, c * FFS : (c + 1) * FFS].astype(BF16)
        wb[c, :, 0:FFS] = fc2[:, c * FFS : (c + 1) * FFS].astype(BF16)
        columns = slice(c * HEADS, (c + 1) * HEADS)
        wb[c, :, FFS:WB] = dense[:, columns].astype(BF16)
        for k in range(3):
            wa[c, :, FFS + k * HEADS : FFS + (k + 1) * HEADS] = qkv_w[k, :, columns].astype(BF16)

    piece_copies, tile_copies, place_copies, wa_copies, wb_copies = [], [], [], [], []
    for k, o in enumerate(OTHERS):
        to = plane.device(*o)
        spot = plane.spot(*o)
        piece_copies.append(remote(tile, pieces.at[k], s_small, r_small, 1 + k, to))
        place_copies.append(remote(place, place_all.at[ctx], s_small, r_small, 15 + k, to))
        wa_copies.append(remote(wa.at[spot], scatter_rows(wa_all), s_small, r_small, 22 + k, to))
        wb_copies.append(remote(wb.at[spot], scatter_rows(wb_all), s_small, r_small, 29 + k, to))
        columns = pl.ds(pl.multiple_of(dp * 128, 128), 128)
        tile_copies.append(
            remote(joined, table.at[:, columns], s_small, r_small, 8 + k, data.device(*o))
        )
    hidden_copy = remote(hid, other, s_small, r_small, 0, partner)
    meet(partners)
    for copy in piece_copies:
        copy.start()
    hidden_copy.start()
    locals_ = [
        pltpu.make_async_copy(wa.at[ctx], scatter_rows(wa_all), local.at[0]),
        pltpu.make_async_copy(wb.at[ctx], scatter_rows(wb_all), local.at[1]),
        pltpu.make_async_copy(grad, act_region(grad_all)(ctx, 0, BLOCK), local.at[2]),
        pltpu.make_async_copy(normed, act_region(normed_all)(ctx, 0, BLOCK), local.at[3]),
    ]
    for copy in locals_[:3]:
        copy.start()

    for copy in piece_copies:
        copy.wait_recv()
    total = tile[...].astype(F32)
    for k in range(7):
        total = total + pieces[k].astype(F32)
    joined[...] = total.astype(BF16)
    table[:, pl.ds(pl.multiple_of(dp * 128, 128), 128)] = total.astype(BF16)
    for copy in tile_copies + wa_copies + place_copies + wb_copies:
        copy.start()
    grad_gather.begin_ring()
    sums[...] = jnp.zeros((8, SEQ), F32)

    a_region, b_region = weight_region(wa_all), weight_region(wb_all)
    wa_gather = Gather(data, a_region(dp, 0, BLOCK), a_region, s_w, r_w, 0)
    wb_gather = Gather(data, b_region(dp, 0, BLOCK), b_region, s_w, r_w, 9)
    for copy in wa_copies:
        copy.wait_recv()
    locals_[0].wait()
    wa_gather.begin_pair()
    wa_gather.begin_ring()
    for copy in tile_copies:
        copy.wait_recv()
    hidden_copy.wait_recv()
    rows = table[...].astype(F32)
    vec_all[...] = rows
    gain, shift = rows[9:10], rows[10:11]
    lanes = lax.broadcasted_iota(jnp.int32, (16, 128), 1)

    def norm(i, carry):
        at = pl.ds(pl.multiple_of(i * 16, 16), 16)
        a, b = hid[at, :].astype(F32), other[at, :].astype(F32)
        mean = (jnp.sum(a, axis=1, keepdims=True) + jnp.sum(b, axis=1, keepdims=True)) / D
        a, b = a - mean, b - mean
        square = jnp.sum(a * a, axis=1, keepdims=True) + jnp.sum(b * b, axis=1, keepdims=True)
        inverse = lax.rsqrt(square / D + NORM_EPS)
        normed[at, :] = (a * inverse * gain + shift).astype(BF16)
        stats[at, :] = jnp.where(lanes < 64, mean, inverse)
        return carry

    lax.fori_loop(0, BLOCK // 16, norm, 0)
    normed_gather.begin_pair()
    normed_gather.begin_ring()
    locals_[3].start()
    for copy in place_copies:
        copy.wait_recv()
    lane = lax.broadcasted_iota(jnp.int32, (BLOCK, HEADS), 1)
    inner = lax.rem(lane, HD)
    first_head = lane < HD
    turning = inner < ROT
    wheel = lax.rem(lax.broadcasted_iota(jnp.int32, (1, HEADS), 1), ROT // 2)
    freq = jnp.zeros((1, HEADS), F32)
    for k in range(ROT // 2):
        freq = jnp.where(wheel == k, float(np.float32(10000.0 ** (-2.0 * k / ROT))), freq)

    def tables(i, carry):
        column = place_all[i].astype(F32).T
        angle = column[:, 1:2] * freq
        wave[0, rows_at(i), :] = jnp.where(turning, jnp.cos(angle), 1.0)
        wave[1, rows_at(i), :] = jnp.where(turning, jnp.sin(angle), 0.0)
        return carry

    lax.fori_loop(0, 8, tables, 0)

    for copy in wb_copies:
        copy.wait_recv()
    locals_[1].wait()
    wa_gather.ring(0)
    wa_gather.pair()
    normed_gather.pair()
    wa_gather.ring(1)
    wb_gather.begin_pair()
    wb_gather.begin_ring()
    normed_gather.ring(0)
    grad_gather.begin_pair()
    wa_gather.far(0)
    wa_gather.far(1)
    normed_gather.far(0)
    my_rows = pl.ds(pl.multiple_of(core * HALF, HALF), HALF)
    their_rows = pl.ds(pl.multiple_of((1 - core) * HALF, HALF), HALF)
    pairs = [
        remote(wa_all.at[their_rows, :], wa_out.at[1], s_pair, r_pair, 0, partner),
        remote(wb_all.at[their_rows, :], wb_out.at[1], s_pair, r_pair, 1, partner),
    ]
    pairs[0].start()
    stores = [
        pltpu.make_async_copy(wa_all.at[my_rows, :], wa_out.at[0], store.at[0]),
        pltpu.make_async_copy(wb_all.at[my_rows, :], wb_out.at[0], store.at[1]),
        pltpu.make_async_copy(wave, wave_out, store.at[2]),
    ]
    stores[0].start()
    stores[2].start()

    qkv_bias = [
        vec_all[c : c + 1, pl.ds(pl.multiple_of(ctx * HEADS, HEADS), HEADS)] for c in range(3)
    ]
    fc1_bias = vec_all[
        pl.ds(3 + lax.div(ctx, 2), 1), pl.ds(pl.multiple_of(lax.rem(ctx, 2) * FFS, FFS), FFS)
    ]

    def project(spot):
        at = rows_at(spot)
        block = normed_all[at, :]
        x = dot_nn(block, wa_all[:, 0:FFS]) + fc1_bias
        square = x * x
        tanh = jnp.tanh(x * (GELU + (GELU * 0.044715) * square))
        half = 0.5 * (1.0 + tanh)
        bend = GELU + (3.0 * 0.044715 * GELU) * square
        slope[at, :] = half + 0.5 * x * (1.0 - tanh * tanh) * bend
        right[at, 0:FFS] = (x * half).astype(BF16)
        qkv = dot_nn(block, wa_all[:, FFS:WA])
        c, s = wave[0, at, :], wave[1, at, :]
        q = turn(qkv[:, 0:HEADS] + qkv_bias[0], c, s, 1.0).astype(BF16).astype(F32) * (HD**-0.5)
        k = turn(qkv[:, HEADS : 2 * HEADS] + qkv_bias[1], c, s, 1.0)
        v = qkv[:, 2 * HEADS : 3 * HEADS] + qkv_bias[2]
        segment = place_all[spot].astype(F32).T[:, 0:1]
        feature = jnp.where(segment == inner.astype(F32), 1.0, 0.0)
        barred = jnp.where(inner < 3, (1.0 - feature) * MASKED, 0.0)
        q_mask[0, at, :] = jnp.where(first_head, q, barred).astype(BF16)
        q_mask[1, at, :] = jnp.where(first_head, barred, q).astype(BF16)
        k_mask[0, at, :] = jnp.where(first_head, k, feature).astype(BF16)
        k_mask[1, at, :] = jnp.where(first_head, feature, k).astype(BF16)
        q_own[at, :] = q.astype(BF16)
        v_own[at, :] = v.astype(BF16)
        k_t[:, at] = k.T.astype(BF16)
        v_t[:, at] = v.T.astype(BF16)

    def project_ring(flip, start, end):
        def step(n, carry):
            project(nth_spot(plane, n, flip))
            return carry

        lax.fori_loop(start, end, step, 0)

    def keep_block(ref, out, o, number):
        at = rows_at(plane.spot(*o))
        copy = pltpu.make_async_copy(ref.at[at, :], out.at[at, :], store.at[number])
        copy.start()
        return copy

    locals_[3].wait()
    for o in ((0, 0), (1, 0), (3, 0), (2, 0)):
        normed_gather.relays[o].wait_recv()
    project_ring(0, 0, 2)
    normed_gather.ring(1)
    grad_gather.ring(0)
    project_ring(0, 2, 4)
    wb_gather.ring(0)
    wb_gather.pair()
    normed_gather.relays[0, 1].wait_recv()
    normed_gather.relays[1, 1].wait_recv()
    project_ring(1, 0, 2)
    grad_gather.pair()
    normed_gather.far(1)
    normed_gather.relays[3, 1].wait_recv()
    normed_gather.relays[2, 1].wait_recv()
    project_ring(1, 2, 4)
    normed_copies = [
        keep_block(normed_all, normed_out, (along, flip), 16 + 2 * along + flip)
        for flip in (0, 1)
        for along in range(4)
    ]
    small_stores = [
        pltpu.make_async_copy(q_own, q_out, store.at[4]),
        pltpu.make_async_copy(k_t, k_out, store.at[5]),
        pltpu.make_async_copy(v_own, v_out, store.at[6]),
    ]
    for copy in small_stores:
        copy.start()

    key_row = lax.broadcasted_iota(jnp.int32, (BLOCK, BLOCK), 0)
    query_col = lax.broadcasted_iota(jnp.int32, (BLOCK, BLOCK), 1)
    causal = key_row <= query_col
    prob_stores, right_copies, right_keeps = {}, [], []
    for i in range(8):
        own = pl.ds(i * BLOCK, BLOCK)
        slot = i % 2

        def raw(j, h):
            return dot_nt(k_mask[h, rows_at(j), :], q_mask[h, own, :])

        def score(j, carry):
            new = []
            for h in range(2):
                s = raw(j, h)
                scores[h, rows_at(j), :] = s
                new.append(jnp.maximum(carry[h], fold(s, jnp.max)))
            return tuple(new)

        low = jnp.full((8, BLOCK), MASKED, F32)
        maxima = lax.fori_loop(0, i, score, (low, low), unroll=True)
        tops = []
        for h in range(2):
            s = jnp.where(causal, raw(i, h), MASKED)
            scores[h, own, :] = s
            top = jnp.maximum(maxima[h], fold(s, jnp.max))
            tops.append(jnp.max(top, axis=0, keepdims=True))
        if i >= 2:
            prob_stores[i - 2].wait()

        def prob(j, carry):
            totals, outs = [], []
            for h in range(2):
                p = jnp.exp(scores[h, rows_at(j), :] - tops[h])
                totals.append(carry[0][h] + fold(p, jnp.sum))
                p = p.astype(BF16)
                probs[slot, h, rows_at(j), :] = p
                outs.append(carry[1][h] + dot_nn(v_t[pl.ds(h * HD, HD), rows_at(j)], p))
            return (tuple(totals), tuple(outs))

        zero_sum, zero_out = jnp.zeros((8, BLOCK), F32), jnp.zeros((HD, BLOCK), F32)
        totals, outs = lax.fori_loop(
            0, i + 1, prob, ((zero_sum, zero_sum), (zero_out, zero_out)), unroll=True
        )
        length = (i + 1) * BLOCK
        prob_stores[i] = pltpu.make_async_copy(
            probs.at[slot, :, pl.ds(0, length), :],
            probs_out.at[i, :, pl.ds(0, length), :],
            p_sem.at[slot],
        )
        prob_stores[i].start()
        scale = [1.0 / jnp.sum(totals[h], axis=0, keepdims=True) for h in range(2)]
        both = jnp.concatenate([outs[h] * scale[h] for h in range(2)], axis=0)
        sums[0:1, own] = scale[0]
        sums[1:2, own] = scale[1]
        att_t[:, own] = both
        right[own, FFS:WB] = both.T.astype(BF16)
        right_copies.append(
            remote(right.at[own, :], right_out.at[1, own, :], s_pair, r_pair, 2 + i, partner)
        )
        right_copies[i].start()
        right_keeps.append(
            pltpu.make_async_copy(right.at[own, :], right_out.at[0, own, :], store.at[7 + i])
        )
        right_keeps[i].start()
        if i == 3:
            wb_gather.ring(1)
        if i == 5:
            grad_gather.far(0)
        if i == 6:
            grad_gather.ring(1)
    wb_gather.far(0)
    wb_gather.far(1)
    pairs[1].start()
    stores[1].start()

    bias_out[...] = jnp.zeros((8, FFS), F32)

    def back(spot):
        at = rows_at(spot)
        block = grad_all[at, :]
        d_pre = dot_nn(block, wb_all[:, 0:FFS]) * slope[at, :]
        rounded = d_pre.astype(BF16)
        left[at, :] = rounded
        whole = rounded.astype(F32)
        bias_out[...] += jnp.sum(whole.reshape(BLOCK // 8, 8, FFS), axis=0)
        d_att = dot_nn(block, wb_all[:, FFS:WB])
        do_own[at, :] = d_att.astype(BF16)
        product = att_t[:, at] * d_att.astype(BF16).astype(F32).T
        sums[2:3, at] = jnp.sum(product[0:HD], axis=0, keepdims=True)
        sums[3:4, at] = jnp.sum(product[HD:], axis=0, keepdims=True)

    def back_ring(flip, start, end):
        def step(n, carry):
            back(nth_spot(plane, n, flip))
            return carry

        lax.fori_loop(start, end, step, 0)

    locals_[2].wait()
    left_copies, left_keeps = [], []

    def send_left(o):
        k = len(left_copies)
        at = rows_at(plane.spot(*o))
        left_copies.append(
            remote(left.at[at, :], left_out.at[1, at, :], s_pair, r_pair, 10 + k, partner)
        )
        left_keeps.append(
            pltpu.make_async_copy(left.at[at, :], left_out.at[0, at, :], store.at[24 + k])
        )
        left_copies[k].start()
        left_keeps[k].start()

    for along in range(4):
        grad_gather.relays[along, 0].wait_recv()
    grad_copies = [
        keep_block(grad_all, grad_out, (along, 0), 32 + 2 * along) for along in range(4)
    ]
    back_ring(0, 0, 4)
    for along in range(4):
        send_left((along, 0))
    for along in (0, 1, 3):
        grad_gather.relays[along, 1].wait_recv()
        grad_copies.append(keep_block(grad_all, grad_out, (along, 1), 33 + 2 * along))
    back_ring(1, 0, 2)
    grad_gather.far(1)
    back_ring(1, 2, 3)
    for along in (0, 1, 3):
        send_left((along, 1))
    grad_gather.relays[2, 1].wait_recv()
    grad_copies.append(keep_block(grad_all, grad_out, (2, 1), 37))
    back_ring(1, 3, 4)
    send_left((2, 1))
    last_stores = [
        pltpu.make_async_copy(do_own, do_out, store.at[40]),
        pltpu.make_async_copy(sums, sums_out, store.at[41]),
    ]
    for copy in last_stores:
        copy.start()

    for gather in (grad_gather, normed_gather):
        for copy in gather.copies:
            copy.wait_send()
        for copy in gather.relays.values():
            copy.wait_send()
    wa_gather.end()
    wb_gather.end()
    hidden_copy.wait_send()
    for copy in piece_copies + tile_copies + wa_copies + wb_copies + place_copies:
        copy.wait_send()
    for copy in pairs + right_copies + left_copies:
        copy.wait()
    for copy in stores + small_stores + right_keeps + left_keeps + last_stores:
        copy.wait()
    for copy in normed_copies + grad_copies + [prob_stores[6], prob_stores[7]]:
        copy.wait()


def forward(*args):
    hbm = pl.BlockSpec(memory_space=pl.ANY)
    vmem = pl.BlockSpec(memory_space=pltpu.VMEM)
    dma = pltpu.SemaphoreType.DMA

    def shape(*dims, kind=BF16):
        return jax.ShapeDtypeStruct(dims, kind)

    return pl.pallas_call(
        forward_kernel,
        out_shape=(
            shape(SEQ, D),
            shape(SEQ, D),
            shape(2, HALF, WA),
            shape(2, HALF, WB),
            shape(2, SEQ, WB),
            shape(2, SEQ, FFS),
            shape(SEQ, HEADS),
            shape(HEADS, SEQ),
            shape(SEQ, HEADS),
            shape(SEQ, HEADS),
            shape(8, 2, SEQ, BLOCK),
            shape(8, SEQ, kind=F32),
            shape(2, SEQ, HEADS, kind=F32),
            shape(16, HALF, kind=F32),
            shape(BLOCK, 128, kind=F32),
            shape(8, FFS, kind=F32),
        ),
        in_specs=[vmem] + [hbm] * 5 + [vmem] * 3,
        out_specs=(hbm,) * 13 + (vmem,) * 3,
        scratch_shapes=[
            pltpu.VMEM((OWN, FF // 2), F32),
            pltpu.VMEM((3, OWN, HALF), F32),
            pltpu.VMEM((OWN, FF // 2), F32),
            pltpu.VMEM((OWN, HALF), F32),
            pltpu.VMEM((8, OWN, WA), BF16),
            pltpu.VMEM((8, OWN, WB), BF16),
            pltpu.VMEM((16, 128), F32),
            pltpu.VMEM((8, BLOCK), jnp.int32),
            pltpu.VMEM((16, 128), BF16),
            pltpu.VMEM((BLOCK, HALF), BF16),
            pltpu.VMEM((BLOCK, HALF), BF16),
            pltpu.VMEM((7, 16, 128), BF16),
            pltpu.VMEM((16, 128), BF16),
            pltpu.VMEM((16, HALF), BF16),
            pltpu.VMEM((8, 8, BLOCK), jnp.int32),
            pltpu.VMEM((SEQ, D), BF16),
            pltpu.VMEM((SEQ, D), BF16),
            pltpu.VMEM((D, WA), BF16),
            pltpu.VMEM((D, WB), BF16),
            pltpu.VMEM((SEQ, FFS), F32),
            pltpu.VMEM((SEQ, WB), BF16),
            pltpu.VMEM((SEQ, FFS), BF16),
            pltpu.VMEM((2, SEQ, HEADS), BF16),
            pltpu.VMEM((2, SEQ, HEADS), BF16),
            pltpu.VMEM((HEADS, SEQ), BF16),
            pltpu.VMEM((HEADS, SEQ), BF16),
            pltpu.VMEM((SEQ, HEADS), BF16),
            pltpu.VMEM((SEQ, HEADS), BF16),
            pltpu.VMEM((SEQ, HEADS), BF16),
            pltpu.VMEM((2, SEQ, BLOCK), F32),
            pltpu.VMEM((2, 2, SEQ, BLOCK), BF16),
            pltpu.VMEM((HEADS, SEQ), F32),
            pltpu.VMEM((2, SEQ, HEADS), F32),
            pltpu.VMEM((8, SEQ), F32),
            dma((4,)),
            dma((4,)),
            dma((24,)),
            dma((24,)),
            dma((16,)),
            dma((16,)),
            dma((18,)),
            dma((18,)),
            dma((36,)),
            dma((36,)),
            dma((18,)),
            dma((18,)),
            dma((42,)),
            dma((2,)),
        ],
        compiler_params=pltpu.CompilerParams(
            collective_id=0, has_side_effects=True, vmem_limit_bytes=62 * 1024 * 1024
        ),
        name="forward",
    )(*args)


def add_rows(dst, terms, count, chunk):
    def step(i, carry):
        at = pl.ds(pl.multiple_of(i * chunk, chunk), chunk)
        total = terms[0][at, :].astype(F32)
        for term in terms[1:]:
            total = total + term[at, :].astype(F32)
        dst[at, :] = total.astype(dst.dtype)
        return carry

    lax.fori_loop(0, count // chunk, step, 0)


class Reduce:
    def __init__(self, plane, acc, landing, sends, recvs, base):
        half_up, half_down, up, down, across = landing[:5]
        self.plane, self.acc, self.across = plane, acc, across
        self.near = (half_up, half_down, up, down)
        self.rows = across.shape[0]
        self.early = landing[5] if len(landing) > 5 else None
        self.direct = DIRECT if self.early is not None else 0
        self.sizes = (self.rows - self.direct, self.rows)
        self.copies = []
        for j, flip in ((0, 1), (1, 0)):
            far, size = plane.spot(2, flip), self.sizes[j]
            low, high, most = pl.ds(0, size // 2), pl.ds(size // 2, size // 2), pl.ds(0, size)
            for number, (src, dst, along) in enumerate(
                (
                    (acc.at[far, low, :], half_up.at[j, low, :], 1),
                    (acc.at[far, high, :], half_down.at[j, low, :], 3),
                    (acc.at[plane.spot(1, flip), most, :], up.at[j, most, :], 1),
                    (acc.at[plane.spot(3, flip), most, :], down.at[j, most, :], 3),
                )
            ):
                self.copies.append(
                    remote(src, dst, sends, recvs, base + 4 * j + number, plane.device(along, 0))
                )
        across_device = plane.device(0, 1)
        self.copies.append(
            remote(acc.at[plane.spot(0, 1)], across, sends, recvs, base + 8, across_device)
        )
        if self.direct:
            self.rest = pl.ds(self.sizes[0], self.direct)
            for k, along in enumerate((2, 1, 3)):
                src = acc.at[plane.spot(along, 1), self.rest, :]
                self.copies.append(
                    remote(src, self.early.at[k], sends, recvs, base + 9 + k, across_device)
                )

    def send_early(self):
        self.copies[10].start()
        self.copies[11].start()

    def add_early(self, k, along):
        self.copies[9 + k].wait_recv()
        dst = self.acc.at[self.plane.spot(along, 0), self.rest, :]
        add_rows(dst, [dst, self.early.at[k]], self.direct, 16)

    def first(self, j):
        if self.direct and j:
            self.add_early(0, 2)
        self.copies[4 * j].start()
        self.copies[4 * j + 1].start()
        if self.direct and not j:
            self.copies[9].start()

    def second(self, j):
        if self.direct and j:
            self.add_early(1, 1)
            self.add_early(2, 3)
        half = self.sizes[j] // 2
        for number, along in ((0, 1), (1, 3)):
            self.copies[4 * j + number].wait_recv()
            dst = self.acc.at[self.plane.spot(along, 1 - j), pl.ds(number * half, half), :]
            add_rows(dst, [dst, self.near[number].at[j]], half, 16)
            self.copies[4 * j + number + 2].start()

    def third(self):
        self.copies[2].wait_recv()
        self.copies[3].wait_recv()
        dst = self.acc.at[self.plane.spot(0, 1)]
        add_rows(dst, [dst, self.near[2].at[0], self.near[3].at[0]], self.sizes[0], 16)
        self.copies[8].start()

    def arrived(self):
        for k in (6, 7, 8):
            self.copies[k].wait_recv()
        mine = self.acc.at[self.plane.spot(0, 0)]
        return [mine, self.near[2].at[1], self.near[3].at[1], self.across]

    def last(self, dst):
        add_rows(dst, self.arrived(), self.rows, 16)

    def end(self):
        for copy in self.copies:
            copy.wait_send()


def backward_kernel(
    right_in, wb_in, left_in, wa_in, normed, grads, q_in, k_in, v_in, do_in,
    probs_in, sums, wave_in, hid, grad, stats, vec_all, bias_in,
    hidden_out, grad_in, gb_all, ga_all, vec_sum,
    right, left, weight, stream, q_all, k_t, v_all, do_all, probs_odd, probs_even, wave, d_k, d_v,
    out_acc, dx_acc, gb_acc, ga_acc,
    out_a, out_b, out_c, out_d, out_e, out_f, dx_a, dx_b, dx_c, dx_d, dx_e, dx_f, gb_a, gb_b, gb_c, gb_d, gb_e,
    ga_a, ga_b, ga_c, ga_d, ga_e, gb_done, ga_done, bias, final, vec, vec_in, vec_tile, tile_in, row_own, row_in,
    load, s_stream, s_probs, s_pair, r_pair, s_red, r_red, s_small, r_small, keep,
):
    plane, data = Plane(True), Plane(False)
    ctx, dp, core = plane.ctx, plane.dp, plane.core
    partner = (dp, ctx, 1 - core)
    loads = {
        "weight": pltpu.make_async_copy(wb_in, weight.at[:, :, pl.ds(0, WB)], load.at[0]),
        "right": pltpu.make_async_copy(right_in, right, load.at[1]),
        "left": pltpu.make_async_copy(left_in, left.at[:, :, pl.ds(0, FFS)], load.at[2]),
        "q": pltpu.make_async_copy(q_in, q_all, load.at[4]),
        "k": pltpu.make_async_copy(k_in, k_t, load.at[5]),
        "v": pltpu.make_async_copy(v_in, v_all, load.at[6]),
        "do": pltpu.make_async_copy(do_in, do_all, load.at[7]),
    }
    loads["weight"].start()
    loads["right"].start()
    partners = partners_of(plane, data)
    greet(partners)

    out = Reduce(plane, out_acc, (out_a, out_b, out_c, out_d, out_e, out_f), s_red, r_red, 0)
    dx = Reduce(plane, dx_acc, (dx_a, dx_b, dx_c, dx_d, dx_e, dx_f), s_red, r_red, 12)
    gb = Reduce(data, gb_acc, (gb_a, gb_b, gb_c, gb_d, gb_e), s_red, r_red, 24)
    ga = Reduce(data, ga_acc, (ga_a, ga_b, ga_c, ga_d, ga_e), s_red, r_red, 33)

    def spot_of(where, n):
        group = lax.div(n + 2, 4)
        inside = n + 2 - 4 * group
        near = 1 - lax.rem(group + 1, 2)
        along = near * (1 + 2 * lax.rem(inside, 2)) + (1 - near) * (2 - group)
        flip = near * (1 - lax.div(inside, 2)) + (1 - near) * (1 - lax.rem(inside, 2))
        return where.spot_at(along, flip)

    def out_block(n, carry):
        spot = spot_of(plane, n)
        at = rows_at(spot)
        total = dot_nt(right[0, at, :], weight[0, :, 0:WB])
        total = total + dot_nt(right[1, at, :], weight[1, :, 0:WB])
        out_acc[spot] = total.astype(BF16)
        return carry

    def dx_block(n, carry):
        spot = spot_of(plane, n)
        at = rows_at(spot)
        total = dot_nt(left[0, at, :], weight[0])
        total = total + dot_nt(left[1, at, :], weight[1])
        dx_acc[spot] = total.astype(BF16)
        return carry

    def fetch(source, n):
        columns = rows_at(spot_of(data, n))
        slot = lax.rem(n, 2)
        return pltpu.make_async_copy(source.at[:, columns], stream.at[slot], s_stream.at[slot])

    def weight_blocks(source, factor, acc, start, end):
        def step(n, carry):
            @pl.when(n < 7)
            def _():
                fetch(source, n + 1).start()

            fetch(source, n).wait()
            total = dot_tn(stream[lax.rem(n, 2)], factor[0])
            acc[spot_of(data, n)] = total.astype(BF16)
            return carry

        lax.fori_loop(start, end, step, 0)

    loads["weight"].wait()
    loads["right"].wait()
    fetch(grads, 0).start()
    lax.fori_loop(0, 1, out_block, 0)
    meet(partners)
    out.first(0)
    for name in ("q", "k", "v", "do", "left"):
        loads[name].start()
    lax.fori_loop(1, 4, out_block, 0)
    out.send_early()
    lax.fori_loop(4, 8, out_block, 0)
    weight_load = pltpu.make_async_copy(wa_in, weight, load.at[8])
    weight_load.start()
    out.second(0)
    out.first(1)
    weight_blocks(grads, right, gb_acc, 0, 1)
    gb.first(0)
    weight_blocks(grads, right, gb_acc, 1, 6)
    gb.second(0)
    gb.first(1)
    weight_blocks(grads, right, gb_acc, 6, 8)
    fetch(normed, 0).start()

    lane = lax.broadcasted_iota(jnp.int32, (BLOCK, HEADS), 1)
    heads = (lane < HD, lane >= HD)
    bias[...] = jnp.zeros((8, 3 * HEADS), F32)

    def clear(i, carry):
        d_k[rows_at(i), :] = jnp.zeros((BLOCK, HEADS), F32)
        d_v[rows_at(i), :] = jnp.zeros((BLOCK, HEADS), F32)
        return carry

    lax.fori_loop(0, 8, clear, 0)

    def probs_of(i):
        length = pl.ds(0, (i + 1) * BLOCK)
        buffer = probs_odd if i % 2 else probs_even
        return [
            pltpu.make_async_copy(
                probs_in.at[i, :, length, :], buffer.at[:, length, :], s_probs.at[i % 2]
            ),
            pltpu.make_async_copy(
                wave_in.at[:, pl.ds(i * BLOCK, BLOCK), :], wave.at[i % 2], s_probs.at[2 + i % 2]
            ),
        ]

    for name in ("q", "k", "v", "do"):
        loads[name].wait()
    arriving = {7: probs_of(7)}
    for copy in arriving[7]:
        copy.start()
    swaps = []
    for i in range(7, -1, -1):
        own = pl.ds(i * BLOCK, BLOCK)
        if i:
            arriving[i - 1] = probs_of(i - 1)
            for copy in arriving[i - 1]:
                copy.start()
        for copy in arriving[i]:
            copy.wait()
        probs = probs_odd if i % 2 else probs_even
        scale = [sums[h : h + 1, own] for h in range(2)]
        delta = [sums[2 + h : 3 + h, own] for h in range(2)]
        q, do = q_all[own, :].astype(F32), do_all[own, :].astype(F32)
        q_plain = [jnp.where(heads[h], q, 0.0).astype(BF16) for h in range(2)]
        do_plain = [jnp.where(heads[h], do, 0.0).astype(BF16) for h in range(2)]

        def back(j, carry):
            at, new = rows_at(j), []
            add_k, add_v = d_k[at, :], d_v[at, :]
            for h in range(2):
                p = probs[h, at, :].astype(F32) * scale[h]
                d_p = dot_nt(v_all[at, :], do_plain[h])
                d_s = (p * (d_p - delta[h])).astype(BF16)
                add_v = add_v + dot_nn(p.astype(BF16), do_plain[h])
                add_k = add_k + dot_nn(d_s, q_plain[h])
                new.append(carry[h] + dot_nn(k_t[pl.ds(h * HD, HD), at], d_s))
            d_k[at, :] = add_k
            d_v[at, :] = add_v
            return tuple(new)

        zero_out = jnp.zeros((HD, BLOCK), F32)
        d_q = lax.fori_loop(0, i + 1, back, (zero_out, zero_out), unroll=True)
        d_q = jnp.concatenate(d_q, axis=0).T * (HD**-0.5)
        c, s = wave[i % 2, 0], wave[i % 2, 1]
        parts = (turn(d_q, c, s, -1.0), turn(d_k[own, :], c, s, -1.0), d_v[own, :])
        for k, part in enumerate(parts):
            rounded = part.astype(BF16)
            whole = rounded.astype(F32)
            left[0, own, FFS + k * HEADS : FFS + (k + 1) * HEADS] = rounded
            columns = slice(k * HEADS, (k + 1) * HEADS)
            bias[:, columns] += jnp.sum(whole.reshape(BLOCK // 8, 8, HEADS), axis=0)
        span = pl.ds(FFS, 3 * HEADS)
        swap = remote(
            left.at[0, own, span], left.at[1, own, span], s_pair, r_pair, i, partner
        )
        swap.start()
        swaps.append(swap)
        if i == 7:
            gb.second(1)
        if i == 6:
            out.second(1)
        if i == 3:
            out.third()
            gb.third()

    loads["left"].wait()
    weight_load.wait()
    for swap in swaps:
        swap.wait_recv()
    lax.fori_loop(0, 1, dx_block, 0)
    dx.first(0)
    weight_blocks(normed, left, ga_acc, 0, 1)
    ga.first(0)
    lax.fori_loop(1, 4, dx_block, 0)
    dx.send_early()
    weight_blocks(normed, left, ga_acc, 1, 2)
    dx.second(0)
    dx.first(1)
    weight_blocks(normed, left, ga_acc, 2, 4)
    ga.second(0)
    ga.first(1)
    lax.fori_loop(4, 8, dx_block, 0)
    dx.third()
    weight_blocks(normed, left, ga_acc, 4, 6)
    dx.second(1)
    weight_blocks(normed, left, ga_acc, 6, 7)
    ga.third()
    weight_blocks(normed, left, ga_acc, 7, 8)
    ga.second(1)
    gb.last(gb_done)

    copies = {}
    keeps = []
    for n, (name, done, landed) in enumerate(
        (("gb", gb_done, gb_all), ("ga", ga_done, ga_all))
    ):
        copies[name] = [
            remote(
                done.at[rows_at(plane.spot(*o), OWN), :],
                landed.at[ctx],
                s_small,
                r_small,
                15 + 7 * n + k,
                plane.device(*o),
            )
            for k, o in enumerate(OTHERS)
        ]
        keeps.append(
            pltpu.make_async_copy(done.at[rows_at(ctx, OWN), :], landed.at[ctx], keep.at[n])
        )
    for copy in copies["gb"]:
        copy.start()
    keeps[0].start()

    out.last(final)
    bias_rows = vec_all[7:8, :] + vec_all[8:9, :]

    def add_hidden(i, carry):
        at = pl.ds(pl.multiple_of(i * 16, 16), 16)
        hidden_out[at, :] = (hid[at, :].astype(F32) + final[at, :] + bias_rows).astype(BF16)
        return carry

    lax.fori_loop(0, BLOCK // 16, add_hidden, 0)
    dx.last(final)
    gain = vec_all[9:10, :]
    lanes = lax.broadcasted_iota(jnp.int32, (16, 128), 1)

    def lean(i, carry):
        at = pl.ds(pl.multiple_of(i * 16, 16), 16)
        d, h, stat = final[at, :], hid[at, :].astype(F32), stats[at, :]
        normal = (h - stat[:, 0:1]) * stat[:, 64:65]
        product = d * normal
        one = jnp.sum(d * gain, axis=1, keepdims=True)
        two = jnp.sum(product * gain, axis=1, keepdims=True)
        row_own[at, :] = jnp.where(lanes < 64, one, two)
        return (carry[0] + d, carry[1] + product, carry[2] + grad[at, :].astype(F32))

    zero = jnp.zeros((16, HALF), F32)
    rows = lax.fori_loop(0, BLOCK // 16, lean, (zero, zero, zero))
    row_copy = remote(row_own, row_in, s_small, r_small, 0, partner)
    row_copy.start()
    shift_grad, gain_grad, bias_grad = [jnp.sum(r, axis=0, keepdims=True) for r in rows]
    number = lax.broadcasted_iota(jnp.int32, (16, HALF), 0)
    vec[...] = jnp.where(
        number == 9,
        gain_grad,
        jnp.where(
            number == 10, shift_grad, jnp.where((number == 7) | (number == 8), bias_grad, 0.0)
        ),
    )
    columns = pl.ds(pl.multiple_of(ctx * HEADS, HEADS), HEADS)
    for k in range(3):
        part = jnp.sum(bias[:, k * HEADS : (k + 1) * HEADS], axis=0, keepdims=True)
        vec[k : k + 1, columns] = part
    columns = pl.ds(pl.multiple_of(lax.rem(ctx, 2) * FFS, FFS), FFS)
    part = jnp.sum(bias_in[...], axis=0, keepdims=True)
    vec[:, columns] = jnp.where(
        lax.broadcasted_iota(jnp.int32, (16, FFS), 0) == 3 + lax.div(ctx, 2), part, vec[:, columns]
    )
    vec_copies, tile_copies = [], []
    for k, o in enumerate(OTHERS):
        columns = pl.ds(pl.multiple_of(data.spot(*o) * 128, 128), 128)
        vec_copies.append(
            remote(vec.at[:, columns], vec_in.at[k], s_small, r_small, 1 + k, data.device(*o))
        )
        tile_copies.append(
            remote(vec_tile, tile_in.at[k], s_small, r_small, 8 + k, plane.device(*o))
        )
    for copy in vec_copies:
        copy.start()
    ga.last(ga_done)
    for copy in copies["ga"]:
        copy.start()
    keeps[1].start()
    for copy in vec_copies:
        copy.wait_recv()
    total = vec[:, pl.ds(pl.multiple_of(dp * 128, 128), 128)]
    for k in range(7):
        total = total + vec_in[k]
    vec_tile[...] = total
    for copy in tile_copies:
        copy.start()

    row_copy.wait()

    def tilt(i, carry):
        at = pl.ds(pl.multiple_of(i * 16, 16), 16)
        d, h, stat = final[at, :], hid[at, :].astype(F32), stats[at, :]
        inverse = stat[:, 64:65]
        normal = (h - stat[:, 0:1]) * inverse
        row = (row_own[at, :] + row_in[at, :]) / D
        change = inverse * (d * gain - row[:, 0:1] - normal * row[:, 64:65])
        grad_in[at, :] = (grad[at, :].astype(F32) + change).astype(BF16)
        return carry

    lax.fori_loop(0, BLOCK // 16, tilt, 0)
    for copy in tile_copies:
        copy.wait_recv()
    total = vec_tile[...]
    for k in range(7):
        total = total + tile_in[k]
    vec_sum[...] = total

    for name in copies:
        for copy in copies[name]:
            copy.wait()
    for copy in keeps:
        copy.wait()
    for copy in vec_copies + tile_copies + swaps:
        copy.wait_send()
    for red in (dx, out, gb, ga):
        red.end()


def backward(*args):
    hbm = pl.BlockSpec(memory_space=pl.ANY)
    vmem = pl.BlockSpec(memory_space=pltpu.VMEM)
    dma = pltpu.SemaphoreType.DMA

    def landing(rows, width):
        half = pltpu.VMEM((2, rows // 2, width), BF16)
        whole = pltpu.VMEM((2, rows, width), BF16)
        return [half, half, whole, whole, pltpu.VMEM((rows, width), BF16)]

    def shape(*dims, kind=BF16):
        return jax.ShapeDtypeStruct(dims, kind)

    return pl.pallas_call(
        backward_kernel,
        out_shape=(
            shape(BLOCK, HALF),
            shape(BLOCK, HALF),
            shape(8, OWN, WB),
            shape(8, OWN, WA),
            shape(16, 128, kind=F32),
        ),
        in_specs=[hbm] * 11 + [vmem, hbm] + [vmem] * 5,
        out_specs=(vmem, vmem, hbm, hbm, vmem),
        scratch_shapes=[
            pltpu.VMEM((2, SEQ, WB), BF16),
            pltpu.VMEM((2, SEQ, WA), BF16),
            pltpu.VMEM((2, HALF, WA), BF16),
            pltpu.VMEM((2, SEQ, BLOCK), BF16),
            pltpu.VMEM((SEQ, HEADS), BF16),
            pltpu.VMEM((HEADS, SEQ), BF16),
            pltpu.VMEM((SEQ, HEADS), BF16),
            pltpu.VMEM((SEQ, HEADS), BF16),
            pltpu.VMEM((2, SEQ, BLOCK), BF16),
            pltpu.VMEM((2, SEQ - BLOCK, BLOCK), BF16),
            pltpu.VMEM((2, 2, BLOCK, HEADS), F32),
            pltpu.VMEM((SEQ, HEADS), F32),
            pltpu.VMEM((SEQ, HEADS), F32),
            pltpu.VMEM((8, BLOCK, HALF), BF16),
            pltpu.VMEM((8, BLOCK, HALF), BF16),
            pltpu.VMEM((8, BLOCK, WB), BF16),
            pltpu.VMEM((8, BLOCK, WA), BF16),
            *landing(BLOCK, HALF),
            pltpu.VMEM((3, DIRECT, HALF), BF16),
            *landing(BLOCK, HALF),
            pltpu.VMEM((3, DIRECT, HALF), BF16),
            *landing(BLOCK, WB),
            *landing(BLOCK, WA),
            pltpu.VMEM((BLOCK, WB), BF16),
            pltpu.VMEM((BLOCK, WA), BF16),
            pltpu.VMEM((8, 3 * HEADS), F32),
            pltpu.VMEM((BLOCK, HALF), F32),
            pltpu.VMEM((16, HALF), F32),
            pltpu.VMEM((7, 16, 128), F32),
            pltpu.VMEM((16, 128), F32),
            pltpu.VMEM((7, 16, 128), F32),
            pltpu.VMEM((BLOCK, 128), F32),
            pltpu.VMEM((BLOCK, 128), F32),
            dma((10,)),
            dma((2,)),
            dma((4,)),
            dma((8,)),
            dma((8,)),
            dma((42,)),
            dma((42,)),
            dma((36,)),
            dma((36,)),
            dma((3,)),
        ],
        compiler_params=pltpu.CompilerParams(
            collective_id=1, has_side_effects=True, vmem_limit_bytes=62 * 1024 * 1024
        ),
        name="backward",
    )(*args)


def adam_step(weight, first, second, gradient, rate):
    first_new = BETA_ONE * first + (1.0 - BETA_ONE) * gradient
    second_new = BETA_TWO * second + (1.0 - BETA_TWO) * gradient * gradient
    fix_one = 1.0 - BETA_ONE**STEP
    fix_two = 1.0 - BETA_TWO**STEP
    update = first_new / fix_one / (jnp.sqrt(second_new / fix_two) + ADAM_EPS)
    return (first_new, second_new, weight - rate * (update + DECAY * weight))


def update_kernel(
    ga, gb, vec_sum, hidden, back,
    qkv_w, qkv_m, qkv_v, dense_w, dense_m, dense_v, fc1_w, fc1_m, fc1_v, fc2_w, fc2_m, fc2_v,
    vec_w, vec_m, vec_v,
    hidden_out, back_out,
    qkv_mo, qkv_vo, qkv_wo, dense_mo, dense_vo, dense_wo, fc1_mo, fc1_vo, fc1_wo,
    fc2_mo, fc2_vo, fc2_wo, vec_mo, vec_vo, vec_wo,
):
    hidden_out[...] = hidden[...]
    back_out[...] = back[...]

    fc1 = (fc1_w, fc1_m, fc1_v, fc1_mo, fc1_vo, fc1_wo)
    fc2 = (fc2_w, fc2_m, fc2_v, fc2_mo, fc2_vo, fc2_wo)
    dense = (dense_w, dense_m, dense_v, dense_mo, dense_vo, dense_wo)
    qkv = (qkv_w, qkv_m, qkv_v, qkv_mo, qkv_vo, qkv_wo)
    vec = (vec_w, vec_m, vec_v, vec_mo, vec_vo, vec_wo)

    def step(refs, gradient, rate, *at):
        w, m, v, mo, vo, wo = refs
        mo[at], vo[at], wo[at] = adam_step(w[at], m[at], v[at], gradient, rate)

    for c in range(8):
        wide, narrow = slice(c * FFS, (c + 1) * FFS), slice(c * HEADS, (c + 1) * HEADS)
        step(fc1, ga[c, :, 0:FFS].astype(F32), RATES[0], slice(None), wide)
        step(fc2, gb[c, :, 0:FFS].astype(F32), RATES[1], slice(None), wide)
        step(dense, gb[c, :, FFS:WB].astype(F32), RATES[2], slice(None), narrow)
        for k in range(3):
            columns = slice(FFS + k * HEADS, FFS + (k + 1) * HEADS)
            step(qkv, ga[c, :, columns].astype(F32), RATES[0], k, slice(None), narrow)

    @pl.when(pl.program_id(0) == 0)
    def _():
        mine = pltpu.roll(vec_sum[...], lax.rem(128 - 16 * lax.axis_index("ctx"), 128), 1)
        for k in range(11):
            step(vec, mine[k : k + 1, 0:16], RATES[3], k)


def update(ga, gb, vec_sum, hidden, back, *state):
    steps = 2
    rows = OWN // steps

    def part(width):
        return pl.BlockSpec((rows, width), lambda n: (n, 0))

    vec = pl.BlockSpec((11, 1, 16), lambda n: (0, 0, 0))
    token = pl.BlockSpec((BLOCK // steps, HALF), lambda n: (n, 0))
    sets = (
        [pl.BlockSpec((3, rows, HALF), lambda n: (0, n, 0))] * 3
        + [part(HALF)] * 3
        + [part(FF // 2)] * 6
        + [vec] * 3
    )
    wide = [pl.BlockSpec((8, rows, w), lambda n: (0, n, 0)) for w in (WA, WB)]
    shapes = [jax.ShapeDtypeStruct(x.shape, x.dtype) for x in (hidden, back, *state)]
    return pl.pallas_call(
        update_kernel,
        grid=(steps,),
        out_shape=shapes,
        in_specs=wide + [pl.BlockSpec((16, 128), lambda n: (0, 0)), token, token] + sets,
        out_specs=[token, token] + sets,
        compiler_params=pltpu.CompilerParams(vmem_limit_bytes=62 * 1024 * 1024),
        name="update",
    )(ga, gb, vec_sum, hidden, back, *state)


def on_device(
    hidden_in,
    grad_out,
    segment_ids,
    positions,
    qkv_weight,
    dense_weight,
    fc1_weight,
    fc2_weight,
    vectors,
    qkv_first,
    qkv_second,
    dense_first,
    dense_second,
    fc1_first,
    fc1_second,
    fc2_first,
    fc2_second,
    vector_first,
    vector_second,
):
    hid = hidden_in.reshape(BLOCK, HALF)
    grad = grad_out.reshape(BLOCK, HALF)

    def turned(array):
        return jnp.moveaxis(array, 1, 0)

    (
        normed, grads, wa2, wb2, right, left, q, k_t, v, do, probs, sums, wave, vec_all, stats, bias,
    ) = forward(
        hid, grad, fc1_weight, turned(qkv_weight), fc2_weight, dense_weight, turned(vectors),
        segment_ids, positions,
    )
    hidden_out, grad_in, gb_all, ga_all, vec_sum = backward(
        right, wb2, left, wa2, normed, grads, q, k_t, v, do, probs, sums, wave,
        hid, grad, stats, vec_all, bias,
    )
    new = update(
        ga_all, gb_all, vec_sum, hidden_out, grad_in,
        turned(qkv_weight), turned(qkv_first), turned(qkv_second),
        dense_weight, dense_first, dense_second,
        fc1_weight, fc1_first, fc1_second, fc2_weight, fc2_first, fc2_second,
        turned(vectors), turned(vector_first), turned(vector_second),
    )
    return (
        new[0].reshape(hidden_in.shape),
        new[1].reshape(grad_out.shape),
        *(turned(x) for x in new[2:5]),
        *new[5:14],
        *(turned(x) for x in new[14:]),
    )


def solution(mesh):
    rows = P("dp", "ctx", "tensor")
    tokens = P("dp", "ctx")
    cube = P(("dp", "ctx"), None, "tensor")
    plain = P(("dp", "ctx"), "tensor")
    packed = P("tensor", None, ("dp", "ctx"))
    return jax.shard_map(
        on_device,
        mesh=mesh,
        in_specs=(rows, rows, tokens, tokens, cube, plain, plain, plain, packed)
        + (cube,) * 2
        + (plain,) * 6
        + (packed,) * 2,
        out_specs=(rows, rows) + (cube,) * 3 + (plain,) * 9 + (packed,) * 3,
        check_vma=False,
    )
```

```python
import functools
import math

import jax
import jax.numpy as jnp
import numpy as np
from jax import lax
from jax.experimental import pallas as pl
from jax.experimental.pallas import tpu as pltpu
from jax.sharding import PartitionSpec as P

D = 2048
HD = 64
ROT = 32
FF = 8192
STEP = 10
SEQ = 2048
BLOCK = 256
HALF = 1024
FFS = 512
HEADS = 128
WA = FFS + 3 * HEADS
WB = FFS + HEADS
OWN = 32
DIRECT = 64

BETA_ONE = 0.9
BETA_TWO = 0.95
ADAM_EPS = 1e-08
DECAY = 0.1
NORM_EPS = 1e-05
MASKED = -1e30
GELU = math.sqrt(2.0 / math.pi)

RATES = (2.0 / math.sqrt(D), 2.0 / math.sqrt(FF), 2.0 / math.sqrt(D // 16), 0.6)
MESH = pl.DeviceIdType.MESH
F32 = jnp.float32
BF16 = jnp.bfloat16
OTHERS = tuple((k // 2, k % 2) for k in range(1, 8))


class Plane:
    def __init__(self, over_ctx):
        self.dp = lax.axis_index("dp")
        self.ctx = lax.axis_index("ctx")
        self.core = lax.axis_index("tensor")
        self.over_ctx = over_ctx
        if over_ctx:
            self.ring, self.pair = lax.div(self.ctx, 2), lax.rem(self.ctx, 2)
        else:
            self.ring, self.pair = lax.rem(self.dp, 4), lax.div(self.dp, 4)

    def spot(self, along, flip):
        ring = lax.rem(self.ring + along, 4) if along else self.ring
        pair = 1 - self.pair if flip else self.pair
        return ring * 2 + pair if self.over_ctx else pair * 4 + ring

    def spot_at(self, along, flip):
        ring, pair = lax.rem(self.ring + along, 4), lax.rem(self.pair + flip, 2)
        return ring * 2 + pair if self.over_ctx else pair * 4 + ring

    def device(self, along, flip):
        spot = self.spot(along, flip)
        return (self.dp, spot, self.core) if self.over_ctx else (spot, self.ctx, self.core)


def rows_at(index, size=BLOCK):
    return pl.ds(pl.multiple_of(index * size, size), size)


def remote(src, dst, sends, recvs, number, device):
    return pltpu.make_async_remote_copy(
        src_ref=src,
        dst_ref=dst,
        send_sem=sends.at[number],
        recv_sem=recvs.at[number],
        device_id=device,
        device_id_type=MESH,
    )


def partners_of(ctx_plane, dp_plane):
    partners = [ctx_plane.device(*o) for o in OTHERS] + [dp_plane.device(*o) for o in OTHERS]
    return partners + [(ctx_plane.dp, ctx_plane.ctx, 1 - ctx_plane.core)]


def greet(partners):
    barrier = pltpu.get_barrier_semaphore()
    for partner in partners:
        pl.semaphore_signal(barrier, inc=1, device_id=partner, device_id_type=MESH)


def meet(partners):
    pl.semaphore_wait(pltpu.get_barrier_semaphore(), len(partners))


class Gather:
    def __init__(self, plane, own, region, sends, recvs, base, direct=0):
        self.direct = direct
        near, half = BLOCK - direct, BLOCK // 2
        whole, most, rest = (0, BLOCK), (0, near), (near, direct)
        plans = [
            ((0, 0), whole, (1, 0)),
            ((0, 0), whole, (3, 0)),
            ((0, 0), whole, (0, 1)),
            ((3, 0), (0, half), (1, 0)),
            ((1, 0), (half, half), (3, 0)),
            ((0, 1), most, (1, 0)),
            ((0, 1), most, (3, 0)),
            ((3, 1), (0, near // 2), (1, 0)),
            ((1, 1), (near // 2, near // 2), (3, 0)),
        ]
        if direct:
            plans += [((along, 0), rest, (0, 1)) for along in (3, 1, 2)]
        self.copies = []
        for number, (block, span, to) in enumerate(plans):
            dst = region(plane.spot(*block), *span)
            src = own if number < 3 else dst
            self.copies.append(
                remote(src, dst, sends, recvs, base + number, plane.device(*to))
            )

    def begin_ring(self):
        self.copies[0].start()
        self.copies[1].start()

    def begin_pair(self):
        self.copies[2].start()

    def ring(self, flip):
        first, relay = (5, 7) if flip else (0, 3)
        for k in (0, 1):
            self.copies[first + k].wait_recv()
            self.copies[relay + k].start()
            if self.direct and not flip:
                self.copies[9 + k].start()
        if self.direct and flip:
            self.copies[9].wait_recv()
            self.copies[10].wait_recv()

    def pair(self):
        self.copies[2].wait_recv()
        self.copies[5].start()
        self.copies[6].start()

    def far(self, flip):
        for k in (7, 8) if flip else (3, 4):
            self.copies[k].wait_recv()
        if self.direct:
            if flip:
                self.copies[11].wait_recv()
            else:
                self.copies[11].start()

    def end(self):
        for copy in self.copies:
            copy.wait_send()


class GatherCores(Gather):
    def __init__(self, plane, own, region, sends, recvs, base, core_sends, core_recvs, core_base):
        super().__init__(plane, own, region, sends, recvs, base, DIRECT)
        partner = (plane.dp, plane.ctx, 1 - plane.core)
        self.relays = {}
        for number, (along, flip) in enumerate(((0, 0),) + OTHERS):
            dst = region(plane.spot(along, flip), 0, BLOCK)
            src = dst if number else own
            self.relays[along, flip] = remote(
                src, dst, core_sends, core_recvs, core_base + number, partner
            )

    def begin_ring(self):
        super().begin_ring()
        self.relays[0, 0].start()

    def ring(self, flip):
        super().ring(flip)
        self.relays[3, flip].start()
        self.relays[1, flip].start()

    def pair(self):
        super().pair()
        self.relays[0, 1].start()

    def far(self, flip):
        super().far(flip)
        self.relays[2, flip].start()

    def end(self):
        super().end()
        for copy in self.relays.values():
            copy.wait()


def dot_nt(left, right):
    return lax.dot_general(left, right, (((1,), (1,)), ((), ())), preferred_element_type=F32)


def dot_nn(left, right):
    return jnp.dot(left, right, preferred_element_type=F32)


def dot_tn(left, right):
    return lax.dot_general(left, right, (((0,), (0,)), ((), ())), preferred_element_type=F32)


def turn(values, cosine, sine, sign):
    lane = lax.rem(lax.broadcasted_iota(jnp.int32, values.shape, 1), HD)
    low = jnp.where(lane < ROT // 2, sine, 0.0)
    high = sine - low
    up = pltpu.roll(values, HEADS - ROT // 2, 1)
    down = pltpu.roll(values, ROT // 2, 1)
    return values * cosine + sign * (down * high - up * low)


def fold(values, op):
    return op(values.reshape(BLOCK // 8, 8, BLOCK), axis=0)


def nth_spot(plane, n, flip):
    along = n + lax.div(n, 2) - 2 * lax.div(n, 3)
    return plane.spot_at(along, flip)


def forward_kernel(
    hid, grad, fc1_in, qkv_in, fc2_in, dense_in, vectors, segments, positions,
    normed_out, grad_out, wa_out, wb_out, right_out, left_out,
    q_out, k_out, v_out, do_out, probs_out, sums_out, wave_out, vec_all, stats, bias_out,
    fc1, qkv_w, fc2, dense, wa, wb, vec, place, joined, other, normed, pieces, tile, table, place_all,
    normed_all, grad_all, wa_all, wb_all, slope, right, left, q_mask, k_mask, v_t, k_t, q_own, v_own, do_own,
    scores, probs, att_t, wave, sums,
    load, local, s_act, r_act, s_core, r_core, s_w, r_w, s_small, r_small, s_pair, r_pair, store, p_sem,
):
    plane, data = Plane(True), Plane(False)
    ctx, dp, core = plane.ctx, plane.dp, plane.core
    partner = (dp, ctx, 1 - core)

    def span_at(spot, start, size):
        return pl.ds(pl.multiple_of(spot * BLOCK + start, 32), size)

    def act_region(ref):
        columns = pl.ds(pl.multiple_of(core * HALF, HALF), HALF)
        return lambda *span: ref.at[span_at(*span), columns]

    def weight_region(ref):
        return lambda *span: ref.at[span_at(*span), :]

    def scatter_rows(ref):
        start = pl.multiple_of(dp * BLOCK + ctx * OWN, OWN)
        return ref.at[pl.ds(start, OWN), :]

    normed_gather = GatherCores(
        plane, normed, act_region(normed_all), s_act, r_act, 0, s_core, r_core, 0
    )
    grad_gather = GatherCores(
        plane, grad, act_region(grad_all), s_act, r_act, 12, s_core, r_core, 8
    )

    loads = [
        pltpu.make_async_copy(src, dst, load.at[k])
        for k, (src, dst) in enumerate(
            ((fc1_in, fc1), (qkv_in, qkv_w), (fc2_in, fc2), (dense_in, dense))
        )
    ]
    for copy in loads:
        copy.start()
    partners = partners_of(plane, data)
    greet(partners)
    vec_lane = lax.broadcasted_iota(jnp.int32, (1, 128), 1)
    vec[...] = jnp.zeros((16, 128), F32)
    for k in range(11):
        spread = jnp.concatenate([vectors[k]] * 8, axis=1)
        vec[k : k + 1, :] = jnp.where(lax.div(vec_lane, 16) == ctx, spread, 0.0)
    tile[...] = vec[...].astype(BF16)
    place[...] = jnp.zeros((8, BLOCK), jnp.int32)
    place[0:1, :] = segments[...]
    place[1:2, :] = positions[...]
    place_all[ctx] = place[...]
    for copy in loads:
        copy.wait()
    for c in range(8):
        wa[c, :, 0:FFS] = fc1[:, c * FFS : (c + 1) * FFS].astype(BF16)
        wb[c, :, 0:FFS] = fc2[:, c * FFS : (c + 1) * FFS].astype(BF16)
        columns = slice(c * HEADS, (c + 1) * HEADS)
        wb[c, :, FFS:WB] = dense[:, columns].astype(BF16)
        for k in range(3):
            wa[c, :, FFS + k * HEADS : FFS + (k + 1) * HEADS] = qkv_w[k, :, columns].astype(BF16)

    piece_copies, tile_copies, place_copies, wa_copies, wb_copies = [], [], [], [], []
    for k, o in enumerate(OTHERS):
        to = plane.device(*o)
        spot = plane.spot(*o)
        piece_copies.append(remote(tile, pieces.at[k], s_small, r_small, 1 + k, to))
        place_copies.append(remote(place, place_all.at[ctx], s_small, r_small, 15 + k, to))
        wa_copies.append(remote(wa.at[spot], scatter_rows(wa_all), s_small, r_small, 22 + k, to))
        wb_copies.append(remote(wb.at[spot], scatter_rows(wb_all), s_small, r_small, 29 + k, to))
        columns = pl.ds(pl.multiple_of(dp * 128, 128), 128)
        tile_copies.append(
            remote(joined, table.at[:, columns], s_small, r_small, 8 + k, data.device(*o))
        )
    hidden_copy = remote(hid, other, s_small, r_small, 0, partner)
    meet(partners)
    for copy in piece_copies:
        copy.start()
    hidden_copy.start()
    locals_ = [
        pltpu.make_async_copy(wa.at[ctx], scatter_rows(wa_all), local.at[0]),
        pltpu.make_async_copy(wb.at[ctx], scatter_rows(wb_all), local.at[1]),
        pltpu.make_async_copy(grad, act_region(grad_all)(ctx, 0, BLOCK), local.at[2]),
        pltpu.make_async_copy(normed, act_region(normed_all)(ctx, 0, BLOCK), local.at[3]),
    ]
    for copy in locals_[:3]:
        copy.start()

    for copy in piece_copies:
        copy.wait_recv()
    total = tile[...].astype(F32)
    for k in range(7):
        total = total + pieces[k].astype(F32)
    joined[...] = total.astype(BF16)
    table[:, pl.ds(pl.multiple_of(dp * 128, 128), 128)] = total.astype(BF16)
    for copy in tile_copies + wa_copies + place_copies + wb_copies:
        copy.start()
    grad_gather.begin_ring()
    sums[...] = jnp.zeros((8, SEQ), F32)

    a_region, b_region = weight_region(wa_all), weight_region(wb_all)
    wa_gather = Gather(data, a_region(dp, 0, BLOCK), a_region, s_w, r_w, 0)
    wb_gather = Gather(data, b_region(dp, 0, BLOCK), b_region, s_w, r_w, 9)
    for copy in wa_copies:
        copy.wait_recv()
    locals_[0].wait()
    wa_gather.begin_pair()
    wa_gather.begin_ring()
    for copy in tile_copies:
        copy.wait_recv()
    hidden_copy.wait_recv()
    rows = table[...].astype(F32)
    vec_all[...] = rows
    gain, shift = rows[9:10], rows[10:11]
    lanes = lax.broadcasted_iota(jnp.int32, (16, 128), 1)

    def norm(i, carry):
        at = pl.ds(pl.multiple_of(i * 16, 16), 16)
        a, b = hid[at, :].astype(F32), other[at, :].astype(F32)
        mean = (jnp.sum(a, axis=1, keepdims=True) + jnp.sum(b, axis=1, keepdims=True)) / D
        a, b = a - mean, b - mean
        square = jnp.sum(a * a, axis=1, keepdims=True) + jnp.sum(b * b, axis=1, keepdims=True)
        inverse = lax.rsqrt(square / D + NORM_EPS)
        normed[at, :] = (a * inverse * gain + shift).astype(BF16)
        stats[at, :] = jnp.where(lanes < 64, mean, inverse)
        return carry

    lax.fori_loop(0, BLOCK // 16, norm, 0)
    normed_gather.begin_pair()
    normed_gather.begin_ring()
    locals_[3].start()
    for copy in place_copies:
        copy.wait_recv()
    lane = lax.broadcasted_iota(jnp.int32, (BLOCK, HEADS), 1)
    inner = lax.rem(lane, HD)
    first_head = lane < HD
    turning = inner < ROT
    wheel = lax.rem(lax.broadcasted_iota(jnp.int32, (1, HEADS), 1), ROT // 2)
    freq = jnp.zeros((1, HEADS), F32)
    for k in range(ROT // 2):
        freq = jnp.where(wheel == k, float(np.float32(10000.0 ** (-2.0 * k / ROT))), freq)

    def tables(i, carry):
        column = place_all[i].astype(F32).T
        angle = column[:, 1:2] * freq
        wave[0, rows_at(i), :] = jnp.where(turning, jnp.cos(angle), 1.0)
        wave[1, rows_at(i), :] = jnp.where(turning, jnp.sin(angle), 0.0)
        return carry

    lax.fori_loop(0, 8, tables, 0)

    for copy in wb_copies:
        copy.wait_recv()
    locals_[1].wait()
    wa_gather.ring(0)
    wa_gather.pair()
    normed_gather.pair()
    wa_gather.ring(1)
    wb_gather.begin_pair()
    wb_gather.begin_ring()
    normed_gather.ring(0)
    grad_gather.begin_pair()
    wa_gather.far(0)
    wa_gather.far(1)
    normed_gather.far(0)
    my_rows = pl.ds(pl.multiple_of(core * HALF, HALF), HALF)
    their_rows = pl.ds(pl.multiple_of((1 - core) * HALF, HALF), HALF)
    pairs = [
        remote(wa_all.at[their_rows, :], wa_out.at[1], s_pair, r_pair, 0, partner),
        remote(wb_all.at[their_rows, :], wb_out.at[1], s_pair, r_pair, 1, partner),
    ]
    pairs[0].start()
    stores = [
        pltpu.make_async_copy(wa_all.at[my_rows, :], wa_out.at[0], store.at[0]),
        pltpu.make_async_copy(wb_all.at[my_rows, :], wb_out.at[0], store.at[1]),
        pltpu.make_async_copy(wave, wave_out, store.at[2]),
    ]
    stores[0].start()
    stores[2].start()

    qkv_bias = [
        vec_all[c : c + 1, pl.ds(pl.multiple_of(ctx * HEADS, HEADS), HEADS)] for c in range(3)
    ]
    fc1_bias = vec_all[
        pl.ds(3 + lax.div(ctx, 2), 1), pl.ds(pl.multiple_of(lax.rem(ctx, 2) * FFS, FFS), FFS)
    ]

    def project(spot):
        at = rows_at(spot)
        block = normed_all[at, :]
        x = dot_nn(block, wa_all[:, 0:FFS]) + fc1_bias
        square = x * x
        tanh = jnp.tanh(x * (GELU + (GELU * 0.044715) * square))
        half = 0.5 * (1.0 + tanh)
        bend = GELU + (3.0 * 0.044715 * GELU) * square
        slope[at, :] = half + 0.5 * x * (1.0 - tanh * tanh) * bend
        right[at, 0:FFS] = (x * half).astype(BF16)
        qkv = dot_nn(block, wa_all[:, FFS:WA])
        c, s = wave[0, at, :], wave[1, at, :]
        q = turn(qkv[:, 0:HEADS] + qkv_bias[0], c, s, 1.0).astype(BF16).astype(F32) * (HD**-0.5)
        k = turn(qkv[:, HEADS : 2 * HEADS] + qkv_bias[1], c, s, 1.0)
        v = qkv[:, 2 * HEADS : 3 * HEADS] + qkv_bias[2]
        segment = place_all[spot].astype(F32).T[:, 0:1]
        feature = jnp.where(segment == inner.astype(F32), 1.0, 0.0)
        barred = jnp.where(inner < 3, (1.0 - feature) * MASKED, 0.0)
        q_mask[0, at, :] = jnp.where(first_head, q, barred).astype(BF16)
        q_mask[1, at, :] = jnp.where(first_head, barred, q).astype(BF16)
        k_mask[0, at, :] = jnp.where(first_head, k, feature).astype(BF16)
        k_mask[1, at, :] = jnp.where(first_head, feature, k).astype(BF16)
        q_own[at, :] = q.astype(BF16)
        v_own[at, :] = v.astype(BF16)
        k_t[:, at] = k.T.astype(BF16)
        v_t[:, at] = v.T.astype(BF16)

    def project_ring(flip, start, end):
        def step(n, carry):
            project(nth_spot(plane, n, flip))
            return carry

        lax.fori_loop(start, end, step, 0)

    def keep_block(ref, out, o, number):
        at = rows_at(plane.spot(*o))
        copy = pltpu.make_async_copy(ref.at[at, :], out.at[at, :], store.at[number])
        copy.start()
        return copy

    locals_[3].wait()
    for o in ((0, 0), (1, 0), (3, 0), (2, 0)):
        normed_gather.relays[o].wait_recv()
    project_ring(0, 0, 2)
    normed_gather.ring(1)
    grad_gather.ring(0)
    project_ring(0, 2, 4)
    wb_gather.ring(0)
    wb_gather.pair()
    normed_gather.relays[0, 1].wait_recv()
    normed_gather.relays[1, 1].wait_recv()
    project_ring(1, 0, 2)
    grad_gather.pair()
    normed_gather.far(1)
    normed_gather.relays[3, 1].wait_recv()
    normed_gather.relays[2, 1].wait_recv()
    project_ring(1, 2, 4)
    normed_copies = [
        keep_block(normed_all, normed_out, (along, flip), 16 + 2 * along + flip)
        for flip in (0, 1)
        for along in range(4)
    ]
    small_stores = [
        pltpu.make_async_copy(q_own, q_out, store.at[4]),
        pltpu.make_async_copy(k_t, k_out, store.at[5]),
        pltpu.make_async_copy(v_own, v_out, store.at[6]),
    ]
    for copy in small_stores:
        copy.start()

    key_row = lax.broadcasted_iota(jnp.int32, (BLOCK, BLOCK), 0)
    query_col = lax.broadcasted_iota(jnp.int32, (BLOCK, BLOCK), 1)
    causal = key_row <= query_col
    prob_stores, right_copies, right_keeps = {}, [], []
    for i in range(8):
        own = pl.ds(i * BLOCK, BLOCK)
        slot = i % 2

        def raw(j, h):
            return dot_nt(k_mask[h, rows_at(j), :], q_mask[h, own, :])

        def score(j, carry):
            new = []
            for h in range(2):
                s = raw(j, h)
                scores[h, rows_at(j), :] = s
                new.append(jnp.maximum(carry[h], fold(s, jnp.max)))
            return tuple(new)

        low = jnp.full((8, BLOCK), MASKED, F32)
        maxima = lax.fori_loop(0, i, score, (low, low), unroll=True)
        tops = []
        for h in range(2):
            s = jnp.where(causal, raw(i, h), MASKED)
            scores[h, own, :] = s
            top = jnp.maximum(maxima[h], fold(s, jnp.max))
            tops.append(jnp.max(top, axis=0, keepdims=True))
        if i >= 2:
            prob_stores[i - 2].wait()

        def prob(j, carry):
            totals, outs = [], []
            for h in range(2):
                p = jnp.exp(scores[h, rows_at(j), :] - tops[h])
                totals.append(carry[0][h] + fold(p, jnp.sum))
                p = p.astype(BF16)
                probs[slot, h, rows_at(j), :] = p
                outs.append(carry[1][h] + dot_nn(v_t[pl.ds(h * HD, HD), rows_at(j)], p))
            return (tuple(totals), tuple(outs))

        zero_sum, zero_out = jnp.zeros((8, BLOCK), F32), jnp.zeros((HD, BLOCK), F32)
        totals, outs = lax.fori_loop(
            0, i + 1, prob, ((zero_sum, zero_sum), (zero_out, zero_out)), unroll=True
        )
        length = (i + 1) * BLOCK
        prob_stores[i] = pltpu.make_async_copy(
            probs.at[slot, :, pl.ds(0, length), :],
            probs_out.at[i, :, pl.ds(0, length), :],
            p_sem.at[slot],
        )
        prob_stores[i].start()
        scale = [1.0 / jnp.sum(totals[h], axis=0, keepdims=True) for h in range(2)]
        both = jnp.concatenate([outs[h] * scale[h] for h in range(2)], axis=0)
        sums[0:1, own] = scale[0]
        sums[1:2, own] = scale[1]
        att_t[:, own] = both
        right[own, FFS:WB] = both.T.astype(BF16)
        right_copies.append(
            remote(right.at[own, :], right_out.at[1, own, :], s_pair, r_pair, 2 + i, partner)
        )
        right_copies[i].start()
        right_keeps.append(
            pltpu.make_async_copy(right.at[own, :], right_out.at[0, own, :], store.at[7 + i])
        )
        right_keeps[i].start()
        if i == 3:
            wb_gather.ring(1)
        if i == 5:
            grad_gather.far(0)
        if i == 6:
            grad_gather.ring(1)
    wb_gather.far(0)
    wb_gather.far(1)
    pairs[1].start()
    stores[1].start()

    bias_out[...] = jnp.zeros((8, FFS), F32)

    def back(spot):
        at = rows_at(spot)
        block = grad_all[at, :]
        d_pre = dot_nn(block, wb_all[:, 0:FFS]) * slope[at, :]
        rounded = d_pre.astype(BF16)
        left[at, :] = rounded
        whole = rounded.astype(F32)
        bias_out[...] += jnp.sum(whole.reshape(BLOCK // 8, 8, FFS), axis=0)
        d_att = dot_nn(block, wb_all[:, FFS:WB])
        do_own[at, :] = d_att.astype(BF16)
        product = att_t[:, at] * d_att.astype(BF16).astype(F32).T
        sums[2:3, at] = jnp.sum(product[0:HD], axis=0, keepdims=True)
        sums[3:4, at] = jnp.sum(product[HD:], axis=0, keepdims=True)

    def back_ring(flip, start, end):
        def step(n, carry):
            back(nth_spot(plane, n, flip))
            return carry

        lax.fori_loop(start, end, step, 0)

    locals_[2].wait()
    left_copies, left_keeps = [], []

    def send_left(o):
        k = len(left_copies)
        at = rows_at(plane.spot(*o))
        left_copies.append(
            remote(left.at[at, :], left_out.at[1, at, :], s_pair, r_pair, 10 + k, partner)
        )
        left_keeps.append(
            pltpu.make_async_copy(left.at[at, :], left_out.at[0, at, :], store.at[24 + k])
        )
        left_copies[k].start()
        left_keeps[k].start()

    for along in range(4):
        grad_gather.relays[along, 0].wait_recv()
    grad_copies = [
        keep_block(grad_all, grad_out, (along, 0), 32 + 2 * along) for along in range(4)
    ]
    back_ring(0, 0, 4)
    for along in range(4):
        send_left((along, 0))
    for along in (0, 1, 3):
        grad_gather.relays[along, 1].wait_recv()
        grad_copies.append(keep_block(grad_all, grad_out, (along, 1), 33 + 2 * along))
    back_ring(1, 0, 2)
    grad_gather.far(1)
    back_ring(1, 2, 3)
    for along in (0, 1, 3):
        send_left((along, 1))
    grad_gather.relays[2, 1].wait_recv()
    grad_copies.append(keep_block(grad_all, grad_out, (2, 1), 37))
    back_ring(1, 3, 4)
    send_left((2, 1))
    last_stores = [
        pltpu.make_async_copy(do_own, do_out, store.at[40]),
        pltpu.make_async_copy(sums, sums_out, store.at[41]),
    ]
    for copy in last_stores:
        copy.start()

    for gather in (grad_gather, normed_gather):
        for copy in gather.copies:
            copy.wait_send()
        for copy in gather.relays.values():
            copy.wait_send()
    wa_gather.end()
    wb_gather.end()
    hidden_copy.wait_send()
    for copy in piece_copies + tile_copies + wa_copies + wb_copies + place_copies:
        copy.wait_send()
    for copy in pairs + right_copies + left_copies:
        copy.wait()
    for copy in stores + small_stores + right_keeps + left_keeps + last_stores:
        copy.wait()
    for copy in normed_copies + grad_copies + [prob_stores[6], prob_stores[7]]:
        copy.wait()


def forward(*args):
    hbm = pl.BlockSpec(memory_space=pl.ANY)
    vmem = pl.BlockSpec(memory_space=pltpu.VMEM)
    dma = pltpu.SemaphoreType.DMA

    def shape(*dims, kind=BF16):
        return jax.ShapeDtypeStruct(dims, kind)

    return pl.pallas_call(
        forward_kernel,
        out_shape=(
            shape(SEQ, D),
            shape(SEQ, D),
            shape(2, HALF, WA),
            shape(2, HALF, WB),
            shape(2, SEQ, WB),
            shape(2, SEQ, FFS),
            shape(SEQ, HEADS),
            shape(HEADS, SEQ),
            shape(SEQ, HEADS),
            shape(SEQ, HEADS),
            shape(8, 2, SEQ, BLOCK),
            shape(8, SEQ, kind=F32),
            shape(2, SEQ, HEADS, kind=F32),
            shape(16, HALF, kind=F32),
            shape(BLOCK, 128, kind=F32),
            shape(8, FFS, kind=F32),
        ),
        in_specs=[vmem] + [hbm] * 5 + [vmem] * 3,
        out_specs=(hbm,) * 13 + (vmem,) * 3,
        scratch_shapes=[
            pltpu.VMEM((OWN, FF // 2), F32),
            pltpu.VMEM((3, OWN, HALF), F32),
            pltpu.VMEM((OWN, FF // 2), F32),
            pltpu.VMEM((OWN, HALF), F32),
            pltpu.VMEM((8, OWN, WA), BF16),
            pltpu.VMEM((8, OWN, WB), BF16),
            pltpu.VMEM((16, 128), F32),
            pltpu.VMEM((8, BLOCK), jnp.int32),
            pltpu.VMEM((16, 128), BF16),
            pltpu.VMEM((BLOCK, HALF), BF16),
            pltpu.VMEM((BLOCK, HALF), BF16),
            pltpu.VMEM((7, 16, 128), BF16),
            pltpu.VMEM((16, 128), BF16),
            pltpu.VMEM((16, HALF), BF16),
            pltpu.VMEM((8, 8, BLOCK), jnp.int32),
            pltpu.VMEM((SEQ, D), BF16),
            pltpu.VMEM((SEQ, D), BF16),
            pltpu.VMEM((D, WA), BF16),
            pltpu.VMEM((D, WB), BF16),
            pltpu.VMEM((SEQ, FFS), F32),
            pltpu.VMEM((SEQ, WB), BF16),
            pltpu.VMEM((SEQ, FFS), BF16),
            pltpu.VMEM((2, SEQ, HEADS), BF16),
            pltpu.VMEM((2, SEQ, HEADS), BF16),
            pltpu.VMEM((HEADS, SEQ), BF16),
            pltpu.VMEM((HEADS, SEQ), BF16),
            pltpu.VMEM((SEQ, HEADS), BF16),
            pltpu.VMEM((SEQ, HEADS), BF16),
            pltpu.VMEM((SEQ, HEADS), BF16),
            pltpu.VMEM((2, SEQ, BLOCK), F32),
            pltpu.VMEM((2, 2, SEQ, BLOCK), BF16),
            pltpu.VMEM((HEADS, SEQ), F32),
            pltpu.VMEM((2, SEQ, HEADS), F32),
            pltpu.VMEM((8, SEQ), F32),
            dma((4,)),
            dma((4,)),
            dma((24,)),
            dma((24,)),
            dma((16,)),
            dma((16,)),
            dma((18,)),
            dma((18,)),
            dma((36,)),
            dma((36,)),
            dma((18,)),
            dma((18,)),
            dma((42,)),
            dma((2,)),
        ],
        compiler_params=pltpu.CompilerParams(
            collective_id=0, has_side_effects=True, vmem_limit_bytes=62 * 1024 * 1024
        ),
        name="forward",
    )(*args)


def add_rows(dst, terms, count, chunk):
    def step(i, carry):
        at = pl.ds(pl.multiple_of(i * chunk, chunk), chunk)
        total = terms[0][at, :].astype(F32)
        for term in terms[1:]:
            total = total + term[at, :].astype(F32)
        dst[at, :] = total.astype(dst.dtype)
        return carry

    lax.fori_loop(0, count // chunk, step, 0)


class Reduce:
    def __init__(self, plane, acc, landing, sends, recvs, base):
        half_up, half_down, up, down, across = landing[:5]
        self.plane, self.acc, self.across = plane, acc, across
        self.near = (half_up, half_down, up, down)
        self.rows = across.shape[0]
        self.early = landing[5] if len(landing) > 5 else None
        self.direct = DIRECT if self.early is not None else 0
        self.sizes = (self.rows - self.direct, self.rows)
        self.copies = []
        for j, flip in ((0, 1), (1, 0)):
            far, size = plane.spot(2, flip), self.sizes[j]
            low, high, most = pl.ds(0, size // 2), pl.ds(size // 2, size // 2), pl.ds(0, size)
            for number, (src, dst, along) in enumerate(
                (
                    (acc.at[far, low, :], half_up.at[j, low, :], 1),
                    (acc.at[far, high, :], half_down.at[j, low, :], 3),
                    (acc.at[plane.spot(1, flip), most, :], up.at[j, most, :], 1),
                    (acc.at[plane.spot(3, flip), most, :], down.at[j, most, :], 3),
                )
            ):
                self.copies.append(
                    remote(src, dst, sends, recvs, base + 4 * j + number, plane.device(along, 0))
                )
        across_device = plane.device(0, 1)
        self.copies.append(
            remote(acc.at[plane.spot(0, 1)], across, sends, recvs, base + 8, across_device)
        )
        if self.direct:
            self.rest = pl.ds(self.sizes[0], self.direct)
            for k, along in enumerate((2, 1, 3)):
                src = acc.at[plane.spot(along, 1), self.rest, :]
                self.copies.append(
                    remote(src, self.early.at[k], sends, recvs, base + 9 + k, across_device)
                )

    def send_early(self):
        self.copies[10].start()
        self.copies[11].start()

    def add_early(self, k, along):
        self.copies[9 + k].wait_recv()
        dst = self.acc.at[self.plane.spot(along, 0), self.rest, :]
        add_rows(dst, [dst, self.early.at[k]], self.direct, 16)

    def first(self, j):
        if self.direct and j:
            self.add_early(0, 2)
        self.copies[4 * j].start()
        self.copies[4 * j + 1].start()
        if self.direct and not j:
            self.copies[9].start()

    def second(self, j):
        if self.direct and j:
            self.add_early(1, 1)
            self.add_early(2, 3)
        half = self.sizes[j] // 2
        for number, along in ((0, 1), (1, 3)):
            self.copies[4 * j + number].wait_recv()
            dst = self.acc.at[self.plane.spot(along, 1 - j), pl.ds(number * half, half), :]
            add_rows(dst, [dst, self.near[number].at[j]], half, 16)
            self.copies[4 * j + number + 2].start()

    def third(self):
        self.copies[2].wait_recv()
        self.copies[3].wait_recv()
        dst = self.acc.at[self.plane.spot(0, 1)]
        add_rows(dst, [dst, self.near[2].at[0], self.near[3].at[0]], self.sizes[0], 16)
        self.copies[8].start()

    def arrived(self):
        for k in (6, 7, 8):
            self.copies[k].wait_recv()
        mine = self.acc.at[self.plane.spot(0, 0)]
        return [mine, self.near[2].at[1], self.near[3].at[1], self.across]

    def last(self, dst):
        add_rows(dst, self.arrived(), self.rows, 16)

    def end(self):
        for copy in self.copies:
            copy.wait_send()


def backward_kernel(
    right_in, wb_in, left_in, wa_in, normed, grads, q_in, k_in, v_in, do_in,
    probs_in, sums, wave_in, hid, grad, stats, vec_all, bias_in,
    hidden_out, grad_in, gb_all, ga_all, vec_sum,
    right, left, weight, stream, q_all, k_t, v_all, do_all, probs_odd, probs_even, wave, d_k, d_v,
    out_acc, dx_acc, gb_acc, ga_acc,
    out_a, out_b, out_c, out_d, out_e, out_f, dx_a, dx_b, dx_c, dx_d, dx_e, dx_f, gb_a, gb_b, gb_c, gb_d, gb_e,
    ga_a, ga_b, ga_c, ga_d, ga_e, gb_done, ga_done, bias, final, vec, vec_in, vec_tile, tile_in, row_own, row_in,
    load, s_stream, s_probs, s_pair, r_pair, s_red, r_red, s_small, r_small, keep,
):
    plane, data = Plane(True), Plane(False)
    ctx, dp, core = plane.ctx, plane.dp, plane.core
    partner = (dp, ctx, 1 - core)
    loads = {
        "weight": pltpu.make_async_copy(wb_in, weight.at[:, :, pl.ds(0, WB)], load.at[0]),
        "right": pltpu.make_async_copy(right_in, right, load.at[1]),
        "left": pltpu.make_async_copy(left_in, left.at[:, :, pl.ds(0, FFS)], load.at[2]),
        "q": pltpu.make_async_copy(q_in, q_all, load.at[4]),
        "k": pltpu.make_async_copy(k_in, k_t, load.at[5]),
        "v": pltpu.make_async_copy(v_in, v_all, load.at[6]),
        "do": pltpu.make_async_copy(do_in, do_all, load.at[7]),
    }
    loads["weight"].start()
    loads["right"].start()
    partners = partners_of(plane, data)
    greet(partners)

    out = Reduce(plane, out_acc, (out_a, out_b, out_c, out_d, out_e, out_f), s_red, r_red, 0)
    dx = Reduce(plane, dx_acc, (dx_a, dx_b, dx_c, dx_d, dx_e, dx_f), s_red, r_red, 12)
    gb = Reduce(data, gb_acc, (gb_a, gb_b, gb_c, gb_d, gb_e), s_red, r_red, 24)
    ga = Reduce(data, ga_acc, (ga_a, ga_b, ga_c, ga_d, ga_e), s_red, r_red, 33)

    def spot_of(where, n):
        group = lax.div(n + 2, 4)
        inside = n + 2 - 4 * group
        near = 1 - lax.rem(group + 1, 2)
        along = near * (1 + 2 * lax.rem(inside, 2)) + (1 - near) * (2 - group)
        flip = near * (1 - lax.div(inside, 2)) + (1 - near) * (1 - lax.rem(inside, 2))
        return where.spot_at(along, flip)

    def out_block(n, carry):
        spot = spot_of(plane, n)
        at = rows_at(spot)
        total = dot_nt(right[0, at, :], weight[0, :, 0:WB])
        total = total + dot_nt(right[1, at, :], weight[1, :, 0:WB])
        out_acc[spot] = total.astype(BF16)
        return carry

    def dx_block(n, carry):
        spot = spot_of(plane, n)
        at = rows_at(spot)
        total = dot_nt(left[0, at, :], weight[0])
        total = total + dot_nt(left[1, at, :], weight[1])
        dx_acc[spot] = total.astype(BF16)
        return carry

    def fetch(source, n):
        columns = rows_at(spot_of(data, n))
        slot = lax.rem(n, 2)
        return pltpu.make_async_copy(source.at[:, columns], stream.at[slot], s_stream.at[slot])

    def weight_blocks(source, factor, acc, start, end):
        def step(n, carry):
            @pl.when(n < 7)
            def _():
                fetch(source, n + 1).start()

            fetch(source, n).wait()
            total = dot_tn(stream[lax.rem(n, 2)], factor[0])
            acc[spot_of(data, n)] = total.astype(BF16)
            return carry

        lax.fori_loop(start, end, step, 0)

    loads["weight"].wait()
    loads["right"].wait()
    fetch(grads, 0).start()
    lax.fori_loop(0, 1, out_block, 0)
    meet(partners)
    out.first(0)
    for name in ("q", "k", "v", "do", "left"):
        loads[name].start()
    lax.fori_loop(1, 4, out_block, 0)
    out.send_early()
    lax.fori_loop(4, 8, out_block, 0)
    weight_load = pltpu.make_async_copy(wa_in, weight, load.at[8])
    weight_load.start()
    out.second(0)
    out.first(1)
    weight_blocks(grads, right, gb_acc, 0, 1)
    gb.first(0)
    weight_blocks(grads, right, gb_acc, 1, 4)

    lane = lax.broadcasted_iota(jnp.int32, (BLOCK, HEADS), 1)
    heads = (lane < HD, lane >= HD)
    bias[...] = jnp.zeros((8, 3 * HEADS), F32)

    def clear(i, carry):
        d_k[rows_at(i), :] = jnp.zeros((BLOCK, HEADS), F32)
        d_v[rows_at(i), :] = jnp.zeros((BLOCK, HEADS), F32)
        return carry

    lax.fori_loop(0, 8, clear, 0)

    def probs_of(i):
        length = pl.ds(0, (i + 1) * BLOCK)
        buffer = probs_odd if i % 2 else probs_even
        return [
            pltpu.make_async_copy(
                probs_in.at[i, :, length, :], buffer.at[:, length, :], s_probs.at[i % 2]
            ),
            pltpu.make_async_copy(
                wave_in.at[:, pl.ds(i * BLOCK, BLOCK), :], wave.at[i % 2], s_probs.at[2 + i % 2]
            ),
        ]

    for name in ("q", "k", "v", "do"):
        loads[name].wait()
    arriving = {7: probs_of(7)}
    for copy in arriving[7]:
        copy.start()
    swaps = []
    for i in range(7, -1, -1):
        own = pl.ds(i * BLOCK, BLOCK)
        if i:
            arriving[i - 1] = probs_of(i - 1)
            for copy in arriving[i - 1]:
                copy.start()
        for copy in arriving[i]:
            copy.wait()
        probs = probs_odd if i % 2 else probs_even
        scale = [sums[h : h + 1, own] for h in range(2)]
        delta = [sums[2 + h : 3 + h, own] for h in range(2)]
        q, do = q_all[own, :].astype(F32), do_all[own, :].astype(F32)
        q_plain = [jnp.where(heads[h], q, 0.0).astype(BF16) for h in range(2)]
        do_plain = [jnp.where(heads[h], do, 0.0).astype(BF16) for h in range(2)]

        def back(j, carry):
            at, new = rows_at(j), []
            add_k, add_v = d_k[at, :], d_v[at, :]
            for h in range(2):
                p = probs[h, at, :].astype(F32) * scale[h]
                d_p = dot_nt(v_all[at, :], do_plain[h])
                d_s = (p * (d_p - delta[h])).astype(BF16)
                add_v = add_v + dot_nn(p.astype(BF16), do_plain[h])
                add_k = add_k + dot_nn(d_s, q_plain[h])
                new.append(carry[h] + dot_nn(k_t[pl.ds(h * HD, HD), at], d_s))
            d_k[at, :] = add_k
            d_v[at, :] = add_v
            return tuple(new)

        zero_out = jnp.zeros((HD, BLOCK), F32)
        d_q = lax.fori_loop(0, i + 1, back, (zero_out, zero_out), unroll=True)
        d_q = jnp.concatenate(d_q, axis=0).T * (HD**-0.5)
        c, s = wave[i % 2, 0], wave[i % 2, 1]
        parts = (turn(d_q, c, s, -1.0), turn(d_k[own, :], c, s, -1.0), d_v[own, :])
        for k, part in enumerate(parts):
            rounded = part.astype(BF16)
            whole = rounded.astype(F32)
            left[0, own, FFS + k * HEADS : FFS + (k + 1) * HEADS] = rounded
            columns = slice(k * HEADS, (k + 1) * HEADS)
            bias[:, columns] += jnp.sum(whole.reshape(BLOCK // 8, 8, HEADS), axis=0)
        span = pl.ds(FFS, 3 * HEADS)
        swap = remote(
            left.at[0, own, span], left.at[1, own, span], s_pair, r_pair, i, partner
        )
        swap.start()
        swaps.append(swap)
        if i == 7:
            gb.second(0)
            gb.first(1)
        if i == 6:
            out.second(1)
        if i == 3:
            out.third()

    loads["left"].wait()
    weight_load.wait()
    for swap in swaps:
        swap.wait_recv()
    lax.fori_loop(0, 1, dx_block, 0)
    dx.first(0)
    weight_blocks(grads, right, gb_acc, 4, 6)
    gb.second(1)
    weight_blocks(grads, right, gb_acc, 6, 8)
    fetch(normed, 0).start()
    gb.third()
    weight_blocks(normed, left, ga_acc, 0, 1)
    ga.first(0)
    lax.fori_loop(1, 4, dx_block, 0)
    dx.send_early()
    weight_blocks(normed, left, ga_acc, 1, 2)
    dx.second(0)
    dx.first(1)
    weight_blocks(normed, left, ga_acc, 2, 4)
    ga.second(0)
    ga.first(1)
    lax.fori_loop(4, 8, dx_block, 0)
    dx.third()
    weight_blocks(normed, left, ga_acc, 4, 6)
    dx.second(1)
    weight_blocks(normed, left, ga_acc, 6, 7)
    ga.third()
    weight_blocks(normed, left, ga_acc, 7, 8)
    ga.second(1)
    gb.last(gb_done)

    copies = {}
    keeps = []
    for n, (name, done, landed) in enumerate(
        (("gb", gb_done, gb_all), ("ga", ga_done, ga_all))
    ):
        copies[name] = [
            remote(
                done.at[rows_at(plane.spot(*o), OWN), :],
                landed.at[ctx],
                s_small,
                r_small,
                15 + 7 * n + k,
                plane.device(*o),
            )
            for k, o in enumerate(OTHERS)
        ]
        keeps.append(
            pltpu.make_async_copy(done.at[rows_at(ctx, OWN), :], landed.at[ctx], keep.at[n])
        )
    for copy in copies["gb"]:
        copy.start()
    keeps[0].start()

    out.last(final)
    bias_rows = vec_all[7:8, :] + vec_all[8:9, :]

    def add_hidden(i, carry):
        at = pl.ds(pl.multiple_of(i * 16, 16), 16)
        hidden_out[at, :] = (hid[at, :].astype(F32) + final[at, :] + bias_rows).astype(BF16)
        return carry

    lax.fori_loop(0, BLOCK // 16, add_hidden, 0)
    dx.last(final)
    gain = vec_all[9:10, :]
    lanes = lax.broadcasted_iota(jnp.int32, (16, 128), 1)

    def lean(i, carry):
        at = pl.ds(pl.multiple_of(i * 16, 16), 16)
        d, h, stat = final[at, :], hid[at, :].astype(F32), stats[at, :]
        normal = (h - stat[:, 0:1]) * stat[:, 64:65]
        product = d * normal
        one = jnp.sum(d * gain, axis=1, keepdims=True)
        two = jnp.sum(product * gain, axis=1, keepdims=True)
        row_own[at, :] = jnp.where(lanes < 64, one, two)
        return (carry[0] + d, carry[1] + product, carry[2] + grad[at, :].astype(F32))

    zero = jnp.zeros((16, HALF), F32)
    rows = lax.fori_loop(0, BLOCK // 16, lean, (zero, zero, zero))
    row_copy = remote(row_own, row_in, s_small, r_small, 0, partner)
    row_copy.start()
    shift_grad, gain_grad, bias_grad = [jnp.sum(r, axis=0, keepdims=True) for r in rows]
    number = lax.broadcasted_iota(jnp.int32, (16, HALF), 0)
    vec[...] = jnp.where(
        number == 9,
        gain_grad,
        jnp.where(
            number == 10, shift_grad, jnp.where((number == 7) | (number == 8), bias_grad, 0.0)
        ),
    )
    columns = pl.ds(pl.multiple_of(ctx * HEADS, HEADS), HEADS)
    for k in range(3):
        part = jnp.sum(bias[:, k * HEADS : (k + 1) * HEADS], axis=0, keepdims=True)
        vec[k : k + 1, columns] = part
    columns = pl.ds(pl.multiple_of(lax.rem(ctx, 2) * FFS, FFS), FFS)
    part = jnp.sum(bias_in[...], axis=0, keepdims=True)
    vec[:, columns] = jnp.where(
        lax.broadcasted_iota(jnp.int32, (16, FFS), 0) == 3 + lax.div(ctx, 2), part, vec[:, columns]
    )
    vec_copies, tile_copies = [], []
    for k, o in enumerate(OTHERS):
        columns = pl.ds(pl.multiple_of(data.spot(*o) * 128, 128), 128)
        vec_copies.append(
            remote(vec.at[:, columns], vec_in.at[k], s_small, r_small, 1 + k, data.device(*o))
        )
        tile_copies.append(
            remote(vec_tile, tile_in.at[k], s_small, r_small, 8 + k, plane.device(*o))
        )
    for copy in vec_copies:
        copy.start()
    ga.last(ga_done)
    for copy in copies["ga"]:
        copy.start()
    keeps[1].start()
    for copy in vec_copies:
        copy.wait_recv()
    total = vec[:, pl.ds(pl.multiple_of(dp * 128, 128), 128)]
    for k in range(7):
        total = total + vec_in[k]
    vec_tile[...] = total
    for copy in tile_copies:
        copy.start()

    row_copy.wait()

    def tilt(i, carry):
        at = pl.ds(pl.multiple_of(i * 16, 16), 16)
        d, h, stat = final[at, :], hid[at, :].astype(F32), stats[at, :]
        inverse = stat[:, 64:65]
        normal = (h - stat[:, 0:1]) * inverse
        row = (row_own[at, :] + row_in[at, :]) / D
        change = inverse * (d * gain - row[:, 0:1] - normal * row[:, 64:65])
        grad_in[at, :] = (grad[at, :].astype(F32) + change).astype(BF16)
        return carry

    lax.fori_loop(0, BLOCK // 16, tilt, 0)
    for copy in tile_copies:
        copy.wait_recv()
    total = vec_tile[...]
    for k in range(7):
        total = total + tile_in[k]
    vec_sum[...] = total

    for name in copies:
        for copy in copies[name]:
            copy.wait()
    for copy in keeps:
        copy.wait()
    for copy in vec_copies + tile_copies + swaps:
        copy.wait_send()
    for red in (dx, out, gb, ga):
        red.end()


def backward(*args):
    hbm = pl.BlockSpec(memory_space=pl.ANY)
    vmem = pl.BlockSpec(memory_space=pltpu.VMEM)
    dma = pltpu.SemaphoreType.DMA

    def landing(rows, width):
        half = pltpu.VMEM((2, rows // 2, width), BF16)
        whole = pltpu.VMEM((2, rows, width), BF16)
        return [half, half, whole, whole, pltpu.VMEM((rows, width), BF16)]

    def shape(*dims, kind=BF16):
        return jax.ShapeDtypeStruct(dims, kind)

    return pl.pallas_call(
        backward_kernel,
        out_shape=(
            shape(BLOCK, HALF),
            shape(BLOCK, HALF),
            shape(8, OWN, WB),
            shape(8, OWN, WA),
            shape(16, 128, kind=F32),
        ),
        in_specs=[hbm] * 11 + [vmem, hbm] + [vmem] * 5,
        out_specs=(vmem, vmem, hbm, hbm, vmem),
        scratch_shapes=[
            pltpu.VMEM((2, SEQ, WB), BF16),
            pltpu.VMEM((2, SEQ, WA), BF16),
            pltpu.VMEM((2, HALF, WA), BF16),
            pltpu.VMEM((2, SEQ, BLOCK), BF16),
            pltpu.VMEM((SEQ, HEADS), BF16),
            pltpu.VMEM((HEADS, SEQ), BF16),
            pltpu.VMEM((SEQ, HEADS), BF16),
            pltpu.VMEM((SEQ, HEADS), BF16),
            pltpu.VMEM((2, SEQ, BLOCK), BF16),
            pltpu.VMEM((2, SEQ - BLOCK, BLOCK), BF16),
            pltpu.VMEM((2, 2, BLOCK, HEADS), F32),
            pltpu.VMEM((SEQ, HEADS), F32),
            pltpu.VMEM((SEQ, HEADS), F32),
            pltpu.VMEM((8, BLOCK, HALF), BF16),
            pltpu.VMEM((8, BLOCK, HALF), BF16),
            pltpu.VMEM((8, BLOCK, WB), BF16),
            pltpu.VMEM((8, BLOCK, WA), BF16),
            *landing(BLOCK, HALF),
            pltpu.VMEM((3, DIRECT, HALF), BF16),
            *landing(BLOCK, HALF),
            pltpu.VMEM((3, DIRECT, HALF), BF16),
            *landing(BLOCK, WB),
            *landing(BLOCK, WA),
            pltpu.VMEM((BLOCK, WB), BF16),
            pltpu.VMEM((BLOCK, WA), BF16),
            pltpu.VMEM((8, 3 * HEADS), F32),
            pltpu.VMEM((BLOCK, HALF), F32),
            pltpu.VMEM((16, HALF), F32),
            pltpu.VMEM((7, 16, 128), F32),
            pltpu.VMEM((16, 128), F32),
            pltpu.VMEM((7, 16, 128), F32),
            pltpu.VMEM((BLOCK, 128), F32),
            pltpu.VMEM((BLOCK, 128), F32),
            dma((10,)),
            dma((2,)),
            dma((4,)),
            dma((8,)),
            dma((8,)),
            dma((42,)),
            dma((42,)),
            dma((36,)),
            dma((36,)),
            dma((3,)),
        ],
        compiler_params=pltpu.CompilerParams(
            collective_id=1, has_side_effects=True, vmem_limit_bytes=62 * 1024 * 1024
        ),
        name="backward",
    )(*args)


def adam_step(weight, first, second, gradient, rate):
    first_new = BETA_ONE * first + (1.0 - BETA_ONE) * gradient
    second_new = BETA_TWO * second + (1.0 - BETA_TWO) * gradient * gradient
    fix_one = 1.0 - BETA_ONE**STEP
    fix_two = 1.0 - BETA_TWO**STEP
    update = first_new / fix_one / (jnp.sqrt(second_new / fix_two) + ADAM_EPS)
    return (first_new, second_new, weight - rate * (update + DECAY * weight))


def update_kernel(
    ga, gb, vec_sum, hidden, back,
    qkv_w, qkv_m, qkv_v, dense_w, dense_m, dense_v, fc1_w, fc1_m, fc1_v, fc2_w, fc2_m, fc2_v,
    vec_w, vec_m, vec_v,
    hidden_out, back_out,
    qkv_mo, qkv_vo, qkv_wo, dense_mo, dense_vo, dense_wo, fc1_mo, fc1_vo, fc1_wo,
    fc2_mo, fc2_vo, fc2_wo, vec_mo, vec_vo, vec_wo,
):
    hidden_out[...] = hidden[...]
    back_out[...] = back[...]

    fc1 = (fc1_w, fc1_m, fc1_v, fc1_mo, fc1_vo, fc1_wo)
    fc2 = (fc2_w, fc2_m, fc2_v, fc2_mo, fc2_vo, fc2_wo)
    dense = (dense_w, dense_m, dense_v, dense_mo, dense_vo, dense_wo)
    qkv = (qkv_w, qkv_m, qkv_v, qkv_mo, qkv_vo, qkv_wo)
    vec = (vec_w, vec_m, vec_v, vec_mo, vec_vo, vec_wo)

    def step(refs, gradient, rate, *at):
        w, m, v, mo, vo, wo = refs
        mo[at], vo[at], wo[at] = adam_step(w[at], m[at], v[at], gradient, rate)

    for c in range(8):
        wide, narrow = slice(c * FFS, (c + 1) * FFS), slice(c * HEADS, (c + 1) * HEADS)
        step(fc1, ga[c, :, 0:FFS].astype(F32), RATES[0], slice(None), wide)
        step(fc2, gb[c, :, 0:FFS].astype(F32), RATES[1], slice(None), wide)
        step(dense, gb[c, :, FFS:WB].astype(F32), RATES[2], slice(None), narrow)
        for k in range(3):
            columns = slice(FFS + k * HEADS, FFS + (k + 1) * HEADS)
            step(qkv, ga[c, :, columns].astype(F32), RATES[0], k, slice(None), narrow)

    @pl.when(pl.program_id(0) == 0)
    def _():
        mine = pltpu.roll(vec_sum[...], lax.rem(128 - 16 * lax.axis_index("ctx"), 128), 1)
        for k in range(11):
            step(vec, mine[k : k + 1, 0:16], RATES[3], k)


def update(ga, gb, vec_sum, hidden, back, *state):
    steps = 2
    rows = OWN // steps

    def part(width):
        return pl.BlockSpec((rows, width), lambda n: (n, 0))

    vec = pl.BlockSpec((11, 1, 16), lambda n: (0, 0, 0))
    token = pl.BlockSpec((BLOCK // steps, HALF), lambda n: (n, 0))
    sets = (
        [pl.BlockSpec((3, rows, HALF), lambda n: (0, n, 0))] * 3
        + [part(HALF)] * 3
        + [part(FF // 2)] * 6
        + [vec] * 3
    )
    wide = [pl.BlockSpec((8, rows, w), lambda n: (0, n, 0)) for w in (WA, WB)]
    shapes = [jax.ShapeDtypeStruct(x.shape, x.dtype) for x in (hidden, back, *state)]
    return pl.pallas_call(
        update_kernel,
        grid=(steps,),
        out_shape=shapes,
        in_specs=wide + [pl.BlockSpec((16, 128), lambda n: (0, 0)), token, token] + sets,
        out_specs=[token, token] + sets,
        compiler_params=pltpu.CompilerParams(vmem_limit_bytes=62 * 1024 * 1024),
        name="update",
    )(ga, gb, vec_sum, hidden, back, *state)


def on_device(
    hidden_in,
    grad_out,
    segment_ids,
    positions,
    qkv_weight,
    dense_weight,
    fc1_weight,
    fc2_weight,
    vectors,
    qkv_first,
    qkv_second,
    dense_first,
    dense_second,
    fc1_first,
    fc1_second,
    fc2_first,
    fc2_second,
    vector_first,
    vector_second,
):
    hid = hidden_in.reshape(BLOCK, HALF)
    grad = grad_out.reshape(BLOCK, HALF)

    def turned(array):
        return jnp.moveaxis(array, 1, 0)

    (
        normed, grads, wa2, wb2, right, left, q, k_t, v, do, probs, sums, wave, vec_all, stats, bias,
    ) = forward(
        hid, grad, fc1_weight, turned(qkv_weight), fc2_weight, dense_weight, turned(vectors),
        segment_ids, positions,
    )
    hidden_out, grad_in, gb_all, ga_all, vec_sum = backward(
        right, wb2, left, wa2, normed, grads, q, k_t, v, do, probs, sums, wave,
        hid, grad, stats, vec_all, bias,
    )
    new = update(
        ga_all, gb_all, vec_sum, hidden_out, grad_in,
        turned(qkv_weight), turned(qkv_first), turned(qkv_second),
        dense_weight, dense_first, dense_second,
        fc1_weight, fc1_first, fc1_second, fc2_weight, fc2_first, fc2_second,
        turned(vectors), turned(vector_first), turned(vector_second),
    )
    return (
        new[0].reshape(hidden_in.shape),
        new[1].reshape(grad_out.shape),
        *(turned(x) for x in new[2:5]),
        *new[5:14],
        *(turned(x) for x in new[14:]),
    )


def solution(mesh):
    rows = P("dp", "ctx", "tensor")
    tokens = P("dp", "ctx")
    cube = P(("dp", "ctx"), None, "tensor")
    plain = P(("dp", "ctx"), "tensor")
    packed = P("tensor", None, ("dp", "ctx"))
    return jax.shard_map(
        on_device,
        mesh=mesh,
        in_specs=(rows, rows, tokens, tokens, cube, plain, plain, plain, packed)
        + (cube,) * 2
        + (plain,) * 6
        + (packed,) * 2,
        out_specs=(rows, rows) + (cube,) * 3 + (plain,) * 9 + (packed,) * 3,
        check_vma=False,
    )
```

```python
import functools
import math

import jax
import jax.numpy as jnp
import numpy as np
from jax import lax
from jax.experimental import pallas as pl
from jax.experimental.pallas import tpu as pltpu
from jax.sharding import PartitionSpec as P

D = 2048
HD = 64
ROT = 32
FF = 8192
STEP = 10
SEQ = 2048
BLOCK = 256
HALF = 1024
FFS = 512
HEADS = 128
WA = FFS + 3 * HEADS
WB = FFS + HEADS
OWN = 32
DIRECT = 64

BETA_ONE = 0.9
BETA_TWO = 0.95
ADAM_EPS = 1e-08
DECAY = 0.1
NORM_EPS = 1e-05
MASKED = -1e30
GELU = math.sqrt(2.0 / math.pi)

RATES = (2.0 / math.sqrt(D), 2.0 / math.sqrt(FF), 2.0 / math.sqrt(D // 16), 0.6)
MESH = pl.DeviceIdType.MESH
F32 = jnp.float32
BF16 = jnp.bfloat16
OTHERS = tuple((k // 2, k % 2) for k in range(1, 8))


class Plane:
    def __init__(self, over_ctx):
        self.dp = lax.axis_index("dp")
        self.ctx = lax.axis_index("ctx")
        self.core = lax.axis_index("tensor")
        self.over_ctx = over_ctx
        if over_ctx:
            self.ring, self.pair = lax.div(self.ctx, 2), lax.rem(self.ctx, 2)
        else:
            self.ring, self.pair = lax.rem(self.dp, 4), lax.div(self.dp, 4)

    def spot(self, along, flip):
        ring = lax.rem(self.ring + along, 4) if along else self.ring
        pair = 1 - self.pair if flip else self.pair
        return ring * 2 + pair if self.over_ctx else pair * 4 + ring

    def spot_at(self, along, flip):
        ring, pair = lax.rem(self.ring + along, 4), lax.rem(self.pair + flip, 2)
        return ring * 2 + pair if self.over_ctx else pair * 4 + ring

    def device(self, along, flip):
        spot = self.spot(along, flip)
        return (self.dp, spot, self.core) if self.over_ctx else (spot, self.ctx, self.core)


def rows_at(index, size=BLOCK):
    return pl.ds(pl.multiple_of(index * size, size), size)


def remote(src, dst, sends, recvs, number, device):
    return pltpu.make_async_remote_copy(
        src_ref=src,
        dst_ref=dst,
        send_sem=sends.at[number],
        recv_sem=recvs.at[number],
        device_id=device,
        device_id_type=MESH,
    )


def partners_of(ctx_plane, dp_plane):
    partners = [ctx_plane.device(*o) for o in OTHERS] + [dp_plane.device(*o) for o in OTHERS]
    return partners + [(ctx_plane.dp, ctx_plane.ctx, 1 - ctx_plane.core)]


def greet(partners):
    barrier = pltpu.get_barrier_semaphore()
    for partner in partners:
        pl.semaphore_signal(barrier, inc=1, device_id=partner, device_id_type=MESH)


def meet(partners):
    pl.semaphore_wait(pltpu.get_barrier_semaphore(), len(partners))


class Gather:
    def __init__(self, plane, own, region, sends, recvs, base, direct=0):
        self.direct = direct
        near, half = BLOCK - direct, BLOCK // 2
        whole, most, rest = (0, BLOCK), (0, near), (near, direct)
        plans = [
            ((0, 0), whole, (1, 0)),
            ((0, 0), whole, (3, 0)),
            ((0, 0), whole, (0, 1)),
            ((3, 0), (0, half), (1, 0)),
            ((1, 0), (half, half), (3, 0)),
            ((0, 1), most, (1, 0)),
            ((0, 1), most, (3, 0)),
            ((3, 1), (0, near // 2), (1, 0)),
            ((1, 1), (near // 2, near // 2), (3, 0)),
        ]
        if direct:
            plans += [((along, 0), rest, (0, 1)) for along in (3, 1, 2)]
        self.copies = []
        for number, (block, span, to) in enumerate(plans):
            dst = region(plane.spot(*block), *span)
            src = own if number < 3 else dst
            self.copies.append(
                remote(src, dst, sends, recvs, base + number, plane.device(*to))
            )

    def begin_ring(self):
        self.copies[0].start()
        self.copies[1].start()

    def begin_pair(self):
        self.copies[2].start()

    def ring(self, flip):
        first, relay = (5, 7) if flip else (0, 3)
        for k in (0, 1):
            self.copies[first + k].wait_recv()
            self.copies[relay + k].start()
            if self.direct and not flip:
                self.copies[9 + k].start()
        if self.direct and flip:
            self.copies[9].wait_recv()
            self.copies[10].wait_recv()

    def pair(self):
        self.copies[2].wait_recv()
        self.copies[5].start()
        self.copies[6].start()

    def far(self, flip):
        for k in (7, 8) if flip else (3, 4):
            self.copies[k].wait_recv()
        if self.direct:
            if flip:
                self.copies[11].wait_recv()
            else:
                self.copies[11].start()

    def end(self):
        for copy in self.copies:
            copy.wait_send()


class GatherCores(Gather):
    def __init__(self, plane, own, region, sends, recvs, base, core_sends, core_recvs, core_base):
        super().__init__(plane, own, region, sends, recvs, base, DIRECT)
        partner = (plane.dp, plane.ctx, 1 - plane.core)
        self.relays = {}
        for number, (along, flip) in enumerate(((0, 0),) + OTHERS):
            dst = region(plane.spot(along, flip), 0, BLOCK)
            src = dst if number else own
            self.relays[along, flip] = remote(
                src, dst, core_sends, core_recvs, core_base + number, partner
            )

    def begin_ring(self):
        super().begin_ring()
        self.relays[0, 0].start()

    def ring(self, flip):
        super().ring(flip)
        self.relays[3, flip].start()
        self.relays[1, flip].start()

    def pair(self):
        super().pair()
        self.relays[0, 1].start()

    def far(self, flip):
        super().far(flip)
        self.relays[2, flip].start()

    def end(self):
        super().end()
        for copy in self.relays.values():
            copy.wait()


def dot_nt(left, right):
    return lax.dot_general(left, right, (((1,), (1,)), ((), ())), preferred_element_type=F32)


def dot_nn(left, right):
    return jnp.dot(left, right, preferred_element_type=F32)


def dot_tn(left, right):
    return lax.dot_general(left, right, (((0,), (0,)), ((), ())), preferred_element_type=F32)


def turn(values, cosine, sine, sign):
    lane = lax.rem(lax.broadcasted_iota(jnp.int32, values.shape, 1), HD)
    low = jnp.where(lane < ROT // 2, sine, 0.0)
    high = sine - low
    up = pltpu.roll(values, HEADS - ROT // 2, 1)
    down = pltpu.roll(values, ROT // 2, 1)
    return values * cosine + sign * (down * high - up * low)


def fold(values, op):
    return op(values.reshape(BLOCK // 8, 8, BLOCK), axis=0)


def nth_spot(plane, n, flip):
    along = n + lax.div(n, 2) - 2 * lax.div(n, 3)
    return plane.spot_at(along, flip)


def forward_kernel(
    hid, grad, fc1_in, qkv_in, fc2_in, dense_in, vectors, segments, positions,
    normed_out, grad_out, wa_out, wb_out, right_out, left_out,
    q_out, k_out, v_out, do_out, probs_out, sums_out, wave_out, vec_all, stats, bias_out,
    fc1, qkv_w, fc2, dense, wa, wb, vec, place, joined, other, normed, pieces, tile, table, place_all,
    normed_all, grad_all, wa_all, wb_all, slope, right, left, q_mask, k_mask, v_t, k_t, q_own, v_own, do_own,
    scores, probs, att_t, wave, sums,
    load, local, s_act, r_act, s_core, r_core, s_w, r_w, s_small, r_small, s_pair, r_pair, store, p_sem,
):
    plane, data = Plane(True), Plane(False)
    ctx, dp, core = plane.ctx, plane.dp, plane.core
    partner = (dp, ctx, 1 - core)

    def span_at(spot, start, size):
        return pl.ds(pl.multiple_of(spot * BLOCK + start, 32), size)

    def act_region(ref):
        columns = pl.ds(pl.multiple_of(core * HALF, HALF), HALF)
        return lambda *span: ref.at[span_at(*span), columns]

    def weight_region(ref):
        return lambda *span: ref.at[span_at(*span), :]

    def scatter_rows(ref):
        start = pl.multiple_of(dp * BLOCK + ctx * OWN, OWN)
        return ref.at[pl.ds(start, OWN), :]

    normed_gather = GatherCores(
        plane, normed, act_region(normed_all), s_act, r_act, 0, s_core, r_core, 0
    )
    grad_gather = GatherCores(
        plane, grad, act_region(grad_all), s_act, r_act, 12, s_core, r_core, 8
    )

    loads = [
        pltpu.make_async_copy(src, dst, load.at[k])
        for k, (src, dst) in enumerate(
            ((fc1_in, fc1), (qkv_in, qkv_w), (fc2_in, fc2), (dense_in, dense))
        )
    ]
    for copy in loads:
        copy.start()
    partners = partners_of(plane, data)
    greet(partners)
    vec_lane = lax.broadcasted_iota(jnp.int32, (1, 128), 1)
    vec[...] = jnp.zeros((16, 128), F32)
    for k in range(11):
        spread = jnp.concatenate([vectors[k]] * 8, axis=1)
        vec[k : k + 1, :] = jnp.where(lax.div(vec_lane, 16) == ctx, spread, 0.0)
    tile[...] = vec[...].astype(BF16)
    place[...] = jnp.zeros((8, BLOCK), jnp.int32)
    place[0:1, :] = segments[...]
    place[1:2, :] = positions[...]
    place_all[ctx] = place[...]
    for copy in loads:
        copy.wait()
    for c in range(8):
        wa[c, :, 0:FFS] = fc1[:, c * FFS : (c + 1) * FFS].astype(BF16)
        wb[c, :, 0:FFS] = fc2[:, c * FFS : (c + 1) * FFS].astype(BF16)
        columns = slice(c * HEADS, (c + 1) * HEADS)
        wb[c, :, FFS:WB] = dense[:, columns].astype(BF16)
        for k in range(3):
            wa[c, :, FFS + k * HEADS : FFS + (k + 1) * HEADS] = qkv_w[k, :, columns].astype(BF16)

    piece_copies, tile_copies, place_copies, wa_copies, wb_copies = [], [], [], [], []
    for k, o in enumerate(OTHERS):
        to = plane.device(*o)
        spot = plane.spot(*o)
        piece_copies.append(remote(tile, pieces.at[k], s_small, r_small, 1 + k, to))
        place_copies.append(remote(place, place_all.at[ctx], s_small, r_small, 15 + k, to))
        wa_copies.append(remote(wa.at[spot], scatter_rows(wa_all), s_small, r_small, 22 + k, to))
        wb_copies.append(remote(wb.at[spot], scatter_rows(wb_all), s_small, r_small, 29 + k, to))
        columns = pl.ds(pl.multiple_of(dp * 128, 128), 128)
        tile_copies.append(
            remote(joined, table.at[:, columns], s_small, r_small, 8 + k, data.device(*o))
        )
    hidden_copy = remote(hid, other, s_small, r_small, 0, partner)
    meet(partners)
    for copy in piece_copies:
        copy.start()
    hidden_copy.start()
    locals_ = [
        pltpu.make_async_copy(wa.at[ctx], scatter_rows(wa_all), local.at[0]),
        pltpu.make_async_copy(wb.at[ctx], scatter_rows(wb_all), local.at[1]),
        pltpu.make_async_copy(grad, act_region(grad_all)(ctx, 0, BLOCK), local.at[2]),
        pltpu.make_async_copy(normed, act_region(normed_all)(ctx, 0, BLOCK), local.at[3]),
    ]
    for copy in locals_[:3]:
        copy.start()

    for copy in piece_copies:
        copy.wait_recv()
    total = tile[...].astype(F32)
    for k in range(7):
        total = total + pieces[k].astype(F32)
    joined[...] = total.astype(BF16)
    table[:, pl.ds(pl.multiple_of(dp * 128, 128), 128)] = total.astype(BF16)
    for copy in tile_copies + wa_copies + place_copies + wb_copies:
        copy.start()
    grad_gather.begin_ring()
    sums[...] = jnp.zeros((8, SEQ), F32)

    a_region, b_region = weight_region(wa_all), weight_region(wb_all)
    wa_gather = Gather(data, a_region(dp, 0, BLOCK), a_region, s_w, r_w, 0)
    wb_gather = Gather(data, b_region(dp, 0, BLOCK), b_region, s_w, r_w, 9)
    for copy in wa_copies:
        copy.wait_recv()
    locals_[0].wait()
    wa_gather.begin_pair()
    wa_gather.begin_ring()
    for copy in tile_copies:
        copy.wait_recv()
    hidden_copy.wait_recv()
    rows = table[...].astype(F32)
    vec_all[...] = rows
    gain, shift = rows[9:10], rows[10:11]
    lanes = lax.broadcasted_iota(jnp.int32, (16, 128), 1)

    def norm(i, carry):
        at = pl.ds(pl.multiple_of(i * 16, 16), 16)
        a, b = hid[at, :].astype(F32), other[at, :].astype(F32)
        mean = (jnp.sum(a, axis=1, keepdims=True) + jnp.sum(b, axis=1, keepdims=True)) / D
        a, b = a - mean, b - mean
        square = jnp.sum(a * a, axis=1, keepdims=True) + jnp.sum(b * b, axis=1, keepdims=True)
        inverse = lax.rsqrt(square / D + NORM_EPS)
        normed[at, :] = (a * inverse * gain + shift).astype(BF16)
        stats[at, :] = jnp.where(lanes < 64, mean, inverse)
        return carry

    lax.fori_loop(0, BLOCK // 16, norm, 0)
    normed_gather.begin_pair()
    normed_gather.begin_ring()
    locals_[3].start()
    for copy in place_copies:
        copy.wait_recv()
    lane = lax.broadcasted_iota(jnp.int32, (BLOCK, HEADS), 1)
    inner = lax.rem(lane, HD)
    first_head = lane < HD
    turning = inner < ROT
    wheel = lax.rem(lax.broadcasted_iota(jnp.int32, (1, HEADS), 1), ROT // 2)
    freq = jnp.zeros((1, HEADS), F32)
    for k in range(ROT // 2):
        freq = jnp.where(wheel == k, float(np.float32(10000.0 ** (-2.0 * k / ROT))), freq)

    def tables(i, carry):
        column = place_all[i].astype(F32).T
        angle = column[:, 1:2] * freq
        wave[0, rows_at(i), :] = jnp.where(turning, jnp.cos(angle), 1.0)
        wave[1, rows_at(i), :] = jnp.where(turning, jnp.sin(angle), 0.0)
        return carry

    lax.fori_loop(0, 8, tables, 0)

    for copy in wb_copies:
        copy.wait_recv()
    locals_[1].wait()
    wa_gather.ring(0)
    wa_gather.pair()
    normed_gather.pair()
    wa_gather.ring(1)
    wb_gather.begin_pair()
    wb_gather.begin_ring()
    normed_gather.ring(0)
    grad_gather.begin_pair()
    wa_gather.far(0)
    wa_gather.far(1)
    normed_gather.far(0)
    my_rows = pl.ds(pl.multiple_of(core * HALF, HALF), HALF)
    their_rows = pl.ds(pl.multiple_of((1 - core) * HALF, HALF), HALF)
    pairs = [
        remote(wa_all.at[their_rows, :], wa_out.at[1], s_pair, r_pair, 0, partner),
        remote(wb_all.at[their_rows, :], wb_out.at[1], s_pair, r_pair, 1, partner),
    ]
    pairs[0].start()
    stores = [
        pltpu.make_async_copy(wa_all.at[my_rows, :], wa_out.at[0], store.at[0]),
        pltpu.make_async_copy(wb_all.at[my_rows, :], wb_out.at[0], store.at[1]),
        pltpu.make_async_copy(wave, wave_out, store.at[2]),
    ]
    stores[0].start()
    stores[2].start()

    qkv_bias = [
        vec_all[c : c + 1, pl.ds(pl.multiple_of(ctx * HEADS, HEADS), HEADS)] for c in range(3)
    ]
    fc1_bias = vec_all[
        pl.ds(3 + lax.div(ctx, 2), 1), pl.ds(pl.multiple_of(lax.rem(ctx, 2) * FFS, FFS), FFS)
    ]

    def project(spot):
        at = rows_at(spot)
        block = normed_all[at, :]
        x = dot_nn(block, wa_all[:, 0:FFS]) + fc1_bias
        square = x * x
        tanh = jnp.tanh(x * (GELU + (GELU * 0.044715) * square))
        half = 0.5 * (1.0 + tanh)
        bend = GELU + (3.0 * 0.044715 * GELU) * square
        slope[at, :] = half + 0.5 * x * (1.0 - tanh * tanh) * bend
        right[at, 0:FFS] = (x * half).astype(BF16)
        qkv = dot_nn(block, wa_all[:, FFS:WA])
        c, s = wave[0, at, :], wave[1, at, :]
        q = turn(qkv[:, 0:HEADS] + qkv_bias[0], c, s, 1.0).astype(BF16).astype(F32) * (HD**-0.5)
        k = turn(qkv[:, HEADS : 2 * HEADS] + qkv_bias[1], c, s, 1.0)
        v = qkv[:, 2 * HEADS : 3 * HEADS] + qkv_bias[2]
        segment = place_all[spot].astype(F32).T[:, 0:1]
        feature = jnp.where(segment == inner.astype(F32), 1.0, 0.0)
        barred = jnp.where(inner < 3, (1.0 - feature) * MASKED, 0.0)
        q_mask[0, at, :] = jnp.where(first_head, q, barred).astype(BF16)
        q_mask[1, at, :] = jnp.where(first_head, barred, q).astype(BF16)
        k_mask[0, at, :] = jnp.where(first_head, k, feature).astype(BF16)
        k_mask[1, at, :] = jnp.where(first_head, feature, k).astype(BF16)
        q_own[at, :] = q.astype(BF16)
        v_own[at, :] = v.astype(BF16)
        k_t[:, at] = k.T.astype(BF16)
        v_t[:, at] = v.T.astype(BF16)

    def project_ring(flip, start, end):
        def step(n, carry):
            project(nth_spot(plane, n, flip))
            return carry

        lax.fori_loop(start, end, step, 0)

    def keep_block(ref, out, o, number):
        at = rows_at(plane.spot(*o))
        copy = pltpu.make_async_copy(ref.at[at, :], out.at[at, :], store.at[number])
        copy.start()
        return copy

    locals_[3].wait()
    for o in ((0, 0), (1, 0), (3, 0), (2, 0)):
        normed_gather.relays[o].wait_recv()
    project_ring(0, 0, 2)
    normed_gather.ring(1)
    grad_gather.ring(0)
    project_ring(0, 2, 4)
    wb_gather.ring(0)
    wb_gather.pair()
    normed_gather.relays[0, 1].wait_recv()
    normed_gather.relays[1, 1].wait_recv()
    project_ring(1, 0, 2)
    grad_gather.pair()
    normed_gather.far(1)
    normed_gather.relays[3, 1].wait_recv()
    normed_gather.relays[2, 1].wait_recv()
    project_ring(1, 2, 4)
    normed_copies = [
        keep_block(normed_all, normed_out, (along, flip), 16 + 2 * along + flip)
        for flip in (0, 1)
        for along in range(4)
    ]
    small_stores = [
        pltpu.make_async_copy(q_own, q_out, store.at[4]),
        pltpu.make_async_copy(k_t, k_out, store.at[5]),
        pltpu.make_async_copy(v_own, v_out, store.at[6]),
    ]
    for copy in small_stores:
        copy.start()

    key_row = lax.broadcasted_iota(jnp.int32, (BLOCK, BLOCK), 0)
    query_col = lax.broadcasted_iota(jnp.int32, (BLOCK, BLOCK), 1)
    causal = key_row <= query_col
    prob_stores, right_copies, right_keeps = {}, [], []
    for i in range(8):
        own = pl.ds(i * BLOCK, BLOCK)
        slot = i % 2

        def raw(j, h):
            return dot_nt(k_mask[h, rows_at(j), :], q_mask[h, own, :])

        def score(j, carry):
            new = []
            for h in range(2):
                s = raw(j, h)
                scores[h, rows_at(j), :] = s
                new.append(jnp.maximum(carry[h], fold(s, jnp.max)))
            return tuple(new)

        low = jnp.full((8, BLOCK), MASKED, F32)
        maxima = lax.fori_loop(0, i, score, (low, low), unroll=True)
        tops = []
        for h in range(2):
            s = jnp.where(causal, raw(i, h), MASKED)
            scores[h, own, :] = s
            top = jnp.maximum(maxima[h], fold(s, jnp.max))
            tops.append(jnp.max(top, axis=0, keepdims=True))
        if i >= 2:
            prob_stores[i - 2].wait()

        def prob(j, carry):
            totals, outs = [], []
            for h in range(2):
                p = jnp.exp(scores[h, rows_at(j), :] - tops[h])
                totals.append(carry[0][h] + fold(p, jnp.sum))
                p = p.astype(BF16)
                probs[slot, h, rows_at(j), :] = p
                outs.append(carry[1][h] + dot_nn(v_t[pl.ds(h * HD, HD), rows_at(j)], p))
            return (tuple(totals), tuple(outs))

        zero_sum, zero_out = jnp.zeros((8, BLOCK), F32), jnp.zeros((HD, BLOCK), F32)
        totals, outs = lax.fori_loop(
            0, i + 1, prob, ((zero_sum, zero_sum), (zero_out, zero_out)), unroll=True
        )
        length = (i + 1) * BLOCK
        prob_stores[i] = pltpu.make_async_copy(
            probs.at[slot, :, pl.ds(0, length), :],
            probs_out.at[i, :, pl.ds(0, length), :],
            p_sem.at[slot],
        )
        prob_stores[i].start()
        scale = [1.0 / jnp.sum(totals[h], axis=0, keepdims=True) for h in range(2)]
        both = jnp.concatenate([outs[h] * scale[h] for h in range(2)], axis=0)
        sums[0:1, own] = scale[0]
        sums[1:2, own] = scale[1]
        att_t[:, own] = both
        right[own, FFS:WB] = both.T.astype(BF16)
        right_copies.append(
            remote(right.at[own, :], right_out.at[1, own, :], s_pair, r_pair, 2 + i, partner)
        )
        right_copies[i].start()
        right_keeps.append(
            pltpu.make_async_copy(right.at[own, :], right_out.at[0, own, :], store.at[7 + i])
        )
        right_keeps[i].start()
        if i == 3:
            wb_gather.ring(1)
        if i == 5:
            grad_gather.far(0)
        if i == 6:
            grad_gather.ring(1)
    wb_gather.far(0)
    wb_gather.far(1)
    pairs[1].start()
    stores[1].start()

    bias_out[...] = jnp.zeros((8, FFS), F32)

    def back(spot):
        at = rows_at(spot)
        block = grad_all[at, :]
        d_pre = dot_nn(block, wb_all[:, 0:FFS]) * slope[at, :]
        rounded = d_pre.astype(BF16)
        left[at, :] = rounded
        whole = rounded.astype(F32)
        bias_out[...] += jnp.sum(whole.reshape(BLOCK // 8, 8, FFS), axis=0)
        d_att = dot_nn(block, wb_all[:, FFS:WB])
        do_own[at, :] = d_att.astype(BF16)
        product = att_t[:, at] * d_att.astype(BF16).astype(F32).T
        sums[2:3, at] = jnp.sum(product[0:HD], axis=0, keepdims=True)
        sums[3:4, at] = jnp.sum(product[HD:], axis=0, keepdims=True)

    def back_ring(flip, start, end):
        def step(n, carry):
            back(nth_spot(plane, n, flip))
            return carry

        lax.fori_loop(start, end, step, 0)

    locals_[2].wait()
    left_copies, left_keeps = [], []

    def send_left(o):
        k = len(left_copies)
        at = rows_at(plane.spot(*o))
        left_copies.append(
            remote(left.at[at, :], left_out.at[1, at, :], s_pair, r_pair, 10 + k, partner)
        )
        left_keeps.append(
            pltpu.make_async_copy(left.at[at, :], left_out.at[0, at, :], store.at[24 + k])
        )
        left_copies[k].start()
        left_keeps[k].start()

    for along in range(4):
        grad_gather.relays[along, 0].wait_recv()
    grad_copies = [
        keep_block(grad_all, grad_out, (along, 0), 32 + 2 * along) for along in range(4)
    ]
    back_ring(0, 0, 4)
    for along in range(4):
        send_left((along, 0))
    for along in (0, 1, 3):
        grad_gather.relays[along, 1].wait_recv()
        grad_copies.append(keep_block(grad_all, grad_out, (along, 1), 33 + 2 * along))
    back_ring(1, 0, 2)
    grad_gather.far(1)
    back_ring(1, 2, 3)
    for along in (0, 1, 3):
        send_left((along, 1))
    grad_gather.relays[2, 1].wait_recv()
    grad_copies.append(keep_block(grad_all, grad_out, (2, 1), 37))
    back_ring(1, 3, 4)
    send_left((2, 1))
    last_stores = [
        pltpu.make_async_copy(do_own, do_out, store.at[40]),
        pltpu.make_async_copy(sums, sums_out, store.at[41]),
    ]
    for copy in last_stores:
        copy.start()

    for gather in (grad_gather, normed_gather):
        for copy in gather.copies:
            copy.wait_send()
        for copy in gather.relays.values():
            copy.wait_send()
    wa_gather.end()
    wb_gather.end()
    hidden_copy.wait_send()
    for copy in piece_copies + tile_copies + wa_copies + wb_copies + place_copies:
        copy.wait_send()
    for copy in pairs + right_copies + left_copies:
        copy.wait()
    for copy in stores + small_stores + right_keeps + left_keeps + last_stores:
        copy.wait()
    for copy in normed_copies + grad_copies + [prob_stores[6], prob_stores[7]]:
        copy.wait()


def forward(*args):
    hbm = pl.BlockSpec(memory_space=pl.ANY)
    vmem = pl.BlockSpec(memory_space=pltpu.VMEM)
    dma = pltpu.SemaphoreType.DMA

    def shape(*dims, kind=BF16):
        return jax.ShapeDtypeStruct(dims, kind)

    return pl.pallas_call(
        forward_kernel,
        out_shape=(
            shape(SEQ, D),
            shape(SEQ, D),
            shape(2, HALF, WA),
            shape(2, HALF, WB),
            shape(2, SEQ, WB),
            shape(2, SEQ, FFS),
            shape(SEQ, HEADS),
            shape(HEADS, SEQ),
            shape(SEQ, HEADS),
            shape(SEQ, HEADS),
            shape(8, 2, SEQ, BLOCK),
            shape(8, SEQ, kind=F32),
            shape(2, SEQ, HEADS, kind=F32),
            shape(16, HALF, kind=F32),
            shape(BLOCK, 128, kind=F32),
            shape(8, FFS, kind=F32),
        ),
        in_specs=[vmem] + [hbm] * 5 + [vmem] * 3,
        out_specs=(hbm,) * 13 + (vmem,) * 3,
        scratch_shapes=[
            pltpu.VMEM((OWN, FF // 2), F32),
            pltpu.VMEM((3, OWN, HALF), F32),
            pltpu.VMEM((OWN, FF // 2), F32),
            pltpu.VMEM((OWN, HALF), F32),
            pltpu.VMEM((8, OWN, WA), BF16),
            pltpu.VMEM((8, OWN, WB), BF16),
            pltpu.VMEM((16, 128), F32),
            pltpu.VMEM((8, BLOCK), jnp.int32),
            pltpu.VMEM((16, 128), BF16),
            pltpu.VMEM((BLOCK, HALF), BF16),
            pltpu.VMEM((BLOCK, HALF), BF16),
            pltpu.VMEM((7, 16, 128), BF16),
            pltpu.VMEM((16, 128), BF16),
            pltpu.VMEM((16, HALF), BF16),
            pltpu.VMEM((8, 8, BLOCK), jnp.int32),
            pltpu.VMEM((SEQ, D), BF16),
            pltpu.VMEM((SEQ, D), BF16),
            pltpu.VMEM((D, WA), BF16),
            pltpu.VMEM((D, WB), BF16),
            pltpu.VMEM((SEQ, FFS), F32),
            pltpu.VMEM((SEQ, WB), BF16),
            pltpu.VMEM((SEQ, FFS), BF16),
            pltpu.VMEM((2, SEQ, HEADS), BF16),
            pltpu.VMEM((2, SEQ, HEADS), BF16),
            pltpu.VMEM((HEADS, SEQ), BF16),
            pltpu.VMEM((HEADS, SEQ), BF16),
            pltpu.VMEM((SEQ, HEADS), BF16),
            pltpu.VMEM((SEQ, HEADS), BF16),
            pltpu.VMEM((SEQ, HEADS), BF16),
            pltpu.VMEM((2, SEQ, BLOCK), F32),
            pltpu.VMEM((2, 2, SEQ, BLOCK), BF16),
            pltpu.VMEM((HEADS, SEQ), F32),
            pltpu.VMEM((2, SEQ, HEADS), F32),
            pltpu.VMEM((8, SEQ), F32),
            dma((4,)),
            dma((4,)),
            dma((24,)),
            dma((24,)),
            dma((16,)),
            dma((16,)),
            dma((18,)),
            dma((18,)),
            dma((36,)),
            dma((36,)),
            dma((18,)),
            dma((18,)),
            dma((42,)),
            dma((2,)),
        ],
        compiler_params=pltpu.CompilerParams(
            collective_id=0, has_side_effects=True, vmem_limit_bytes=62 * 1024 * 1024
        ),
        name="forward",
    )(*args)


def add_rows(dst, terms, count, chunk):
    def step(i, carry):
        at = pl.ds(pl.multiple_of(i * chunk, chunk), chunk)
        total = terms[0][at, :].astype(F32)
        for term in terms[1:]:
            total = total + term[at, :].astype(F32)
        dst[at, :] = total.astype(dst.dtype)
        return carry

    lax.fori_loop(0, count // chunk, step, 0)


class Reduce:
    def __init__(self, plane, acc, landing, sends, recvs, base):
        half_up, half_down, up, down, across = landing[:5]
        self.plane, self.acc, self.across = plane, acc, across
        self.near = (half_up, half_down, up, down)
        self.rows = across.shape[0]
        self.early = landing[5] if len(landing) > 5 else None
        self.direct = DIRECT if self.early is not None else 0
        self.sizes = (self.rows - self.direct, self.rows)
        self.copies = []
        for j, flip in ((0, 1), (1, 0)):
            far, size = plane.spot(2, flip), self.sizes[j]
            low, high, most = pl.ds(0, size // 2), pl.ds(size // 2, size // 2), pl.ds(0, size)
            for number, (src, dst, along) in enumerate(
                (
                    (acc.at[far, low, :], half_up.at[j, low, :], 1),
                    (acc.at[far, high, :], half_down.at[j, low, :], 3),
                    (acc.at[plane.spot(1, flip), most, :], up.at[j, most, :], 1),
                    (acc.at[plane.spot(3, flip), most, :], down.at[j, most, :], 3),
                )
            ):
                self.copies.append(
                    remote(src, dst, sends, recvs, base + 4 * j + number, plane.device(along, 0))
                )
        across_device = plane.device(0, 1)
        self.copies.append(
            remote(acc.at[plane.spot(0, 1)], across, sends, recvs, base + 8, across_device)
        )
        if self.direct:
            self.rest = pl.ds(self.sizes[0], self.direct)
            for k, along in enumerate((2, 1, 3)):
                src = acc.at[plane.spot(along, 1), self.rest, :]
                self.copies.append(
                    remote(src, self.early.at[k], sends, recvs, base + 9 + k, across_device)
                )

    def send_early(self):
        self.copies[10].start()
        self.copies[11].start()

    def add_early(self, k, along):
        self.copies[9 + k].wait_recv()
        dst = self.acc.at[self.plane.spot(along, 0), self.rest, :]
        add_rows(dst, [dst, self.early.at[k]], self.direct, 16)

    def first(self, j):
        if self.direct and j:
            self.add_early(0, 2)
        self.copies[4 * j].start()
        self.copies[4 * j + 1].start()
        if self.direct and not j:
            self.copies[9].start()

    def second(self, j):
        if self.direct and j:
            self.add_early(1, 1)
            self.add_early(2, 3)
        half = self.sizes[j] // 2
        for number, along in ((0, 1), (1, 3)):
            self.copies[4 * j + number].wait_recv()
            dst = self.acc.at[self.plane.spot(along, 1 - j), pl.ds(number * half, half), :]
            add_rows(dst, [dst, self.near[number].at[j]], half, 16)
            self.copies[4 * j + number + 2].start()

    def third(self):
        self.copies[2].wait_recv()
        self.copies[3].wait_recv()
        dst = self.acc.at[self.plane.spot(0, 1)]
        add_rows(dst, [dst, self.near[2].at[0], self.near[3].at[0]], self.sizes[0], 16)
        self.copies[8].start()

    def arrived(self):
        for k in (6, 7, 8):
            self.copies[k].wait_recv()
        mine = self.acc.at[self.plane.spot(0, 0)]
        return [mine, self.near[2].at[1], self.near[3].at[1], self.across]

    def last(self, dst):
        add_rows(dst, self.arrived(), self.rows, 16)

    def end(self):
        for copy in self.copies:
            copy.wait_send()


def backward_kernel(
    right_in, wb_in, left_in, wa_in, normed, grads, q_in, k_in, v_in, do_in,
    probs_in, sums, wave_in, hid, grad, stats, vec_all, bias_in,
    hidden_out, grad_in, gb_all, ga_all, vec_sum,
    right, left, weight, stream, q_all, k_t, v_all, do_all, probs_odd, probs_even, wave, d_k, d_v,
    out_acc, dx_acc, gb_acc, ga_acc,
    out_a, out_b, out_c, out_d, out_e, out_f, dx_a, dx_b, dx_c, dx_d, dx_e, dx_f, gb_a, gb_b, gb_c, gb_d, gb_e,
    ga_a, ga_b, ga_c, ga_d, ga_e, gb_done, ga_done, bias, final, vec, vec_in, vec_tile, tile_in, row_own, row_in,
    load, s_stream, s_probs, s_pair, r_pair, s_red, r_red, s_small, r_small, keep,
):
    plane, data = Plane(True), Plane(False)
    ctx, dp, core = plane.ctx, plane.dp, plane.core
    partner = (dp, ctx, 1 - core)
    loads = {
        "weight": pltpu.make_async_copy(wb_in, weight.at[:, :, pl.ds(0, WB)], load.at[0]),
        "right": pltpu.make_async_copy(right_in, right, load.at[1]),
        "left": pltpu.make_async_copy(left_in, left.at[:, :, pl.ds(0, FFS)], load.at[2]),
        "q": pltpu.make_async_copy(q_in, q_all, load.at[4]),
        "k": pltpu.make_async_copy(k_in, k_t, load.at[5]),
        "v": pltpu.make_async_copy(v_in, v_all, load.at[6]),
        "do": pltpu.make_async_copy(do_in, do_all, load.at[7]),
    }
    loads["weight"].start()
    loads["right"].start()
    partners = partners_of(plane, data)
    greet(partners)

    out = Reduce(plane, out_acc, (out_a, out_b, out_c, out_d, out_e, out_f), s_red, r_red, 0)
    dx = Reduce(plane, dx_acc, (dx_a, dx_b, dx_c, dx_d, dx_e, dx_f), s_red, r_red, 12)
    gb = Reduce(data, gb_acc, (gb_a, gb_b, gb_c, gb_d, gb_e), s_red, r_red, 24)
    ga = Reduce(data, ga_acc, (ga_a, ga_b, ga_c, ga_d, ga_e), s_red, r_red, 33)

    def spot_of(where, n):
        group = lax.div(n + 2, 4)
        inside = n + 2 - 4 * group
        near = 1 - lax.rem(group + 1, 2)
        along = near * (1 + 2 * lax.rem(inside, 2)) + (1 - near) * (2 - group)
        flip = near * (1 - lax.div(inside, 2)) + (1 - near) * (1 - lax.rem(inside, 2))
        return where.spot_at(along, flip)

    def out_block(n, carry):
        spot = spot_of(plane, n)
        at = rows_at(spot)
        total = dot_nt(right[0, at, :], weight[0, :, 0:WB])
        total = total + dot_nt(right[1, at, :], weight[1, :, 0:WB])
        out_acc[spot] = total.astype(BF16)
        return carry

    def dx_block(n, carry):
        spot = spot_of(plane, n)
        at = rows_at(spot)
        total = dot_nt(left[0, at, :], weight[0])
        total = total + dot_nt(left[1, at, :], weight[1])
        dx_acc[spot] = total.astype(BF16)
        return carry

    def fetch(source, n):
        columns = rows_at(spot_of(data, n))
        slot = lax.rem(n, 2)
        return pltpu.make_async_copy(source.at[:, columns], stream.at[slot], s_stream.at[slot])

    def weight_blocks(source, factor, acc, start, end):
        def step(n, carry):
            @pl.when(n < 7)
            def _():
                fetch(source, n + 1).start()

            fetch(source, n).wait()
            total = dot_tn(stream[lax.rem(n, 2)], factor[0])
            acc[spot_of(data, n)] = total.astype(BF16)
            return carry

        lax.fori_loop(start, end, step, 0)

    loads["weight"].wait()
    loads["right"].wait()
    fetch(grads, 0).start()
    lax.fori_loop(0, 1, out_block, 0)
    meet(partners)
    out.first(0)
    for name in ("q", "k", "v", "do", "left"):
        loads[name].start()
    lax.fori_loop(1, 4, out_block, 0)
    out.send_early()
    lax.fori_loop(4, 8, out_block, 0)
    weight_load = pltpu.make_async_copy(wa_in, weight, load.at[8])
    weight_load.start()
    out.second(0)
    out.first(1)
    weight_blocks(grads, right, gb_acc, 0, 1)
    gb.first(0)
    weight_blocks(grads, right, gb_acc, 1, 4)

    lane = lax.broadcasted_iota(jnp.int32, (BLOCK, HEADS), 1)
    heads = (lane < HD, lane >= HD)
    bias[...] = jnp.zeros((8, 3 * HEADS), F32)

    def clear(i, carry):
        d_k[rows_at(i), :] = jnp.zeros((BLOCK, HEADS), F32)
        d_v[rows_at(i), :] = jnp.zeros((BLOCK, HEADS), F32)
        return carry

    lax.fori_loop(0, 8, clear, 0)

    def probs_of(i):
        length = pl.ds(0, (i + 1) * BLOCK)
        buffer = probs_odd if i % 2 else probs_even
        return [
            pltpu.make_async_copy(
                probs_in.at[i, :, length, :], buffer.at[:, length, :], s_probs.at[i % 2]
            ),
            pltpu.make_async_copy(
                wave_in.at[:, pl.ds(i * BLOCK, BLOCK), :], wave.at[i % 2], s_probs.at[2 + i % 2]
            ),
        ]

    for name in ("q", "k", "v", "do"):
        loads[name].wait()
    arriving = {7: probs_of(7)}
    for copy in arriving[7]:
        copy.start()
    swaps = []
    for i in range(7, -1, -1):
        own = pl.ds(i * BLOCK, BLOCK)
        if i:
            arriving[i - 1] = probs_of(i - 1)
            for copy in arriving[i - 1]:
                copy.start()
        for copy in arriving[i]:
            copy.wait()
        probs = probs_odd if i % 2 else probs_even
        scale = [sums[h : h + 1, own] for h in range(2)]
        delta = [sums[2 + h : 3 + h, own] for h in range(2)]
        q, do = q_all[own, :].astype(F32), do_all[own, :].astype(F32)
        q_plain = [jnp.where(heads[h], q, 0.0).astype(BF16) for h in range(2)]
        do_plain = [jnp.where(heads[h], do, 0.0).astype(BF16) for h in range(2)]

        def back(j, carry):
            at, new = rows_at(j), []
            add_k, add_v = d_k[at, :], d_v[at, :]
            for h in range(2):
                p = probs[h, at, :].astype(F32) * scale[h]
                d_p = dot_nt(v_all[at, :], do_plain[h])
                d_s = (p * (d_p - delta[h])).astype(BF16)
                add_v = add_v + dot_nn(p.astype(BF16), do_plain[h])
                add_k = add_k + dot_nn(d_s, q_plain[h])
                new.append(carry[h] + dot_nn(k_t[pl.ds(h * HD, HD), at], d_s))
            d_k[at, :] = add_k
            d_v[at, :] = add_v
            return tuple(new)

        zero_out = jnp.zeros((HD, BLOCK), F32)
        d_q = lax.fori_loop(0, i + 1, back, (zero_out, zero_out), unroll=True)
        d_q = jnp.concatenate(d_q, axis=0).T * (HD**-0.5)
        c, s = wave[i % 2, 0], wave[i % 2, 1]
        parts = (turn(d_q, c, s, -1.0), turn(d_k[own, :], c, s, -1.0), d_v[own, :])
        for k, part in enumerate(parts):
            rounded = part.astype(BF16)
            whole = rounded.astype(F32)
            left[0, own, FFS + k * HEADS : FFS + (k + 1) * HEADS] = rounded
            columns = slice(k * HEADS, (k + 1) * HEADS)
            bias[:, columns] += jnp.sum(whole.reshape(BLOCK // 8, 8, HEADS), axis=0)
        span = pl.ds(FFS, 3 * HEADS)
        swap = remote(
            left.at[0, own, span], left.at[1, own, span], s_pair, r_pair, i, partner
        )
        swap.start()
        swaps.append(swap)
        if i == 7:
            gb.second(0)
            gb.first(1)
        if i == 5:
            out.second(1)
        if i == 3:
            out.third()

    loads["left"].wait()
    weight_load.wait()
    for swap in swaps:
        swap.wait_recv()
    lax.fori_loop(0, 1, dx_block, 0)
    dx.first(0)
    lax.fori_loop(1, 4, dx_block, 0)
    dx.send_early()
    weight_blocks(grads, right, gb_acc, 4, 6)
    dx.second(0)
    dx.first(1)
    gb.second(1)
    weight_blocks(grads, right, gb_acc, 6, 8)
    fetch(normed, 0).start()
    weight_blocks(normed, left, ga_acc, 0, 1)
    ga.first(0)
    weight_blocks(normed, left, ga_acc, 1, 4)
    gb.third()
    ga.second(0)
    ga.first(1)
    lax.fori_loop(4, 8, dx_block, 0)
    dx.third()
    weight_blocks(normed, left, ga_acc, 4, 6)
    dx.second(1)
    weight_blocks(normed, left, ga_acc, 6, 7)
    ga.third()
    weight_blocks(normed, left, ga_acc, 7, 8)
    ga.second(1)
    gb.last(gb_done)

    copies = {}
    keeps = []
    for n, (name, done, landed) in enumerate(
        (("gb", gb_done, gb_all), ("ga", ga_done, ga_all))
    ):
        copies[name] = [
            remote(
                done.at[rows_at(plane.spot(*o), OWN), :],
                landed.at[ctx],
                s_small,
                r_small,
                15 + 7 * n + k,
                plane.device(*o),
            )
            for k, o in enumerate(OTHERS)
        ]
        keeps.append(
            pltpu.make_async_copy(done.at[rows_at(ctx, OWN), :], landed.at[ctx], keep.at[n])
        )
    for copy in copies["gb"]:
        copy.start()
    keeps[0].start()

    out.last(final)
    bias_rows = vec_all[7:8, :] + vec_all[8:9, :]

    def add_hidden(i, carry):
        at = pl.ds(pl.multiple_of(i * 16, 16), 16)
        hidden_out[at, :] = (hid[at, :].astype(F32) + final[at, :] + bias_rows).astype(BF16)
        return carry

    lax.fori_loop(0, BLOCK // 16, add_hidden, 0)
    dx.last(final)
    gain = vec_all[9:10, :]
    lanes = lax.broadcasted_iota(jnp.int32, (16, 128), 1)

    def lean(i, carry):
        at = pl.ds(pl.multiple_of(i * 16, 16), 16)
        d, h, stat = final[at, :], hid[at, :].astype(F32), stats[at, :]
        normal = (h - stat[:, 0:1]) * stat[:, 64:65]
        product = d * normal
        one = jnp.sum(d * gain, axis=1, keepdims=True)
        two = jnp.sum(product * gain, axis=1, keepdims=True)
        row_own[at, :] = jnp.where(lanes < 64, one, two)
        return (carry[0] + d, carry[1] + product, carry[2] + grad[at, :].astype(F32))

    zero = jnp.zeros((16, HALF), F32)
    rows = lax.fori_loop(0, BLOCK // 16, lean, (zero, zero, zero))
    row_copy = remote(row_own, row_in, s_small, r_small, 0, partner)
    row_copy.start()
    shift_grad, gain_grad, bias_grad = [jnp.sum(r, axis=0, keepdims=True) for r in rows]
    number = lax.broadcasted_iota(jnp.int32, (16, HALF), 0)
    vec[...] = jnp.where(
        number == 9,
        gain_grad,
        jnp.where(
            number == 10, shift_grad, jnp.where((number == 7) | (number == 8), bias_grad, 0.0)
        ),
    )
    columns = pl.ds(pl.multiple_of(ctx * HEADS, HEADS), HEADS)
    for k in range(3):
        part = jnp.sum(bias[:, k * HEADS : (k + 1) * HEADS], axis=0, keepdims=True)
        vec[k : k + 1, columns] = part
    columns = pl.ds(pl.multiple_of(lax.rem(ctx, 2) * FFS, FFS), FFS)
    part = jnp.sum(bias_in[...], axis=0, keepdims=True)
    vec[:, columns] = jnp.where(
        lax.broadcasted_iota(jnp.int32, (16, FFS), 0) == 3 + lax.div(ctx, 2), part, vec[:, columns]
    )
    vec_copies, tile_copies = [], []
    for k, o in enumerate(OTHERS):
        columns = pl.ds(pl.multiple_of(data.spot(*o) * 128, 128), 128)
        vec_copies.append(
            remote(vec.at[:, columns], vec_in.at[k], s_small, r_small, 1 + k, data.device(*o))
        )
        tile_copies.append(
            remote(vec_tile, tile_in.at[k], s_small, r_small, 8 + k, plane.device(*o))
        )
    for copy in vec_copies:
        copy.start()
    ga.last(ga_done)
    for copy in copies["ga"]:
        copy.start()
    keeps[1].start()
    for copy in vec_copies:
        copy.wait_recv()
    total = vec[:, pl.ds(pl.multiple_of(dp * 128, 128), 128)]
    for k in range(7):
        total = total + vec_in[k]
    vec_tile[...] = total
    for copy in tile_copies:
        copy.start()

    row_copy.wait()

    def tilt(i, carry):
        at = pl.ds(pl.multiple_of(i * 16, 16), 16)
        d, h, stat = final[at, :], hid[at, :].astype(F32), stats[at, :]
        inverse = stat[:, 64:65]
        normal = (h - stat[:, 0:1]) * inverse
        row = (row_own[at, :] + row_in[at, :]) / D
        change = inverse * (d * gain - row[:, 0:1] - normal * row[:, 64:65])
        grad_in[at, :] = (grad[at, :].astype(F32) + change).astype(BF16)
        return carry

    lax.fori_loop(0, BLOCK // 16, tilt, 0)
    for copy in tile_copies:
        copy.wait_recv()
    total = vec_tile[...]
    for k in range(7):
        total = total + tile_in[k]
    vec_sum[...] = total

    for name in copies:
        for copy in copies[name]:
            copy.wait()
    for copy in keeps:
        copy.wait()
    for copy in vec_copies + tile_copies + swaps:
        copy.wait_send()
    for red in (dx, out, gb, ga):
        red.end()


def backward(*args):
    hbm = pl.BlockSpec(memory_space=pl.ANY)
    vmem = pl.BlockSpec(memory_space=pltpu.VMEM)
    dma = pltpu.SemaphoreType.DMA

    def landing(rows, width):
        half = pltpu.VMEM((2, rows // 2, width), BF16)
        whole = pltpu.VMEM((2, rows, width), BF16)
        return [half, half, whole, whole, pltpu.VMEM((rows, width), BF16)]

    def shape(*dims, kind=BF16):
        return jax.ShapeDtypeStruct(dims, kind)

    return pl.pallas_call(
        backward_kernel,
        out_shape=(
            shape(BLOCK, HALF),
            shape(BLOCK, HALF),
            shape(8, OWN, WB),
            shape(8, OWN, WA),
            shape(16, 128, kind=F32),
        ),
        in_specs=[hbm] * 11 + [vmem, hbm] + [vmem] * 5,
        out_specs=(vmem, vmem, hbm, hbm, vmem),
        scratch_shapes=[
            pltpu.VMEM((2, SEQ, WB), BF16),
            pltpu.VMEM((2, SEQ, WA), BF16),
            pltpu.VMEM((2, HALF, WA), BF16),
            pltpu.VMEM((2, SEQ, BLOCK), BF16),
            pltpu.VMEM((SEQ, HEADS), BF16),
            pltpu.VMEM((HEADS, SEQ), BF16),
            pltpu.VMEM((SEQ, HEADS), BF16),
            pltpu.VMEM((SEQ, HEADS), BF16),
            pltpu.VMEM((2, SEQ, BLOCK), BF16),
            pltpu.VMEM((2, SEQ - BLOCK, BLOCK), BF16),
            pltpu.VMEM((2, 2, BLOCK, HEADS), F32),
            pltpu.VMEM((SEQ, HEADS), F32),
            pltpu.VMEM((SEQ, HEADS), F32),
            pltpu.VMEM((8, BLOCK, HALF), BF16),
            pltpu.VMEM((8, BLOCK, HALF), BF16),
            pltpu.VMEM((8, BLOCK, WB), BF16),
            pltpu.VMEM((8, BLOCK, WA), BF16),
            *landing(BLOCK, HALF),
            pltpu.VMEM((3, DIRECT, HALF), BF16),
            *landing(BLOCK, HALF),
            pltpu.VMEM((3, DIRECT, HALF), BF16),
            *landing(BLOCK, WB),
            *landing(BLOCK, WA),
            pltpu.VMEM((BLOCK, WB), BF16),
            pltpu.VMEM((BLOCK, WA), BF16),
            pltpu.VMEM((8, 3 * HEADS), F32),
            pltpu.VMEM((BLOCK, HALF), F32),
            pltpu.VMEM((16, HALF), F32),
            pltpu.VMEM((7, 16, 128), F32),
            pltpu.VMEM((16, 128), F32),
            pltpu.VMEM((7, 16, 128), F32),
            pltpu.VMEM((BLOCK, 128), F32),
            pltpu.VMEM((BLOCK, 128), F32),
            dma((10,)),
            dma((2,)),
            dma((4,)),
            dma((8,)),
            dma((8,)),
            dma((42,)),
            dma((42,)),
            dma((36,)),
            dma((36,)),
            dma((3,)),
        ],
        compiler_params=pltpu.CompilerParams(
            collective_id=1, has_side_effects=True, vmem_limit_bytes=62 * 1024 * 1024
        ),
        name="backward",
    )(*args)


def adam_step(weight, first, second, gradient, rate):
    first_new = BETA_ONE * first + (1.0 - BETA_ONE) * gradient
    second_new = BETA_TWO * second + (1.0 - BETA_TWO) * gradient * gradient
    fix_one = 1.0 - BETA_ONE**STEP
    fix_two = 1.0 - BETA_TWO**STEP
    update = first_new / fix_one / (jnp.sqrt(second_new / fix_two) + ADAM_EPS)
    return (first_new, second_new, weight - rate * (update + DECAY * weight))


def update_kernel(
    ga, gb, vec_sum, hidden, back,
    qkv_w, qkv_m, qkv_v, dense_w, dense_m, dense_v, fc1_w, fc1_m, fc1_v, fc2_w, fc2_m, fc2_v,
    vec_w, vec_m, vec_v,
    hidden_out, back_out,
    qkv_mo, qkv_vo, qkv_wo, dense_mo, dense_vo, dense_wo, fc1_mo, fc1_vo, fc1_wo,
    fc2_mo, fc2_vo, fc2_wo, vec_mo, vec_vo, vec_wo,
):
    hidden_out[...] = hidden[...]
    back_out[...] = back[...]

    fc1 = (fc1_w, fc1_m, fc1_v, fc1_mo, fc1_vo, fc1_wo)
    fc2 = (fc2_w, fc2_m, fc2_v, fc2_mo, fc2_vo, fc2_wo)
    dense = (dense_w, dense_m, dense_v, dense_mo, dense_vo, dense_wo)
    qkv = (qkv_w, qkv_m, qkv_v, qkv_mo, qkv_vo, qkv_wo)
    vec = (vec_w, vec_m, vec_v, vec_mo, vec_vo, vec_wo)

    def step(refs, gradient, rate, *at):
        w, m, v, mo, vo, wo = refs
        mo[at], vo[at], wo[at] = adam_step(w[at], m[at], v[at], gradient, rate)

    for c in range(8):
        wide, narrow = slice(c * FFS, (c + 1) * FFS), slice(c * HEADS, (c + 1) * HEADS)
        step(fc1, ga[c, :, 0:FFS].astype(F32), RATES[0], slice(None), wide)
        step(fc2, gb[c, :, 0:FFS].astype(F32), RATES[1], slice(None), wide)
        step(dense, gb[c, :, FFS:WB].astype(F32), RATES[2], slice(None), narrow)
        for k in range(3):
            columns = slice(FFS + k * HEADS, FFS + (k + 1) * HEADS)
            step(qkv, ga[c, :, columns].astype(F32), RATES[0], k, slice(None), narrow)

    @pl.when(pl.program_id(0) == 0)
    def _():
        mine = pltpu.roll(vec_sum[...], lax.rem(128 - 16 * lax.axis_index("ctx"), 128), 1)
        for k in range(11):
            step(vec, mine[k : k + 1, 0:16], RATES[3], k)


def update(ga, gb, vec_sum, hidden, back, *state):
    steps = 2
    rows = OWN // steps

    def part(width):
        return pl.BlockSpec((rows, width), lambda n: (n, 0))

    vec = pl.BlockSpec((11, 1, 16), lambda n: (0, 0, 0))
    token = pl.BlockSpec((BLOCK // steps, HALF), lambda n: (n, 0))
    sets = (
        [pl.BlockSpec((3, rows, HALF), lambda n: (0, n, 0))] * 3
        + [part(HALF)] * 3
        + [part(FF // 2)] * 6
        + [vec] * 3
    )
    wide = [pl.BlockSpec((8, rows, w), lambda n: (0, n, 0)) for w in (WA, WB)]
    shapes = [jax.ShapeDtypeStruct(x.shape, x.dtype) for x in (hidden, back, *state)]
    return pl.pallas_call(
        update_kernel,
        grid=(steps,),
        out_shape=shapes,
        in_specs=wide + [pl.BlockSpec((16, 128), lambda n: (0, 0)), token, token] + sets,
        out_specs=[token, token] + sets,
        compiler_params=pltpu.CompilerParams(vmem_limit_bytes=62 * 1024 * 1024),
        name="update",
    )(ga, gb, vec_sum, hidden, back, *state)


def on_device(
    hidden_in,
    grad_out,
    segment_ids,
    positions,
    qkv_weight,
    dense_weight,
    fc1_weight,
    fc2_weight,
    vectors,
    qkv_first,
    qkv_second,
    dense_first,
    dense_second,
    fc1_first,
    fc1_second,
    fc2_first,
    fc2_second,
    vector_first,
    vector_second,
):
    hid = hidden_in.reshape(BLOCK, HALF)
    grad = grad_out.reshape(BLOCK, HALF)

    def turned(array):
        return jnp.moveaxis(array, 1, 0)

    (
        normed, grads, wa2, wb2, right, left, q, k_t, v, do, probs, sums, wave, vec_all, stats, bias,
    ) = forward(
        hid, grad, fc1_weight, turned(qkv_weight), fc2_weight, dense_weight, turned(vectors),
        segment_ids, positions,
    )
    hidden_out, grad_in, gb_all, ga_all, vec_sum = backward(
        right, wb2, left, wa2, normed, grads, q, k_t, v, do, probs, sums, wave,
        hid, grad, stats, vec_all, bias,
    )
    new = update(
        ga_all, gb_all, vec_sum, hidden_out, grad_in,
        turned(qkv_weight), turned(qkv_first), turned(qkv_second),
        dense_weight, dense_first, dense_second,
        fc1_weight, fc1_first, fc1_second, fc2_weight, fc2_first, fc2_second,
        turned(vectors), turned(vector_first), turned(vector_second),
    )
    return (
        new[0].reshape(hidden_in.shape),
        new[1].reshape(grad_out.shape),
        *(turned(x) for x in new[2:5]),
        *new[5:14],
        *(turned(x) for x in new[14:]),
    )


def solution(mesh):
    rows = P("dp", "ctx", "tensor")
    tokens = P("dp", "ctx")
    cube = P(("dp", "ctx"), None, "tensor")
    plain = P(("dp", "ctx"), "tensor")
    packed = P("tensor", None, ("dp", "ctx"))
    return jax.shard_map(
        on_device,
        mesh=mesh,
        in_specs=(rows, rows, tokens, tokens, cube, plain, plain, plain, packed)
        + (cube,) * 2
        + (plain,) * 6
        + (packed,) * 2,
        out_specs=(rows, rows) + (cube,) * 3 + (plain,) * 9 + (packed,) * 3,
        check_vma=False,
    )
```
